32 devices in a mesh: px: 8 (over z, x), py: 4 (over y, core).
Axes of the slice: x: 2, y: 2, z: 4, core: 2. Of those that a mesh axis runs over, the one named last changes fastest.
Arguments:
- state_field: bfloat16 [32, 16, 128, 128], P(None, 'px', 'py'), may hold values from -6 to 6
- conv_weight: bfloat16 [32, 32, 3, 3, 3], replicated, may hold values from -0.21875 to 0.21875
- conv_bias: float32 [32], replicated, may hold values from -4 to 4
- spectral_weight: float32 [2, 16, 32, 16, 32, 16], P(None, 'py', 'px'), may hold values from -1 to 1
Outputs:
- layer_out: bfloat16 [32, 16, 128, 128], P(None, 'px', 'py')
The draws below stay inside these ranges and needn't reach their ends.
All inputs are finite; a program needn't handle non-finite values.
Results may differ from the reference program's by a relative error of at most 0.0063.
Values may be sent and summed in bfloat16 or wider, within the bound.
No kernel may reach another device: no remote copies, remote signals or barrier semaphores. Data moves between devices by JAX's collectives and lax.ppermute only.
A program may use at most 64 MiB of HBM per device.

```python
import math
import jax
import jax.numpy as jnp
from jax import lax

C = 32
KX = 16
KY = 16
KZ = 16
NZ = 128
NX = 16
NY = 128


def block_levels(rng, dims, pieces, low, largest):
    def one(dim, shards_of):
        draws = jax.random.uniform(jax.random.fold_in(jax.random.fold_in(rng, 6), dim), (shards_of,), jnp.float32, low / len(pieces), largest / len(pieces))
        return jnp.repeat(jnp.exp(draws), dims[dim] // shards_of).reshape((-1,) + (1,) * (len(dims) - dim - 1))

    factor_of = one(*pieces[0])
    for cut in pieces[1:]:
        factor_of = factor_of * one(*cut)
    return factor_of


def bell_draw(own_key, dims, width, most, split=(), held_as=jnp.bfloat16):
    values = jax.random.normal(own_key, dims, jnp.float32) * width
    if len(split) > 0:
        values = block_levels(own_key, dims, split, -0.22, 0.18) * values
    return jnp.clip(values, min=-most, max=most).astype(held_as)


def setup_inputs(seed: int = 0) -> dict:
    keys = jax.random.split(jax.random.key(seed), 5)
    return {
        "state_field": bell_draw(keys[0], (C, NX, NY, NZ), 1.0, 6.0, ((1, 8), (2, 4))),
        "conv_weight": bell_draw(keys[1], (C, C, 3, 3, 3), (27 * C) ** -0.5, 0.21875),
        "conv_bias": bell_draw(keys[2], (C,), 1.0, 4.0, (), jnp.float32),
        "spectral_weight": bell_draw(keys[3], (2, KZ, 2 * KY, C // 2, C, KX), C ** -0.5, 1.0, ((1, 4), (2, 8)), jnp.float32),
    }


def mode_numbers(count):
    indices = jnp.arange(count, dtype=jnp.int32)
    return jnp.where(indices < count // 2, indices, indices - count)


def trig_pair(numbers, points, offset, length, factor, out_type):
    positions = offset + jnp.arange(points, dtype=jnp.int32)
    phases = (positions[:, None] * numbers[None, :]) % length
    angles = phases.astype(jnp.float32) * (2.0 * math.pi / length)
    return (jnp.cos(angles) * factor).astype(out_type), (jnp.sin(angles) * factor).astype(out_type)


def last_product(source, table, precision=None):
    flat = source.reshape(-1, source.shape[-1])
    result = jnp.dot(flat, table, preferred_element_type=jnp.float32, precision=precision)
    return result.reshape(source.shape[:-1] + (table.shape[1],))


def forward_last(source, cosine, sine_table, precision=None):
    real_part = source[..., 0, :]
    imag_part = source[..., 1, :]
    real_out = last_product(real_part, cosine, precision) + last_product(imag_part, sine_table, precision)
    imag_out = last_product(imag_part, cosine, precision) - last_product(real_part, sine_table, precision)
    return jnp.stack([real_out, imag_out], axis=-2)


def inverse_last(source, cosine, sine_table, precision=None):
    real_part = source[..., 0, :]
    imag_part = source[..., 1, :]
    real_out = last_product(real_part, cosine, precision) - last_product(imag_part, sine_table, precision)
    imag_out = last_product(real_part, sine_table, precision) + last_product(imag_part, cosine, precision)
    return jnp.stack([real_out, imag_out], axis=-2)


def reference(state_field, conv_weight, conv_bias, spectral_weight):
    highest = lax.Precision.HIGHEST
    convolved = lax.conv_general_dilated(
        state_field[None].astype(jnp.float32), conv_weight.astype(jnp.float32), (1, 1, 1),
        ((1, 1), (1, 1), (1, 1)), dimension_numbers=("NCDHW", "OIDHW", "NCDHW"),
        precision=highest)[0]
    z_cos, z_sin = trig_pair(jnp.arange(KZ, dtype=jnp.int32), NZ, 0, NZ, NZ ** -0.5, jnp.bfloat16)
    z_table = jnp.stack([z_cos, -z_sin], axis=1).reshape(NZ, 2 * KZ)
    z_modes = last_product(state_field, z_table).astype(jnp.bfloat16)
    z_modes = z_modes.reshape(C, NX, NY, 2, KZ).transpose(4, 0, 1, 3, 2)
    y_cos, y_sin = trig_pair(mode_numbers(KY), NY, 0, NY, NY ** -0.5, jnp.bfloat16)
    y_modes = forward_last(z_modes, y_cos, y_sin).astype(jnp.bfloat16)
    x_cos, x_sin = trig_pair(mode_numbers(KX), NX, 0, NX, NX ** -0.5, jnp.bfloat16)
    x_modes = forward_last(y_modes.transpose(0, 1, 4, 3, 2), x_cos, x_sin)
    weights = spectral_weight.reshape(2, KZ, 2, KY, C // 2, C, KX).transpose(0, 1, 3, 2, 4, 5, 6)
    weights = weights.reshape(2, KZ, KY, C, C, KX)
    real_in = x_modes[:, :, :, 0, :]
    imag_in = x_modes[:, :, :, 1, :]
    mixed_real = (jnp.einsum("zyiok,ziyk->zyok", weights[0], real_in, precision=highest)
                  - jnp.einsum("zyiok,ziyk->zyok", weights[1], imag_in, precision=highest))
    mixed_imag = (jnp.einsum("zyiok,ziyk->zyok", weights[0], imag_in, precision=highest)
                  + jnp.einsum("zyiok,ziyk->zyok", weights[1], real_in, precision=highest))
    mixed_modes = jnp.stack([mixed_real, mixed_imag], axis=3)
    ix_cos, ix_sin = trig_pair(mode_numbers(KX), NX, 0, NX, KX ** -0.5, jnp.float32)
    x_values = inverse_last(mixed_modes, ix_cos.T, ix_sin.T, highest).astype(jnp.bfloat16)
    iy_cos, iy_sin = trig_pair(mode_numbers(KY), NY, 0, NY, KY ** -0.5, jnp.bfloat16)
    y_values = inverse_last(x_values.transpose(0, 2, 4, 3, 1), iy_cos.T, iy_sin.T).astype(jnp.bfloat16)
    iz_cos, iz_sin = trig_pair(jnp.arange(KZ, dtype=jnp.int32), NZ, 0, NZ, KZ ** -0.5, jnp.bfloat16)
    iz_table = jnp.stack([iz_cos.T, -iz_sin.T], axis=0).reshape(2 * KZ, NZ)
    spectral = last_product(y_values.transpose(1, 2, 4, 3, 0).reshape(C, NX, NY, 2 * KZ), iz_table)
    total = convolved + spectral + conv_bias[:, None, None, None]
    return jax.nn.gelu(total, approximate=False).astype(jnp.bfloat16)
```

```python
import functools
import math

import jax
import jax.numpy as jnp
import ml_dtypes
import numpy as np
from jax import lax
from jax.experimental import pallas as pl
from jax.experimental.pallas import tpu as pltpu
from jax.sharding import PartitionSpec as P

KX = 16
KY = 16
KZ = 16


def extended(cells, sides, width):
    for axis, dim in sides:
        count = lax.axis_size(axis)
        ends = count - 1
        head = lax.slice_in_dim(cells, 0, width, axis=dim)
        tail = lax.slice_in_dim(cells, cells.shape[dim] - width, cells.shape[dim], axis=dim)
        cells = jnp.concatenate(
            [
                lax.ppermute(tail, axis, [(i, (i + 1) % count) for i in range(ends)]),
                cells,
                lax.ppermute(head, axis, [((i + 1) % count, i) for i in range(ends)]),
            ],
            axis=dim,
        )
    return cells


def swapped(value, axis, distance):
    mask = 2**distance
    pairs = [(source, source ^ mask) for source in range(lax.axis_size(axis))]
    return lax.ppermute(value, axis, pairs)


def mode_numbers(count):
    indices = jnp.arange(count, dtype=jnp.int32)
    return jnp.where(indices < count // 2, indices, indices - count)


def trig_pair(numbers, points, length, factor, out_type):
    positions = jnp.arange(points, dtype=jnp.int32)
    phases = positions[:, None] * numbers[None, :] % length
    angles = phases.astype(jnp.float32) * (2.0 * math.pi / length)
    return (
        (jnp.cos(angles) * factor).astype(out_type),
        (jnp.sin(angles) * factor).astype(out_type),
    )


def last_product(source, table, precision=None):
    flat = source.reshape(-1, source.shape[-1])
    result = jnp.dot(flat, table, preferred_element_type=jnp.float32, precision=precision)
    return result.reshape(source.shape[:-1] + (table.shape[1],))


def forward_last(source, cosine, sine_table, precision=None):
    real_part = source[..., 0, :]
    imag_part = source[..., 1, :]
    real_out = last_product(real_part, cosine, precision) + last_product(
        imag_part, sine_table, precision
    )
    imag_out = last_product(imag_part, cosine, precision) - last_product(
        real_part, sine_table, precision
    )
    return jnp.stack([real_out, imag_out], axis=-2)


def inverse_last(source, cosine, sine_table, precision=None):
    real_part = source[..., 0, :]
    imag_part = source[..., 1, :]
    real_out = last_product(real_part, cosine, precision) - last_product(
        imag_part, sine_table, precision
    )
    imag_out = last_product(real_part, sine_table, precision) + last_product(
        imag_part, cosine, precision
    )
    return jnp.stack([real_out, imag_out], axis=-2)


def mix_block(spectral_weight, x_block):
    highest = lax.Precision.HIGHEST
    real_in = x_block[:, :, :, 0, :]
    imag_in = x_block[:, :, :, 1, :]
    partial_real = jnp.einsum(
        "zucok,uzck->uzok", spectral_weight[0], real_in, precision=highest
    ) - jnp.einsum("zucok,uzck->uzok", spectral_weight[1], imag_in, precision=highest)
    partial_imag = jnp.einsum(
        "zucok,uzck->uzok", spectral_weight[0], imag_in, precision=highest
    ) + jnp.einsum("zucok,uzck->uzok", spectral_weight[1], real_in, precision=highest)
    return jnp.stack([partial_real, partial_imag], axis=3)


def general_body(state_field, conv_weight, conv_bias, spectral_weight):
    channels, cells_x, cells_y, depth = state_field.shape
    count_x = lax.axis_size("px")
    count_y = lax.axis_size("py")
    width_x = cells_x * count_x
    width_y = cells_y * count_y
    index_x = lax.axis_index("px")
    kz_local = KZ // count_y
    units = 2 * KY // count_x
    highest = lax.Precision.HIGHEST
    padded = extended(state_field, (("px", 1), ("py", 2)), 1)
    convolved = lax.conv_general_dilated(
        padded[None],
        conv_weight,
        (1, 1, 1),
        ((0, 0), (0, 0), (1, 1)),
        dimension_numbers=("NCDHW", "OIDHW", "NCDHW"),
        preferred_element_type=jnp.float32,
    )[0]
    z_cos, z_sin = trig_pair(
        jnp.arange(KZ, dtype=jnp.int32), depth, depth, depth ** (-0.5), jnp.bfloat16
    )
    z_table = jnp.stack([z_cos, -z_sin], axis=1)
    z_modes = jnp.einsum(
        "cxyn,nwk->kcxwy", state_field, z_table, preferred_element_type=jnp.float32
    ).astype(jnp.bfloat16)
    y_cos, y_sin = trig_pair(mode_numbers(KY), width_y, width_y, width_y ** (-0.5), jnp.bfloat16)
    full_rows = lax.all_to_all(z_modes, "py", split_axis=0, concat_axis=4, tiled=True)
    y_modes = forward_last(full_rows, y_cos, y_sin)
    y_modes = y_modes.astype(jnp.bfloat16)
    by_unit = y_modes.reshape(kz_local, 2, channels // 2, cells_x, 2, KY).transpose(
        1, 5, 0, 2, 4, 3
    )
    by_unit = by_unit.reshape(2 * KY, kz_local, channels // 2, 2, cells_x)
    x_rows = lax.all_to_all(by_unit, "px", split_axis=0, concat_axis=4, tiled=True)
    x_cos, x_sin = trig_pair(mode_numbers(KX), width_x, width_x, width_x ** (-0.5), jnp.bfloat16)
    x_modes = forward_last(x_rows, x_cos, x_sin)
    partial_modes = mix_block(spectral_weight, x_modes)
    partial_modes = partial_modes.reshape(units, kz_local, 2, channels // 2, 2, KX)
    half_index = index_x * units // KY
    own_half = lax.dynamic_index_in_dim(partial_modes, half_index, 2, keepdims=False)
    other_half = lax.dynamic_index_in_dim(partial_modes, 1 - half_index, 2, keepdims=False)
    mixed_modes = own_half + swapped(other_half, "px", count_x.bit_length() - 2)
    ix_cos, ix_sin = trig_pair(mode_numbers(KX), width_x, width_x, KX ** (-0.5), jnp.float32)
    x_values = inverse_last(mixed_modes, ix_cos.T, ix_sin.T, highest).astype(jnp.bfloat16)
    returned = lax.all_to_all(x_values, "px", split_axis=4, concat_axis=0, tiled=True)
    returned = returned.reshape(2, KY, kz_local, channels // 2, 2, cells_x).transpose(
        2, 0, 3, 5, 4, 1
    )
    returned = returned.reshape(kz_local, channels, cells_x, 2, KY)
    iy_cos, iy_sin = trig_pair(mode_numbers(KY), width_y, width_y, KY ** (-0.5), jnp.bfloat16)
    expanded = inverse_last(returned, iy_cos.T, iy_sin.T).astype(jnp.bfloat16)
    y_values = lax.all_to_all(expanded, "py", split_axis=4, concat_axis=0, tiled=True)
    iz_cos, iz_sin = trig_pair(
        jnp.arange(KZ, dtype=jnp.int32), depth, depth, KZ ** (-0.5), jnp.bfloat16
    )
    iz_table = jnp.stack([iz_cos.T, -iz_sin.T], axis=0)
    spectral = jnp.einsum("kcxwy,wkn->cxyn", y_values, iz_table, preferred_element_type=jnp.float32)
    total = convolved + spectral + conv_bias[:, None, None, None]
    return jax.nn.gelu(total, approximate=False).astype(jnp.bfloat16)


def angle_tables(numbers, points, length, factor):
    phases = (np.arange(points)[:, None] * numbers[None, :]) % length
    angles = phases.astype(np.float32) * np.float32(2.0 * math.pi / length)
    return (
        np.cos(angles).astype(np.float32) * np.float32(factor),
        np.sin(angles).astype(np.float32) * np.float32(factor),
    )


def signed_modes(count):
    indices = np.arange(count)
    return np.where(indices < count // 2, indices, indices - count)


def narrow(table):
    return table.astype(ml_dtypes.bfloat16).astype(np.float32)


def forward_pair(cosine, sine):
    return np.stack([np.stack([cosine, -sine]), np.stack([sine, cosine])])


def inverse_pair(cosine, sine):
    return np.stack([np.stack([cosine, sine]), np.stack([-sine, cosine])])


@functools.cache
def tables(count_x, count_y, cells_x, cells_y, depth):
    width_x, width_y = count_x * cells_x, count_y * cells_y
    kzl, units = KZ // count_y, 2 * KY // count_x
    groups = KY // units
    zc, zs = angle_tables(np.arange(KZ), depth, depth, depth**-0.5)
    z_forward = np.concatenate([zc.T, -zs.T])
    yc, ys = angle_tables(signed_modes(KY), width_y, width_y, width_y**-0.5)
    pair = forward_pair(yc, ys).reshape(2, 2, count_y, cells_y, groups, units)
    y_forward = np.einsum("rsqygk,d,w->qrygwskd", pair, np.ones(8), np.ones(cells_x))
    y_forward = y_forward.reshape(count_y, 2 * cells_y, groups * 2 * cells_x * units * 8)
    xc, xs = angle_tables(signed_modes(KX), width_x, width_x, width_x**-0.5)
    pair = forward_pair(xc, xs).reshape(2, 2, count_x, cells_x, KX)
    x_forward = np.einsum("rspxk,gh,q->gskpqhxr", pair, np.eye(2), np.ones(count_y))
    x_forward = x_forward.reshape(4 * KX, count_x * count_y * 4 * cells_x)
    xc, xs = angle_tables(signed_modes(KX), width_x, width_x, KX**-0.5)
    pair = inverse_pair(xc, xs).reshape(2, 2, count_x, cells_x, KX)
    x_inverse = np.einsum("rspxk,zv->pxzsvrk", pair, np.eye(kzl))
    x_inverse = x_inverse.reshape(count_x * cells_x * kzl * 2, kzl * 2 * KX)
    zc, zs = angle_tables(np.arange(KZ), depth, depth, KZ**-0.5)
    pair = inverse_pair(zc, zs).reshape(2, 2, depth, count_y, kzl)
    z_inverse = np.einsum("rsnqz,xw,h->hqxzrwsn", pair, np.eye(cells_x), np.ones(2))
    z_inverse = z_inverse.reshape(4 * cells_x * KZ, cells_x * 2 * depth)
    yc, ys = angle_tables(signed_modes(KY), width_y, width_y, KY**-0.5)
    pair = np.stack([yc, -ys]).reshape(2, count_y, cells_y, KY)
    y_inverse = np.einsum("rqyk,i->qyrki", pair, np.ones(16))
    y_inverse = y_inverse.reshape(count_y, cells_y, 32 * KY)
    return (
        narrow(z_forward),
        narrow(y_forward),
        narrow(x_forward),
        x_inverse.astype(np.float32),
        narrow(z_inverse),
        narrow(y_inverse),
    )


def block_moves(value):
    rows = value.shape[0]
    tiles = value.reshape(rows // 8, 8, 128)
    row = lax.broadcasted_iota(jnp.int32, tiles.shape, 1) % 4
    block = lax.broadcasted_iota(jnp.int32, tiles.shape, 2) // 32
    result = tiles
    for lane_step in (1, 2, 3):
        moved = pltpu.roll(tiles, 128 - 32 * lane_step, 2)
        result = jnp.where(row - block == lane_step, pltpu.roll(moved, lane_step, 1), result)
        result = jnp.where(
            row - block == lane_step - 4, pltpu.roll(moved, 8 + lane_step - 4, 1), result
        )
    return result


def forward_kernel(index_ref, state_ref, z_ref, y_ref, out_ref, table_ref):
    span = state_ref.shape[1]
    table = y_ref[index_ref[0]]
    lane = lax.broadcasted_iota(jnp.int32, (span, table.shape[1]), 1)
    for x in range(2):
        for c in range(8):
            own = (lane % 8 == c) & (lane // 64 % 2 == x)
            for part in range(2):
                first = part * 16 * span + (c * 2 + x) * span
                block = jnp.where(own, table[part * span : (part + 1) * span], 0.0)
                table_ref[first : first + span] = block.astype(jnp.bfloat16)
    rows = state_ref.shape[0] * state_ref.shape[1]
    state = state_ref[...].reshape(rows, state_ref.shape[2])
    z_modes = lax.dot_general(
        z_ref[...].astype(jnp.bfloat16), state, (((1,), (1,)), ((), ())), preferred_element_type=jnp.float32
    ).astype(jnp.bfloat16)
    span = rows // 4
    pieces = [
        jnp.concatenate(
            [z_modes[:KZ, g * span : (g + 1) * span], z_modes[KZ:, g * span : (g + 1) * span]], axis=1
        )
        for g in range(4)
    ]
    stacked = jnp.concatenate(pieces, axis=0)
    modes = jnp.dot(stacked, table_ref[...], preferred_element_type=jnp.float32)
    for group in range(4):
        moved = block_moves(modes[:, group * 128 : (group + 1) * 128])
        for half in range(2):
            for pair in range(2):
                first = moved[half * 4 + pair]
                second = moved[half * 4 + 2 + pair]
                for side in range(2):
                    rows4 = slice(4 * side, 4 * side + 4)
                    chunk = jnp.concatenate([first[rows4], second[rows4]], axis=0)
                    out_ref[(half * 4 + group) * 4 + 2 * pair + side] = chunk.astype(jnp.bfloat16)


def forward_modes(index_y, state, z_table, y_table):
    return pl.pallas_call(
        forward_kernel,
        out_shape=jax.ShapeDtypeStruct((32, 8, 128), jnp.bfloat16),
        in_specs=[
            pl.BlockSpec(memory_space=pltpu.SMEM),
            pl.BlockSpec(memory_space=pltpu.VMEM),
            pl.BlockSpec(memory_space=pltpu.VMEM),
            pl.BlockSpec(memory_space=pltpu.VMEM),
        ],
        out_specs=pl.BlockSpec(memory_space=pltpu.VMEM),
        scratch_shapes=[pltpu.VMEM((32 * state.shape[1], y_table.shape[2]), jnp.bfloat16)],
        compiler_params=pltpu.CompilerParams(vmem_limit_bytes=40 * 2**20),
        cost_estimate=pl.CostEstimate(flops=2**27, bytes_accessed=2**21, transcendentals=0),
        name="forward_modes",
    )(index_y, state, z_table, y_table)


def prepare_kernel(weight_ref, conv_ref, weight_out, conv_out):
    for part in range(2):
        for kz in range(4):
            for c in range(16):
                weight_out[part, kz, c] = jnp.concatenate(
                    [weight_ref[part, kz, u, c] for u in range(4)], axis=1
                )
    zero = jnp.zeros((32, 32), jnp.float32)
    for dz in range(3):
        taps = {
            (dx, dy): conv_ref[dx, dy, dz].astype(jnp.float32)
            for dx in range(3)
            for dy in range(3)
        }
        for y_out in range(2):
            for x_out in range(2):
                row = ((dz * 2 + y_out) * 2 + x_out) * 32
                for y_in in range(4):
                    blocks = [taps.get((x_in - x_out, y_in - y_out), zero) for x_in in range(4)]
                    conv_out[row : row + 32, y_in * 128 : (y_in + 1) * 128] = jnp.concatenate(
                        blocks, axis=1
                    ).astype(jnp.bfloat16)


def prepare(spectral_weight, conv_weight):
    vmem = pl.BlockSpec(memory_space=pltpu.VMEM)
    return pl.pallas_call(
        prepare_kernel,
        out_shape=(
            jax.ShapeDtypeStruct((2, 4, 16, KX, 128), jnp.float32),
            jax.ShapeDtypeStruct((384, 512), jnp.bfloat16),
        ),
        in_specs=[vmem, vmem],
        out_specs=(vmem, vmem),
        compiler_params=pltpu.CompilerParams(vmem_limit_bytes=40 * 2**20),
        cost_estimate=pl.CostEstimate(flops=2**20, bytes_accessed=6 * 2**20, transcendentals=0),
        name="prepare_weights",
    )(spectral_weight, conv_weight)


def mix_kernel(modes_ref, forward_ref, weight_ref, inverse_ref, out_ref):
    received = modes_ref[...].astype(jnp.float32).reshape(256, 128).astype(jnp.bfloat16)
    x_modes = jnp.dot(
        forward_ref[...].astype(jnp.bfloat16), received, preferred_element_type=jnp.float32)
    lane = lax.broadcasted_iota(jnp.int32, (16, 128), 1)
    base = (lane // 32) * 8
    mixed = []
    for kz in range(4):
        real_sum = imag_sum = None
        for c in range(16):
            half, c8 = c // 8, c % 8
            index = base + (kz * 32 + c8)
            real_in = jnp.take_along_axis(x_modes[half * 32 : half * 32 + 16], index, axis=1)
            imag_in = jnp.take_along_axis(x_modes[half * 32 + 16 : half * 32 + 32], index, axis=1)
            real_weight = weight_ref[0, kz, c]
            imag_weight = weight_ref[1, kz, c]
            real_term = real_weight * real_in - imag_weight * imag_in
            imag_term = real_weight * imag_in + imag_weight * real_in
            real_sum = real_term if real_sum is None else real_sum + real_term
            imag_sum = imag_term if imag_sum is None else imag_sum + imag_term
        mixed += [real_sum, imag_sum]
    values = jnp.dot(
        inverse_ref[...],
        jnp.concatenate(mixed, axis=0),
        preferred_element_type=jnp.float32,
        precision=lax.Precision.HIGHEST,
    ).astype(jnp.bfloat16)
    for x in range(8):
        for y in range(4):
            out_ref[x * 4 + y] = values[16 * x : 16 * x + 16]


def mix_modes(modes, forward_table, weights, inverse_table):
    vmem = pl.BlockSpec(memory_space=pltpu.VMEM)
    return pl.pallas_call(
        mix_kernel,
        out_shape=jax.ShapeDtypeStruct((32, 16, 128), jnp.bfloat16),
        in_specs=[vmem] * 4,
        out_specs=vmem,
        compiler_params=pltpu.CompilerParams(vmem_limit_bytes=40 * 2**20),
        cost_estimate=pl.CostEstimate(flops=2**22, bytes_accessed=2**21, transcendentals=0),
        name="mix_modes",
    )(modes, forward_table, weights, inverse_table)


def arrange_kernel(left_ref, state_ref, right_ref, out_ref, first_ref, last_ref, wide):
    cells_y = state_ref.shape[2]
    planes = [left_ref[:, 0], state_ref[:, 0], state_ref[:, 1], right_ref[:, 0]]
    for x, plane in enumerate(planes):
        wide[x] = plane.astype(jnp.float32).reshape(32 * cells_y, 128)
    for y in range(cells_y):
        for x in range(4):
            rows = wide[x, pl.ds(y, 32, stride=cells_y), :].astype(jnp.bfloat16)
            out_ref[y, 32 * x : 32 * x + 32] = rows
            if y == 0:
                first_ref[32 * x : 32 * x + 32] = rows
            if y == cells_y - 1:
                last_ref[32 * x : 32 * x + 32] = rows


def arrange(left, state, right):
    vmem = pl.BlockSpec(memory_space=pltpu.VMEM)
    cells_y = state.shape[2]
    return pl.pallas_call(
        arrange_kernel,
        out_shape=(
            jax.ShapeDtypeStruct((cells_y, 128, 128), jnp.bfloat16),
            jax.ShapeDtypeStruct((128, 128), jnp.bfloat16),
            jax.ShapeDtypeStruct((128, 128), jnp.bfloat16),
        ),
        in_specs=[vmem] * 3,
        out_specs=(vmem,) * 3,
        scratch_shapes=[pltpu.VMEM((4, 32 * cells_y, 128), jnp.float32)],
        compiler_params=pltpu.CompilerParams(vmem_limit_bytes=40 * 2**20),
        cost_estimate=pl.CostEstimate(flops=2**20, bytes_accessed=2**21, transcendentals=0),
        name="arrange_cells",
    )(left, state, right)


def convolve_kernel(cells_ref, before_ref, after_ref, weight_ref, out_ref):
    cells_y = cells_ref.shape[0]
    lane = lax.broadcasted_iota(jnp.int32, (128, 256), 1) % 128
    weight = weight_ref[...]

    def row(y):
        if y < 0:
            return before_ref[...]
        return after_ref[...] if y >= cells_y else cells_ref[y]

    for quad in range(cells_y // 4):
        windows = []
        for pair in range(2):
            start = quad * 4 + pair * 2 - 1
            windows.append(jnp.concatenate([row(start + i) for i in range(4)], axis=0))
        product = jnp.dot(
            weight, jnp.concatenate(windows, axis=1), preferred_element_type=jnp.float32
        )
        below = pltpu.roll(product[:128], 1, 1)
        above = pltpu.roll(product[256:], 255, 1)
        total = product[128:256] + jnp.where(lane == 0, 0.0, below)
        total = total + jnp.where(lane == 127, 0.0, above)
        for pair in range(2):
            for y_out in range(2):
                for x_out in range(2):
                    first = (y_out * 2 + x_out) * 32
                    value = total[first : first + 32, pair * 128 : (pair + 1) * 128]
                    y = quad * 4 + pair * 2 + y_out
                    out_ref[pl.ds(x_out * cells_y + y, 32, stride=2 * cells_y), :] = value


def convolve(cells, before, after, weight):
    vmem = pl.BlockSpec(memory_space=pltpu.VMEM)
    cells_y = cells.shape[0]
    return pl.pallas_call(
        convolve_kernel,
        out_shape=jax.ShapeDtypeStruct((64 * cells_y, 128), jnp.float32),
        in_specs=[vmem] * 4,
        out_specs=vmem,
        compiler_params=pltpu.CompilerParams(vmem_limit_bytes=40 * 2**20),
        cost_estimate=pl.CostEstimate(flops=2**31, bytes_accessed=2**21, transcendentals=0),
        name="convolve_cells",
    )(cells, before, after, weight)


def gelu(value):
    return 0.5 * value * (1.0 + lax.erf(value * math.sqrt(0.5)))


def finish_kernel(index_ref, bias_ref, values_ref, z_ref, y_ref, conv_ref, out_ref):
    table = y_ref[index_ref[0]]
    lane = lax.broadcasted_iota(jnp.int32, table.shape, 1) % 16
    blocks = [jnp.where(lane == o, table, 0.0).astype(jnp.bfloat16) for o in range(16)]
    columns = []
    for group in range(4):
        columns.append(
            jnp.concatenate(
                [values_ref[(h * 4 + group) * 4 + q] for h in range(2) for q in range(4)], axis=0
            )
        )
    packed = jnp.concatenate(columns, axis=1)
    z_values = lax.dot_general(
        packed, z_ref[...].astype(jnp.bfloat16), (((0,), (0,)), ((), ())), preferred_element_type=jnp.float32
    ).astype(jnp.bfloat16)
    for half in range(2):
        sides = []
        for x in range(2):
            parts = []
            for part in range(2):
                lanes = slice((x * 2 + part) * 128, (x * 2 + part + 1) * 128)
                parts += [
                    z_values[ky * 32 + half * 16 : ky * 32 + half * 16 + 16, lanes]
                    for ky in range(KY)
                ]
            sides.append(jnp.concatenate(parts, axis=0))
        right = jnp.concatenate(sides, axis=1)
        for block in range(4):
            spectral = jnp.dot(
                jnp.concatenate(blocks[block * 4 : block * 4 + 4], axis=0),
                right,
                preferred_element_type=jnp.float32,
            )
            for o4 in range(4):
                o = half * 16 + block * 4 + o4
                for x in range(2):
                    total = (
                        spectral[o4 * 32 : o4 * 32 + 32, x * 128 : (x + 1) * 128]
                        + conv_ref[o, x]
                        + bias_ref[o]
                    )
                    out_ref[o, x] = gelu(total).astype(jnp.bfloat16)


def finish(index_y, bias, values, z_table, y_table, convolved):
    vmem = pl.BlockSpec(memory_space=pltpu.VMEM)
    return pl.pallas_call(
        finish_kernel,
        out_shape=jax.ShapeDtypeStruct(convolved.shape, jnp.bfloat16),
        in_specs=[
            pl.BlockSpec(memory_space=pltpu.SMEM),
            pl.BlockSpec(memory_space=pltpu.SMEM),
            vmem,
            vmem,
            vmem,
            vmem,
        ],
        out_specs=vmem,
        compiler_params=pltpu.CompilerParams(vmem_limit_bytes=40 * 2**20),
        cost_estimate=pl.CostEstimate(flops=2**28, bytes_accessed=2**22, transcendentals=2**18),
        name="finish_layer",
    )(index_y, bias, values, z_table, y_table, convolved)


def exchanged(value):
    return lax.all_to_all(value, ("px", "py"), split_axis=0, concat_axis=0, tiled=True)


def shifted(value, axis, step):
    count = lax.axis_size(axis)
    pairs = [(i, i + step) for i in range(count) if 0 <= i + step < count]
    return lax.ppermute(value, axis, pairs)


def body(state_field, conv_weight, conv_bias, spectral_weight):
    channels, cells_x, cells_y, depth = state_field.shape
    sizes = (lax.axis_size("px"), lax.axis_size("py"), cells_x, cells_y, depth)
    if sizes != (8, 4, 2, 32, 128):
        return general_body(state_field, conv_weight, conv_bias, spectral_weight)
    z_forward, y_forward, x_forward, x_inverse, z_inverse, y_inverse = tables(*sizes)
    index_y = lax.axis_index("py").reshape(1)
    sent = forward_modes(
        index_y, state_field.reshape(channels * cells_x, cells_y, depth), z_forward, y_forward
    )
    modes = exchanged(sent)
    left = shifted(state_field[:, cells_x - 1 :], "px", 1)
    right = shifted(state_field[:, :1], "px", -1)
    weights, taps = prepare(
        spectral_weight.swapaxes(4, 5), conv_weight.transpose(2, 3, 4, 0, 1)
    )
    cells, first, last = arrange(left, state_field, right)
    before = shifted(last, "py", 1)
    after = shifted(first, "py", -1)
    convolved = convolve(cells, before, after, taps)
    values = exchanged(mix_modes(modes, x_forward, weights, x_inverse))
    return finish(
        index_y,
        conv_bias,
        values,
        z_inverse,
        y_inverse,
        convolved.reshape(channels, cells_x, cells_y, depth),
    )


def solution(mesh):
    in_specs = (P(None, "px", "py", None), P(), P(), P(None, "py", "px", None, None, None))
    out_specs = P(None, "px", "py", None)
    return jax.shard_map(body, mesh=mesh, in_specs=in_specs, out_specs=out_specs, check_vma=False)
```

```python
import functools
import math

import jax
import jax.numpy as jnp
import ml_dtypes
import numpy as np
from jax import lax
from jax.experimental import pallas as pl
from jax.experimental.pallas import tpu as pltpu
from jax.sharding import PartitionSpec as P

KX = 16
KY = 16
KZ = 16


def extended(cells, sides, width):
    for axis, dim in sides:
        count = lax.axis_size(axis)
        ends = count - 1
        head = lax.slice_in_dim(cells, 0, width, axis=dim)
        tail = lax.slice_in_dim(cells, cells.shape[dim] - width, cells.shape[dim], axis=dim)
        cells = jnp.concatenate(
            [
                lax.ppermute(tail, axis, [(i, (i + 1) % count) for i in range(ends)]),
                cells,
                lax.ppermute(head, axis, [((i + 1) % count, i) for i in range(ends)]),
            ],
            axis=dim,
        )
    return cells


def swapped(value, axis, distance):
    mask = 2**distance
    pairs = [(source, source ^ mask) for source in range(lax.axis_size(axis))]
    return lax.ppermute(value, axis, pairs)


def mode_numbers(count):
    indices = jnp.arange(count, dtype=jnp.int32)
    return jnp.where(indices < count // 2, indices, indices - count)


def trig_pair(numbers, points, length, factor, out_type):
    positions = jnp.arange(points, dtype=jnp.int32)
    phases = positions[:, None] * numbers[None, :] % length
    angles = phases.astype(jnp.float32) * (2.0 * math.pi / length)
    return (
        (jnp.cos(angles) * factor).astype(out_type),
        (jnp.sin(angles) * factor).astype(out_type),
    )


def last_product(source, table, precision=None):
    flat = source.reshape(-1, source.shape[-1])
    result = jnp.dot(flat, table, preferred_element_type=jnp.float32, precision=precision)
    return result.reshape(source.shape[:-1] + (table.shape[1],))


def forward_last(source, cosine, sine_table, precision=None):
    real_part = source[..., 0, :]
    imag_part = source[..., 1, :]
    real_out = last_product(real_part, cosine, precision) + last_product(
        imag_part, sine_table, precision
    )
    imag_out = last_product(imag_part, cosine, precision) - last_product(
        real_part, sine_table, precision
    )
    return jnp.stack([real_out, imag_out], axis=-2)


def inverse_last(source, cosine, sine_table, precision=None):
    real_part = source[..., 0, :]
    imag_part = source[..., 1, :]
    real_out = last_product(real_part, cosine, precision) - last_product(
        imag_part, sine_table, precision
    )
    imag_out = last_product(real_part, sine_table, precision) + last_product(
        imag_part, cosine, precision
    )
    return jnp.stack([real_out, imag_out], axis=-2)


def mix_block(spectral_weight, x_block):
    highest = lax.Precision.HIGHEST
    real_in = x_block[:, :, :, 0, :]
    imag_in = x_block[:, :, :, 1, :]
    partial_real = jnp.einsum(
        "zucok,uzck->uzok", spectral_weight[0], real_in, precision=highest
    ) - jnp.einsum("zucok,uzck->uzok", spectral_weight[1], imag_in, precision=highest)
    partial_imag = jnp.einsum(
        "zucok,uzck->uzok", spectral_weight[0], imag_in, precision=highest
    ) + jnp.einsum("zucok,uzck->uzok", spectral_weight[1], real_in, precision=highest)
    return jnp.stack([partial_real, partial_imag], axis=3)


def general_body(state_field, conv_weight, conv_bias, spectral_weight):
    channels, cells_x, cells_y, depth = state_field.shape
    count_x = lax.axis_size("px")
    count_y = lax.axis_size("py")
    width_x = cells_x * count_x
    width_y = cells_y * count_y
    index_x = lax.axis_index("px")
    kz_local = KZ // count_y
    units = 2 * KY // count_x
    highest = lax.Precision.HIGHEST
    padded = extended(state_field, (("px", 1), ("py", 2)), 1)
    convolved = lax.conv_general_dilated(
        padded[None],
        conv_weight,
        (1, 1, 1),
        ((0, 0), (0, 0), (1, 1)),
        dimension_numbers=("NCDHW", "OIDHW", "NCDHW"),
        preferred_element_type=jnp.float32,
    )[0]
    z_cos, z_sin = trig_pair(
        jnp.arange(KZ, dtype=jnp.int32), depth, depth, depth ** (-0.5), jnp.bfloat16
    )
    z_table = jnp.stack([z_cos, -z_sin], axis=1)
    z_modes = jnp.einsum(
        "cxyn,nwk->kcxwy", state_field, z_table, preferred_element_type=jnp.float32
    ).astype(jnp.bfloat16)
    y_cos, y_sin = trig_pair(mode_numbers(KY), width_y, width_y, width_y ** (-0.5), jnp.bfloat16)
    full_rows = lax.all_to_all(z_modes, "py", split_axis=0, concat_axis=4, tiled=True)
    y_modes = forward_last(full_rows, y_cos, y_sin)
    y_modes = y_modes.astype(jnp.bfloat16)
    by_unit = y_modes.reshape(kz_local, 2, channels // 2, cells_x, 2, KY).transpose(
        1, 5, 0, 2, 4, 3
    )
    by_unit = by_unit.reshape(2 * KY, kz_local, channels // 2, 2, cells_x)
    x_rows = lax.all_to_all(by_unit, "px", split_axis=0, concat_axis=4, tiled=True)
    x_cos, x_sin = trig_pair(mode_numbers(KX), width_x, width_x, width_x ** (-0.5), jnp.bfloat16)
    x_modes = forward_last(x_rows, x_cos, x_sin)
    partial_modes = mix_block(spectral_weight, x_modes)
    partial_modes = partial_modes.reshape(units, kz_local, 2, channels // 2, 2, KX)
    half_index = index_x * units // KY
    own_half = lax.dynamic_index_in_dim(partial_modes, half_index, 2, keepdims=False)
    other_half = lax.dynamic_index_in_dim(partial_modes, 1 - half_index, 2, keepdims=False)
    mixed_modes = own_half + swapped(other_half, "px", count_x.bit_length() - 2)
    ix_cos, ix_sin = trig_pair(mode_numbers(KX), width_x, width_x, KX ** (-0.5), jnp.float32)
    x_values = inverse_last(mixed_modes, ix_cos.T, ix_sin.T, highest).astype(jnp.bfloat16)
    returned = lax.all_to_all(x_values, "px", split_axis=4, concat_axis=0, tiled=True)
    returned = returned.reshape(2, KY, kz_local, channels // 2, 2, cells_x).transpose(
        2, 0, 3, 5, 4, 1
    )
    returned = returned.reshape(kz_local, channels, cells_x, 2, KY)
    iy_cos, iy_sin = trig_pair(mode_numbers(KY), width_y, width_y, KY ** (-0.5), jnp.bfloat16)
    expanded = inverse_last(returned, iy_cos.T, iy_sin.T).astype(jnp.bfloat16)
    y_values = lax.all_to_all(expanded, "py", split_axis=4, concat_axis=0, tiled=True)
    iz_cos, iz_sin = trig_pair(
        jnp.arange(KZ, dtype=jnp.int32), depth, depth, KZ ** (-0.5), jnp.bfloat16
    )
    iz_table = jnp.stack([iz_cos.T, -iz_sin.T], axis=0)
    spectral = jnp.einsum("kcxwy,wkn->cxyn", y_values, iz_table, preferred_element_type=jnp.float32)
    total = convolved + spectral + conv_bias[:, None, None, None]
    return jax.nn.gelu(total, approximate=False).astype(jnp.bfloat16)


def angle_tables(numbers, points, length, factor):
    phases = (np.arange(points)[:, None] * numbers[None, :]) % length
    angles = phases.astype(np.float32) * np.float32(2.0 * math.pi / length)
    return (
        np.cos(angles).astype(np.float32) * np.float32(factor),
        np.sin(angles).astype(np.float32) * np.float32(factor),
    )


def signed_modes(count):
    indices = np.arange(count)
    return np.where(indices < count // 2, indices, indices - count)


def narrow(table):
    return table.astype(ml_dtypes.bfloat16).astype(np.float32)


def forward_pair(cosine, sine):
    return np.stack([np.stack([cosine, -sine]), np.stack([sine, cosine])])


def inverse_pair(cosine, sine):
    return np.stack([np.stack([cosine, sine]), np.stack([-sine, cosine])])


@functools.cache
def tables(count_x, count_y, cells_x, cells_y, depth):
    width_x, width_y = count_x * cells_x, count_y * cells_y
    kzl, units = KZ // count_y, 2 * KY // count_x
    groups = KY // units
    zc, zs = angle_tables(np.arange(KZ), depth, depth, depth**-0.5)
    z_forward = np.concatenate([zc.T, -zs.T])
    yc, ys = angle_tables(signed_modes(KY), width_y, width_y, width_y**-0.5)
    pair = forward_pair(yc, ys).reshape(2, 2, count_y, cells_y, groups, units)
    y_forward = np.einsum("rsqygk,d,w->qrygwskd", pair, np.ones(8), np.ones(cells_x))
    y_forward = y_forward.reshape(count_y, 2 * cells_y, groups * 2 * cells_x * units * 8)
    xc, xs = angle_tables(signed_modes(KX), width_x, width_x, width_x**-0.5)
    pair = forward_pair(xc, xs).reshape(2, 2, count_x, cells_x, KX)
    x_forward = np.einsum("rspxk,gh,q->gskpqhxr", pair, np.eye(2), np.ones(count_y))
    x_forward = x_forward.reshape(4 * KX, count_x * count_y * 4 * cells_x)
    xc, xs = angle_tables(signed_modes(KX), width_x, width_x, KX**-0.5)
    pair = inverse_pair(xc, xs).reshape(2, 2, count_x, cells_x, KX)
    x_inverse = np.einsum("rspxk,zv->pxzsvrk", pair, np.eye(kzl))
    x_inverse = x_inverse.reshape(count_x * cells_x * kzl * 2, kzl * 2 * KX)
    zc, zs = angle_tables(np.arange(KZ), depth, depth, KZ**-0.5)
    pair = inverse_pair(zc, zs).reshape(2, 2, depth, count_y, kzl)
    z_inverse = np.einsum("rsnqz,xw,h->hqxzrwsn", pair, np.eye(cells_x), np.ones(2))
    z_inverse = z_inverse.reshape(4 * cells_x * KZ, cells_x * 2 * depth)
    yc, ys = angle_tables(signed_modes(KY), width_y, width_y, KY**-0.5)
    pair = np.stack([yc, -ys]).reshape(2, count_y, cells_y, KY)
    y_inverse = np.einsum("rqyk,i->qyrki", pair, np.ones(16))
    y_inverse = y_inverse.reshape(count_y, cells_y, 32 * KY)
    return (
        narrow(z_forward),
        narrow(y_forward),
        narrow(x_forward),
        x_inverse.astype(np.float32),
        narrow(z_inverse),
        narrow(y_inverse),
    )


def block_moves(value):
    rows = value.shape[0]
    tiles = value.reshape(rows // 8, 8, 128)
    row = lax.broadcasted_iota(jnp.int32, tiles.shape, 1) % 4
    block = lax.broadcasted_iota(jnp.int32, tiles.shape, 2) // 32
    result = tiles
    for lane_step in (1, 2, 3):
        moved = pltpu.roll(tiles, 128 - 32 * lane_step, 2)
        result = jnp.where(row - block == lane_step, pltpu.roll(moved, lane_step, 1), result)
        result = jnp.where(
            row - block == lane_step - 4, pltpu.roll(moved, 8 + lane_step - 4, 1), result
        )
    return result


def forward_kernel(state_hbm, z_hbm, y_hbm, out_ref, state_ref, z_ref, y_ref, table_ref, sems):
    count = state_ref.shape[0] // 4
    span = state_ref.shape[1]
    y_copy = pltpu.make_async_copy(y_hbm.at[lax.axis_index("py")], y_ref, sems.at[0])
    z_copy = pltpu.make_async_copy(z_hbm, z_ref, sems.at[1])
    copies = [
        pltpu.make_async_copy(
            state_hbm.at[pl.ds(g * count, count)],
            state_ref.at[pl.ds(g * count, count)],
            sems.at[2 + g],
        )
        for g in range(4)
    ]
    for copy in [y_copy, z_copy] + copies:
        copy.start()
    y_copy.wait()
    table = y_ref[...]
    lane = lax.broadcasted_iota(jnp.int32, (span, table.shape[1]), 1)
    for x in range(2):
        for c in range(8):
            own = (lane % 8 == c) & (lane // 64 % 2 == x)
            for part in range(2):
                first = part * 16 * span + (c * 2 + x) * span
                block = jnp.where(own, table[part * span : (part + 1) * span], 0.0)
                table_ref[first : first + span] = block.astype(jnp.bfloat16)
    z_copy.wait()
    z_table = z_ref[...].astype(jnp.bfloat16)
    pieces = []
    for g in range(4):
        copies[g].wait()
        cells = state_ref[g * count : (g + 1) * count].reshape(count * span, state_ref.shape[2])
        z_modes = lax.dot_general(
            z_table, cells, (((1,), (1,)), ((), ())), preferred_element_type=jnp.float32
        ).astype(jnp.bfloat16)
        pieces.append(jnp.concatenate([z_modes[:KZ], z_modes[KZ:]], axis=1))
    stacked = jnp.concatenate(pieces, axis=0)
    modes = jnp.dot(stacked, table_ref[...], preferred_element_type=jnp.float32)
    for group in range(4):
        moved = block_moves(modes[:, group * 128 : (group + 1) * 128])
        for half in range(2):
            for pair in range(2):
                first = moved[half * 4 + pair]
                second = moved[half * 4 + 2 + pair]
                for side in range(2):
                    rows4 = slice(4 * side, 4 * side + 4)
                    chunk = jnp.concatenate([first[rows4], second[rows4]], axis=0)
                    out_ref[(half * 4 + group) * 4 + 2 * pair + side] = chunk.astype(jnp.bfloat16)


def forward_modes(state, z_table, y_table):
    return pl.pallas_call(
        forward_kernel,
        out_shape=jax.ShapeDtypeStruct((32, 8, 128), jnp.bfloat16),
        in_specs=[pl.BlockSpec(memory_space=pltpu.HBM)] * 3,
        out_specs=pl.BlockSpec(memory_space=pltpu.VMEM),
        scratch_shapes=[
            pltpu.VMEM(state.shape, jnp.bfloat16),
            pltpu.VMEM(z_table.shape, jnp.float32),
            pltpu.VMEM(y_table.shape[1:], jnp.float32),
            pltpu.VMEM((32 * state.shape[1], y_table.shape[2]), jnp.bfloat16),
            pltpu.SemaphoreType.DMA((6,)),
        ],
        compiler_params=pltpu.CompilerParams(vmem_limit_bytes=40 * 2**20),
        cost_estimate=pl.CostEstimate(flops=2**27, bytes_accessed=2**21, transcendentals=0),
        name="forward_modes",
    )(*(pltpu.with_memory_space_constraint(v, pltpu.HBM) for v in (state, z_table, y_table)))


def prepare_kernel(
    after_ref, weight_hbm, conv_ref, y_ref, weight_out, conv_out, y_out, weight_ref, sems
):
    copies = [
        pltpu.make_async_copy(
            weight_hbm.at[part, kz], weight_ref.at[part, kz], sems.at[part * 4 + kz]
        )
        for part in range(2)
        for kz in range(4)
    ]
    for copy in copies:
        copy.start()
    odd_x = lax.rem(lax.axis_index("px"), 2) == 1
    zero = jnp.zeros((32, 32), jnp.float32)
    for dz in range(3):
        taps = {
            (dx, dy): conv_ref[dx, dy, dz].astype(jnp.float32)
            for dx in range(3)
            for dy in range(3)
        }
        for y_at in range(2):
            for x_at in range(2):
                row = ((dz * 2 + y_at) * 2 + x_at) * 32
                for y_in in range(4):
                    low, *inner, high = [
                        taps.get((x_in - x_at, y_in - y_at), zero) for x_in in range(4)
                    ]
                    blocks = [jnp.where(odd_x, low, high)] + inner + [jnp.where(odd_x, high, low)]
                    conv_out[row : row + 32, y_in * 128 : (y_in + 1) * 128] = jnp.concatenate(
                        blocks, axis=1
                    ).astype(jnp.bfloat16)
    table = y_ref[lax.axis_index("py")]
    lane = lax.broadcasted_iota(jnp.int32, table.shape, 1) % 16
    span = table.shape[0]
    for o in range(16):
        y_out[o * span : (o + 1) * span] = jnp.where(lane == o, table, 0.0).astype(jnp.bfloat16)
    for part in range(2):
        for kz in range(4):
            copies[part * 4 + kz].wait()
            for c in range(16):
                weight_out[part, kz, c] = jnp.concatenate(
                    [weight_ref[part, kz, u, c] for u in range(4)], axis=1
                )


def prepare(after, spectral_weight, conv_weight, y_table):
    vmem = pl.BlockSpec(memory_space=pltpu.VMEM)
    return pl.pallas_call(
        prepare_kernel,
        out_shape=(
            jax.ShapeDtypeStruct((2, 4, 16, KX, 128), jnp.float32),
            jax.ShapeDtypeStruct((384, 512), jnp.bfloat16),
            jax.ShapeDtypeStruct((16 * y_table.shape[1], y_table.shape[2]), jnp.bfloat16),
        ),
        in_specs=[
            pl.BlockSpec(memory_space=pl.ANY),
            pl.BlockSpec(memory_space=pltpu.HBM),
            vmem,
            vmem,
        ],
        out_specs=(vmem,) * 3,
        scratch_shapes=[
            pltpu.VMEM(spectral_weight.shape, jnp.float32),
            pltpu.SemaphoreType.DMA((8,)),
        ],
        compiler_params=pltpu.CompilerParams(vmem_limit_bytes=40 * 2**20),
        cost_estimate=pl.CostEstimate(flops=2**20, bytes_accessed=6 * 2**20, transcendentals=0),
        name="prepare_weights",
    )(
        after,
        pltpu.with_memory_space_constraint(spectral_weight, pltpu.HBM),
        conv_weight,
        y_table,
    )


def mix_kernel(modes_ref, forward_ref, weight_ref, inverse_ref, out_ref):
    received = modes_ref[...].astype(jnp.float32).reshape(256, 128).astype(jnp.bfloat16)
    x_modes = jnp.dot(
        forward_ref[...].astype(jnp.bfloat16), received, preferred_element_type=jnp.float32)
    lane = lax.broadcasted_iota(jnp.int32, (16, 128), 1)
    base = (lane // 32) * 8
    mixed = []
    for kz in range(4):
        real_sum = imag_sum = None
        for c in range(16):
            half, c8 = c // 8, c % 8
            index = base + (kz * 32 + c8)
            real_in = jnp.take_along_axis(x_modes[half * 32 : half * 32 + 16], index, axis=1)
            imag_in = jnp.take_along_axis(x_modes[half * 32 + 16 : half * 32 + 32], index, axis=1)
            real_weight = weight_ref[0, kz, c]
            imag_weight = weight_ref[1, kz, c]
            real_term = real_weight * real_in - imag_weight * imag_in
            imag_term = real_weight * imag_in + imag_weight * real_in
            real_sum = real_term if real_sum is None else real_sum + real_term
            imag_sum = imag_term if imag_sum is None else imag_sum + imag_term
        mixed += [real_sum, imag_sum]
    values = jnp.dot(
        inverse_ref[...],
        jnp.concatenate(mixed, axis=0),
        preferred_element_type=jnp.float32,
        precision=lax.Precision.HIGHEST,
    ).astype(jnp.bfloat16)
    for x in range(8):
        for y in range(4):
            out_ref[x * 4 + y] = values[16 * x : 16 * x + 16]


def mix_modes(modes, forward_table, weights, inverse_table):
    vmem = pl.BlockSpec(memory_space=pltpu.VMEM)
    return pl.pallas_call(
        mix_kernel,
        out_shape=jax.ShapeDtypeStruct((32, 16, 128), jnp.bfloat16),
        in_specs=[vmem] * 4,
        out_specs=vmem,
        compiler_params=pltpu.CompilerParams(vmem_limit_bytes=40 * 2**20),
        cost_estimate=pl.CostEstimate(flops=2**22, bytes_accessed=2**21, transcendentals=0),
        name="mix_modes",
    )(modes, forward_table, weights, inverse_table)


def arrange_kernel(after_ref, state_ref, own_ref, wide):
    cells_y = state_ref.shape[2]
    for x in range(2):
        wide[x] = state_ref[:, x].astype(jnp.float32).reshape(32 * cells_y, 128)
    for y in range(cells_y):
        for x in range(2):
            own_ref[x, y] = wide[x, pl.ds(y, 32, stride=cells_y), :].astype(jnp.bfloat16)


def arrange(after, state):
    vmem = pl.BlockSpec(memory_space=pltpu.VMEM)
    cells_y = state.shape[2]
    return pl.pallas_call(
        arrange_kernel,
        out_shape=jax.ShapeDtypeStruct((2, cells_y, 32, 128), jnp.bfloat16),
        in_specs=[pl.BlockSpec(memory_space=pl.ANY), vmem],
        out_specs=vmem,
        scratch_shapes=[pltpu.VMEM((2, 32 * cells_y, 128), jnp.float32)],
        compiler_params=pltpu.CompilerParams(vmem_limit_bytes=40 * 2**20),
        cost_estimate=pl.CostEstimate(flops=2**20, bytes_accessed=2**21, transcendentals=0),
        name="arrange_cells",
    )(after, state)


def convolve_quad(quad, row, weight, place, out_ref):
    lane = lax.broadcasted_iota(jnp.int32, (128, 256), 1) % 128
    windows = []
    for pair in range(2):
        start = quad * 4 + pair * 2 - 1
        windows.append(jnp.concatenate([row(start + i) for i in range(4)], axis=0))
    product = jnp.dot(weight, jnp.concatenate(windows, axis=1), preferred_element_type=jnp.float32)
    below = pltpu.roll(product[:128], 1, 1)
    above = pltpu.roll(product[256:], 255, 1)
    total = product[128:256] + jnp.where(lane == 0, 0.0, below)
    total = total + jnp.where(lane == 127, 0.0, above)
    for pair in range(2):
        for y_out in range(2):
            for x_out in range(2):
                first = (y_out * 2 + x_out) * 32
                value = total[first : first + 32, pair * 128 : (pair + 1) * 128]
                y = quad * 4 + pair * 2 + y_out
                at, span = place(y)
                out_ref[pl.ds(x_out * span + at, 32, stride=2 * span), :] = value


def interior_kernel(own_ref, first_ref, second_ref, weight_ref, out_ref):
    cells_y = own_ref.shape[1]

    def row(y):
        return jnp.concatenate([first_ref[y], own_ref[0, y], own_ref[1, y], second_ref[y]], axis=0)

    weight = weight_ref[...]
    for quad in range(1, cells_y // 4 - 1):
        convolve_quad(quad, row, weight, lambda y: (y, cells_y), out_ref)


def edge_kernel(
    own_ref, first_ref, second_ref, first_row, second_row, weight_ref, out_ref
):
    cells_y = own_ref.shape[1]
    odd_y = lax.rem(lax.axis_index("py"), 2) == 1

    def row(y):
        if y < 0:
            return jnp.where(odd_y, first_row[...], second_row[...])
        if y >= cells_y:
            return jnp.where(odd_y, second_row[...], first_row[...])
        return jnp.concatenate([first_ref[y], own_ref[0, y], own_ref[1, y], second_ref[y]], axis=0)

    weight = weight_ref[...]
    for quad in (0, cells_y // 4 - 1):
        convolve_quad(quad, row, weight, lambda y: (y % 8, 8), out_ref)


def convolve(kernel, name, operands, rows):
    vmem = pl.BlockSpec(memory_space=pltpu.VMEM)
    return pl.pallas_call(
        kernel,
        out_shape=jax.ShapeDtypeStruct((rows, 128), jnp.float32),
        in_specs=[vmem] * len(operands),
        out_specs=vmem,
        compiler_params=pltpu.CompilerParams(vmem_limit_bytes=40 * 2**20),
        cost_estimate=pl.CostEstimate(flops=2**30, bytes_accessed=2**21, transcendentals=0),
        name=name,
    )(*operands)


def gelu(value):
    return 0.5 * value * (1.0 + lax.erf(value * math.sqrt(0.5)))


def finish_kernel(
    bias_ref, values_ref, z_ref, y_ref, conv_ref, edge_ref, out_hbm, out_ref, sems
):
    upper = lax.broadcasted_iota(jnp.int32, (8, 128), 0) < 4
    columns = []
    for group in range(4):
        columns.append(
            jnp.concatenate(
                [values_ref[(h * 4 + group) * 4 + q] for h in range(2) for q in range(4)], axis=0
            )
        )
    packed = jnp.concatenate(columns, axis=1)
    z_values = lax.dot_general(
        packed,
        z_ref[...].astype(jnp.bfloat16),
        (((0,), (0,)), ((), ())),
        preferred_element_type=jnp.float32,
    ).astype(jnp.bfloat16)
    copies = []
    for half in range(2):
        sides = []
        for x in range(2):
            parts = []
            for part in range(2):
                lanes = slice((x * 2 + part) * 128, (x * 2 + part + 1) * 128)
                parts += [
                    z_values[ky * 32 + half * 16 : ky * 32 + half * 16 + 16, lanes]
                    for ky in range(KY)
                ]
            sides.append(jnp.concatenate(parts, axis=0))
        right = jnp.concatenate(sides, axis=1)
        for block in range(4):
            spectral = jnp.dot(
                y_ref[block * 128 : (block + 1) * 128], right, preferred_element_type=jnp.float32
            )
            for o4 in range(4):
                o = half * 16 + block * 4 + o4
                for x in range(2):
                    inner, edge = conv_ref[o, x], edge_ref[o, x]
                    convolved = jnp.concatenate(
                        [
                            jnp.where(upper, edge, inner[:8]),
                            inner[8:-8],
                            jnp.where(upper, inner[-8:], edge),
                        ],
                        axis=0,
                    )
                    total = spectral[o4 * 32 : o4 * 32 + 32, x * 128 : (x + 1) * 128]
                    total = total + convolved + bias_ref[o]
                    out_ref[o, x] = gelu(total).astype(jnp.bfloat16)
            number = half * 4 + block
            copy = pltpu.make_async_copy(
                out_ref.at[pl.ds(number * 4, 4)], out_hbm.at[pl.ds(number * 4, 4)], sems.at[number]
            )
            copy.start()
            copies.append(copy)
    for copy in copies:
        copy.wait()


def finish(bias, values, z_table, y_table, convolved, edges):
    vmem = pl.BlockSpec(memory_space=pltpu.VMEM)
    return pl.pallas_call(
        finish_kernel,
        out_shape=jax.ShapeDtypeStruct(convolved.shape, jnp.bfloat16),
        in_specs=[pl.BlockSpec(memory_space=pltpu.SMEM)] + [vmem] * 5,
        out_specs=pl.BlockSpec(memory_space=pltpu.HBM),
        scratch_shapes=[
            pltpu.VMEM(convolved.shape, jnp.bfloat16),
            pltpu.SemaphoreType.DMA((8,)),
        ],
        compiler_params=pltpu.CompilerParams(vmem_limit_bytes=40 * 2**20),
        cost_estimate=pl.CostEstimate(flops=2**28, bytes_accessed=2**22, transcendentals=2**18),
        name="finish_layer",
    )(bias, values, z_table, y_table, convolved, edges)


def exchanged(value):
    return lax.all_to_all(value, ("px", "py"), split_axis=0, concat_axis=0, tiled=True)


def swaps(first, second, axis):
    count = lax.axis_size(axis)
    inside = [(i, i ^ 1) for i in range(count)]
    across = [(i, i + 1 if i % 2 else i - 1) for i in range(1, count - 1)]
    return lax.ppermute(first, axis, inside), lax.ppermute(second, axis, across)


def body(state_field, conv_weight, conv_bias, spectral_weight):
    channels, cells_x, cells_y, depth = state_field.shape
    sizes = (lax.axis_size("px"), lax.axis_size("py"), cells_x, cells_y, depth)
    if sizes != (8, 4, 2, 32, 128):
        return general_body(state_field, conv_weight, conv_bias, spectral_weight)
    z_forward, y_forward, x_forward, x_inverse, z_inverse, y_inverse = tables(*sizes)
    sent = forward_modes(
        state_field.reshape(channels * cells_x, cells_y, depth), z_forward, y_forward
    )
    modes = exchanged(sent)
    own = arrange(sent, state_field)
    odd_x = lax.axis_index("px") % 2
    odd_y = lax.axis_index("py") % 2
    first_plane, second_plane = swaps(
        lax.dynamic_index_in_dim(own, 1 - odd_x, 0, keepdims=False),
        lax.dynamic_index_in_dim(own, odd_x, 0, keepdims=False),
        "px",
    )
    weights, taps, y_expanded = prepare(
        sent, spectral_weight.swapaxes(4, 5), conv_weight.transpose(2, 3, 4, 0, 1), y_inverse
    )
    values = exchanged(mix_modes(modes, x_forward, weights, x_inverse))

    def edge(y):
        pieces = [first_plane, own[0], own[1], second_plane]
        return jnp.concatenate([lax.dynamic_index_in_dim(p, y, 0, keepdims=False) for p in pieces])

    first_row, second_row = swaps(
        edge((1 - odd_y) * (cells_y - 1)), edge(odd_y * (cells_y - 1)), "py"
    )
    planes = (own, first_plane, second_plane)
    rows = channels * cells_x * cells_y
    interior = convolve(interior_kernel, "convolve_interior", planes + (taps,), rows)
    edges = convolve(
        edge_kernel, "convolve_edges", planes + (first_row, second_row, taps), rows // cells_y * 8
    )
    return finish(
        conv_bias,
        values,
        z_inverse,
        y_expanded,
        interior.reshape(channels, cells_x, cells_y, depth),
        edges.reshape(channels, cells_x, 8, depth),
    )


def solution(mesh):
    in_specs = (P(None, "px", "py", None), P(), P(), P(None, "py", "px", None, None, None))
    out_specs = P(None, "px", "py", None)
    return jax.shard_map(body, mesh=mesh, in_specs=in_specs, out_specs=out_specs, check_vma=False)
```

```python
import functools
import math

import jax
import jax.numpy as jnp
import ml_dtypes
import numpy as np
from jax import lax
from jax.experimental import pallas as pl
from jax.experimental.pallas import tpu as pltpu
from jax.sharding import PartitionSpec as P

KX = 16
KY = 16
KZ = 16


def extended(cells, sides, width):
    for axis, dim in sides:
        count = lax.axis_size(axis)
        ends = count - 1
        head = lax.slice_in_dim(cells, 0, width, axis=dim)
        tail = lax.slice_in_dim(cells, cells.shape[dim] - width, cells.shape[dim], axis=dim)
        cells = jnp.concatenate(
            [
                lax.ppermute(tail, axis, [(i, (i + 1) % count) for i in range(ends)]),
                cells,
                lax.ppermute(head, axis, [((i + 1) % count, i) for i in range(ends)]),
            ],
            axis=dim,
        )
    return cells


def swapped(value, axis, distance):
    mask = 2**distance
    pairs = [(source, source ^ mask) for source in range(lax.axis_size(axis))]
    return lax.ppermute(value, axis, pairs)


def mode_numbers(count):
    indices = jnp.arange(count, dtype=jnp.int32)
    return jnp.where(indices < count // 2, indices, indices - count)


def trig_pair(numbers, points, length, factor, out_type):
    positions = jnp.arange(points, dtype=jnp.int32)
    phases = positions[:, None] * numbers[None, :] % length
    angles = phases.astype(jnp.float32) * (2.0 * math.pi / length)
    return (
        (jnp.cos(angles) * factor).astype(out_type),
        (jnp.sin(angles) * factor).astype(out_type),
    )


def last_product(source, table, precision=None):
    flat = source.reshape(-1, source.shape[-1])
    result = jnp.dot(flat, table, preferred_element_type=jnp.float32, precision=precision)
    return result.reshape(source.shape[:-1] + (table.shape[1],))


def forward_last(source, cosine, sine_table, precision=None):
    real_part = source[..., 0, :]
    imag_part = source[..., 1, :]
    real_out = last_product(real_part, cosine, precision) + last_product(
        imag_part, sine_table, precision
    )
    imag_out = last_product(imag_part, cosine, precision) - last_product(
        real_part, sine_table, precision
    )
    return jnp.stack([real_out, imag_out], axis=-2)


def inverse_last(source, cosine, sine_table, precision=None):
    real_part = source[..., 0, :]
    imag_part = source[..., 1, :]
    real_out = last_product(real_part, cosine, precision) - last_product(
        imag_part, sine_table, precision
    )
    imag_out = last_product(real_part, sine_table, precision) + last_product(
        imag_part, cosine, precision
    )
    return jnp.stack([real_out, imag_out], axis=-2)


def mix_block(spectral_weight, x_block):
    highest = lax.Precision.HIGHEST
    real_in = x_block[:, :, :, 0, :]
    imag_in = x_block[:, :, :, 1, :]
    partial_real = jnp.einsum(
        "zucok,uzck->uzok", spectral_weight[0], real_in, precision=highest
    ) - jnp.einsum("zucok,uzck->uzok", spectral_weight[1], imag_in, precision=highest)
    partial_imag = jnp.einsum(
        "zucok,uzck->uzok", spectral_weight[0], imag_in, precision=highest
    ) + jnp.einsum("zucok,uzck->uzok", spectral_weight[1], real_in, precision=highest)
    return jnp.stack([partial_real, partial_imag], axis=3)


def general_body(state_field, conv_weight, conv_bias, spectral_weight):
    channels, cells_x, cells_y, depth = state_field.shape
    count_x = lax.axis_size("px")
    count_y = lax.axis_size("py")
    width_x = cells_x * count_x
    width_y = cells_y * count_y
    index_x = lax.axis_index("px")
    kz_local = KZ // count_y
    units = 2 * KY // count_x
    highest = lax.Precision.HIGHEST
    padded = extended(state_field, (("px", 1), ("py", 2)), 1)
    convolved = lax.conv_general_dilated(
        padded[None],
        conv_weight,
        (1, 1, 1),
        ((0, 0), (0, 0), (1, 1)),
        dimension_numbers=("NCDHW", "OIDHW", "NCDHW"),
        preferred_element_type=jnp.float32,
    )[0]
    z_cos, z_sin = trig_pair(
        jnp.arange(KZ, dtype=jnp.int32), depth, depth, depth ** (-0.5), jnp.bfloat16
    )
    z_table = jnp.stack([z_cos, -z_sin], axis=1)
    z_modes = jnp.einsum(
        "cxyn,nwk->kcxwy", state_field, z_table, preferred_element_type=jnp.float32
    ).astype(jnp.bfloat16)
    y_cos, y_sin = trig_pair(mode_numbers(KY), width_y, width_y, width_y ** (-0.5), jnp.bfloat16)
    full_rows = lax.all_to_all(z_modes, "py", split_axis=0, concat_axis=4, tiled=True)
    y_modes = forward_last(full_rows, y_cos, y_sin)
    y_modes = y_modes.astype(jnp.bfloat16)
    by_unit = y_modes.reshape(kz_local, 2, channels // 2, cells_x, 2, KY).transpose(
        1, 5, 0, 2, 4, 3
    )
    by_unit = by_unit.reshape(2 * KY, kz_local, channels // 2, 2, cells_x)
    x_rows = lax.all_to_all(by_unit, "px", split_axis=0, concat_axis=4, tiled=True)
    x_cos, x_sin = trig_pair(mode_numbers(KX), width_x, width_x, width_x ** (-0.5), jnp.bfloat16)
    x_modes = forward_last(x_rows, x_cos, x_sin)
    partial_modes = mix_block(spectral_weight, x_modes)
    partial_modes = partial_modes.reshape(units, kz_local, 2, channels // 2, 2, KX)
    half_index = index_x * units // KY
    own_half = lax.dynamic_index_in_dim(partial_modes, half_index, 2, keepdims=False)
    other_half = lax.dynamic_index_in_dim(partial_modes, 1 - half_index, 2, keepdims=False)
    mixed_modes = own_half + swapped(other_half, "px", count_x.bit_length() - 2)
    ix_cos, ix_sin = trig_pair(mode_numbers(KX), width_x, width_x, KX ** (-0.5), jnp.float32)
    x_values = inverse_last(mixed_modes, ix_cos.T, ix_sin.T, highest).astype(jnp.bfloat16)
    returned = lax.all_to_all(x_values, "px", split_axis=4, concat_axis=0, tiled=True)
    returned = returned.reshape(2, KY, kz_local, channels // 2, 2, cells_x).transpose(
        2, 0, 3, 5, 4, 1
    )
    returned = returned.reshape(kz_local, channels, cells_x, 2, KY)
    iy_cos, iy_sin = trig_pair(mode_numbers(KY), width_y, width_y, KY ** (-0.5), jnp.bfloat16)
    expanded = inverse_last(returned, iy_cos.T, iy_sin.T).astype(jnp.bfloat16)
    y_values = lax.all_to_all(expanded, "py", split_axis=4, concat_axis=0, tiled=True)
    iz_cos, iz_sin = trig_pair(
        jnp.arange(KZ, dtype=jnp.int32), depth, depth, KZ ** (-0.5), jnp.bfloat16
    )
    iz_table = jnp.stack([iz_cos.T, -iz_sin.T], axis=0)
    spectral = jnp.einsum("kcxwy,wkn->cxyn", y_values, iz_table, preferred_element_type=jnp.float32)
    total = convolved + spectral + conv_bias[:, None, None, None]
    return jax.nn.gelu(total, approximate=False).astype(jnp.bfloat16)


def angle_tables(numbers, points, length, factor):
    phases = (np.arange(points)[:, None] * numbers[None, :]) % length
    angles = phases.astype(np.float32) * np.float32(2.0 * math.pi / length)
    return (
        np.cos(angles).astype(np.float32) * np.float32(factor),
        np.sin(angles).astype(np.float32) * np.float32(factor),
    )


def signed_modes(count):
    indices = np.arange(count)
    return np.where(indices < count // 2, indices, indices - count)


def narrow(table):
    return table.astype(ml_dtypes.bfloat16).astype(np.float32)


def forward_pair(cosine, sine):
    return np.stack([np.stack([cosine, -sine]), np.stack([sine, cosine])])


def inverse_pair(cosine, sine):
    return np.stack([np.stack([cosine, sine]), np.stack([-sine, cosine])])


@functools.cache
def tables(count_x, count_y, cells_x, cells_y, depth):
    width_x, width_y = count_x * cells_x, count_y * cells_y
    kzl, units = KZ // count_y, 2 * KY // count_x
    groups = KY // units
    zc, zs = angle_tables(np.arange(KZ), depth, depth, depth**-0.5)
    z_forward = np.concatenate([zc.T, -zs.T])
    yc, ys = angle_tables(signed_modes(KY), width_y, width_y, width_y**-0.5)
    pair = forward_pair(yc, ys).reshape(2, 2, count_y, cells_y, groups, units)
    y_forward = np.einsum("rsqygk,d,w->qrygwskd", pair, np.ones(8), np.ones(cells_x))
    y_forward = y_forward.reshape(count_y, 2 * cells_y, groups * 2 * cells_x * units * 8)
    xc, xs = angle_tables(signed_modes(KX), width_x, width_x, width_x**-0.5)
    pair = forward_pair(xc, xs).reshape(2, 2, count_x, cells_x, KX)
    x_forward = np.einsum("rspxk,gh,q->gskpqhxr", pair, np.eye(2), np.ones(count_y))
    x_forward = x_forward.reshape(4 * KX, count_x * count_y * 4 * cells_x)
    xc, xs = angle_tables(signed_modes(KX), width_x, width_x, KX**-0.5)
    pair = inverse_pair(xc, xs).reshape(2, 2, count_x, cells_x, KX)
    x_inverse = np.einsum("rspxk,zv->pxzsvrk", pair, np.eye(kzl))
    x_inverse = x_inverse.reshape(count_x * cells_x * kzl * 2, kzl * 2 * KX)
    zc, zs = angle_tables(np.arange(KZ), depth, depth, KZ**-0.5)
    pair = inverse_pair(zc, zs).reshape(2, 2, depth, count_y, kzl)
    z_inverse = np.einsum("rsnqz,xw,h->hqxzrwsn", pair, np.eye(cells_x), np.ones(2))
    z_inverse = z_inverse.reshape(4 * cells_x * KZ, cells_x * 2 * depth)
    yc, ys = angle_tables(signed_modes(KY), width_y, width_y, KY**-0.5)
    pair = np.stack([yc, -ys]).reshape(2, count_y, cells_y, KY)
    y_inverse = np.einsum("rqyk,i->qyrki", pair, np.ones(16))
    y_inverse = y_inverse.reshape(count_y, cells_y, 32 * KY)
    return (
        narrow(z_forward),
        narrow(y_forward),
        narrow(x_forward),
        x_inverse.astype(np.float32),
        narrow(z_inverse),
        narrow(y_inverse),
    )


def block_moves(value):
    rows = value.shape[0]
    tiles = value.reshape(rows // 8, 8, 128)
    row = lax.broadcasted_iota(jnp.int32, tiles.shape, 1) % 4
    block = lax.broadcasted_iota(jnp.int32, tiles.shape, 2) // 32
    result = tiles
    for lane_step in (1, 2, 3):
        moved = pltpu.roll(tiles, 128 - 32 * lane_step, 2)
        result = jnp.where(row - block == lane_step, pltpu.roll(moved, lane_step, 1), result)
        result = jnp.where(
            row - block == lane_step - 4, pltpu.roll(moved, 8 + lane_step - 4, 1), result
        )
    return result


def forward_kernel(state_hbm, z_hbm, y_hbm, out_ref, state_ref, z_ref, y_ref, table_ref, sems):
    count = state_ref.shape[0] // 4
    span = state_ref.shape[1]
    y_copy = pltpu.make_async_copy(y_hbm.at[lax.axis_index("py")], y_ref, sems.at[0])
    z_copy = pltpu.make_async_copy(z_hbm, z_ref, sems.at[1])
    copies = [
        pltpu.make_async_copy(
            state_hbm.at[pl.ds(g * count, count)],
            state_ref.at[pl.ds(g * count, count)],
            sems.at[2 + g],
        )
        for g in range(4)
    ]
    for copy in [y_copy, z_copy] + copies:
        copy.start()
    y_copy.wait()
    table = y_ref[...]
    lane = lax.broadcasted_iota(jnp.int32, (span, table.shape[1]), 1)
    for x in range(2):
        for c in range(8):
            own = (lane % 8 == c) & (lane // 64 % 2 == x)
            for part in range(2):
                first = part * 16 * span + (c * 2 + x) * span
                block = jnp.where(own, table[part * span : (part + 1) * span], 0.0)
                table_ref[first : first + span] = block.astype(jnp.bfloat16)
    z_copy.wait()
    z_table = z_ref[...].astype(jnp.bfloat16)
    pieces = []
    for g in range(4):
        copies[g].wait()
        cells = state_ref[g * count : (g + 1) * count].reshape(count * span, state_ref.shape[2])
        z_modes = lax.dot_general(
            z_table, cells, (((1,), (1,)), ((), ())), preferred_element_type=jnp.float32
        ).astype(jnp.bfloat16)
        pieces.append(jnp.concatenate([z_modes[:KZ], z_modes[KZ:]], axis=1))
    stacked = jnp.concatenate(pieces, axis=0)
    modes = jnp.dot(stacked, table_ref[...], preferred_element_type=jnp.float32)
    for group in range(4):
        moved = block_moves(modes[:, group * 128 : (group + 1) * 128])
        for half in range(2):
            for pair in range(2):
                first = moved[half * 4 + pair]
                second = moved[half * 4 + 2 + pair]
                for side in range(2):
                    rows4 = slice(4 * side, 4 * side + 4)
                    chunk = jnp.concatenate([first[rows4], second[rows4]], axis=0)
                    out_ref[(half * 4 + group) * 4 + 2 * pair + side] = chunk.astype(jnp.bfloat16)


def forward_modes(state, z_table, y_table):
    return pl.pallas_call(
        forward_kernel,
        out_shape=jax.ShapeDtypeStruct((32, 8, 128), jnp.bfloat16),
        in_specs=[pl.BlockSpec(memory_space=pltpu.HBM)] * 3,
        out_specs=pl.BlockSpec(memory_space=pltpu.VMEM),
        scratch_shapes=[
            pltpu.VMEM(state.shape, jnp.bfloat16),
            pltpu.VMEM(z_table.shape, jnp.float32),
            pltpu.VMEM(y_table.shape[1:], jnp.float32),
            pltpu.VMEM((32 * state.shape[1], y_table.shape[2]), jnp.bfloat16),
            pltpu.SemaphoreType.DMA((6,)),
        ],
        compiler_params=pltpu.CompilerParams(vmem_limit_bytes=40 * 2**20),
        cost_estimate=pl.CostEstimate(flops=2**27, bytes_accessed=2**21, transcendentals=0),
        name="forward_modes",
    )(*(pltpu.with_memory_space_constraint(v, pltpu.HBM) for v in (state, z_table, y_table)))


def prepare_kernel(
    after_ref, weight_hbm, conv_ref, y_ref, weight_out, conv_out, y_out, weight_ref, sems
):
    copies = [
        pltpu.make_async_copy(
            weight_hbm.at[part, kz], weight_ref.at[part, kz], sems.at[part * 4 + kz]
        )
        for part in range(2)
        for kz in range(4)
    ]
    for copy in copies:
        copy.start()
    odd_x = lax.rem(lax.axis_index("px"), 2) == 1
    zero = jnp.zeros((32, 32), jnp.float32)
    for dz in range(3):
        taps = {
            (dx, dy): conv_ref[dx, dy, dz].astype(jnp.float32)
            for dx in range(3)
            for dy in range(3)
        }
        for y_at in range(2):
            for x_at in range(2):
                row = ((dz * 2 + y_at) * 2 + x_at) * 32
                for y_in in range(4):
                    blocks = [taps.get((x_in - x_at, y_in - y_at), zero) for x_in in range(4)]
                    blocks = [jnp.where(odd_x, blocks[i], blocks[3 - i]) for i in range(4)]
                    conv_out[row : row + 32, y_in * 128 : (y_in + 1) * 128] = jnp.concatenate(
                        blocks, axis=1
                    ).astype(jnp.bfloat16)
    table = y_ref[lax.axis_index("py")]
    lane = lax.broadcasted_iota(jnp.int32, table.shape, 1) % 16
    span = table.shape[0]
    for o in range(16):
        y_out[o * span : (o + 1) * span] = jnp.where(lane == o, table, 0.0).astype(jnp.bfloat16)
    for part in range(2):
        for kz in range(4):
            copies[part * 4 + kz].wait()
            for c in range(16):
                weight_out[part, kz, c] = jnp.concatenate(
                    [weight_ref[part, kz, u, c] for u in range(4)], axis=1
                )


def prepare(after, spectral_weight, conv_weight, y_table):
    vmem = pl.BlockSpec(memory_space=pltpu.VMEM)
    return pl.pallas_call(
        prepare_kernel,
        out_shape=(
            jax.ShapeDtypeStruct((2, 4, 16, KX, 128), jnp.float32),
            jax.ShapeDtypeStruct((384, 512), jnp.bfloat16),
            jax.ShapeDtypeStruct((16 * y_table.shape[1], y_table.shape[2]), jnp.bfloat16),
        ),
        in_specs=[
            pl.BlockSpec(memory_space=pl.ANY),
            pl.BlockSpec(memory_space=pltpu.HBM),
            vmem,
            vmem,
        ],
        out_specs=(vmem,) * 3,
        scratch_shapes=[
            pltpu.VMEM(spectral_weight.shape, jnp.float32),
            pltpu.SemaphoreType.DMA((8,)),
        ],
        compiler_params=pltpu.CompilerParams(vmem_limit_bytes=40 * 2**20),
        cost_estimate=pl.CostEstimate(flops=2**20, bytes_accessed=6 * 2**20, transcendentals=0),
        name="prepare_weights",
    )(
        after,
        pltpu.with_memory_space_constraint(spectral_weight, pltpu.HBM),
        conv_weight,
        y_table,
    )


def mix_kernel(modes_ref, forward_ref, weight_ref, inverse_ref, out_ref):
    received = modes_ref[...].astype(jnp.float32).reshape(256, 128).astype(jnp.bfloat16)
    x_modes = jnp.dot(
        forward_ref[...].astype(jnp.bfloat16), received, preferred_element_type=jnp.float32)
    lane = lax.broadcasted_iota(jnp.int32, (16, 128), 1)
    base = (lane // 32) * 8
    mixed = []
    for kz in range(4):
        real_sum = imag_sum = None
        for c in range(16):
            half, c8 = c // 8, c % 8
            index = base + (kz * 32 + c8)
            real_in = jnp.take_along_axis(x_modes[half * 32 : half * 32 + 16], index, axis=1)
            imag_in = jnp.take_along_axis(x_modes[half * 32 + 16 : half * 32 + 32], index, axis=1)
            real_weight = weight_ref[0, kz, c]
            imag_weight = weight_ref[1, kz, c]
            real_term = real_weight * real_in - imag_weight * imag_in
            imag_term = real_weight * imag_in + imag_weight * real_in
            real_sum = real_term if real_sum is None else real_sum + real_term
            imag_sum = imag_term if imag_sum is None else imag_sum + imag_term
        mixed += [real_sum, imag_sum]
    values = jnp.dot(
        inverse_ref[...],
        jnp.concatenate(mixed, axis=0),
        preferred_element_type=jnp.float32,
        precision=lax.Precision.HIGHEST,
    ).astype(jnp.bfloat16)
    for x in range(8):
        for y in range(4):
            out_ref[x * 4 + y] = values[16 * x : 16 * x + 16]


def mix_modes(modes, forward_table, weights, inverse_table):
    vmem = pl.BlockSpec(memory_space=pltpu.VMEM)
    return pl.pallas_call(
        mix_kernel,
        out_shape=jax.ShapeDtypeStruct((32, 16, 128), jnp.bfloat16),
        in_specs=[vmem] * 4,
        out_specs=vmem,
        compiler_params=pltpu.CompilerParams(vmem_limit_bytes=40 * 2**20),
        cost_estimate=pl.CostEstimate(flops=2**22, bytes_accessed=2**21, transcendentals=0),
        name="mix_modes",
    )(modes, forward_table, weights, inverse_table)


def arrange_kernel(after_ref, state_ref, first_ref, second_ref, wide):
    cells_y = state_ref.shape[2]
    odd_x = lax.rem(lax.axis_index("px"), 2)
    for out_ref, x in ((first_ref, 1 - odd_x), (second_ref, odd_x)):
        wide[...] = state_ref[:, x].astype(jnp.float32).reshape(32 * cells_y, 128)
        for y in range(cells_y):
            out_ref[y] = wide[pl.ds(y, 32, stride=cells_y), :].astype(jnp.bfloat16)


def arrange(after, state):
    vmem = pl.BlockSpec(memory_space=pltpu.VMEM)
    cells_y = state.shape[2]
    plane = jax.ShapeDtypeStruct((cells_y, 32, 128), jnp.bfloat16)
    return pl.pallas_call(
        arrange_kernel,
        out_shape=(plane, plane),
        in_specs=[pl.BlockSpec(memory_space=pl.ANY), vmem],
        out_specs=(vmem, vmem),
        scratch_shapes=[pltpu.VMEM((32 * cells_y, 128), jnp.float32)],
        compiler_params=pltpu.CompilerParams(vmem_limit_bytes=40 * 2**20),
        cost_estimate=pl.CostEstimate(flops=2**20, bytes_accessed=2**21, transcendentals=0),
        name="arrange_cells",
    )(after, state)


def cell_row(planes, y):
    return jnp.concatenate([plane[y] for plane in planes], axis=0)


def edge_rows_kernel(*refs):
    *planes, first_ref, second_ref = refs
    end = planes[0].shape[0] - 1
    odd_y = lax.rem(lax.axis_index("py"), 2)
    first_ref[...] = cell_row(planes, (1 - odd_y) * end)
    second_ref[...] = cell_row(planes, odd_y * end)


def edge_rows(planes):
    vmem = pl.BlockSpec(memory_space=pltpu.VMEM)
    row = jax.ShapeDtypeStruct((128, 128), jnp.bfloat16)
    return pl.pallas_call(
        edge_rows_kernel,
        out_shape=(row, row),
        in_specs=[vmem] * 4,
        out_specs=(vmem, vmem),
        compiler_params=pltpu.CompilerParams(vmem_limit_bytes=40 * 2**20),
        cost_estimate=pl.CostEstimate(flops=2**10, bytes_accessed=2**17, transcendentals=0),
        name="edge_rows",
    )(*planes)


def convolve_quad(quad, row, weight, place, out_ref):
    lane = lax.broadcasted_iota(jnp.int32, (128, 256), 1) % 128
    windows = []
    for pair in range(2):
        start = quad * 4 + pair * 2 - 1
        windows.append(jnp.concatenate([row(start + i) for i in range(4)], axis=0))
    product = jnp.dot(weight, jnp.concatenate(windows, axis=1), preferred_element_type=jnp.float32)
    below = pltpu.roll(product[:128], 1, 1)
    above = pltpu.roll(product[256:], 255, 1)
    total = product[128:256] + jnp.where(lane == 0, 0.0, below)
    total = total + jnp.where(lane == 127, 0.0, above)
    for pair in range(2):
        for y_out in range(2):
            for x_out in range(2):
                first = (y_out * 2 + x_out) * 32
                value = total[first : first + 32, pair * 128 : (pair + 1) * 128]
                y = quad * 4 + pair * 2 + y_out
                at, span = place(y)
                out_ref[pl.ds(x_out * span + at, 32, stride=2 * span), :] = value


def interior_kernel(*refs):
    *planes, weight_ref, out_ref = refs
    cells_y = planes[0].shape[0]
    weight = weight_ref[...]
    for quad in range(1, cells_y // 4 - 1):
        convolve_quad(
            quad, lambda y: cell_row(planes, y), weight, lambda y: (y, cells_y), out_ref
        )


def edge_kernel(*refs):
    *planes, first_row, second_row, weight_ref, out_ref = refs
    cells_y = planes[0].shape[0]
    odd_y = lax.rem(lax.axis_index("py"), 2) == 1

    def row(y):
        if y < 0:
            return jnp.where(odd_y, first_row[...], second_row[...])
        if y >= cells_y:
            return jnp.where(odd_y, second_row[...], first_row[...])
        return cell_row(planes, y)

    weight = weight_ref[...]
    for quad in (0, cells_y // 4 - 1):
        convolve_quad(quad, row, weight, lambda y: (y % 8, 8), out_ref)


def convolve(kernel, name, operands, rows):
    vmem = pl.BlockSpec(memory_space=pltpu.VMEM)
    return pl.pallas_call(
        kernel,
        out_shape=jax.ShapeDtypeStruct((rows, 128), jnp.float32),
        in_specs=[vmem] * len(operands),
        out_specs=vmem,
        compiler_params=pltpu.CompilerParams(vmem_limit_bytes=40 * 2**20),
        cost_estimate=pl.CostEstimate(flops=2**30, bytes_accessed=2**21, transcendentals=0),
        name=name,
    )(*operands)


def gelu(value):
    return 0.5 * value * (1.0 + lax.erf(value * math.sqrt(0.5)))


def finish_kernel(
    bias_ref, values_ref, z_ref, y_ref, conv_ref, edge_ref, out_hbm, out_ref, sems
):
    upper = lax.broadcasted_iota(jnp.int32, (8, 128), 0) < 4
    columns = []
    for group in range(4):
        columns.append(
            jnp.concatenate(
                [values_ref[(h * 4 + group) * 4 + q] for h in range(2) for q in range(4)], axis=0
            )
        )
    packed = jnp.concatenate(columns, axis=1)
    z_values = lax.dot_general(
        packed,
        z_ref[...].astype(jnp.bfloat16),
        (((0,), (0,)), ((), ())),
        preferred_element_type=jnp.float32,
    ).astype(jnp.bfloat16)
    copies = []
    for half in range(2):
        sides = []
        for x in range(2):
            parts = []
            for part in range(2):
                lanes = slice((x * 2 + part) * 128, (x * 2 + part + 1) * 128)
                parts += [
                    z_values[ky * 32 + half * 16 : ky * 32 + half * 16 + 16, lanes]
                    for ky in range(KY)
                ]
            sides.append(jnp.concatenate(parts, axis=0))
        right = jnp.concatenate(sides, axis=1)
        for block in range(4):
            spectral = jnp.dot(
                y_ref[block * 128 : (block + 1) * 128], right, preferred_element_type=jnp.float32
            )
            for o4 in range(4):
                o = half * 16 + block * 4 + o4
                for x in range(2):
                    inner, edge = conv_ref[o, x], edge_ref[o, x]
                    convolved = jnp.concatenate(
                        [
                            jnp.where(upper, edge, inner[:8]),
                            inner[8:-8],
                            jnp.where(upper, inner[-8:], edge),
                        ],
                        axis=0,
                    )
                    total = spectral[o4 * 32 : o4 * 32 + 32, x * 128 : (x + 1) * 128]
                    total = total + convolved + bias_ref[o]
                    out_ref[o, x] = gelu(total).astype(jnp.bfloat16)
            number = half * 4 + block
            copy = pltpu.make_async_copy(
                out_ref.at[pl.ds(number * 4, 4)], out_hbm.at[pl.ds(number * 4, 4)], sems.at[number]
            )
            copy.start()
            copies.append(copy)
    for copy in copies:
        copy.wait()


def finish(bias, values, z_table, y_table, convolved, edges):
    vmem = pl.BlockSpec(memory_space=pltpu.VMEM)
    return pl.pallas_call(
        finish_kernel,
        out_shape=jax.ShapeDtypeStruct(convolved.shape, jnp.bfloat16),
        in_specs=[pl.BlockSpec(memory_space=pltpu.SMEM)] + [vmem] * 5,
        out_specs=pl.BlockSpec(memory_space=pltpu.HBM),
        scratch_shapes=[
            pltpu.VMEM(convolved.shape, jnp.bfloat16),
            pltpu.SemaphoreType.DMA((8,)),
        ],
        compiler_params=pltpu.CompilerParams(vmem_limit_bytes=40 * 2**20),
        cost_estimate=pl.CostEstimate(flops=2**28, bytes_accessed=2**22, transcendentals=2**18),
        name="finish_layer",
    )(bias, values, z_table, y_table, convolved, edges)


def exchanged(value):
    return lax.all_to_all(value, ("px", "py"), split_axis=0, concat_axis=0, tiled=True)


def swaps(first, second, axis):
    count = lax.axis_size(axis)
    inside = [(i, i ^ 1) for i in range(count)]
    across = [(i, i + 1 if i % 2 else i - 1) for i in range(1, count - 1)]
    return lax.ppermute(first, axis, inside), lax.ppermute(second, axis, across)


def body(state_field, conv_weight, conv_bias, spectral_weight):
    channels, cells_x, cells_y, depth = state_field.shape
    sizes = (lax.axis_size("px"), lax.axis_size("py"), cells_x, cells_y, depth)
    if sizes != (8, 4, 2, 32, 128):
        return general_body(state_field, conv_weight, conv_bias, spectral_weight)
    z_forward, y_forward, x_forward, x_inverse, z_inverse, y_inverse = tables(*sizes)
    sent = forward_modes(
        state_field.reshape(channels * cells_x, cells_y, depth), z_forward, y_forward
    )
    modes = exchanged(sent)
    weights, taps, y_expanded = prepare(
        sent, spectral_weight.swapaxes(4, 5), conv_weight.transpose(2, 3, 4, 0, 1), y_inverse
    )
    first_own, second_own = arrange(taps, state_field)
    first_plane, second_plane = swaps(first_own, second_own, "px")
    values = exchanged(mix_modes(modes, x_forward, weights, x_inverse))
    planes = (first_plane, first_own, second_own, second_plane)
    first_row, second_row = swaps(*edge_rows(planes), "py")
    rows = channels * cells_x * cells_y
    interior = convolve(interior_kernel, "convolve_interior", planes + (taps,), rows)
    edges = convolve(
        edge_kernel, "convolve_edges", planes + (first_row, second_row, taps), rows // cells_y * 8
    )
    return finish(
        conv_bias,
        values,
        z_inverse,
        y_expanded,
        interior.reshape(channels, cells_x, cells_y, depth),
        edges.reshape(channels, cells_x, 8, depth),
    )


def solution(mesh):
    in_specs = (P(None, "px", "py", None), P(), P(), P(None, "py", "px", None, None, None))
    out_specs = P(None, "px", "py", None)
    return jax.shard_map(body, mesh=mesh, in_specs=in_specs, out_specs=out_specs, check_vma=False)
```

```python
import functools
import math

import jax
import jax.numpy as jnp
import ml_dtypes
import numpy as np
from jax import lax
from jax.experimental import pallas as pl
from jax.experimental.pallas import tpu as pltpu
from jax.sharding import PartitionSpec as P

KX = 16
KY = 16
KZ = 16


def extended(cells, sides, width):
    for axis, dim in sides:
        count = lax.axis_size(axis)
        ends = count - 1
        head = lax.slice_in_dim(cells, 0, width, axis=dim)
        tail = lax.slice_in_dim(cells, cells.shape[dim] - width, cells.shape[dim], axis=dim)
        cells = jnp.concatenate(
            [
                lax.ppermute(tail, axis, [(i, (i + 1) % count) for i in range(ends)]),
                cells,
                lax.ppermute(head, axis, [((i + 1) % count, i) for i in range(ends)]),
            ],
            axis=dim,
        )
    return cells


def swapped(value, axis, distance):
    mask = 2**distance
    pairs = [(source, source ^ mask) for source in range(lax.axis_size(axis))]
    return lax.ppermute(value, axis, pairs)


def mode_numbers(count):
    indices = jnp.arange(count, dtype=jnp.int32)
    return jnp.where(indices < count // 2, indices, indices - count)


def trig_pair(numbers, points, length, factor, out_type):
    positions = jnp.arange(points, dtype=jnp.int32)
    phases = positions[:, None] * numbers[None, :] % length
    angles = phases.astype(jnp.float32) * (2.0 * math.pi / length)
    return (
        (jnp.cos(angles) * factor).astype(out_type),
        (jnp.sin(angles) * factor).astype(out_type),
    )


def last_product(source, table, precision=None):
    flat = source.reshape(-1, source.shape[-1])
    result = jnp.dot(flat, table, preferred_element_type=jnp.float32, precision=precision)
    return result.reshape(source.shape[:-1] + (table.shape[1],))


def forward_last(source, cosine, sine_table, precision=None):
    real_part = source[..., 0, :]
    imag_part = source[..., 1, :]
    real_out = last_product(real_part, cosine, precision) + last_product(
        imag_part, sine_table, precision
    )
    imag_out = last_product(imag_part, cosine, precision) - last_product(
        real_part, sine_table, precision
    )
    return jnp.stack([real_out, imag_out], axis=-2)


def inverse_last(source, cosine, sine_table, precision=None):
    real_part = source[..., 0, :]
    imag_part = source[..., 1, :]
    real_out = last_product(real_part, cosine, precision) - last_product(
        imag_part, sine_table, precision
    )
    imag_out = last_product(real_part, sine_table, precision) + last_product(
        imag_part, cosine, precision
    )
    return jnp.stack([real_out, imag_out], axis=-2)


def mix_block(spectral_weight, x_block):
    highest = lax.Precision.HIGHEST
    real_in = x_block[:, :, :, 0, :]
    imag_in = x_block[:, :, :, 1, :]
    partial_real = jnp.einsum(
        "zucok,uzck->uzok", spectral_weight[0], real_in, precision=highest
    ) - jnp.einsum("zucok,uzck->uzok", spectral_weight[1], imag_in, precision=highest)
    partial_imag = jnp.einsum(
        "zucok,uzck->uzok", spectral_weight[0], imag_in, precision=highest
    ) + jnp.einsum("zucok,uzck->uzok", spectral_weight[1], real_in, precision=highest)
    return jnp.stack([partial_real, partial_imag], axis=3)


def general_body(state_field, conv_weight, conv_bias, spectral_weight):
    channels, cells_x, cells_y, depth = state_field.shape
    count_x = lax.axis_size("px")
    count_y = lax.axis_size("py")
    width_x = cells_x * count_x
    width_y = cells_y * count_y
    index_x = lax.axis_index("px")
    kz_local = KZ // count_y
    units = 2 * KY // count_x
    highest = lax.Precision.HIGHEST
    padded = extended(state_field, (("px", 1), ("py", 2)), 1)
    convolved = lax.conv_general_dilated(
        padded[None],
        conv_weight,
        (1, 1, 1),
        ((0, 0), (0, 0), (1, 1)),
        dimension_numbers=("NCDHW", "OIDHW", "NCDHW"),
        preferred_element_type=jnp.float32,
    )[0]
    z_cos, z_sin = trig_pair(
        jnp.arange(KZ, dtype=jnp.int32), depth, depth, depth ** (-0.5), jnp.bfloat16
    )
    z_table = jnp.stack([z_cos, -z_sin], axis=1)
    z_modes = jnp.einsum(
        "cxyn,nwk->kcxwy", state_field, z_table, preferred_element_type=jnp.float32
    ).astype(jnp.bfloat16)
    y_cos, y_sin = trig_pair(mode_numbers(KY), width_y, width_y, width_y ** (-0.5), jnp.bfloat16)
    full_rows = lax.all_to_all(z_modes, "py", split_axis=0, concat_axis=4, tiled=True)
    y_modes = forward_last(full_rows, y_cos, y_sin)
    y_modes = y_modes.astype(jnp.bfloat16)
    by_unit = y_modes.reshape(kz_local, 2, channels // 2, cells_x, 2, KY).transpose(
        1, 5, 0, 2, 4, 3
    )
    by_unit = by_unit.reshape(2 * KY, kz_local, channels // 2, 2, cells_x)
    x_rows = lax.all_to_all(by_unit, "px", split_axis=0, concat_axis=4, tiled=True)
    x_cos, x_sin = trig_pair(mode_numbers(KX), width_x, width_x, width_x ** (-0.5), jnp.bfloat16)
    x_modes = forward_last(x_rows, x_cos, x_sin)
    partial_modes = mix_block(spectral_weight, x_modes)
    partial_modes = partial_modes.reshape(units, kz_local, 2, channels // 2, 2, KX)
    half_index = index_x * units // KY
    own_half = lax.dynamic_index_in_dim(partial_modes, half_index, 2, keepdims=False)
    other_half = lax.dynamic_index_in_dim(partial_modes, 1 - half_index, 2, keepdims=False)
    mixed_modes = own_half + swapped(other_half, "px", count_x.bit_length() - 2)
    ix_cos, ix_sin = trig_pair(mode_numbers(KX), width_x, width_x, KX ** (-0.5), jnp.float32)
    x_values = inverse_last(mixed_modes, ix_cos.T, ix_sin.T, highest).astype(jnp.bfloat16)
    returned = lax.all_to_all(x_values, "px", split_axis=4, concat_axis=0, tiled=True)
    returned = returned.reshape(2, KY, kz_local, channels // 2, 2, cells_x).transpose(
        2, 0, 3, 5, 4, 1
    )
    returned = returned.reshape(kz_local, channels, cells_x, 2, KY)
    iy_cos, iy_sin = trig_pair(mode_numbers(KY), width_y, width_y, KY ** (-0.5), jnp.bfloat16)
    expanded = inverse_last(returned, iy_cos.T, iy_sin.T).astype(jnp.bfloat16)
    y_values = lax.all_to_all(expanded, "py", split_axis=4, concat_axis=0, tiled=True)
    iz_cos, iz_sin = trig_pair(
        jnp.arange(KZ, dtype=jnp.int32), depth, depth, KZ ** (-0.5), jnp.bfloat16
    )
    iz_table = jnp.stack([iz_cos.T, -iz_sin.T], axis=0)
    spectral = jnp.einsum("kcxwy,wkn->cxyn", y_values, iz_table, preferred_element_type=jnp.float32)
    total = convolved + spectral + conv_bias[:, None, None, None]
    return jax.nn.gelu(total, approximate=False).astype(jnp.bfloat16)


def angle_tables(numbers, points, length, factor):
    phases = (np.arange(points)[:, None] * numbers[None, :]) % length
    angles = phases.astype(np.float32) * np.float32(2.0 * math.pi / length)
    return (
        np.cos(angles).astype(np.float32) * np.float32(factor),
        np.sin(angles).astype(np.float32) * np.float32(factor),
    )


def signed_modes(count):
    indices = np.arange(count)
    return np.where(indices < count // 2, indices, indices - count)


def narrow(table):
    return table.astype(ml_dtypes.bfloat16).astype(np.float32)


def forward_pair(cosine, sine):
    return np.stack([np.stack([cosine, -sine]), np.stack([sine, cosine])])


def inverse_pair(cosine, sine):
    return np.stack([np.stack([cosine, sine]), np.stack([-sine, cosine])])


@functools.cache
def tables(count_x, count_y, cells_x, cells_y, depth):
    width_x, width_y = count_x * cells_x, count_y * cells_y
    kzl, units = KZ // count_y, 2 * KY // count_x
    groups = KY // units
    zc, zs = angle_tables(np.arange(KZ), depth, depth, depth**-0.5)
    z_forward = np.concatenate([zc.T, -zs.T])
    yc, ys = angle_tables(signed_modes(KY), width_y, width_y, width_y**-0.5)
    pair = forward_pair(yc, ys).reshape(2, 2, count_y, cells_y, groups, units)
    y_forward = np.einsum("rsqygk,d,w->qrygwskd", pair, np.ones(8), np.ones(cells_x))
    y_forward = y_forward.reshape(count_y, 2 * cells_y, groups * 2 * cells_x * units * 8)
    xc, xs = angle_tables(signed_modes(KX), width_x, width_x, width_x**-0.5)
    pair = forward_pair(xc, xs).reshape(2, 2, count_x, cells_x, KX)
    x_forward = np.einsum("rspxk,gh,q->gskpqhxr", pair, np.eye(2), np.ones(count_y))
    x_forward = x_forward.reshape(4 * KX, count_x * count_y * 4 * cells_x)
    xc, xs = angle_tables(signed_modes(KX), width_x, width_x, KX**-0.5)
    pair = inverse_pair(xc, xs).reshape(2, 2, count_x, cells_x, KX)
    x_inverse = np.einsum("rspxk,zv->pxzsvrk", pair, np.eye(kzl))
    x_inverse = x_inverse.reshape(count_x * cells_x * kzl * 2, kzl * 2 * KX)
    zc, zs = angle_tables(np.arange(KZ), depth, depth, KZ**-0.5)
    pair = inverse_pair(zc, zs).reshape(2, 2, depth, count_y, kzl)
    z_inverse = np.einsum("rsnqz,xw,h->hqxzrwsn", pair, np.eye(cells_x), np.ones(2))
    z_inverse = z_inverse.reshape(4 * cells_x * KZ, cells_x * 2 * depth)
    yc, ys = angle_tables(signed_modes(KY), width_y, width_y, KY**-0.5)
    pair = np.stack([yc, -ys]).reshape(2, count_y, cells_y, KY)
    y_inverse = np.einsum("rqyk,i->qyrki", pair, np.ones(16))
    y_inverse = y_inverse.reshape(count_y, cells_y, 32 * KY)
    return (
        narrow(z_forward),
        narrow(y_forward),
        narrow(x_forward),
        x_inverse.astype(np.float32),
        narrow(z_inverse),
        narrow(y_inverse),
    )


def block_moves(value):
    rows = value.shape[0]
    tiles = value.reshape(rows // 8, 8, 128)
    row = lax.broadcasted_iota(jnp.int32, tiles.shape, 1) % 4
    block = lax.broadcasted_iota(jnp.int32, tiles.shape, 2) // 32
    result = tiles
    for lane_step in (1, 2, 3):
        moved = pltpu.roll(tiles, 128 - 32 * lane_step, 2)
        result = jnp.where(row - block == lane_step, pltpu.roll(moved, lane_step, 1), result)
        result = jnp.where(
            row - block == lane_step - 4, pltpu.roll(moved, 8 + lane_step - 4, 1), result
        )
    return result


def forward_kernel(state_hbm, z_hbm, y_hbm, out_ref, state_ref, z_ref, y_ref, table_ref, sems):
    count = state_ref.shape[0] // 4
    span = state_ref.shape[1]
    y_copy = pltpu.make_async_copy(y_hbm.at[lax.axis_index("py")], y_ref, sems.at[0])
    z_copy = pltpu.make_async_copy(z_hbm, z_ref, sems.at[1])
    copies = [
        pltpu.make_async_copy(
            state_hbm.at[pl.ds(g * count, count)],
            state_ref.at[pl.ds(g * count, count)],
            sems.at[2 + g],
        )
        for g in range(4)
    ]
    for copy in [y_copy, z_copy] + copies:
        copy.start()
    y_copy.wait()
    table = y_ref[...]
    lane = lax.broadcasted_iota(jnp.int32, (span, table.shape[1]), 1)
    for x in range(2):
        for c in range(8):
            own = (lane % 8 == c) & (lane // 64 % 2 == x)
            for part in range(2):
                first = part * 16 * span + (c * 2 + x) * span
                block = jnp.where(own, table[part * span : (part + 1) * span], 0.0)
                table_ref[first : first + span] = block.astype(jnp.bfloat16)
    z_copy.wait()
    z_table = z_ref[...].astype(jnp.bfloat16)
    pieces = []
    for g in range(4):
        copies[g].wait()
        cells = state_ref[g * count : (g + 1) * count].reshape(count * span, state_ref.shape[2])
        z_modes = lax.dot_general(
            z_table, cells, (((1,), (1,)), ((), ())), preferred_element_type=jnp.float32
        ).astype(jnp.bfloat16)
        pieces.append(jnp.concatenate([z_modes[:KZ], z_modes[KZ:]], axis=1))
    stacked = jnp.concatenate(pieces, axis=0)
    modes = jnp.dot(stacked, table_ref[...], preferred_element_type=jnp.float32)
    for group in range(4):
        moved = block_moves(modes[:, group * 128 : (group + 1) * 128])
        for half in range(2):
            for pair in range(2):
                first = moved[half * 4 + pair]
                second = moved[half * 4 + 2 + pair]
                for side in range(2):
                    rows4 = slice(4 * side, 4 * side + 4)
                    chunk = jnp.concatenate([first[rows4], second[rows4]], axis=0)
                    out_ref[(half * 4 + group) * 4 + 2 * pair + side] = chunk.astype(jnp.bfloat16)


def forward_modes(state, z_table, y_table):
    return pl.pallas_call(
        forward_kernel,
        out_shape=jax.ShapeDtypeStruct((32, 8, 128), jnp.bfloat16),
        in_specs=[pl.BlockSpec(memory_space=pltpu.HBM)] * 3,
        out_specs=pl.BlockSpec(memory_space=pltpu.VMEM),
        scratch_shapes=[
            pltpu.VMEM(state.shape, jnp.bfloat16),
            pltpu.VMEM(z_table.shape, jnp.float32),
            pltpu.VMEM(y_table.shape[1:], jnp.float32),
            pltpu.VMEM((32 * state.shape[1], y_table.shape[2]), jnp.bfloat16),
            pltpu.SemaphoreType.DMA((6,)),
        ],
        compiler_params=pltpu.CompilerParams(vmem_limit_bytes=16 * 2**20),
        cost_estimate=pl.CostEstimate(flops=2**27, bytes_accessed=2**21, transcendentals=0),
        name="forward_modes",
    )(*(pltpu.with_memory_space_constraint(v, pltpu.HBM) for v in (state, z_table, y_table)))


def prepare_kernel(
    after_ref,
    weight_hbm,
    conv_hbm,
    y_hbm,
    weight_out,
    conv_out,
    y_out,
    weight_ref,
    conv_ref,
    y_ref,
    sems,
):
    conv_copy = pltpu.make_async_copy(conv_hbm, conv_ref, sems.at[8])
    y_copy = pltpu.make_async_copy(y_hbm.at[lax.axis_index("py")], y_ref, sems.at[9])
    conv_copy.start()
    y_copy.start()
    copies = [
        pltpu.make_async_copy(
            weight_hbm.at[part, kz], weight_ref.at[part, kz], sems.at[part * 4 + kz]
        )
        for part in range(2)
        for kz in range(4)
    ]
    for copy in copies:
        copy.start()
    odd_x = lax.rem(lax.axis_index("px"), 2) == 1
    conv_copy.wait()
    zero = jnp.zeros((32, 32), jnp.float32)
    for dz in range(3):
        taps = {
            (dx, dy): conv_ref[dx, dy, dz].astype(jnp.float32)
            for dx in range(3)
            for dy in range(3)
        }
        for y_at in range(2):
            for x_at in range(2):
                row = ((dz * 2 + y_at) * 2 + x_at) * 32
                for y_in in range(4):
                    blocks = [taps.get((x_in - x_at, y_in - y_at), zero) for x_in in range(4)]
                    blocks = [jnp.where(odd_x, blocks[i], blocks[3 - i]) for i in range(4)]
                    conv_out[row : row + 32, y_in * 128 : (y_in + 1) * 128] = jnp.concatenate(
                        blocks, axis=1
                    ).astype(jnp.bfloat16)
    y_copy.wait()
    table = y_ref[...]
    lane = lax.broadcasted_iota(jnp.int32, table.shape, 1) % 16
    span = table.shape[0]
    for o in range(16):
        y_out[o * span : (o + 1) * span] = jnp.where(lane == o, table, 0.0).astype(jnp.bfloat16)
    for part in range(2):
        for kz in range(4):
            copies[part * 4 + kz].wait()
            for c in range(16):
                weight_out[part, kz, c] = jnp.concatenate(
                    [weight_ref[part, kz, u, c] for u in range(4)], axis=1
                )


def prepare(after, spectral_weight, conv_weight, y_table):
    vmem = pl.BlockSpec(memory_space=pltpu.VMEM)
    return pl.pallas_call(
        prepare_kernel,
        out_shape=(
            jax.ShapeDtypeStruct((2, 4, 16, KX, 128), jnp.float32),
            jax.ShapeDtypeStruct((384, 512), jnp.bfloat16),
            jax.ShapeDtypeStruct((16 * y_table.shape[1], y_table.shape[2]), jnp.bfloat16),
        ),
        in_specs=[pl.BlockSpec(memory_space=pl.ANY)] + [pl.BlockSpec(memory_space=pltpu.HBM)] * 3,
        out_specs=(vmem,) * 3,
        scratch_shapes=[
            pltpu.VMEM(spectral_weight.shape, jnp.float32),
            pltpu.VMEM(conv_weight.shape, jnp.bfloat16),
            pltpu.VMEM(y_table.shape[1:], jnp.float32),
            pltpu.SemaphoreType.DMA((10,)),
        ],
        compiler_params=pltpu.CompilerParams(vmem_limit_bytes=16 * 2**20),
        cost_estimate=pl.CostEstimate(flops=2**10, bytes_accessed=2**10, transcendentals=0),
        name="prepare_weights",
    )(
        after,
        *(
            pltpu.with_memory_space_constraint(v, pltpu.HBM)
            for v in (spectral_weight, conv_weight, y_table)
        ),
    )


def mix_kernel(modes_ref, forward_ref, weight_ref, inverse_ref, out_ref):
    received = modes_ref[...].astype(jnp.float32).reshape(256, 128).astype(jnp.bfloat16)
    x_modes = jnp.dot(
        forward_ref[...].astype(jnp.bfloat16), received, preferred_element_type=jnp.float32)
    lane = lax.broadcasted_iota(jnp.int32, (16, 128), 1)
    base = (lane // 32) * 8
    mixed = []
    for kz in range(4):
        real_sum = imag_sum = None
        for c in range(16):
            half, c8 = c // 8, c % 8
            index = base + (kz * 32 + c8)
            real_in = jnp.take_along_axis(x_modes[half * 32 : half * 32 + 16], index, axis=1)
            imag_in = jnp.take_along_axis(x_modes[half * 32 + 16 : half * 32 + 32], index, axis=1)
            real_weight = weight_ref[0, kz, c]
            imag_weight = weight_ref[1, kz, c]
            real_term = real_weight * real_in - imag_weight * imag_in
            imag_term = real_weight * imag_in + imag_weight * real_in
            real_sum = real_term if real_sum is None else real_sum + real_term
            imag_sum = imag_term if imag_sum is None else imag_sum + imag_term
        mixed += [real_sum, imag_sum]
    values = jnp.dot(
        inverse_ref[...],
        jnp.concatenate(mixed, axis=0),
        preferred_element_type=jnp.float32,
        precision=lax.Precision.HIGHEST,
    ).astype(jnp.bfloat16)
    for x in range(8):
        for y in range(4):
            out_ref[x * 4 + y] = values[16 * x : 16 * x + 16]


def mix_modes(modes, forward_table, weights, inverse_table):
    vmem = pl.BlockSpec(memory_space=pltpu.VMEM)
    return pl.pallas_call(
        mix_kernel,
        out_shape=jax.ShapeDtypeStruct((32, 16, 128), jnp.bfloat16),
        in_specs=[vmem] * 4,
        out_specs=vmem,
        compiler_params=pltpu.CompilerParams(vmem_limit_bytes=16 * 2**20),
        cost_estimate=pl.CostEstimate(flops=2**35, bytes_accessed=2**21, transcendentals=0),
        name="mix_modes",
    )(modes, forward_table, weights, inverse_table)


def arrange_kernel(after_ref, state_ref, first_ref, second_ref, wide):
    cells_y = state_ref.shape[2]
    odd_x = lax.rem(lax.axis_index("px"), 2)
    for out_ref, x in ((first_ref, 1 - odd_x), (second_ref, odd_x)):
        wide[...] = state_ref[:, x].astype(jnp.float32).reshape(32 * cells_y, 128)
        for y in range(cells_y):
            out_ref[y] = wide[pl.ds(y, 32, stride=cells_y), :].astype(jnp.bfloat16)


def arrange(after, state):
    vmem = pl.BlockSpec(memory_space=pltpu.VMEM)
    cells_y = state.shape[2]
    plane = jax.ShapeDtypeStruct((cells_y, 32, 128), jnp.bfloat16)
    return pl.pallas_call(
        arrange_kernel,
        out_shape=(plane, plane),
        in_specs=[pl.BlockSpec(memory_space=pl.ANY), vmem],
        out_specs=(vmem, vmem),
        scratch_shapes=[pltpu.VMEM((32 * cells_y, 128), jnp.float32)],
        compiler_params=pltpu.CompilerParams(vmem_limit_bytes=16 * 2**20),
        cost_estimate=pl.CostEstimate(flops=2**10, bytes_accessed=2**10, transcendentals=0),
        name="arrange_cells",
    )(after, state)


def cell_row(planes, y):
    return jnp.concatenate([plane[y] for plane in planes], axis=0)


def edge_rows_kernel(*refs):
    *planes, first_ref, second_ref = refs
    end = planes[0].shape[0] - 1
    odd_y = lax.rem(lax.axis_index("py"), 2)
    first_ref[...] = cell_row(planes, (1 - odd_y) * end)
    second_ref[...] = cell_row(planes, odd_y * end)


def edge_rows(planes):
    vmem = pl.BlockSpec(memory_space=pltpu.VMEM)
    row = jax.ShapeDtypeStruct((128, 128), jnp.bfloat16)
    return pl.pallas_call(
        edge_rows_kernel,
        out_shape=(row, row),
        in_specs=[vmem] * 4,
        out_specs=(vmem, vmem),
        compiler_params=pltpu.CompilerParams(vmem_limit_bytes=16 * 2**20),
        cost_estimate=pl.CostEstimate(flops=2**10, bytes_accessed=2**17, transcendentals=0),
        name="edge_rows",
    )(*planes)


def convolve_quad(quad, row, weight, place, out_ref):
    lane = lax.broadcasted_iota(jnp.int32, (128, 256), 1) % 128
    windows = []
    for pair in range(2):
        start = quad * 4 + pair * 2 - 1
        windows.append(jnp.concatenate([row(start + i) for i in range(4)], axis=0))
    product = jnp.dot(weight, jnp.concatenate(windows, axis=1), preferred_element_type=jnp.float32)
    below = pltpu.roll(product[:128], 1, 1)
    above = pltpu.roll(product[256:], 255, 1)
    total = product[128:256] + jnp.where(lane == 0, 0.0, below)
    total = total + jnp.where(lane == 127, 0.0, above)
    for pair in range(2):
        for y_out in range(2):
            for x_out in range(2):
                first = (y_out * 2 + x_out) * 32
                value = total[first : first + 32, pair * 128 : (pair + 1) * 128]
                y = quad * 4 + pair * 2 + y_out
                at, span = place(y)
                out_ref[pl.ds(x_out * span + at, 32, stride=2 * span), :] = value


def interior_kernel(*refs):
    *planes, weight_ref, out_ref = refs
    cells_y = planes[0].shape[0]
    weight = weight_ref[...]
    for quad in range(1, cells_y // 4 - 1):
        convolve_quad(
            quad, lambda y: cell_row(planes, y), weight, lambda y: (y, cells_y), out_ref
        )


def edge_kernel(*refs):
    *planes, first_row, second_row, weight_ref, out_ref = refs
    cells_y = planes[0].shape[0]
    odd_y = lax.rem(lax.axis_index("py"), 2) == 1

    def row(y):
        if y < 0:
            return jnp.where(odd_y, first_row[...], second_row[...])
        if y >= cells_y:
            return jnp.where(odd_y, second_row[...], first_row[...])
        return cell_row(planes, y)

    weight = weight_ref[...]
    for quad in (0, cells_y // 4 - 1):
        convolve_quad(quad, row, weight, lambda y: (y % 8, 8), out_ref)


def convolve(kernel, name, operands, rows):
    vmem = pl.BlockSpec(memory_space=pltpu.VMEM)
    return pl.pallas_call(
        kernel,
        out_shape=jax.ShapeDtypeStruct((rows, 128), jnp.float32),
        in_specs=[vmem] * len(operands),
        out_specs=vmem,
        compiler_params=pltpu.CompilerParams(vmem_limit_bytes=16 * 2**20),
        cost_estimate=pl.CostEstimate(flops=2**30, bytes_accessed=2**21, transcendentals=0),
        name=name,
    )(*operands)


def gelu(value):
    return 0.5 * value * (1.0 + lax.erf(value * math.sqrt(0.5)))


def finish_kernel(
    bias_ref, values_ref, z_ref, y_ref, conv_ref, edge_ref, out_hbm, out_ref, sems
):
    upper = lax.broadcasted_iota(jnp.int32, (8, 128), 0) < 4
    columns = []
    for group in range(4):
        columns.append(
            jnp.concatenate(
                [values_ref[(h * 4 + group) * 4 + q] for h in range(2) for q in range(4)], axis=0
            )
        )
    packed = jnp.concatenate(columns, axis=1)
    z_values = lax.dot_general(
        packed,
        z_ref[...].astype(jnp.bfloat16),
        (((0,), (0,)), ((), ())),
        preferred_element_type=jnp.float32,
    ).astype(jnp.bfloat16)
    copies = []
    for half in range(2):
        sides = []
        for x in range(2):
            parts = []
            for part in range(2):
                lanes = slice((x * 2 + part) * 128, (x * 2 + part + 1) * 128)
                parts += [
                    z_values[ky * 32 + half * 16 : ky * 32 + half * 16 + 16, lanes]
                    for ky in range(KY)
                ]
            sides.append(jnp.concatenate(parts, axis=0))
        right = jnp.concatenate(sides, axis=1)
        for block in range(4):
            spectral = jnp.dot(
                y_ref[block * 128 : (block + 1) * 128], right, preferred_element_type=jnp.float32
            )
            for o4 in range(4):
                o = half * 16 + block * 4 + o4
                for x in range(2):
                    inner, edge = conv_ref[o, x], edge_ref[o, x]
                    convolved = jnp.concatenate(
                        [
                            jnp.where(upper, edge, inner[:8]),
                            inner[8:-8],
                            jnp.where(upper, inner[-8:], edge),
                        ],
                        axis=0,
                    )
                    total = spectral[o4 * 32 : o4 * 32 + 32, x * 128 : (x + 1) * 128]
                    total = total + convolved + bias_ref[o]
                    out_ref[o, x] = gelu(total).astype(jnp.bfloat16)
            number = half * 4 + block
            copy = pltpu.make_async_copy(
                out_ref.at[pl.ds(number * 4, 4)], out_hbm.at[pl.ds(number * 4, 4)], sems.at[number]
            )
            copy.start()
            copies.append(copy)
    for copy in copies:
        copy.wait()


def finish(bias, values, z_table, y_table, convolved, edges):
    vmem = pl.BlockSpec(memory_space=pltpu.VMEM)
    return pl.pallas_call(
        finish_kernel,
        out_shape=jax.ShapeDtypeStruct(convolved.shape, jnp.bfloat16),
        in_specs=[pl.BlockSpec(memory_space=pltpu.SMEM)] + [vmem] * 5,
        out_specs=pl.BlockSpec(memory_space=pltpu.HBM),
        scratch_shapes=[
            pltpu.VMEM(convolved.shape, jnp.bfloat16),
            pltpu.SemaphoreType.DMA((8,)),
        ],
        compiler_params=pltpu.CompilerParams(vmem_limit_bytes=16 * 2**20),
        cost_estimate=pl.CostEstimate(flops=2**28, bytes_accessed=2**22, transcendentals=2**18),
        name="finish_layer",
    )(bias, values, z_table, y_table, convolved, edges)


def exchanged(value):
    return lax.all_to_all(value, ("px", "py"), split_axis=0, concat_axis=0, tiled=True)


def swaps(first, second, axis):
    count = lax.axis_size(axis)
    inside = [(i, i ^ 1) for i in range(count)]
    across = [(i, i + 1 if i % 2 else i - 1) for i in range(1, count - 1)]
    return lax.ppermute(first, axis, inside), lax.ppermute(second, axis, across)


def body(state_field, conv_weight, conv_bias, spectral_weight):
    channels, cells_x, cells_y, depth = state_field.shape
    sizes = (lax.axis_size("px"), lax.axis_size("py"), cells_x, cells_y, depth)
    if sizes != (8, 4, 2, 32, 128):
        return general_body(state_field, conv_weight, conv_bias, spectral_weight)
    z_forward, y_forward, x_forward, x_inverse, z_inverse, y_inverse = tables(*sizes)
    sent = forward_modes(
        state_field.reshape(channels * cells_x, cells_y, depth), z_forward, y_forward
    )
    modes = exchanged(sent)
    weights, taps, y_expanded = prepare(
        sent, spectral_weight.swapaxes(4, 5), conv_weight.transpose(2, 3, 4, 0, 1), y_inverse
    )
    first_own, second_own = arrange(taps, state_field)
    first_plane, second_plane = swaps(first_own, second_own, "px")
    values = exchanged(mix_modes(modes, x_forward, weights, x_inverse))
    planes = (first_plane, first_own, second_own, second_plane)
    first_row, second_row = swaps(*edge_rows(planes), "py")
    rows = channels * cells_x * cells_y
    interior = convolve(interior_kernel, "convolve_interior", planes + (taps,), rows)
    edges = convolve(
        edge_kernel, "convolve_edges", planes + (first_row, second_row, taps), rows // cells_y * 8
    )
    return finish(
        conv_bias,
        values,
        z_inverse,
        y_expanded,
        interior.reshape(channels, cells_x, cells_y, depth),
        edges.reshape(channels, cells_x, 8, depth),
    )


def solution(mesh):
    in_specs = (P(None, "px", "py", None), P(), P(), P(None, "py", "px", None, None, None))
    out_specs = P(None, "px", "py", None)
    return jax.shard_map(body, mesh=mesh, in_specs=in_specs, out_specs=out_specs, check_vma=False)
```

```python
import functools
import math

import jax
import jax.numpy as jnp
import ml_dtypes
import numpy as np
from jax import lax
from jax.experimental import pallas as pl
from jax.experimental.pallas import tpu as pltpu
from jax.sharding import PartitionSpec as P

KX = 16
KY = 16
KZ = 16


def extended(cells, sides, width):
    for axis, dim in sides:
        count = lax.axis_size(axis)
        ends = count - 1
        head = lax.slice_in_dim(cells, 0, width, axis=dim)
        tail = lax.slice_in_dim(cells, cells.shape[dim] - width, cells.shape[dim], axis=dim)
        cells = jnp.concatenate(
            [
                lax.ppermute(tail, axis, [(i, (i + 1) % count) for i in range(ends)]),
                cells,
                lax.ppermute(head, axis, [((i + 1) % count, i) for i in range(ends)]),
            ],
            axis=dim,
        )
    return cells


def swapped(value, axis, distance):
    mask = 2**distance
    pairs = [(source, source ^ mask) for source in range(lax.axis_size(axis))]
    return lax.ppermute(value, axis, pairs)


def mode_numbers(count):
    indices = jnp.arange(count, dtype=jnp.int32)
    return jnp.where(indices < count // 2, indices, indices - count)


def trig_pair(numbers, points, length, factor, out_type):
    positions = jnp.arange(points, dtype=jnp.int32)
    phases = positions[:, None] * numbers[None, :] % length
    angles = phases.astype(jnp.float32) * (2.0 * math.pi / length)
    return (
        (jnp.cos(angles) * factor).astype(out_type),
        (jnp.sin(angles) * factor).astype(out_type),
    )


def last_product(source, table, precision=None):
    flat = source.reshape(-1, source.shape[-1])
    result = jnp.dot(flat, table, preferred_element_type=jnp.float32, precision=precision)
    return result.reshape(source.shape[:-1] + (table.shape[1],))


def forward_last(source, cosine, sine_table, precision=None):
    real_part = source[..., 0, :]
    imag_part = source[..., 1, :]
    real_out = last_product(real_part, cosine, precision) + last_product(
        imag_part, sine_table, precision
    )
    imag_out = last_product(imag_part, cosine, precision) - last_product(
        real_part, sine_table, precision
    )
    return jnp.stack([real_out, imag_out], axis=-2)


def inverse_last(source, cosine, sine_table, precision=None):
    real_part = source[..., 0, :]
    imag_part = source[..., 1, :]
    real_out = last_product(real_part, cosine, precision) - last_product(
        imag_part, sine_table, precision
    )
    imag_out = last_product(real_part, sine_table, precision) + last_product(
        imag_part, cosine, precision
    )
    return jnp.stack([real_out, imag_out], axis=-2)


def mix_block(spectral_weight, x_block):
    highest = lax.Precision.HIGHEST
    real_in = x_block[:, :, :, 0, :]
    imag_in = x_block[:, :, :, 1, :]
    partial_real = jnp.einsum(
        "zucok,uzck->uzok", spectral_weight[0], real_in, precision=highest
    ) - jnp.einsum("zucok,uzck->uzok", spectral_weight[1], imag_in, precision=highest)
    partial_imag = jnp.einsum(
        "zucok,uzck->uzok", spectral_weight[0], imag_in, precision=highest
    ) + jnp.einsum("zucok,uzck->uzok", spectral_weight[1], real_in, precision=highest)
    return jnp.stack([partial_real, partial_imag], axis=3)


def general_body(state_field, conv_weight, conv_bias, spectral_weight):
    channels, cells_x, cells_y, depth = state_field.shape
    count_x = lax.axis_size("px")
    count_y = lax.axis_size("py")
    width_x = cells_x * count_x
    width_y = cells_y * count_y
    index_x = lax.axis_index("px")
    kz_local = KZ // count_y
    units = 2 * KY // count_x
    highest = lax.Precision.HIGHEST
    padded = extended(state_field, (("px", 1), ("py", 2)), 1)
    convolved = lax.conv_general_dilated(
        padded[None],
        conv_weight,
        (1, 1, 1),
        ((0, 0), (0, 0), (1, 1)),
        dimension_numbers=("NCDHW", "OIDHW", "NCDHW"),
        preferred_element_type=jnp.float32,
    )[0]
    z_cos, z_sin = trig_pair(
        jnp.arange(KZ, dtype=jnp.int32), depth, depth, depth ** (-0.5), jnp.bfloat16
    )
    z_table = jnp.stack([z_cos, -z_sin], axis=1)
    z_modes = jnp.einsum(
        "cxyn,nwk->kcxwy", state_field, z_table, preferred_element_type=jnp.float32
    ).astype(jnp.bfloat16)
    y_cos, y_sin = trig_pair(mode_numbers(KY), width_y, width_y, width_y ** (-0.5), jnp.bfloat16)
    full_rows = lax.all_to_all(z_modes, "py", split_axis=0, concat_axis=4, tiled=True)
    y_modes = forward_last(full_rows, y_cos, y_sin)
    y_modes = y_modes.astype(jnp.bfloat16)
    by_unit = y_modes.reshape(kz_local, 2, channels // 2, cells_x, 2, KY).transpose(
        1, 5, 0, 2, 4, 3
    )
    by_unit = by_unit.reshape(2 * KY, kz_local, channels // 2, 2, cells_x)
    x_rows = lax.all_to_all(by_unit, "px", split_axis=0, concat_axis=4, tiled=True)
    x_cos, x_sin = trig_pair(mode_numbers(KX), width_x, width_x, width_x ** (-0.5), jnp.bfloat16)
    x_modes = forward_last(x_rows, x_cos, x_sin)
    partial_modes = mix_block(spectral_weight, x_modes)
    partial_modes = partial_modes.reshape(units, kz_local, 2, channels // 2, 2, KX)
    half_index = index_x * units // KY
    own_half = lax.dynamic_index_in_dim(partial_modes, half_index, 2, keepdims=False)
    other_half = lax.dynamic_index_in_dim(partial_modes, 1 - half_index, 2, keepdims=False)
    mixed_modes = own_half + swapped(other_half, "px", count_x.bit_length() - 2)
    ix_cos, ix_sin = trig_pair(mode_numbers(KX), width_x, width_x, KX ** (-0.5), jnp.float32)
    x_values = inverse_last(mixed_modes, ix_cos.T, ix_sin.T, highest).astype(jnp.bfloat16)
    returned = lax.all_to_all(x_values, "px", split_axis=4, concat_axis=0, tiled=True)
    returned = returned.reshape(2, KY, kz_local, channels // 2, 2, cells_x).transpose(
        2, 0, 3, 5, 4, 1
    )
    returned = returned.reshape(kz_local, channels, cells_x, 2, KY)
    iy_cos, iy_sin = trig_pair(mode_numbers(KY), width_y, width_y, KY ** (-0.5), jnp.bfloat16)
    expanded = inverse_last(returned, iy_cos.T, iy_sin.T).astype(jnp.bfloat16)
    y_values = lax.all_to_all(expanded, "py", split_axis=4, concat_axis=0, tiled=True)
    iz_cos, iz_sin = trig_pair(
        jnp.arange(KZ, dtype=jnp.int32), depth, depth, KZ ** (-0.5), jnp.bfloat16
    )
    iz_table = jnp.stack([iz_cos.T, -iz_sin.T], axis=0)
    spectral = jnp.einsum("kcxwy,wkn->cxyn", y_values, iz_table, preferred_element_type=jnp.float32)
    total = convolved + spectral + conv_bias[:, None, None, None]
    return jax.nn.gelu(total, approximate=False).astype(jnp.bfloat16)


def angle_tables(numbers, points, length, factor):
    phases = (np.arange(points)[:, None] * numbers[None, :]) % length
    angles = phases.astype(np.float32) * np.float32(2.0 * math.pi / length)
    return (
        np.cos(angles).astype(np.float32) * np.float32(factor),
        np.sin(angles).astype(np.float32) * np.float32(factor),
    )


def signed_modes(count):
    indices = np.arange(count)
    return np.where(indices < count // 2, indices, indices - count)


def narrow(table):
    return table.astype(ml_dtypes.bfloat16).astype(np.float32)


def forward_pair(cosine, sine):
    return np.stack([np.stack([cosine, -sine]), np.stack([sine, cosine])])


def inverse_pair(cosine, sine):
    return np.stack([np.stack([cosine, sine]), np.stack([-sine, cosine])])


@functools.cache
def tables(count_x, count_y, cells_x, cells_y, depth):
    width_x, width_y = count_x * cells_x, count_y * cells_y
    kzl, units = KZ // count_y, 2 * KY // count_x
    groups = KY // units
    zc, zs = angle_tables(np.arange(KZ), depth, depth, depth**-0.5)
    z_forward = np.concatenate([zc.T, -zs.T])
    yc, ys = angle_tables(signed_modes(KY), width_y, width_y, width_y**-0.5)
    pair = forward_pair(yc, ys).reshape(2, 2, count_y, cells_y, groups, units)
    y_forward = np.einsum("rsqygk,d,w->qrygwskd", pair, np.ones(8), np.ones(cells_x))
    y_forward = y_forward.reshape(count_y, 2 * cells_y, groups * 2 * cells_x * units * 8)
    xc, xs = angle_tables(signed_modes(KX), width_x, width_x, width_x**-0.5)
    pair = forward_pair(xc, xs).reshape(2, 2, count_x, cells_x, KX)
    x_forward = np.einsum("rspxk,gh,q->gskpqhxr", pair, np.eye(2), np.ones(count_y))
    x_forward = x_forward.reshape(4 * KX, count_x * count_y * 4 * cells_x)
    xc, xs = angle_tables(signed_modes(KX), width_x, width_x, KX**-0.5)
    pair = inverse_pair(xc, xs).reshape(2, 2, count_x, cells_x, KX)
    x_inverse = np.einsum("rspxk,zv->pxzsvrk", pair, np.eye(kzl))
    x_inverse = x_inverse.reshape(count_x * cells_x * kzl * 2, kzl * 2 * KX)
    zc, zs = angle_tables(np.arange(KZ), depth, depth, KZ**-0.5)
    pair = inverse_pair(zc, zs).reshape(2, 2, depth, count_y, kzl)
    z_inverse = np.einsum("rsnqz,xw,h->hqxzrwsn", pair, np.eye(cells_x), np.ones(2))
    z_inverse = z_inverse.reshape(4 * cells_x * KZ, cells_x * 2 * depth)
    yc, ys = angle_tables(signed_modes(KY), width_y, width_y, KY**-0.5)
    pair = np.stack([yc, -ys]).reshape(2, count_y, cells_y, KY)
    y_inverse = np.einsum("rqyk,i->qyrki", pair, np.ones(16))
    y_inverse = y_inverse.reshape(count_y, cells_y, 32 * KY)
    return (
        narrow(z_forward),
        narrow(y_forward),
        narrow(x_forward),
        x_inverse.astype(np.float32),
        narrow(z_inverse),
        narrow(y_inverse),
    )


def block_moves(value):
    rows = value.shape[0]
    tiles = value.reshape(rows // 8, 8, 128)
    row = lax.broadcasted_iota(jnp.int32, tiles.shape, 1) % 4
    block = lax.broadcasted_iota(jnp.int32, tiles.shape, 2) // 32
    result = tiles
    for lane_step in (1, 2, 3):
        moved = pltpu.roll(tiles, 128 - 32 * lane_step, 2)
        result = jnp.where(row - block == lane_step, pltpu.roll(moved, lane_step, 1), result)
        result = jnp.where(
            row - block == lane_step - 4, pltpu.roll(moved, 8 + lane_step - 4, 1), result
        )
    return result


def forward_kernel(state_hbm, z_hbm, y_hbm, out_ref, state_ref, z_ref, y_ref, table_ref, sems):
    count = state_ref.shape[0] // 4
    span = state_ref.shape[1]
    y_copy = pltpu.make_async_copy(y_hbm.at[lax.axis_index("py")], y_ref, sems.at[0])
    z_copy = pltpu.make_async_copy(z_hbm, z_ref, sems.at[1])
    copies = [
        pltpu.make_async_copy(
            state_hbm.at[pl.ds(g * count, count)],
            state_ref.at[pl.ds(g * count, count)],
            sems.at[2 + g],
        )
        for g in range(4)
    ]
    for copy in [y_copy, z_copy] + copies:
        copy.start()
    y_copy.wait()
    table = y_ref[...]
    lane = lax.broadcasted_iota(jnp.int32, (span, table.shape[1]), 1)
    for x in range(2):
        for c in range(8):
            own = (lane % 8 == c) & (lane // 64 % 2 == x)
            for part in range(2):
                first = part * 16 * span + (c * 2 + x) * span
                block = jnp.where(own, table[part * span : (part + 1) * span], 0.0)
                table_ref[first : first + span] = block.astype(jnp.bfloat16)
    z_copy.wait()
    z_table = z_ref[...].astype(jnp.bfloat16)
    pieces = []
    for g in range(4):
        copies[g].wait()
        cells = state_ref[g * count : (g + 1) * count].reshape(count * span, state_ref.shape[2])
        z_modes = lax.dot_general(
            z_table, cells, (((1,), (1,)), ((), ())), preferred_element_type=jnp.float32
        ).astype(jnp.bfloat16)
        pieces.append(jnp.concatenate([z_modes[:KZ], z_modes[KZ:]], axis=1))
    stacked = jnp.concatenate(pieces, axis=0)
    modes = jnp.dot(stacked, table_ref[...], preferred_element_type=jnp.float32)
    for group in range(4):
        moved = block_moves(modes[:, group * 128 : (group + 1) * 128])
        for half in range(2):
            for pair in range(2):
                first = moved[half * 4 + pair]
                second = moved[half * 4 + 2 + pair]
                for side in range(2):
                    rows4 = slice(4 * side, 4 * side + 4)
                    chunk = jnp.concatenate([first[rows4], second[rows4]], axis=0)
                    out_ref[(half * 4 + group) * 4 + 2 * pair + side] = chunk.astype(jnp.bfloat16)


def forward_modes(state, z_table, y_table):
    return pl.pallas_call(
        forward_kernel,
        out_shape=jax.ShapeDtypeStruct((32, 8, 128), jnp.bfloat16),
        in_specs=[pl.BlockSpec(memory_space=pltpu.HBM)] * 3,
        out_specs=pl.BlockSpec(memory_space=pltpu.VMEM),
        scratch_shapes=[
            pltpu.VMEM(state.shape, jnp.bfloat16),
            pltpu.VMEM(z_table.shape, jnp.float32),
            pltpu.VMEM(y_table.shape[1:], jnp.float32),
            pltpu.VMEM((32 * state.shape[1], y_table.shape[2]), jnp.bfloat16),
            pltpu.SemaphoreType.DMA((6,)),
        ],
        compiler_params=pltpu.CompilerParams(vmem_limit_bytes=16 * 2**20),
        cost_estimate=pl.CostEstimate(flops=2**27, bytes_accessed=2**21, transcendentals=0),
        name="forward_modes",
    )(*(pltpu.with_memory_space_constraint(v, pltpu.HBM) for v in (state, z_table, y_table)))


def prepare_kernel(
    after_ref,
    state_hbm,
    weight_hbm,
    conv_hbm,
    first_ref,
    second_ref,
    conv_out,
    weight_out,
    state_ref,
    weight_ref,
    conv_ref,
    wide,
    sems,
):
    state_copy = pltpu.make_async_copy(state_hbm, state_ref, sems.at[8])
    conv_copy = pltpu.make_async_copy(conv_hbm, conv_ref, sems.at[9])
    copies = [
        pltpu.make_async_copy(
            weight_hbm.at[part, kz], weight_ref.at[part, kz], sems.at[part * 4 + kz]
        )
        for part in range(2)
        for kz in range(4)
    ]
    for copy in [state_copy, conv_copy] + copies:
        copy.start()
    odd_x = lax.rem(lax.axis_index("px"), 2)
    state_copy.wait()
    cells_y = state_ref.shape[2]
    for slot, (out_ref, x) in enumerate(((first_ref, 1 - odd_x), (second_ref, odd_x))):
        wide[slot] = state_ref[:, x].astype(jnp.float32).reshape(32 * cells_y, 128)
        for y in range(cells_y):
            out_ref[y] = wide[slot, pl.ds(y, 32, stride=cells_y), :].astype(jnp.bfloat16)
    conv_copy.wait()
    zero = jnp.zeros((32, 32), jnp.float32)
    for dz in range(3):
        taps = {
            (dx, dy): conv_ref[dx, dy, dz].astype(jnp.float32)
            for dx in range(3)
            for dy in range(3)
        }
        for y_at in range(2):
            for x_at in range(2):
                row = ((dz * 2 + y_at) * 2 + x_at) * 32
                for y_in in range(4):
                    blocks = [taps.get((x_in - x_at, y_in - y_at), zero) for x_in in range(4)]
                    blocks = [jnp.where(odd_x == 1, blocks[i], blocks[3 - i]) for i in range(4)]
                    conv_out[row : row + 32, y_in * 128 : (y_in + 1) * 128] = jnp.concatenate(
                        blocks, axis=1
                    ).astype(jnp.bfloat16)
    for part in range(2):
        for kz in range(4):
            copies[part * 4 + kz].wait()
            for c in range(16):
                weight_out[part, kz, c] = jnp.concatenate(
                    [weight_ref[part, kz, u, c] for u in range(4)], axis=1
                )


def prepare(after, state, spectral_weight, conv_weight):
    vmem = pl.BlockSpec(memory_space=pltpu.VMEM)
    cells_y = state.shape[2]
    plane = jax.ShapeDtypeStruct((cells_y, 32, 128), jnp.bfloat16)
    return pl.pallas_call(
        prepare_kernel,
        out_shape=(
            plane,
            plane,
            jax.ShapeDtypeStruct((384, 512), jnp.bfloat16),
            jax.ShapeDtypeStruct((2, 4, 16, KX, 128), jnp.float32),
        ),
        in_specs=[pl.BlockSpec(memory_space=pl.ANY)] + [pl.BlockSpec(memory_space=pltpu.HBM)] * 3,
        out_specs=(vmem,) * 4,
        scratch_shapes=[
            pltpu.VMEM(state.shape, jnp.bfloat16),
            pltpu.VMEM(spectral_weight.shape, jnp.float32),
            pltpu.VMEM(conv_weight.shape, jnp.bfloat16),
            pltpu.VMEM((2, 32 * cells_y, 128), jnp.float32),
            pltpu.SemaphoreType.DMA((10,)),
        ],
        compiler_params=pltpu.CompilerParams(vmem_limit_bytes=16 * 2**20),
        cost_estimate=pl.CostEstimate(flops=2**10, bytes_accessed=2**10, transcendentals=0),
        name="prepare_operands",
    )(
        after,
        *(
            pltpu.with_memory_space_constraint(v, pltpu.HBM)
            for v in (state, spectral_weight, conv_weight)
        ),
    )


def mix_kernel(modes_ref, forward_ref, weight_ref, inverse_ref, out_ref):
    received = modes_ref[...].astype(jnp.float32).reshape(256, 128).astype(jnp.bfloat16)
    x_modes = jnp.dot(
        forward_ref[...].astype(jnp.bfloat16), received, preferred_element_type=jnp.float32)
    lane = lax.broadcasted_iota(jnp.int32, (16, 128), 1)
    base = (lane // 32) * 8
    mixed = []
    for kz in range(4):
        real_sum = imag_sum = None
        for c in range(16):
            half, c8 = c // 8, c % 8
            index = base + (kz * 32 + c8)
            real_in = jnp.take_along_axis(x_modes[half * 32 : half * 32 + 16], index, axis=1)
            imag_in = jnp.take_along_axis(x_modes[half * 32 + 16 : half * 32 + 32], index, axis=1)
            real_weight = weight_ref[0, kz, c]
            imag_weight = weight_ref[1, kz, c]
            real_term = real_weight * real_in - imag_weight * imag_in
            imag_term = real_weight * imag_in + imag_weight * real_in
            real_sum = real_term if real_sum is None else real_sum + real_term
            imag_sum = imag_term if imag_sum is None else imag_sum + imag_term
        mixed += [real_sum, imag_sum]
    values = jnp.dot(
        inverse_ref[...],
        jnp.concatenate(mixed, axis=0),
        preferred_element_type=jnp.float32,
        precision=lax.Precision.HIGHEST,
    ).astype(jnp.bfloat16)
    for x in range(8):
        for y in range(4):
            out_ref[x * 4 + y] = values[16 * x : 16 * x + 16]


def mix_modes(modes, forward_table, weights, inverse_table):
    vmem = pl.BlockSpec(memory_space=pltpu.VMEM)
    return pl.pallas_call(
        mix_kernel,
        out_shape=jax.ShapeDtypeStruct((32, 16, 128), jnp.bfloat16),
        in_specs=[vmem] * 4,
        out_specs=vmem,
        compiler_params=pltpu.CompilerParams(vmem_limit_bytes=16 * 2**20),
        cost_estimate=pl.CostEstimate(flops=2**35, bytes_accessed=2**21, transcendentals=0),
        name="mix_modes",
    )(modes, forward_table, weights, inverse_table)


def cell_row(planes, y):
    return jnp.concatenate([plane[y] for plane in planes], axis=0)


def edge_rows_kernel(*refs):
    *planes, first_ref, second_ref = refs
    end = planes[0].shape[0] - 1
    odd_y = lax.rem(lax.axis_index("py"), 2)
    first_ref[...] = cell_row(planes, (1 - odd_y) * end)
    second_ref[...] = cell_row(planes, odd_y * end)


def edge_rows(planes):
    vmem = pl.BlockSpec(memory_space=pltpu.VMEM)
    row = jax.ShapeDtypeStruct((128, 128), jnp.bfloat16)
    return pl.pallas_call(
        edge_rows_kernel,
        out_shape=(row, row),
        in_specs=[vmem] * 4,
        out_specs=(vmem, vmem),
        compiler_params=pltpu.CompilerParams(vmem_limit_bytes=16 * 2**20),
        cost_estimate=pl.CostEstimate(flops=2**10, bytes_accessed=2**17, transcendentals=0),
        name="edge_rows",
    )(*planes)


def convolve_quad(quad, row, weight, place, out_ref):
    lane = lax.broadcasted_iota(jnp.int32, (128, 256), 1) % 128
    windows = []
    for pair in range(2):
        start = quad * 4 + pair * 2 - 1
        windows.append(jnp.concatenate([row(start + i) for i in range(4)], axis=0))
    product = jnp.dot(weight, jnp.concatenate(windows, axis=1), preferred_element_type=jnp.float32)
    below = pltpu.roll(product[:128], 1, 1)
    above = pltpu.roll(product[256:], 255, 1)
    total = product[128:256] + jnp.where(lane == 0, 0.0, below)
    total = total + jnp.where(lane == 127, 0.0, above)
    for pair in range(2):
        for y_out in range(2):
            for x_out in range(2):
                first = (y_out * 2 + x_out) * 32
                value = total[first : first + 32, pair * 128 : (pair + 1) * 128]
                y = quad * 4 + pair * 2 + y_out
                at, span = place(y)
                out_ref[pl.ds(x_out * span + at, 32, stride=2 * span), :] = value


def interior_kernel(*refs):
    *planes, weight_ref, y_ref, out_ref, y_out = refs
    cells_y = planes[0].shape[0]
    table = y_ref[lax.axis_index("py")]
    lane = lax.broadcasted_iota(jnp.int32, table.shape, 1) % 16
    for o in range(16):
        y_out[o * cells_y : (o + 1) * cells_y] = jnp.where(lane == o, table, 0.0).astype(
            jnp.bfloat16
        )
    weight = weight_ref[...]
    for quad in range(1, cells_y // 4 - 1):
        convolve_quad(
            quad, lambda y: cell_row(planes, y), weight, lambda y: (y, cells_y), out_ref
        )


def edge_kernel(*refs):
    *planes, first_row, second_row, weight_ref, out_ref = refs
    cells_y = planes[0].shape[0]
    odd_y = lax.rem(lax.axis_index("py"), 2) == 1

    def row(y):
        if y < 0:
            return jnp.where(odd_y, first_row[...], second_row[...])
        if y >= cells_y:
            return jnp.where(odd_y, second_row[...], first_row[...])
        return cell_row(planes, y)

    weight = weight_ref[...]
    for quad in (0, cells_y // 4 - 1):
        convolve_quad(quad, row, weight, lambda y: (y % 8, 8), out_ref)


def convolve(kernel, name, operands, out_shape):
    vmem = pl.BlockSpec(memory_space=pltpu.VMEM)
    return pl.pallas_call(
        kernel,
        out_shape=out_shape,
        in_specs=[vmem] * len(operands),
        out_specs=(vmem,) * len(out_shape),
        compiler_params=pltpu.CompilerParams(vmem_limit_bytes=16 * 2**20),
        cost_estimate=pl.CostEstimate(flops=2**30, bytes_accessed=2**21, transcendentals=0),
        name=name,
    )(*operands)


def gelu(value):
    return 0.5 * value * (1.0 + lax.erf(value * math.sqrt(0.5)))


def finish_kernel(
    bias_ref, values_ref, z_ref, y_ref, conv_ref, edge_ref, out_hbm, out_ref, sems
):
    upper = lax.broadcasted_iota(jnp.int32, (8, 128), 0) < 4
    columns = []
    for group in range(4):
        columns.append(
            jnp.concatenate(
                [values_ref[(h * 4 + group) * 4 + q] for h in range(2) for q in range(4)], axis=0
            )
        )
    packed = jnp.concatenate(columns, axis=1)
    z_values = lax.dot_general(
        packed,
        z_ref[...].astype(jnp.bfloat16),
        (((0,), (0,)), ((), ())),
        preferred_element_type=jnp.float32,
    ).astype(jnp.bfloat16)
    copies = []
    for half in range(2):
        sides = []
        for x in range(2):
            parts = []
            for part in range(2):
                lanes = slice((x * 2 + part) * 128, (x * 2 + part + 1) * 128)
                parts += [
                    z_values[ky * 32 + half * 16 : ky * 32 + half * 16 + 16, lanes]
                    for ky in range(KY)
                ]
            sides.append(jnp.concatenate(parts, axis=0))
        right = jnp.concatenate(sides, axis=1)
        for block in range(4):
            spectral = jnp.dot(
                y_ref[block * 128 : (block + 1) * 128], right, preferred_element_type=jnp.float32
            )
            for o4 in range(4):
                o = half * 16 + block * 4 + o4
                for x in range(2):
                    inner, edge = conv_ref[o, x], edge_ref[o, x]
                    convolved = jnp.concatenate(
                        [
                            jnp.where(upper, edge, inner[:8]),
                            inner[8:-8],
                            jnp.where(upper, inner[-8:], edge),
                        ],
                        axis=0,
                    )
                    total = spectral[o4 * 32 : o4 * 32 + 32, x * 128 : (x + 1) * 128]
                    total = total + convolved + bias_ref[o]
                    out_ref[o, x] = gelu(total).astype(jnp.bfloat16)
            number = half * 4 + block
            copy = pltpu.make_async_copy(
                out_ref.at[pl.ds(number * 4, 4)], out_hbm.at[pl.ds(number * 4, 4)], sems.at[number]
            )
            copy.start()
            copies.append(copy)
    for copy in copies:
        copy.wait()


def finish(bias, values, z_table, y_table, convolved, edges):
    vmem = pl.BlockSpec(memory_space=pltpu.VMEM)
    return pl.pallas_call(
        finish_kernel,
        out_shape=jax.ShapeDtypeStruct(convolved.shape, jnp.bfloat16),
        in_specs=[pl.BlockSpec(memory_space=pltpu.SMEM)] + [vmem] * 5,
        out_specs=pl.BlockSpec(memory_space=pltpu.HBM),
        scratch_shapes=[
            pltpu.VMEM(convolved.shape, jnp.bfloat16),
            pltpu.SemaphoreType.DMA((8,)),
        ],
        compiler_params=pltpu.CompilerParams(vmem_limit_bytes=16 * 2**20),
        cost_estimate=pl.CostEstimate(flops=2**28, bytes_accessed=2**22, transcendentals=2**18),
        name="finish_layer",
    )(bias, values, z_table, y_table, convolved, edges)


def exchanged(value):
    return lax.all_to_all(value, ("px", "py"), split_axis=0, concat_axis=0, tiled=True)


def swaps(first, second, axis):
    count = lax.axis_size(axis)
    inside = [(i, i ^ 1) for i in range(count)]
    across = [(i, i + 1 if i % 2 else i - 1) for i in range(1, count - 1)]
    return lax.ppermute(first, axis, inside), lax.ppermute(second, axis, across)


def body(state_field, conv_weight, conv_bias, spectral_weight):
    channels, cells_x, cells_y, depth = state_field.shape
    sizes = (lax.axis_size("px"), lax.axis_size("py"), cells_x, cells_y, depth)
    if sizes != (8, 4, 2, 32, 128):
        return general_body(state_field, conv_weight, conv_bias, spectral_weight)
    z_forward, y_forward, x_forward, x_inverse, z_inverse, y_inverse = tables(*sizes)
    sent = forward_modes(
        state_field.reshape(channels * cells_x, cells_y, depth), z_forward, y_forward
    )
    modes = exchanged(sent)
    first_own, second_own, taps, weights = prepare(
        sent, state_field, spectral_weight.swapaxes(4, 5), conv_weight.transpose(2, 3, 4, 0, 1)
    )
    first_plane, second_plane = swaps(first_own, second_own, "px")
    values = exchanged(mix_modes(modes, x_forward, weights, x_inverse))
    planes = (first_plane, first_own, second_own, second_plane)
    first_row, second_row = swaps(*edge_rows(planes), "py")
    rows = channels * cells_x
    interior, y_expanded = convolve(
        interior_kernel,
        "convolve_interior",
        planes + (taps, y_inverse),
        (
            jax.ShapeDtypeStruct((rows * cells_y, depth), jnp.float32),
            jax.ShapeDtypeStruct((16 * cells_y, y_inverse.shape[2]), jnp.bfloat16),
        ),
    )
    (edges,) = convolve(
        edge_kernel,
        "convolve_edges",
        planes + (first_row, second_row, taps),
        (jax.ShapeDtypeStruct((rows * 8, depth), jnp.float32),),
    )
    return finish(
        conv_bias,
        values,
        z_inverse,
        y_expanded,
        interior.reshape(channels, cells_x, cells_y, depth),
        edges.reshape(channels, cells_x, 8, depth),
    )


def solution(mesh):
    in_specs = (P(None, "px", "py", None), P(), P(), P(None, "py", "px", None, None, None))
    out_specs = P(None, "px", "py", None)
    return jax.shard_map(body, mesh=mesh, in_specs=in_specs, out_specs=out_specs, check_vma=False)
```

```python
import functools
import math

import jax
import jax.numpy as jnp
import ml_dtypes
import numpy as np
from jax import lax
from jax.experimental import pallas as pl
from jax.experimental.pallas import tpu as pltpu
from jax.sharding import PartitionSpec as P

KX = 16
KY = 16
KZ = 16


def extended(cells, sides, width):
    for axis, dim in sides:
        count = lax.axis_size(axis)
        ends = count - 1
        head = lax.slice_in_dim(cells, 0, width, axis=dim)
        tail = lax.slice_in_dim(cells, cells.shape[dim] - width, cells.shape[dim], axis=dim)
        cells = jnp.concatenate(
            [
                lax.ppermute(tail, axis, [(i, (i + 1) % count) for i in range(ends)]),
                cells,
                lax.ppermute(head, axis, [((i + 1) % count, i) for i in range(ends)]),
            ],
            axis=dim,
        )
    return cells


def swapped(value, axis, distance):
    mask = 2**distance
    pairs = [(source, source ^ mask) for source in range(lax.axis_size(axis))]
    return lax.ppermute(value, axis, pairs)


def mode_numbers(count):
    indices = jnp.arange(count, dtype=jnp.int32)
    return jnp.where(indices < count // 2, indices, indices - count)


def trig_pair(numbers, points, length, factor, out_type):
    positions = jnp.arange(points, dtype=jnp.int32)
    phases = positions[:, None] * numbers[None, :] % length
    angles = phases.astype(jnp.float32) * (2.0 * math.pi / length)
    return (
        (jnp.cos(angles) * factor).astype(out_type),
        (jnp.sin(angles) * factor).astype(out_type),
    )


def last_product(source, table, precision=None):
    flat = source.reshape(-1, source.shape[-1])
    result = jnp.dot(flat, table, preferred_element_type=jnp.float32, precision=precision)
    return result.reshape(source.shape[:-1] + (table.shape[1],))


def forward_last(source, cosine, sine_table, precision=None):
    real_part = source[..., 0, :]
    imag_part = source[..., 1, :]
    real_out = last_product(real_part, cosine, precision) + last_product(
        imag_part, sine_table, precision
    )
    imag_out = last_product(imag_part, cosine, precision) - last_product(
        real_part, sine_table, precision
    )
    return jnp.stack([real_out, imag_out], axis=-2)


def inverse_last(source, cosine, sine_table, precision=None):
    real_part = source[..., 0, :]
    imag_part = source[..., 1, :]
    real_out = last_product(real_part, cosine, precision) - last_product(
        imag_part, sine_table, precision
    )
    imag_out = last_product(real_part, sine_table, precision) + last_product(
        imag_part, cosine, precision
    )
    return jnp.stack([real_out, imag_out], axis=-2)


def mix_block(spectral_weight, x_block):
    highest = lax.Precision.HIGHEST
    real_in = x_block[:, :, :, 0, :]
    imag_in = x_block[:, :, :, 1, :]
    partial_real = jnp.einsum(
        "zucok,uzck->uzok", spectral_weight[0], real_in, precision=highest
    ) - jnp.einsum("zucok,uzck->uzok", spectral_weight[1], imag_in, precision=highest)
    partial_imag = jnp.einsum(
        "zucok,uzck->uzok", spectral_weight[0], imag_in, precision=highest
    ) + jnp.einsum("zucok,uzck->uzok", spectral_weight[1], real_in, precision=highest)
    return jnp.stack([partial_real, partial_imag], axis=3)


def general_body(state_field, conv_weight, conv_bias, spectral_weight):
    channels, cells_x, cells_y, depth = state_field.shape
    count_x = lax.axis_size("px")
    count_y = lax.axis_size("py")
    width_x = cells_x * count_x
    width_y = cells_y * count_y
    index_x = lax.axis_index("px")
    kz_local = KZ // count_y
    units = 2 * KY // count_x
    highest = lax.Precision.HIGHEST
    padded = extended(state_field, (("px", 1), ("py", 2)), 1)
    convolved = lax.conv_general_dilated(
        padded[None],
        conv_weight,
        (1, 1, 1),
        ((0, 0), (0, 0), (1, 1)),
        dimension_numbers=("NCDHW", "OIDHW", "NCDHW"),
        preferred_element_type=jnp.float32,
    )[0]
    z_cos, z_sin = trig_pair(
        jnp.arange(KZ, dtype=jnp.int32), depth, depth, depth ** (-0.5), jnp.bfloat16
    )
    z_table = jnp.stack([z_cos, -z_sin], axis=1)
    z_modes = jnp.einsum(
        "cxyn,nwk->kcxwy", state_field, z_table, preferred_element_type=jnp.float32
    ).astype(jnp.bfloat16)
    y_cos, y_sin = trig_pair(mode_numbers(KY), width_y, width_y, width_y ** (-0.5), jnp.bfloat16)
    full_rows = lax.all_to_all(z_modes, "py", split_axis=0, concat_axis=4, tiled=True)
    y_modes = forward_last(full_rows, y_cos, y_sin)
    y_modes = y_modes.astype(jnp.bfloat16)
    by_unit = y_modes.reshape(kz_local, 2, channels // 2, cells_x, 2, KY).transpose(
        1, 5, 0, 2, 4, 3
    )
    by_unit = by_unit.reshape(2 * KY, kz_local, channels // 2, 2, cells_x)
    x_rows = lax.all_to_all(by_unit, "px", split_axis=0, concat_axis=4, tiled=True)
    x_cos, x_sin = trig_pair(mode_numbers(KX), width_x, width_x, width_x ** (-0.5), jnp.bfloat16)
    x_modes = forward_last(x_rows, x_cos, x_sin)
    partial_modes = mix_block(spectral_weight, x_modes)
    partial_modes = partial_modes.reshape(units, kz_local, 2, channels // 2, 2, KX)
    half_index = index_x * units // KY
    own_half = lax.dynamic_index_in_dim(partial_modes, half_index, 2, keepdims=False)
    other_half = lax.dynamic_index_in_dim(partial_modes, 1 - half_index, 2, keepdims=False)
    mixed_modes = own_half + swapped(other_half, "px", count_x.bit_length() - 2)
    ix_cos, ix_sin = trig_pair(mode_numbers(KX), width_x, width_x, KX ** (-0.5), jnp.float32)
    x_values = inverse_last(mixed_modes, ix_cos.T, ix_sin.T, highest).astype(jnp.bfloat16)
    returned = lax.all_to_all(x_values, "px", split_axis=4, concat_axis=0, tiled=True)
    returned = returned.reshape(2, KY, kz_local, channels // 2, 2, cells_x).transpose(
        2, 0, 3, 5, 4, 1
    )
    returned = returned.reshape(kz_local, channels, cells_x, 2, KY)
    iy_cos, iy_sin = trig_pair(mode_numbers(KY), width_y, width_y, KY ** (-0.5), jnp.bfloat16)
    expanded = inverse_last(returned, iy_cos.T, iy_sin.T).astype(jnp.bfloat16)
    y_values = lax.all_to_all(expanded, "py", split_axis=4, concat_axis=0, tiled=True)
    iz_cos, iz_sin = trig_pair(
        jnp.arange(KZ, dtype=jnp.int32), depth, depth, KZ ** (-0.5), jnp.bfloat16
    )
    iz_table = jnp.stack([iz_cos.T, -iz_sin.T], axis=0)
    spectral = jnp.einsum("kcxwy,wkn->cxyn", y_values, iz_table, preferred_element_type=jnp.float32)
    total = convolved + spectral + conv_bias[:, None, None, None]
    return jax.nn.gelu(total, approximate=False).astype(jnp.bfloat16)


def angle_tables(numbers, points, length, factor):
    phases = (np.arange(points)[:, None] * numbers[None, :]) % length
    angles = phases.astype(np.float32) * np.float32(2.0 * math.pi / length)
    return (
        np.cos(angles).astype(np.float32) * np.float32(factor),
        np.sin(angles).astype(np.float32) * np.float32(factor),
    )


def signed_modes(count):
    indices = np.arange(count)
    return np.where(indices < count // 2, indices, indices - count)


def narrow(table):
    return table.astype(ml_dtypes.bfloat16).astype(np.float32)


def forward_pair(cosine, sine):
    return np.stack([np.stack([cosine, -sine]), np.stack([sine, cosine])])


def inverse_pair(cosine, sine):
    return np.stack([np.stack([cosine, sine]), np.stack([-sine, cosine])])


@functools.cache
def tables(count_x, count_y, cells_x, cells_y, depth):
    width_x, width_y = count_x * cells_x, count_y * cells_y
    kzl, units = KZ // count_y, 2 * KY // count_x
    groups = KY // units
    zc, zs = angle_tables(np.arange(KZ), depth, depth, depth**-0.5)
    z_forward = np.concatenate([zc.T, -zs.T])
    yc, ys = angle_tables(signed_modes(KY), width_y, width_y, width_y**-0.5)
    pair = forward_pair(yc, ys).reshape(2, 2, count_y, cells_y, groups, units)
    y_forward = np.einsum("rsqygk,d,w->qrygwskd", pair, np.ones(8), np.ones(cells_x))
    y_forward = y_forward.reshape(count_y, 2 * cells_y, groups * 2 * cells_x * units * 8)
    xc, xs = angle_tables(signed_modes(KX), width_x, width_x, width_x**-0.5)
    pair = forward_pair(xc, xs).reshape(2, 2, count_x, cells_x, KX)
    x_forward = np.einsum("rspxk,gh,q->gskpqhxr", pair, np.eye(2), np.ones(count_y))
    x_forward = x_forward.reshape(4 * KX, count_x * count_y * 4 * cells_x)
    xc, xs = angle_tables(signed_modes(KX), width_x, width_x, KX**-0.5)
    pair = inverse_pair(xc, xs).reshape(2, 2, count_x, cells_x, KX)
    x_inverse = np.einsum("rspxk,zv->pxzsvrk", pair, np.eye(kzl))
    x_inverse = x_inverse.reshape(count_x * cells_x * kzl * 2, kzl * 2 * KX)
    zc, zs = angle_tables(np.arange(KZ), depth, depth, KZ**-0.5)
    pair = inverse_pair(zc, zs).reshape(2, 2, depth, count_y, kzl)
    z_inverse = np.einsum("rsnqz,xw,h->hqxzrwsn", pair, np.eye(cells_x), np.ones(2))
    z_inverse = z_inverse.reshape(4 * cells_x * KZ, cells_x * 2 * depth)
    yc, ys = angle_tables(signed_modes(KY), width_y, width_y, KY**-0.5)
    pair = np.stack([yc, -ys]).reshape(2, count_y, cells_y, KY)
    y_inverse = np.einsum("rqyk,i->qyrki", pair, np.ones(16))
    y_inverse = y_inverse.reshape(count_y, cells_y, 32 * KY)
    return (
        narrow(z_forward),
        narrow(y_forward),
        narrow(x_forward),
        x_inverse.astype(np.float32),
        narrow(z_inverse),
        narrow(y_inverse),
    )


def block_moves(value):
    rows = value.shape[0]
    tiles = value.reshape(rows // 8, 8, 128)
    row = lax.broadcasted_iota(jnp.int32, tiles.shape, 1) % 4
    block = lax.broadcasted_iota(jnp.int32, tiles.shape, 2) // 32
    result = tiles
    for lane_step in (1, 2, 3):
        moved = pltpu.roll(tiles, 128 - 32 * lane_step, 2)
        result = jnp.where(row - block == lane_step, pltpu.roll(moved, lane_step, 1), result)
        result = jnp.where(
            row - block == lane_step - 4, pltpu.roll(moved, 8 + lane_step - 4, 1), result
        )
    return result


def forward_kernel(state_hbm, z_hbm, y_hbm, out_ref, state_ref, z_ref, y_ref, table_ref, sems):
    count = state_ref.shape[0] // 4
    span = state_ref.shape[1]
    y_copy = pltpu.make_async_copy(y_hbm.at[lax.axis_index("py")], y_ref, sems.at[0])
    z_copy = pltpu.make_async_copy(z_hbm, z_ref, sems.at[1])
    copies = [
        pltpu.make_async_copy(
            state_hbm.at[pl.ds(g * count, count)],
            state_ref.at[pl.ds(g * count, count)],
            sems.at[2 + g],
        )
        for g in range(4)
    ]
    for copy in [y_copy, z_copy] + copies:
        copy.start()
    y_copy.wait()
    table = y_ref[...]
    lane = lax.broadcasted_iota(jnp.int32, (span, table.shape[1]), 1)
    for x in range(2):
        for c in range(8):
            own = (lane % 8 == c) & (lane // 64 % 2 == x)
            for part in range(2):
                first = part * 16 * span + (c * 2 + x) * span
                block = jnp.where(own, table[part * span : (part + 1) * span], 0.0)
                table_ref[first : first + span] = block.astype(jnp.bfloat16)
    z_copy.wait()
    z_table = z_ref[...].astype(jnp.bfloat16)
    pieces = []
    for g in range(4):
        copies[g].wait()
        cells = state_ref[g * count : (g + 1) * count].reshape(count * span, state_ref.shape[2])
        z_modes = lax.dot_general(
            z_table, cells, (((1,), (1,)), ((), ())), preferred_element_type=jnp.float32
        ).astype(jnp.bfloat16)
        pieces.append(jnp.concatenate([z_modes[:KZ], z_modes[KZ:]], axis=1))
    stacked = jnp.concatenate(pieces, axis=0)
    modes = jnp.dot(stacked, table_ref[...], preferred_element_type=jnp.float32)
    for group in range(4):
        moved = block_moves(modes[:, group * 128 : (group + 1) * 128])
        for half in range(2):
            for pair in range(2):
                first = moved[half * 4 + pair]
                second = moved[half * 4 + 2 + pair]
                for side in range(2):
                    rows4 = slice(4 * side, 4 * side + 4)
                    chunk = jnp.concatenate([first[rows4], second[rows4]], axis=0)
                    out_ref[(half * 4 + group) * 4 + 2 * pair + side] = chunk.astype(jnp.bfloat16)


def forward_modes(state, z_table, y_table):
    return pl.pallas_call(
        forward_kernel,
        out_shape=jax.ShapeDtypeStruct((32, 8, 128), jnp.bfloat16),
        in_specs=[pl.BlockSpec(memory_space=pltpu.HBM)] * 3,
        out_specs=pl.BlockSpec(memory_space=pltpu.VMEM),
        scratch_shapes=[
            pltpu.VMEM(state.shape, jnp.bfloat16),
            pltpu.VMEM(z_table.shape, jnp.float32),
            pltpu.VMEM(y_table.shape[1:], jnp.float32),
            pltpu.VMEM((32 * state.shape[1], y_table.shape[2]), jnp.bfloat16),
            pltpu.SemaphoreType.DMA((6,)),
        ],
        compiler_params=pltpu.CompilerParams(vmem_limit_bytes=16 * 2**20),
        cost_estimate=pl.CostEstimate(flops=2**27, bytes_accessed=2**21, transcendentals=0),
        name="forward_modes",
    )(*(pltpu.with_memory_space_constraint(v, pltpu.HBM) for v in (state, z_table, y_table)))


def arrange_kernel(after_ref, state_ref, conv_ref, first_ref, second_ref, conv_out, wide):
    odd_x = lax.rem(lax.axis_index("px"), 2)
    cells_y = state_ref.shape[2]
    for slot, (out_ref, x) in enumerate(((first_ref, odd_x), (second_ref, 1 - odd_x))):
        wide[slot] = state_ref[:, x].astype(jnp.float32).reshape(32 * cells_y, 128)
        for y in range(cells_y):
            out_ref[y] = wide[slot, pl.ds(y, 32, stride=cells_y), :].astype(jnp.bfloat16)
    zero = jnp.zeros((32, 32), jnp.float32)
    for dz in range(3):
        taps = {
            (dx, dy): conv_ref[dx, dy, dz].astype(jnp.float32)
            for dx in range(3)
            for dy in range(3)
        }
        for y_at in range(2):
            for x_at in range(2):
                row = ((dz * 2 + y_at) * 2 + x_at) * 32
                for y_in in range(4):
                    blocks = [taps.get((x_in - x_at, y_in - y_at), zero) for x_in in range(4)]
                    blocks = [jnp.where(odd_x == 1, blocks[3 - i], blocks[i]) for i in range(4)]
                    conv_out[row : row + 32, y_in * 128 : (y_in + 1) * 128] = jnp.concatenate(
                        blocks, axis=1
                    ).astype(jnp.bfloat16)


def arrange(after, state, conv_weight):
    vmem = pl.BlockSpec(memory_space=pltpu.VMEM)
    cells_y = state.shape[2]
    plane = jax.ShapeDtypeStruct((cells_y, 32, 128), jnp.bfloat16)
    return pl.pallas_call(
        arrange_kernel,
        out_shape=(plane, plane, jax.ShapeDtypeStruct((384, 512), jnp.bfloat16)),
        in_specs=[pl.BlockSpec(memory_space=pl.ANY), vmem, vmem],
        out_specs=(vmem,) * 3,
        scratch_shapes=[pltpu.VMEM((2, 32 * cells_y, 128), jnp.float32)],
        compiler_params=pltpu.CompilerParams(vmem_limit_bytes=16 * 2**20),
        cost_estimate=pl.CostEstimate(flops=2**10, bytes_accessed=2**10, transcendentals=0),
        name="arrange_cells",
    )(after, state, conv_weight)


def pack_kernel(after_ref, weight_ref, weight_out):
    for part in range(2):
        for kz in range(4):
            for c in range(16):
                weight_out[part, kz, c] = jnp.concatenate(
                    [weight_ref[part, kz, u, c] for u in range(4)], axis=1
                )


def pack(after, spectral_weight):
    vmem = pl.BlockSpec(memory_space=pltpu.VMEM)
    return pl.pallas_call(
        pack_kernel,
        out_shape=jax.ShapeDtypeStruct((2, 4, 16, KX, 128), jnp.float32),
        in_specs=[pl.BlockSpec(memory_space=pl.ANY), vmem],
        out_specs=vmem,
        compiler_params=pltpu.CompilerParams(vmem_limit_bytes=16 * 2**20),
        cost_estimate=pl.CostEstimate(flops=2**10, bytes_accessed=2**10, transcendentals=0),
        name="pack_weights",
    )(after, spectral_weight)


def mix_kernel(modes_ref, forward_ref, weight_ref, inverse_ref, out_ref):
    received = modes_ref[...].astype(jnp.float32).reshape(256, 128).astype(jnp.bfloat16)
    x_modes = jnp.dot(
        forward_ref[...].astype(jnp.bfloat16), received, preferred_element_type=jnp.float32)
    lane = lax.broadcasted_iota(jnp.int32, (16, 128), 1)
    base = (lane // 32) * 8
    mixed = []
    for kz in range(4):
        real_sum = imag_sum = None
        for c in range(16):
            half, c8 = c // 8, c % 8
            index = base + (kz * 32 + c8)
            real_in = jnp.take_along_axis(x_modes[half * 32 : half * 32 + 16], index, axis=1)
            imag_in = jnp.take_along_axis(x_modes[half * 32 + 16 : half * 32 + 32], index, axis=1)
            real_weight = weight_ref[0, kz, c]
            imag_weight = weight_ref[1, kz, c]
            real_term = real_weight * real_in - imag_weight * imag_in
            imag_term = real_weight * imag_in + imag_weight * real_in
            real_sum = real_term if real_sum is None else real_sum + real_term
            imag_sum = imag_term if imag_sum is None else imag_sum + imag_term
        mixed += [real_sum, imag_sum]
    values = jnp.dot(
        inverse_ref[...],
        jnp.concatenate(mixed, axis=0),
        preferred_element_type=jnp.float32,
        precision=lax.Precision.HIGHEST,
    ).astype(jnp.bfloat16)
    for x in range(8):
        for y in range(4):
            out_ref[x * 4 + y] = values[16 * x : 16 * x + 16]


def mix_modes(modes, forward_table, weights, inverse_table):
    vmem = pl.BlockSpec(memory_space=pltpu.VMEM)
    return pl.pallas_call(
        mix_kernel,
        out_shape=jax.ShapeDtypeStruct((32, 16, 128), jnp.bfloat16),
        in_specs=[vmem] * 4,
        out_specs=vmem,
        compiler_params=pltpu.CompilerParams(vmem_limit_bytes=16 * 2**20),
        cost_estimate=pl.CostEstimate(flops=2**35, bytes_accessed=2**21, transcendentals=0),
        name="mix_modes",
    )(modes, forward_table, weights, inverse_table)


def cell_row(planes, y):
    return jnp.concatenate([plane[y] for plane in planes], axis=0)


def edge_rows_kernel(*refs):
    *planes, first_ref, second_ref = refs
    end = planes[0].shape[0] - 1
    odd_y = lax.rem(lax.axis_index("py"), 2)
    first_ref[...] = cell_row(planes, odd_y * end)
    second_ref[...] = cell_row(planes, (1 - odd_y) * end)


def edge_rows(planes):
    vmem = pl.BlockSpec(memory_space=pltpu.VMEM)
    row = jax.ShapeDtypeStruct((128, 128), jnp.bfloat16)
    return pl.pallas_call(
        edge_rows_kernel,
        out_shape=(row, row),
        in_specs=[vmem] * 4,
        out_specs=(vmem, vmem),
        compiler_params=pltpu.CompilerParams(vmem_limit_bytes=16 * 2**20),
        cost_estimate=pl.CostEstimate(flops=2**10, bytes_accessed=2**17, transcendentals=0),
        name="edge_rows",
    )(*planes)


def convolve_quad(quad, row, weight, place, out_ref):
    lane = lax.broadcasted_iota(jnp.int32, (128, 256), 1) % 128
    windows = []
    for pair in range(2):
        start = quad * 4 + pair * 2 - 1
        windows.append(jnp.concatenate([row(start + i) for i in range(4)], axis=0))
    product = jnp.dot(weight, jnp.concatenate(windows, axis=1), preferred_element_type=jnp.float32)
    below = pltpu.roll(product[:128], 1, 1)
    above = pltpu.roll(product[256:], 255, 1)
    total = product[128:256] + jnp.where(lane == 0, 0.0, below)
    total = total + jnp.where(lane == 127, 0.0, above)
    for pair in range(2):
        for y_out in range(2):
            for x_out in range(2):
                first = (y_out * 2 + x_out) * 32
                value = total[first : first + 32, pair * 128 : (pair + 1) * 128]
                y = quad * 4 + pair * 2 + y_out
                at, span = place(y)
                out_ref[pl.ds(x_out * span + at, 32, stride=2 * span), :] = value


def interior_kernel(*refs):
    *planes, weight_ref, y_hbm, out_ref, y_out, y_ref, y_sem = refs
    cells_y = planes[0].shape[0]
    y_copy = pltpu.make_async_copy(y_hbm.at[lax.axis_index("py")], y_ref, y_sem)
    y_copy.start()
    weight = weight_ref[...]
    for quad in range(1, cells_y // 4 - 1):
        convolve_quad(
            quad, lambda y: cell_row(planes, y), weight, lambda y: (y, cells_y), out_ref
        )
    y_copy.wait()
    table = y_ref[...]
    lane = lax.broadcasted_iota(jnp.int32, table.shape, 1) % 16
    for o in range(16):
        y_out[o * cells_y : (o + 1) * cells_y] = jnp.where(lane == o, table, 0.0).astype(
            jnp.bfloat16
        )


def edge_kernel(*refs):
    *planes, first_row, second_row, weight_ref, out_ref = refs
    cells_y = planes[0].shape[0]
    odd_y = lax.rem(lax.axis_index("py"), 2) == 1

    def row(y):
        if y < 0:
            return jnp.where(odd_y, second_row[...], first_row[...])
        if y >= cells_y:
            return jnp.where(odd_y, first_row[...], second_row[...])
        return cell_row(planes, y)

    weight = weight_ref[...]
    for quad in (0, cells_y // 4 - 1):
        convolve_quad(quad, row, weight, lambda y: (y % 8, 8), out_ref)


def convolve(kernel, name, operands, out_shape, fetched=(), scratch=()):
    vmem = pl.BlockSpec(memory_space=pltpu.VMEM)
    return pl.pallas_call(
        kernel,
        out_shape=out_shape,
        in_specs=[vmem] * len(operands) + [pl.BlockSpec(memory_space=pltpu.HBM)] * len(fetched),
        out_specs=(vmem,) * len(out_shape),
        scratch_shapes=scratch,
        compiler_params=pltpu.CompilerParams(vmem_limit_bytes=16 * 2**20),
        cost_estimate=pl.CostEstimate(flops=2**30, bytes_accessed=2**21, transcendentals=0),
        name=name,
    )(*operands, *(pltpu.with_memory_space_constraint(v, pltpu.HBM) for v in fetched))


def gelu(value):
    return 0.5 * value * (1.0 + lax.erf(value * math.sqrt(0.5)))


def finish_kernel(
    bias_ref, values_ref, z_ref, y_ref, conv_ref, edge_ref, out_hbm, out_ref, sems
):
    upper = lax.broadcasted_iota(jnp.int32, (8, 128), 0) < 4
    columns = []
    for group in range(4):
        columns.append(
            jnp.concatenate(
                [values_ref[(h * 4 + group) * 4 + q] for h in range(2) for q in range(4)], axis=0
            )
        )
    packed = jnp.concatenate(columns, axis=1)
    z_values = lax.dot_general(
        packed,
        z_ref[...].astype(jnp.bfloat16),
        (((0,), (0,)), ((), ())),
        preferred_element_type=jnp.float32,
    ).astype(jnp.bfloat16)
    copies = []
    for half in range(2):
        sides = []
        for x in range(2):
            parts = []
            for part in range(2):
                lanes = slice((x * 2 + part) * 128, (x * 2 + part + 1) * 128)
                parts += [
                    z_values[ky * 32 + half * 16 : ky * 32 + half * 16 + 16, lanes]
                    for ky in range(KY)
                ]
            sides.append(jnp.concatenate(parts, axis=0))
        right = jnp.concatenate(sides, axis=1)
        for block in range(4):
            spectral = jnp.dot(
                y_ref[block * 128 : (block + 1) * 128], right, preferred_element_type=jnp.float32
            )
            for o4 in range(4):
                o = half * 16 + block * 4 + o4
                for x in range(2):
                    inner, edge = conv_ref[o, x], edge_ref[o, x]
                    convolved = jnp.concatenate(
                        [
                            jnp.where(upper, edge, inner[:8]),
                            inner[8:-8],
                            jnp.where(upper, inner[-8:], edge),
                        ],
                        axis=0,
                    )
                    total = spectral[o4 * 32 : o4 * 32 + 32, x * 128 : (x + 1) * 128]
                    total = total + convolved + bias_ref[o]
                    out_ref[o, x] = gelu(total).astype(jnp.bfloat16)
            number = half * 4 + block
            copy = pltpu.make_async_copy(
                out_ref.at[pl.ds(number * 4, 4)], out_hbm.at[pl.ds(number * 4, 4)], sems.at[number]
            )
            copy.start()
            copies.append(copy)
    for copy in copies:
        copy.wait()


def finish(bias, values, z_table, y_table, convolved, edges):
    vmem = pl.BlockSpec(memory_space=pltpu.VMEM)
    return pl.pallas_call(
        finish_kernel,
        out_shape=jax.ShapeDtypeStruct(convolved.shape, jnp.bfloat16),
        in_specs=[pl.BlockSpec(memory_space=pltpu.SMEM)] + [vmem] * 5,
        out_specs=pl.BlockSpec(memory_space=pltpu.HBM),
        scratch_shapes=[
            pltpu.VMEM(convolved.shape, jnp.bfloat16),
            pltpu.SemaphoreType.DMA((8,)),
        ],
        compiler_params=pltpu.CompilerParams(vmem_limit_bytes=16 * 2**20),
        cost_estimate=pl.CostEstimate(flops=2**28, bytes_accessed=2**22, transcendentals=2**18),
        name="finish_layer",
    )(bias, values, z_table, y_table, convolved, edges)


def exchanged(value):
    return lax.all_to_all(value, ("px", "py"), split_axis=0, concat_axis=0, tiled=True)


def swaps(first, second, axis):
    count = lax.axis_size(axis)
    inside = [(i, i ^ 1) for i in range(count)]
    across = [(i, i + 1 if i % 2 else i - 1) for i in range(1, count - 1)]
    return lax.ppermute(first, axis, across), lax.ppermute(second, axis, inside)


def body(state_field, conv_weight, conv_bias, spectral_weight):
    channels, cells_x, cells_y, depth = state_field.shape
    sizes = (lax.axis_size("px"), lax.axis_size("py"), cells_x, cells_y, depth)
    if sizes != (8, 4, 2, 32, 128):
        return general_body(state_field, conv_weight, conv_bias, spectral_weight)
    z_forward, y_forward, x_forward, x_inverse, z_inverse, y_inverse = tables(*sizes)
    sent = forward_modes(
        state_field.reshape(channels * cells_x, cells_y, depth), z_forward, y_forward
    )
    modes = exchanged(sent)
    first_own, second_own, taps = arrange(sent, state_field, conv_weight.transpose(2, 3, 4, 0, 1))
    weights = pack(taps, spectral_weight.swapaxes(4, 5))
    first_plane, second_plane = swaps(first_own, second_own, "px")
    values = exchanged(mix_modes(modes, x_forward, weights, x_inverse))
    planes = (first_plane, first_own, second_own, second_plane)
    first_row, second_row = swaps(*edge_rows(planes), "py")
    rows = channels * cells_x
    interior, y_expanded = convolve(
        interior_kernel,
        "convolve_interior",
        planes + (taps,),
        (
            jax.ShapeDtypeStruct((rows * cells_y, depth), jnp.float32),
            jax.ShapeDtypeStruct((16 * cells_y, y_inverse.shape[2]), jnp.bfloat16),
        ),
        (y_inverse,),
        (pltpu.VMEM(y_inverse.shape[1:], jnp.float32), pltpu.SemaphoreType.DMA),
    )
    (edges,) = convolve(
        edge_kernel,
        "convolve_edges",
        planes + (first_row, second_row, taps),
        (jax.ShapeDtypeStruct((rows * 8, depth), jnp.float32),),
    )
    return finish(
        conv_bias,
        values,
        z_inverse,
        y_expanded,
        interior.reshape(channels, cells_x, cells_y, depth),
        edges.reshape(channels, cells_x, 8, depth),
    )


def solution(mesh):
    in_specs = (P(None, "px", "py", None), P(), P(), P(None, "py", "px", None, None, None))
    out_specs = P(None, "px", "py", None)
    return jax.shard_map(body, mesh=mesh, in_specs=in_specs, out_specs=out_specs, check_vma=False)
```

```python
import functools
import math

import jax
import jax.numpy as jnp
import ml_dtypes
import numpy as np
from jax import lax
from jax.experimental import pallas as pl
from jax.experimental.pallas import tpu as pltpu
from jax.sharding import PartitionSpec as P

KX = 16
KY = 16
KZ = 16


def extended(cells, sides, width):
    for axis, dim in sides:
        count = lax.axis_size(axis)
        ends = count - 1
        head = lax.slice_in_dim(cells, 0, width, axis=dim)
        tail = lax.slice_in_dim(cells, cells.shape[dim] - width, cells.shape[dim], axis=dim)
        cells = jnp.concatenate(
            [
                lax.ppermute(tail, axis, [(i, (i + 1) % count) for i in range(ends)]),
                cells,
                lax.ppermute(head, axis, [((i + 1) % count, i) for i in range(ends)]),
            ],
            axis=dim,
        )
    return cells


def swapped(value, axis, distance):
    mask = 2**distance
    pairs = [(source, source ^ mask) for source in range(lax.axis_size(axis))]
    return lax.ppermute(value, axis, pairs)


def mode_numbers(count):
    indices = jnp.arange(count, dtype=jnp.int32)
    return jnp.where(indices < count // 2, indices, indices - count)


def trig_pair(numbers, points, length, factor, out_type):
    positions = jnp.arange(points, dtype=jnp.int32)
    phases = positions[:, None] * numbers[None, :] % length
    angles = phases.astype(jnp.float32) * (2.0 * math.pi / length)
    return (
        (jnp.cos(angles) * factor).astype(out_type),
        (jnp.sin(angles) * factor).astype(out_type),
    )


def last_product(source, table, precision=None):
    flat = source.reshape(-1, source.shape[-1])
    result = jnp.dot(flat, table, preferred_element_type=jnp.float32, precision=precision)
    return result.reshape(source.shape[:-1] + (table.shape[1],))


def forward_last(source, cosine, sine_table, precision=None):
    real_part = source[..., 0, :]
    imag_part = source[..., 1, :]
    real_out = last_product(real_part, cosine, precision) + last_product(
        imag_part, sine_table, precision
    )
    imag_out = last_product(imag_part, cosine, precision) - last_product(
        real_part, sine_table, precision
    )
    return jnp.stack([real_out, imag_out], axis=-2)


def inverse_last(source, cosine, sine_table, precision=None):
    real_part = source[..., 0, :]
    imag_part = source[..., 1, :]
    real_out = last_product(real_part, cosine, precision) - last_product(
        imag_part, sine_table, precision
    )
    imag_out = last_product(real_part, sine_table, precision) + last_product(
        imag_part, cosine, precision
    )
    return jnp.stack([real_out, imag_out], axis=-2)


def mix_block(spectral_weight, x_block):
    highest = lax.Precision.HIGHEST
    real_in = x_block[:, :, :, 0, :]
    imag_in = x_block[:, :, :, 1, :]
    partial_real = jnp.einsum(
        "zucok,uzck->uzok", spectral_weight[0], real_in, precision=highest
    ) - jnp.einsum("zucok,uzck->uzok", spectral_weight[1], imag_in, precision=highest)
    partial_imag = jnp.einsum(
        "zucok,uzck->uzok", spectral_weight[0], imag_in, precision=highest
    ) + jnp.einsum("zucok,uzck->uzok", spectral_weight[1], real_in, precision=highest)
    return jnp.stack([partial_real, partial_imag], axis=3)


def general_body(state_field, conv_weight, conv_bias, spectral_weight):
    channels, cells_x, cells_y, depth = state_field.shape
    count_x = lax.axis_size("px")
    count_y = lax.axis_size("py")
    width_x = cells_x * count_x
    width_y = cells_y * count_y
    index_x = lax.axis_index("px")
    kz_local = KZ // count_y
    units = 2 * KY // count_x
    highest = lax.Precision.HIGHEST
    padded = extended(state_field, (("px", 1), ("py", 2)), 1)
    convolved = lax.conv_general_dilated(
        padded[None],
        conv_weight,
        (1, 1, 1),
        ((0, 0), (0, 0), (1, 1)),
        dimension_numbers=("NCDHW", "OIDHW", "NCDHW"),
        preferred_element_type=jnp.float32,
    )[0]
    z_cos, z_sin = trig_pair(
        jnp.arange(KZ, dtype=jnp.int32), depth, depth, depth ** (-0.5), jnp.bfloat16
    )
    z_table = jnp.stack([z_cos, -z_sin], axis=1)
    z_modes = jnp.einsum(
        "cxyn,nwk->kcxwy", state_field, z_table, preferred_element_type=jnp.float32
    ).astype(jnp.bfloat16)
    y_cos, y_sin = trig_pair(mode_numbers(KY), width_y, width_y, width_y ** (-0.5), jnp.bfloat16)
    full_rows = lax.all_to_all(z_modes, "py", split_axis=0, concat_axis=4, tiled=True)
    y_modes = forward_last(full_rows, y_cos, y_sin)
    y_modes = y_modes.astype(jnp.bfloat16)
    by_unit = y_modes.reshape(kz_local, 2, channels // 2, cells_x, 2, KY).transpose(
        1, 5, 0, 2, 4, 3
    )
    by_unit = by_unit.reshape(2 * KY, kz_local, channels // 2, 2, cells_x)
    x_rows = lax.all_to_all(by_unit, "px", split_axis=0, concat_axis=4, tiled=True)
    x_cos, x_sin = trig_pair(mode_numbers(KX), width_x, width_x, width_x ** (-0.5), jnp.bfloat16)
    x_modes = forward_last(x_rows, x_cos, x_sin)
    partial_modes = mix_block(spectral_weight, x_modes)
    partial_modes = partial_modes.reshape(units, kz_local, 2, channels // 2, 2, KX)
    half_index = index_x * units // KY
    own_half = lax.dynamic_index_in_dim(partial_modes, half_index, 2, keepdims=False)
    other_half = lax.dynamic_index_in_dim(partial_modes, 1 - half_index, 2, keepdims=False)
    mixed_modes = own_half + swapped(other_half, "px", count_x.bit_length() - 2)
    ix_cos, ix_sin = trig_pair(mode_numbers(KX), width_x, width_x, KX ** (-0.5), jnp.float32)
    x_values = inverse_last(mixed_modes, ix_cos.T, ix_sin.T, highest).astype(jnp.bfloat16)
    returned = lax.all_to_all(x_values, "px", split_axis=4, concat_axis=0, tiled=True)
    returned = returned.reshape(2, KY, kz_local, channels // 2, 2, cells_x).transpose(
        2, 0, 3, 5, 4, 1
    )
    returned = returned.reshape(kz_local, channels, cells_x, 2, KY)
    iy_cos, iy_sin = trig_pair(mode_numbers(KY), width_y, width_y, KY ** (-0.5), jnp.bfloat16)
    expanded = inverse_last(returned, iy_cos.T, iy_sin.T).astype(jnp.bfloat16)
    y_values = lax.all_to_all(expanded, "py", split_axis=4, concat_axis=0, tiled=True)
    iz_cos, iz_sin = trig_pair(
        jnp.arange(KZ, dtype=jnp.int32), depth, depth, KZ ** (-0.5), jnp.bfloat16
    )
    iz_table = jnp.stack([iz_cos.T, -iz_sin.T], axis=0)
    spectral = jnp.einsum("kcxwy,wkn->cxyn", y_values, iz_table, preferred_element_type=jnp.float32)
    total = convolved + spectral + conv_bias[:, None, None, None]
    return jax.nn.gelu(total, approximate=False).astype(jnp.bfloat16)


def angle_tables(numbers, points, length, factor):
    phases = (np.arange(points)[:, None] * numbers[None, :]) % length
    angles = phases.astype(np.float32) * np.float32(2.0 * math.pi / length)
    return (
        np.cos(angles).astype(np.float32) * np.float32(factor),
        np.sin(angles).astype(np.float32) * np.float32(factor),
    )


def signed_modes(count):
    indices = np.arange(count)
    return np.where(indices < count // 2, indices, indices - count)


def narrow(table):
    return table.astype(ml_dtypes.bfloat16).astype(np.float32)


def forward_pair(cosine, sine):
    return np.stack([np.stack([cosine, -sine]), np.stack([sine, cosine])])


def inverse_pair(cosine, sine):
    return np.stack([np.stack([cosine, sine]), np.stack([-sine, cosine])])


@functools.cache
def tables(count_x, count_y, cells_x, cells_y, depth):
    width_x, width_y = count_x * cells_x, count_y * cells_y
    kzl, units = KZ // count_y, 2 * KY // count_x
    groups = KY // units
    zc, zs = angle_tables(np.arange(KZ), depth, depth, depth**-0.5)
    z_forward = np.concatenate([zc.T, -zs.T])
    yc, ys = angle_tables(signed_modes(KY), width_y, width_y, width_y**-0.5)
    pair = forward_pair(yc, ys).reshape(2, 2, count_y, cells_y, groups, units)
    y_forward = np.einsum("rsqygk,d,w->qrygwskd", pair, np.ones(8), np.ones(cells_x))
    y_forward = y_forward.reshape(count_y, 2 * cells_y, groups * 2 * cells_x * units * 8)
    xc, xs = angle_tables(signed_modes(KX), width_x, width_x, width_x**-0.5)
    pair = forward_pair(xc, xs).reshape(2, 2, count_x, cells_x, KX)
    x_forward = np.einsum("rspxk,gh,q->gskpqhxr", pair, np.eye(2), np.ones(count_y))
    x_forward = x_forward.reshape(4 * KX, count_x * count_y * 4 * cells_x)
    xc, xs = angle_tables(signed_modes(KX), width_x, width_x, KX**-0.5)
    pair = inverse_pair(xc, xs).reshape(2, 2, count_x, cells_x, KX)
    x_inverse = np.einsum("rspxk,zv->pxzsvrk", pair, np.eye(kzl))
    x_inverse = x_inverse.reshape(count_x * cells_x * kzl * 2, kzl * 2 * KX)
    zc, zs = angle_tables(np.arange(KZ), depth, depth, KZ**-0.5)
    pair = inverse_pair(zc, zs).reshape(2, 2, depth, count_y, kzl)
    z_inverse = np.einsum("rsnqz,xw,h->hqxzrwsn", pair, np.eye(cells_x), np.ones(2))
    z_inverse = z_inverse.reshape(4 * cells_x * KZ, cells_x * 2 * depth)
    yc, ys = angle_tables(signed_modes(KY), width_y, width_y, KY**-0.5)
    pair = np.stack([yc, -ys]).reshape(2, count_y, cells_y, KY)
    y_inverse = np.einsum("rqyk,i->qyrki", pair, np.ones(16))
    y_inverse = y_inverse.reshape(count_y, cells_y, 32 * KY)
    return (
        narrow(z_forward),
        narrow(y_forward),
        narrow(x_forward),
        x_inverse.astype(np.float32),
        narrow(z_inverse),
        narrow(y_inverse),
    )


def block_moves(value):
    rows = value.shape[0]
    tiles = value.reshape(rows // 8, 8, 128)
    row = lax.broadcasted_iota(jnp.int32, tiles.shape, 1) % 4
    block = lax.broadcasted_iota(jnp.int32, tiles.shape, 2) // 32
    result = tiles
    for lane_step in (1, 2, 3):
        moved = pltpu.roll(tiles, 128 - 32 * lane_step, 2)
        result = jnp.where(row - block == lane_step, pltpu.roll(moved, lane_step, 1), result)
        result = jnp.where(
            row - block == lane_step - 4, pltpu.roll(moved, 8 + lane_step - 4, 1), result
        )
    return result


def forward_kernel(state_hbm, z_hbm, y_hbm, out_ref, state_ref, z_ref, y_ref, table_ref, sems):
    count = state_ref.shape[0] // 4
    span = state_ref.shape[1]
    y_copy = pltpu.make_async_copy(y_hbm.at[lax.axis_index("py")], y_ref, sems.at[0])
    z_copy = pltpu.make_async_copy(z_hbm, z_ref, sems.at[1])
    copies = [
        pltpu.make_async_copy(
            state_hbm.at[pl.ds(g * count, count)],
            state_ref.at[pl.ds(g * count, count)],
            sems.at[2 + g],
        )
        for g in range(4)
    ]
    for copy in [y_copy, z_copy] + copies:
        copy.start()
    y_copy.wait()
    table = y_ref[...]
    lane = lax.broadcasted_iota(jnp.int32, (span, table.shape[1]), 1)
    for x in range(2):
        for c in range(8):
            own = (lane % 8 == c) & (lane // 64 % 2 == x)
            for part in range(2):
                first = part * 16 * span + (c * 2 + x) * span
                block = jnp.where(own, table[part * span : (part + 1) * span], 0.0)
                table_ref[first : first + span] = block.astype(jnp.bfloat16)
    z_copy.wait()
    z_table = z_ref[...].astype(jnp.bfloat16)
    pieces = []
    for g in range(4):
        copies[g].wait()
        cells = state_ref[g * count : (g + 1) * count].reshape(count * span, state_ref.shape[2])
        z_modes = lax.dot_general(
            z_table, cells, (((1,), (1,)), ((), ())), preferred_element_type=jnp.float32
        ).astype(jnp.bfloat16)
        pieces.append(jnp.concatenate([z_modes[:KZ], z_modes[KZ:]], axis=1))
    stacked = jnp.concatenate(pieces, axis=0)
    modes = jnp.dot(stacked, table_ref[...], preferred_element_type=jnp.float32)
    for group in range(4):
        moved = block_moves(modes[:, group * 128 : (group + 1) * 128])
        for half in range(2):
            for pair in range(2):
                first = moved[half * 4 + pair]
                second = moved[half * 4 + 2 + pair]
                for side in range(2):
                    rows4 = slice(4 * side, 4 * side + 4)
                    chunk = jnp.concatenate([first[rows4], second[rows4]], axis=0)
                    out_ref[(half * 4 + group) * 4 + 2 * pair + side] = chunk.astype(jnp.bfloat16)


def forward_modes(state, z_table, y_table):
    return pl.pallas_call(
        forward_kernel,
        out_shape=(
            jax.ShapeDtypeStruct((32, 8, 128), jnp.bfloat16),
            jax.ShapeDtypeStruct(state.shape, jnp.bfloat16),
        ),
        in_specs=[pl.BlockSpec(memory_space=pltpu.HBM)] * 3,
        out_specs=(pl.BlockSpec(memory_space=pltpu.VMEM),) * 2,
        scratch_shapes=[
            pltpu.VMEM(z_table.shape, jnp.float32),
            pltpu.VMEM(y_table.shape[1:], jnp.float32),
            pltpu.VMEM((32 * state.shape[1], y_table.shape[2]), jnp.bfloat16),
            pltpu.SemaphoreType.DMA((6,)),
        ],
        compiler_params=pltpu.CompilerParams(vmem_limit_bytes=16 * 2**20),
        cost_estimate=pl.CostEstimate(flops=2**27, bytes_accessed=2**21, transcendentals=0),
        name="forward_modes",
    )(*(pltpu.with_memory_space_constraint(v, pltpu.HBM) for v in (state, z_table, y_table)))


def arrange_kernel(state_ref, first_ref, second_ref, wide):
    odd_x = lax.rem(lax.axis_index("px"), 2)
    cells_y = state_ref.shape[2]
    for slot, (out_ref, x) in enumerate(((first_ref, odd_x), (second_ref, 1 - odd_x))):
        wide[slot] = state_ref[:, x].astype(jnp.float32).reshape(32 * cells_y, 128)
        for y in range(cells_y):
            out_ref[y] = wide[slot, pl.ds(y, 32, stride=cells_y), :].astype(jnp.bfloat16)


def arrange(state):
    vmem = pl.BlockSpec(memory_space=pltpu.VMEM)
    cells_y = state.shape[2]
    plane = jax.ShapeDtypeStruct((cells_y, 32, 128), jnp.bfloat16)
    return pl.pallas_call(
        arrange_kernel,
        out_shape=(plane, plane),
        in_specs=[vmem],
        out_specs=(vmem, vmem),
        scratch_shapes=[pltpu.VMEM((2, 32 * cells_y, 128), jnp.float32)],
        compiler_params=pltpu.CompilerParams(vmem_limit_bytes=16 * 2**20),
        cost_estimate=pl.CostEstimate(flops=2**10, bytes_accessed=2**10, transcendentals=0),
        name="arrange_cells",
    )(state)


def pack_kernel(
    after_ref, weight_hbm, conv_hbm, weight_out, conv_out, weight_ref, conv_ref, sems
):
    conv_copy = pltpu.make_async_copy(conv_hbm, conv_ref, sems.at[8])
    copies = [
        pltpu.make_async_copy(
            weight_hbm.at[part, kz], weight_ref.at[part, kz], sems.at[part * 4 + kz]
        )
        for part in range(2)
        for kz in range(4)
    ]
    for copy in [conv_copy] + copies:
        copy.start()
    odd_x = lax.rem(lax.axis_index("px"), 2)
    conv_copy.wait()
    zero = jnp.zeros((32, 32), jnp.float32)
    for dz in range(3):
        taps = {
            (dx, dy): conv_ref[dx, dy, dz].astype(jnp.float32)
            for dx in range(3)
            for dy in range(3)
        }
        for y_at in range(2):
            for x_at in range(2):
                row = ((dz * 2 + y_at) * 2 + x_at) * 32
                for y_in in range(4):
                    blocks = [taps.get((x_in - x_at, y_in - y_at), zero) for x_in in range(4)]
                    blocks = [jnp.where(odd_x == 1, blocks[3 - i], blocks[i]) for i in range(4)]
                    conv_out[row : row + 32, y_in * 128 : (y_in + 1) * 128] = jnp.concatenate(
                        blocks, axis=1
                    ).astype(jnp.bfloat16)
    for part in range(2):
        for kz in range(4):
            copies[part * 4 + kz].wait()
            for c in range(16):
                weight_out[part, kz, c] = jnp.concatenate(
                    [weight_ref[part, kz, u, c] for u in range(4)], axis=1
                )


def pack(after, spectral_weight, conv_weight):
    vmem = pl.BlockSpec(memory_space=pltpu.VMEM)
    return pl.pallas_call(
        pack_kernel,
        out_shape=(
            jax.ShapeDtypeStruct((2, 4, 16, KX, 128), jnp.float32),
            jax.ShapeDtypeStruct((384, 512), jnp.bfloat16),
        ),
        in_specs=[pl.BlockSpec(memory_space=pl.ANY)] + [pl.BlockSpec(memory_space=pltpu.HBM)] * 2,
        out_specs=(vmem, vmem),
        scratch_shapes=[
            pltpu.VMEM(spectral_weight.shape, jnp.float32),
            pltpu.VMEM(conv_weight.shape, jnp.bfloat16),
            pltpu.SemaphoreType.DMA((9,)),
        ],
        compiler_params=pltpu.CompilerParams(vmem_limit_bytes=16 * 2**20),
        cost_estimate=pl.CostEstimate(flops=2**10, bytes_accessed=2**10, transcendentals=0),
        name="pack_weights",
    )(
        after,
        *(pltpu.with_memory_space_constraint(v, pltpu.HBM) for v in (spectral_weight, conv_weight)),
    )


def mix_kernel(modes_ref, forward_ref, weight_ref, inverse_ref, out_ref):
    received = modes_ref[...].astype(jnp.float32).reshape(256, 128).astype(jnp.bfloat16)
    x_modes = jnp.dot(
        forward_ref[...].astype(jnp.bfloat16), received, preferred_element_type=jnp.float32)
    lane = lax.broadcasted_iota(jnp.int32, (16, 128), 1)
    base = (lane // 32) * 8
    mixed = []
    for kz in range(4):
        real_sum = imag_sum = None
        for c in range(16):
            half, c8 = c // 8, c % 8
            index = base + (kz * 32 + c8)
            real_in = jnp.take_along_axis(x_modes[half * 32 : half * 32 + 16], index, axis=1)
            imag_in = jnp.take_along_axis(x_modes[half * 32 + 16 : half * 32 + 32], index, axis=1)
            real_weight = weight_ref[0, kz, c]
            imag_weight = weight_ref[1, kz, c]
            real_term = real_weight * real_in - imag_weight * imag_in
            imag_term = real_weight * imag_in + imag_weight * real_in
            real_sum = real_term if real_sum is None else real_sum + real_term
            imag_sum = imag_term if imag_sum is None else imag_sum + imag_term
        mixed += [real_sum, imag_sum]
    values = jnp.dot(
        inverse_ref[...],
        jnp.concatenate(mixed, axis=0),
        preferred_element_type=jnp.float32,
        precision=lax.Precision.HIGHEST,
    ).astype(jnp.bfloat16)
    for x in range(8):
        for y in range(4):
            out_ref[x * 4 + y] = values[16 * x : 16 * x + 16]


def mix_modes(modes, forward_table, weights, inverse_table):
    vmem = pl.BlockSpec(memory_space=pltpu.VMEM)
    return pl.pallas_call(
        mix_kernel,
        out_shape=jax.ShapeDtypeStruct((32, 16, 128), jnp.bfloat16),
        in_specs=[vmem] * 4,
        out_specs=vmem,
        compiler_params=pltpu.CompilerParams(vmem_limit_bytes=16 * 2**20),
        cost_estimate=pl.CostEstimate(flops=2**35, bytes_accessed=2**21, transcendentals=0),
        name="mix_modes",
    )(modes, forward_table, weights, inverse_table)


def cell_row(planes, y):
    return jnp.concatenate([plane[y] for plane in planes], axis=0)


def edge_rows_kernel(*refs):
    *planes, first_ref, second_ref = refs
    end = planes[0].shape[0] - 1
    odd_y = lax.rem(lax.axis_index("py"), 2)
    first_ref[...] = cell_row(planes, odd_y * end)
    second_ref[...] = cell_row(planes, (1 - odd_y) * end)


def edge_rows(planes):
    vmem = pl.BlockSpec(memory_space=pltpu.VMEM)
    row = jax.ShapeDtypeStruct((128, 128), jnp.bfloat16)
    return pl.pallas_call(
        edge_rows_kernel,
        out_shape=(row, row),
        in_specs=[vmem] * 4,
        out_specs=(vmem, vmem),
        compiler_params=pltpu.CompilerParams(vmem_limit_bytes=16 * 2**20),
        cost_estimate=pl.CostEstimate(flops=2**10, bytes_accessed=2**17, transcendentals=0),
        name="edge_rows",
    )(*planes)


def convolve_quad(quad, row, weight, place, out_ref):
    lane = lax.broadcasted_iota(jnp.int32, (128, 256), 1) % 128
    windows = []
    for pair in range(2):
        start = quad * 4 + pair * 2 - 1
        windows.append(jnp.concatenate([row(start + i) for i in range(4)], axis=0))
    product = jnp.dot(weight, jnp.concatenate(windows, axis=1), preferred_element_type=jnp.float32)
    below = pltpu.roll(product[:128], 1, 1)
    above = pltpu.roll(product[256:], 255, 1)
    total = product[128:256] + jnp.where(lane == 0, 0.0, below)
    total = total + jnp.where(lane == 127, 0.0, above)
    for pair in range(2):
        for y_out in range(2):
            for x_out in range(2):
                first = (y_out * 2 + x_out) * 32
                value = total[first : first + 32, pair * 128 : (pair + 1) * 128]
                y = quad * 4 + pair * 2 + y_out
                at, span = place(y)
                out_ref[pl.ds(x_out * span + at, 32, stride=2 * span), :] = value


def interior_kernel(*refs):
    *planes, weight_ref, out_ref = refs
    cells_y = planes[0].shape[0]
    weight = weight_ref[...]
    for quad in range(1, cells_y // 4 - 1):
        convolve_quad(
            quad, lambda y: cell_row(planes, y), weight, lambda y: (y, cells_y), out_ref
        )


def edge_kernel(*refs):
    *planes, first_row, second_row, weight_ref, out_ref = refs
    cells_y = planes[0].shape[0]
    odd_y = lax.rem(lax.axis_index("py"), 2) == 1

    def row(y):
        if y < 0:
            return jnp.where(odd_y, second_row[...], first_row[...])
        if y >= cells_y:
            return jnp.where(odd_y, first_row[...], second_row[...])
        return cell_row(planes, y)

    weight = weight_ref[...]
    for quad in (0, cells_y // 4 - 1):
        convolve_quad(quad, row, weight, lambda y: (y % 8, 8), out_ref)


def convolve(kernel, name, operands, rows):
    vmem = pl.BlockSpec(memory_space=pltpu.VMEM)
    return pl.pallas_call(
        kernel,
        out_shape=jax.ShapeDtypeStruct((rows, 128), jnp.float32),
        in_specs=[vmem] * len(operands),
        out_specs=vmem,
        compiler_params=pltpu.CompilerParams(vmem_limit_bytes=16 * 2**20),
        cost_estimate=pl.CostEstimate(flops=2**30, bytes_accessed=2**21, transcendentals=0),
        name=name,
    )(*operands)


def gelu(value):
    return 0.5 * value * (1.0 + lax.erf(value * math.sqrt(0.5)))


def finish_kernel(
    bias_ref, values_ref, z_ref, y_ref, conv_ref, edge_ref, out_hbm, out_ref, sems
):
    upper = lax.broadcasted_iota(jnp.int32, (8, 128), 0) < 4
    table = y_ref[lax.axis_index("py")]
    lane = lax.broadcasted_iota(jnp.int32, table.shape, 1) % 16
    expanded = [jnp.where(lane == o, table, 0.0).astype(jnp.bfloat16) for o in range(16)]
    columns = []
    for group in range(4):
        columns.append(
            jnp.concatenate(
                [values_ref[(h * 4 + group) * 4 + q] for h in range(2) for q in range(4)], axis=0
            )
        )
    packed = jnp.concatenate(columns, axis=1)
    z_values = lax.dot_general(
        packed,
        z_ref[...].astype(jnp.bfloat16),
        (((0,), (0,)), ((), ())),
        preferred_element_type=jnp.float32,
    ).astype(jnp.bfloat16)
    copies = []
    for half in range(2):
        sides = []
        for x in range(2):
            parts = []
            for part in range(2):
                lanes = slice((x * 2 + part) * 128, (x * 2 + part + 1) * 128)
                parts += [
                    z_values[ky * 32 + half * 16 : ky * 32 + half * 16 + 16, lanes]
                    for ky in range(KY)
                ]
            sides.append(jnp.concatenate(parts, axis=0))
        right = jnp.concatenate(sides, axis=1)
        for block in range(4):
            spectral = jnp.dot(
                jnp.concatenate(expanded[block * 4 : block * 4 + 4], axis=0),
                right,
                preferred_element_type=jnp.float32,
            )
            for o4 in range(4):
                o = half * 16 + block * 4 + o4
                for x in range(2):
                    inner, edge = conv_ref[o, x], edge_ref[o, x]
                    convolved = jnp.concatenate(
                        [
                            jnp.where(upper, edge, inner[:8]),
                            inner[8:-8],
                            jnp.where(upper, inner[-8:], edge),
                        ],
                        axis=0,
                    )
                    total = spectral[o4 * 32 : o4 * 32 + 32, x * 128 : (x + 1) * 128]
                    total = total + convolved + bias_ref[o]
                    out_ref[o, x] = gelu(total).astype(jnp.bfloat16)
            number = half * 4 + block
            copy = pltpu.make_async_copy(
                out_ref.at[pl.ds(number * 4, 4)], out_hbm.at[pl.ds(number * 4, 4)], sems.at[number]
            )
            copy.start()
            copies.append(copy)
    for copy in copies:
        copy.wait()


def finish(bias, values, z_table, y_table, convolved, edges):
    vmem = pl.BlockSpec(memory_space=pltpu.VMEM)
    return pl.pallas_call(
        finish_kernel,
        out_shape=jax.ShapeDtypeStruct(convolved.shape, jnp.bfloat16),
        in_specs=[pl.BlockSpec(memory_space=pltpu.SMEM)] + [vmem] * 5,
        out_specs=pl.BlockSpec(memory_space=pltpu.HBM),
        scratch_shapes=[
            pltpu.VMEM(convolved.shape, jnp.bfloat16),
            pltpu.SemaphoreType.DMA((8,)),
        ],
        compiler_params=pltpu.CompilerParams(vmem_limit_bytes=16 * 2**20),
        cost_estimate=pl.CostEstimate(flops=2**28, bytes_accessed=2**22, transcendentals=2**18),
        name="finish_layer",
    )(bias, values, z_table, y_table, convolved, edges)


def exchanged(value):
    return lax.all_to_all(value, ("px", "py"), split_axis=0, concat_axis=0, tiled=True)


def swaps(first, second, axis):
    count = lax.axis_size(axis)
    inside = [(i, i ^ 1) for i in range(count)]
    across = [(i, i + 1 if i % 2 else i - 1) for i in range(1, count - 1)]
    return lax.ppermute(first, axis, across), lax.ppermute(second, axis, inside)


def body(state_field, conv_weight, conv_bias, spectral_weight):
    channels, cells_x, cells_y, depth = state_field.shape
    sizes = (lax.axis_size("px"), lax.axis_size("py"), cells_x, cells_y, depth)
    if sizes != (8, 4, 2, 32, 128):
        return general_body(state_field, conv_weight, conv_bias, spectral_weight)
    z_forward, y_forward, x_forward, x_inverse, z_inverse, y_inverse = tables(*sizes)
    sent, held = forward_modes(
        state_field.reshape(channels * cells_x, cells_y, depth), z_forward, y_forward
    )
    modes = exchanged(sent)
    first_own, second_own = arrange(held.reshape(state_field.shape))
    weights, taps = pack(
        first_own, spectral_weight.swapaxes(4, 5), conv_weight.transpose(2, 3, 4, 0, 1)
    )
    first_plane, second_plane = swaps(first_own, second_own, "px")
    values = exchanged(mix_modes(modes, x_forward, weights, x_inverse))
    planes = (first_plane, first_own, second_own, second_plane)
    first_row, second_row = swaps(*edge_rows(planes), "py")
    rows = channels * cells_x
    interior = convolve(interior_kernel, "convolve_interior", planes + (taps,), rows * cells_y)
    edges = convolve(
        edge_kernel, "convolve_edges", planes + (first_row, second_row, taps), rows * 8
    )
    return finish(
        conv_bias,
        values,
        z_inverse,
        y_inverse,
        interior.reshape(channels, cells_x, cells_y, depth),
        edges.reshape(channels, cells_x, 8, depth),
    )


def solution(mesh):
    in_specs = (P(None, "px", "py", None), P(), P(), P(None, "py", "px", None, None, None))
    out_specs = P(None, "px", "py", None)
    return jax.shard_map(body, mesh=mesh, in_specs=in_specs, out_specs=out_specs, check_vma=False)
```

```python
import functools
import math

import jax
import jax.numpy as jnp
import ml_dtypes
import numpy as np
from jax import lax
from jax.experimental import pallas as pl
from jax.experimental.pallas import tpu as pltpu
from jax.sharding import PartitionSpec as P

KX = 16
KY = 16
KZ = 16


def extended(cells, sides, width):
    for axis, dim in sides:
        count = lax.axis_size(axis)
        ends = count - 1
        head = lax.slice_in_dim(cells, 0, width, axis=dim)
        tail = lax.slice_in_dim(cells, cells.shape[dim] - width, cells.shape[dim], axis=dim)
        cells = jnp.concatenate(
            [
                lax.ppermute(tail, axis, [(i, (i + 1) % count) for i in range(ends)]),
                cells,
                lax.ppermute(head, axis, [((i + 1) % count, i) for i in range(ends)]),
            ],
            axis=dim,
        )
    return cells


def swapped(value, axis, distance):
    mask = 2**distance
    pairs = [(source, source ^ mask) for source in range(lax.axis_size(axis))]
    return lax.ppermute(value, axis, pairs)


def mode_numbers(count):
    indices = jnp.arange(count, dtype=jnp.int32)
    return jnp.where(indices < count // 2, indices, indices - count)


def trig_pair(numbers, points, length, factor, out_type):
    positions = jnp.arange(points, dtype=jnp.int32)
    phases = positions[:, None] * numbers[None, :] % length
    angles = phases.astype(jnp.float32) * (2.0 * math.pi / length)
    return (
        (jnp.cos(angles) * factor).astype(out_type),
        (jnp.sin(angles) * factor).astype(out_type),
    )


def last_product(source, table, precision=None):
    flat = source.reshape(-1, source.shape[-1])
    result = jnp.dot(flat, table, preferred_element_type=jnp.float32, precision=precision)
    return result.reshape(source.shape[:-1] + (table.shape[1],))


def forward_last(source, cosine, sine_table, precision=None):
    real_part = source[..., 0, :]
    imag_part = source[..., 1, :]
    real_out = last_product(real_part, cosine, precision) + last_product(
        imag_part, sine_table, precision
    )
    imag_out = last_product(imag_part, cosine, precision) - last_product(
        real_part, sine_table, precision
    )
    return jnp.stack([real_out, imag_out], axis=-2)


def inverse_last(source, cosine, sine_table, precision=None):
    real_part = source[..., 0, :]
    imag_part = source[..., 1, :]
    real_out = last_product(real_part, cosine, precision) - last_product(
        imag_part, sine_table, precision
    )
    imag_out = last_product(real_part, sine_table, precision) + last_product(
        imag_part, cosine, precision
    )
    return jnp.stack([real_out, imag_out], axis=-2)


def mix_block(spectral_weight, x_block):
    highest = lax.Precision.HIGHEST
    real_in = x_block[:, :, :, 0, :]
    imag_in = x_block[:, :, :, 1, :]
    partial_real = jnp.einsum(
        "zucok,uzck->uzok", spectral_weight[0], real_in, precision=highest
    ) - jnp.einsum("zucok,uzck->uzok", spectral_weight[1], imag_in, precision=highest)
    partial_imag = jnp.einsum(
        "zucok,uzck->uzok", spectral_weight[0], imag_in, precision=highest
    ) + jnp.einsum("zucok,uzck->uzok", spectral_weight[1], real_in, precision=highest)
    return jnp.stack([partial_real, partial_imag], axis=3)


def general_body(state_field, conv_weight, conv_bias, spectral_weight):
    channels, cells_x, cells_y, depth = state_field.shape
    count_x = lax.axis_size("px")
    count_y = lax.axis_size("py")
    width_x = cells_x * count_x
    width_y = cells_y * count_y
    index_x = lax.axis_index("px")
    kz_local = KZ // count_y
    units = 2 * KY // count_x
    highest = lax.Precision.HIGHEST
    padded = extended(state_field, (("px", 1), ("py", 2)), 1)
    convolved = lax.conv_general_dilated(
        padded[None],
        conv_weight,
        (1, 1, 1),
        ((0, 0), (0, 0), (1, 1)),
        dimension_numbers=("NCDHW", "OIDHW", "NCDHW"),
        preferred_element_type=jnp.float32,
    )[0]
    z_cos, z_sin = trig_pair(
        jnp.arange(KZ, dtype=jnp.int32), depth, depth, depth ** (-0.5), jnp.bfloat16
    )
    z_table = jnp.stack([z_cos, -z_sin], axis=1)
    z_modes = jnp.einsum(
        "cxyn,nwk->kcxwy", state_field, z_table, preferred_element_type=jnp.float32
    ).astype(jnp.bfloat16)
    y_cos, y_sin = trig_pair(mode_numbers(KY), width_y, width_y, width_y ** (-0.5), jnp.bfloat16)
    full_rows = lax.all_to_all(z_modes, "py", split_axis=0, concat_axis=4, tiled=True)
    y_modes = forward_last(full_rows, y_cos, y_sin)
    y_modes = y_modes.astype(jnp.bfloat16)
    by_unit = y_modes.reshape(kz_local, 2, channels // 2, cells_x, 2, KY).transpose(
        1, 5, 0, 2, 4, 3
    )
    by_unit = by_unit.reshape(2 * KY, kz_local, channels // 2, 2, cells_x)
    x_rows = lax.all_to_all(by_unit, "px", split_axis=0, concat_axis=4, tiled=True)
    x_cos, x_sin = trig_pair(mode_numbers(KX), width_x, width_x, width_x ** (-0.5), jnp.bfloat16)
    x_modes = forward_last(x_rows, x_cos, x_sin)
    partial_modes = mix_block(spectral_weight, x_modes)
    partial_modes = partial_modes.reshape(units, kz_local, 2, channels // 2, 2, KX)
    half_index = index_x * units // KY
    own_half = lax.dynamic_index_in_dim(partial_modes, half_index, 2, keepdims=False)
    other_half = lax.dynamic_index_in_dim(partial_modes, 1 - half_index, 2, keepdims=False)
    mixed_modes = own_half + swapped(other_half, "px", count_x.bit_length() - 2)
    ix_cos, ix_sin = trig_pair(mode_numbers(KX), width_x, width_x, KX ** (-0.5), jnp.float32)
    x_values = inverse_last(mixed_modes, ix_cos.T, ix_sin.T, highest).astype(jnp.bfloat16)
    returned = lax.all_to_all(x_values, "px", split_axis=4, concat_axis=0, tiled=True)
    returned = returned.reshape(2, KY, kz_local, channels // 2, 2, cells_x).transpose(
        2, 0, 3, 5, 4, 1
    )
    returned = returned.reshape(kz_local, channels, cells_x, 2, KY)
    iy_cos, iy_sin = trig_pair(mode_numbers(KY), width_y, width_y, KY ** (-0.5), jnp.bfloat16)
    expanded = inverse_last(returned, iy_cos.T, iy_sin.T).astype(jnp.bfloat16)
    y_values = lax.all_to_all(expanded, "py", split_axis=4, concat_axis=0, tiled=True)
    iz_cos, iz_sin = trig_pair(
        jnp.arange(KZ, dtype=jnp.int32), depth, depth, KZ ** (-0.5), jnp.bfloat16
    )
    iz_table = jnp.stack([iz_cos.T, -iz_sin.T], axis=0)
    spectral = jnp.einsum("kcxwy,wkn->cxyn", y_values, iz_table, preferred_element_type=jnp.float32)
    total = convolved + spectral + conv_bias[:, None, None, None]
    return jax.nn.gelu(total, approximate=False).astype(jnp.bfloat16)


def angle_tables(numbers, points, length, factor):
    phases = (np.arange(points)[:, None] * numbers[None, :]) % length
    angles = phases.astype(np.float32) * np.float32(2.0 * math.pi / length)
    return (
        np.cos(angles).astype(np.float32) * np.float32(factor),
        np.sin(angles).astype(np.float32) * np.float32(factor),
    )


def signed_modes(count):
    indices = np.arange(count)
    return np.where(indices < count // 2, indices, indices - count)


def narrow(table):
    return table.astype(ml_dtypes.bfloat16).astype(np.float32)


def forward_pair(cosine, sine):
    return np.stack([np.stack([cosine, -sine]), np.stack([sine, cosine])])


def inverse_pair(cosine, sine):
    return np.stack([np.stack([cosine, sine]), np.stack([-sine, cosine])])


@functools.cache
def tables(count_x, count_y, cells_x, cells_y, depth):
    width_x, width_y = count_x * cells_x, count_y * cells_y
    kzl, units = KZ // count_y, 2 * KY // count_x
    groups = KY // units
    zc, zs = angle_tables(np.arange(KZ), depth, depth, depth**-0.5)
    z_forward = np.concatenate([zc.T, -zs.T])
    yc, ys = angle_tables(signed_modes(KY), width_y, width_y, width_y**-0.5)
    pair = forward_pair(yc, ys).reshape(2, 2, count_y, cells_y, groups, units)
    y_forward = np.einsum("rsqygk,d,w->qrygwskd", pair, np.ones(8), np.ones(cells_x))
    y_forward = y_forward.reshape(count_y, 2 * cells_y, groups * 2 * cells_x * units * 8)
    xc, xs = angle_tables(signed_modes(KX), width_x, width_x, width_x**-0.5)
    pair = forward_pair(xc, xs).reshape(2, 2, count_x, cells_x, KX)
    x_forward = np.einsum("rspxk,gh,q->gskpqhxr", pair, np.eye(2), np.ones(count_y))
    x_forward = x_forward.reshape(4 * KX, count_x * count_y * 4 * cells_x)
    xc, xs = angle_tables(signed_modes(KX), width_x, width_x, KX**-0.5)
    pair = inverse_pair(xc, xs).reshape(2, 2, count_x, cells_x, KX)
    x_inverse = np.einsum("rspxk,zv->pxzsvrk", pair, np.eye(kzl))
    x_inverse = x_inverse.reshape(count_x * cells_x * kzl * 2, kzl * 2 * KX)
    zc, zs = angle_tables(np.arange(KZ), depth, depth, KZ**-0.5)
    pair = inverse_pair(zc, zs).reshape(2, 2, depth, count_y, kzl)
    z_inverse = np.einsum("rsnqz,xw,h->hqxzrwsn", pair, np.eye(cells_x), np.ones(2))
    z_inverse = z_inverse.reshape(4 * cells_x * KZ, cells_x * 2 * depth)
    yc, ys = angle_tables(signed_modes(KY), width_y, width_y, KY**-0.5)
    pair = np.stack([yc, -ys]).reshape(2, count_y, cells_y, KY)
    y_inverse = np.einsum("rqyk,i->qyrki", pair, np.ones(16))
    y_inverse = y_inverse.reshape(count_y, cells_y, 32 * KY)
    return (
        narrow(z_forward),
        narrow(y_forward),
        narrow(x_forward),
        np.concatenate(
            [narrow(x_inverse), narrow(x_inverse), narrow(x_inverse - narrow(x_inverse))], axis=1
        ),
        narrow(z_inverse),
        narrow(y_inverse),
    )


def block_moves(value):
    rows = value.shape[0]
    tiles = value.reshape(rows // 8, 8, 128)
    row = lax.broadcasted_iota(jnp.int32, tiles.shape, 1) % 4
    block = lax.broadcasted_iota(jnp.int32, tiles.shape, 2) // 32
    result = tiles
    for lane_step in (1, 2, 3):
        moved = pltpu.roll(tiles, 128 - 32 * lane_step, 2)
        result = jnp.where(row - block == lane_step, pltpu.roll(moved, lane_step, 1), result)
        result = jnp.where(
            row - block == lane_step - 4, pltpu.roll(moved, 8 + lane_step - 4, 1), result
        )
    return result


def forward_kernel(
    state_hbm, z_hbm, y_hbm, weight_hbm, out_ref, state_ref, weight_ref, z_ref, y_ref, table_ref, sems
):
    count = state_ref.shape[0] // 4
    span = state_ref.shape[1]
    y_copy = pltpu.make_async_copy(y_hbm.at[lax.axis_index("py")], y_ref, sems.at[0])
    z_copy = pltpu.make_async_copy(z_hbm, z_ref, sems.at[1])
    copies = [
        pltpu.make_async_copy(
            state_hbm.at[pl.ds(g * count, count)],
            state_ref.at[pl.ds(g * count, count)],
            sems.at[2 + g],
        )
        for g in range(4)
    ]
    weight_copy = pltpu.make_async_copy(weight_hbm.at[0], weight_ref, sems.at[6])
    for copy in [y_copy, z_copy] + copies + [weight_copy]:
        copy.start()
    y_copy.wait()
    table = y_ref[...]
    lane = lax.broadcasted_iota(jnp.int32, (span, table.shape[1]), 1)
    for x in range(2):
        for c in range(8):
            own = (lane % 8 == c) & (lane // 64 % 2 == x)
            for part in range(2):
                first = part * 16 * span + (c * 2 + x) * span
                block = jnp.where(own, table[part * span : (part + 1) * span], 0.0)
                table_ref[first : first + span] = block.astype(jnp.bfloat16)
    z_copy.wait()
    z_table = z_ref[...].astype(jnp.bfloat16)
    pieces = []
    for g in range(4):
        copies[g].wait()
        cells = state_ref[g * count : (g + 1) * count].reshape(count * span, state_ref.shape[2])
        z_modes = lax.dot_general(
            z_table, cells, (((1,), (1,)), ((), ())), preferred_element_type=jnp.float32
        ).astype(jnp.bfloat16)
        pieces.append(jnp.concatenate([z_modes[:KZ], z_modes[KZ:]], axis=1))
    stacked = jnp.concatenate(pieces, axis=0)
    modes = jnp.dot(stacked, table_ref[...], preferred_element_type=jnp.float32)
    for group in range(4):
        moved = block_moves(modes[:, group * 128 : (group + 1) * 128])
        for half in range(2):
            for pair in range(2):
                first = moved[half * 4 + pair]
                second = moved[half * 4 + 2 + pair]
                for side in range(2):
                    rows4 = slice(4 * side, 4 * side + 4)
                    chunk = jnp.concatenate([first[rows4], second[rows4]], axis=0)
                    out_ref[(half * 4 + group) * 4 + 2 * pair + side] = chunk.astype(jnp.bfloat16)
    weight_copy.wait()


def forward_modes(state, z_table, y_table, spectral_weight):
    return pl.pallas_call(
        forward_kernel,
        out_shape=(
            jax.ShapeDtypeStruct((32, 8, 128), jnp.bfloat16),
            jax.ShapeDtypeStruct(state.shape, jnp.bfloat16),
            jax.ShapeDtypeStruct(spectral_weight.shape[1:], jnp.float32),
        ),
        in_specs=[pl.BlockSpec(memory_space=pltpu.HBM)] * 4,
        out_specs=(pl.BlockSpec(memory_space=pltpu.VMEM),) * 3,
        scratch_shapes=[
            pltpu.VMEM(z_table.shape, jnp.float32),
            pltpu.VMEM(y_table.shape[1:], jnp.float32),
            pltpu.VMEM((32 * state.shape[1], y_table.shape[2]), jnp.bfloat16),
            pltpu.SemaphoreType.DMA((7,)),
        ],
        compiler_params=pltpu.CompilerParams(vmem_limit_bytes=16 * 2**20),
        cost_estimate=pl.CostEstimate(flops=2**27, bytes_accessed=2**21, transcendentals=0),
        name="forward_modes",
    )(
        *(
            pltpu.with_memory_space_constraint(v, pltpu.HBM)
            for v in (state, z_table, y_table, spectral_weight)
        )
    )


def arrange_kernel(state_ref, first_ref, second_ref, token_ref, wide):
    odd_x = lax.rem(lax.axis_index("px"), 2)
    cells_y = state_ref.shape[2]
    for slot, (out_ref, x) in enumerate(((first_ref, odd_x), (second_ref, 1 - odd_x))):
        wide[slot] = state_ref[:, x].astype(jnp.float32).reshape(32 * cells_y, 128)
        for y in range(cells_y):
            out_ref[y] = wide[slot, pl.ds(y, 32, stride=cells_y), :].astype(jnp.bfloat16)
    token_ref[...] = jnp.zeros_like(token_ref)


def arrange(state):
    vmem = pl.BlockSpec(memory_space=pltpu.VMEM)
    cells_y = state.shape[2]
    plane = jax.ShapeDtypeStruct((cells_y, 32, 128), jnp.bfloat16)
    return pl.pallas_call(
        arrange_kernel,
        out_shape=(plane, plane, jax.ShapeDtypeStruct((8, 128), jnp.float32)),
        in_specs=[vmem],
        out_specs=(vmem,) * 3,
        scratch_shapes=[pltpu.VMEM((2, 32 * cells_y, 128), jnp.float32)],
        compiler_params=pltpu.CompilerParams(vmem_limit_bytes=16 * 2**20),
        cost_estimate=pl.CostEstimate(flops=2**10, bytes_accessed=2**10, transcendentals=0),
        name="arrange_cells",
    )(state)


def pack_kernel(
    after_ref, real_ref, weight_hbm, conv_hbm, weight_out, conv_out, imag_ref, conv_ref, sems
):
    conv_copy = pltpu.make_async_copy(conv_hbm, conv_ref, sems.at[4])
    copies = [
        pltpu.make_async_copy(weight_hbm.at[1, kz], imag_ref.at[kz], sems.at[kz]) for kz in range(4)
    ]
    for copy in [conv_copy] + copies:
        copy.start()
    odd_x = lax.rem(lax.axis_index("px"), 2)
    conv_copy.wait()
    zero = jnp.zeros((32, 32), jnp.float32)
    for dz in range(3):
        taps = {
            (dx, dy): conv_ref[dx, dy, dz].astype(jnp.float32)
            for dx in range(3)
            for dy in range(3)
        }
        for y_at in range(2):
            for x_at in range(2):
                row = ((dz * 2 + y_at) * 2 + x_at) * 32
                for y_in in range(4):
                    blocks = [taps.get((x_in - x_at, y_in - y_at), zero) for x_in in range(4)]
                    blocks = [jnp.where(odd_x == 1, blocks[3 - i], blocks[i]) for i in range(4)]
                    conv_out[row : row + 32, y_in * 128 : (y_in + 1) * 128] = jnp.concatenate(
                        blocks, axis=1
                    ).astype(jnp.bfloat16)
    for part, part_ref in enumerate((real_ref, imag_ref)):
        for kz in range(4):
            if part == 1:
                copies[kz].wait()
            for c in range(16):
                weight_out[part, kz, c] = jnp.concatenate(
                    [part_ref[kz, u, c] for u in range(4)], axis=1
                )


def pack(after, real_weight, spectral_weight, conv_weight):
    vmem = pl.BlockSpec(memory_space=pltpu.VMEM)
    return pl.pallas_call(
        pack_kernel,
        out_shape=(
            jax.ShapeDtypeStruct((2, 4, 16, KX, 128), jnp.float32),
            jax.ShapeDtypeStruct((384, 512), jnp.bfloat16),
        ),
        in_specs=[pl.BlockSpec(memory_space=pl.ANY), vmem]
        + [pl.BlockSpec(memory_space=pltpu.HBM)] * 2,
        out_specs=(vmem, vmem),
        scratch_shapes=[
            pltpu.VMEM(spectral_weight.shape[1:], jnp.float32),
            pltpu.VMEM(conv_weight.shape, jnp.bfloat16),
            pltpu.SemaphoreType.DMA((5,)),
        ],
        compiler_params=pltpu.CompilerParams(vmem_limit_bytes=16 * 2**20),
        cost_estimate=pl.CostEstimate(flops=2**10, bytes_accessed=2**10, transcendentals=0),
        name="pack_weights",
    )(
        after,
        real_weight,
        *(pltpu.with_memory_space_constraint(v, pltpu.HBM) for v in (spectral_weight, conv_weight)),
    )


def mix_kernel(modes_ref, forward_ref, weight_ref, inverse_ref, out_ref):
    received = modes_ref[...].astype(jnp.float32).reshape(256, 128).astype(jnp.bfloat16)
    x_modes = jnp.dot(
        forward_ref[...].astype(jnp.bfloat16), received, preferred_element_type=jnp.float32)
    lane = lax.broadcasted_iota(jnp.int32, (16, 128), 1)
    base = (lane // 32) * 8
    mixed = []
    for kz in range(4):
        real_sum = imag_sum = None
        for c in range(16):
            half, c8 = c // 8, c % 8
            index = base + (kz * 32 + c8)
            real_in = jnp.take_along_axis(x_modes[half * 32 : half * 32 + 16], index, axis=1)
            imag_in = jnp.take_along_axis(x_modes[half * 32 + 16 : half * 32 + 32], index, axis=1)
            real_weight = weight_ref[0, kz, c]
            imag_weight = weight_ref[1, kz, c]
            real_term = real_weight * real_in - imag_weight * imag_in
            imag_term = real_weight * imag_in + imag_weight * real_in
            real_sum = real_term if real_sum is None else real_sum + real_term
            imag_sum = imag_term if imag_sum is None else imag_sum + imag_term
        mixed += [real_sum, imag_sum]
    mixed = jnp.concatenate(mixed, axis=0)
    high = mixed.astype(jnp.bfloat16)
    low = (mixed - high.astype(jnp.float32)).astype(jnp.bfloat16)
    values = jnp.dot(
        inverse_ref[...].astype(jnp.bfloat16),
        jnp.concatenate([high, low, high], axis=0),
        preferred_element_type=jnp.float32,
    ).astype(jnp.bfloat16)
    for x in range(8):
        for y in range(4):
            out_ref[x * 4 + y] = values[16 * x : 16 * x + 16]


def mix_modes(modes, forward_table, weights, inverse_table):
    vmem = pl.BlockSpec(memory_space=pltpu.VMEM)
    return pl.pallas_call(
        mix_kernel,
        out_shape=jax.ShapeDtypeStruct((32, 16, 128), jnp.bfloat16),
        in_specs=[vmem] * 4,
        out_specs=vmem,
        compiler_params=pltpu.CompilerParams(vmem_limit_bytes=16 * 2**20),
        cost_estimate=pl.CostEstimate(flops=2**35, bytes_accessed=2**21, transcendentals=0),
        name="mix_modes",
    )(modes, forward_table, weights, inverse_table)


def cell_row(planes, y):
    return jnp.concatenate([plane[y] for plane in planes], axis=0)


def edge_rows_kernel(*refs):
    *planes, first_ref, second_ref = refs
    end = planes[0].shape[0] - 1
    odd_y = lax.rem(lax.axis_index("py"), 2)
    first_ref[...] = cell_row(planes, odd_y * end)
    second_ref[...] = cell_row(planes, (1 - odd_y) * end)


def edge_rows(planes):
    vmem = pl.BlockSpec(memory_space=pltpu.VMEM)
    row = jax.ShapeDtypeStruct((128, 128), jnp.bfloat16)
    return pl.pallas_call(
        edge_rows_kernel,
        out_shape=(row, row),
        in_specs=[vmem] * 4,
        out_specs=(vmem, vmem),
        compiler_params=pltpu.CompilerParams(vmem_limit_bytes=16 * 2**20),
        cost_estimate=pl.CostEstimate(flops=2**10, bytes_accessed=2**17, transcendentals=0),
        name="edge_rows",
    )(*planes)


def convolve_quad(quad, row, weight, place, out_ref):
    lane = lax.broadcasted_iota(jnp.int32, (128, 256), 1) % 128
    windows = []
    for pair in range(2):
        start = quad * 4 + pair * 2 - 1
        windows.append(jnp.concatenate([row(start + i) for i in range(4)], axis=0))
    product = jnp.dot(weight, jnp.concatenate(windows, axis=1), preferred_element_type=jnp.float32)
    below = pltpu.roll(product[:128], 1, 1)
    above = pltpu.roll(product[256:], 255, 1)
    total = product[128:256] + jnp.where(lane == 0, 0.0, below)
    total = total + jnp.where(lane == 127, 0.0, above)
    for pair in range(2):
        for y_out in range(2):
            for x_out in range(2):
                first = (y_out * 2 + x_out) * 32
                value = total[first : first + 32, pair * 128 : (pair + 1) * 128]
                y = quad * 4 + pair * 2 + y_out
                at, span = place(y)
                out_ref[pl.ds(x_out * span + at, 32, stride=2 * span), :] = value


def interior_kernel(*refs):
    *planes, weight_ref, out_ref = refs
    cells_y = planes[0].shape[0]
    weight = weight_ref[...]
    for quad in range(1, cells_y // 4 - 1):
        convolve_quad(
            quad, lambda y: cell_row(planes, y), weight, lambda y: (y, cells_y), out_ref
        )


def edge_kernel(*refs):
    *planes, first_row, second_row, weight_ref, out_ref = refs
    cells_y = planes[0].shape[0]
    odd_y = lax.rem(lax.axis_index("py"), 2) == 1

    def row(y):
        if y < 0:
            return jnp.where(odd_y, second_row[...], first_row[...])
        if y >= cells_y:
            return jnp.where(odd_y, first_row[...], second_row[...])
        return cell_row(planes, y)

    weight = weight_ref[...]
    for quad in (0, cells_y // 4 - 1):
        convolve_quad(quad, row, weight, lambda y: (y % 8, 8), out_ref)


def convolve(kernel, name, operands, rows):
    vmem = pl.BlockSpec(memory_space=pltpu.VMEM)
    return pl.pallas_call(
        kernel,
        out_shape=jax.ShapeDtypeStruct((rows, 128), jnp.float32),
        in_specs=[vmem] * len(operands),
        out_specs=vmem,
        compiler_params=pltpu.CompilerParams(vmem_limit_bytes=16 * 2**20),
        cost_estimate=pl.CostEstimate(flops=2**30, bytes_accessed=2**21, transcendentals=0),
        name=name,
    )(*operands)


def gelu(value):
    return 0.5 * value * (1.0 + lax.erf(value * math.sqrt(0.5)))


def finish_kernel(
    bias_ref, values_ref, z_ref, y_ref, conv_ref, edge_ref, out_hbm, out_ref, sems
):
    upper = lax.broadcasted_iota(jnp.int32, (8, 128), 0) < 4
    table = y_ref[lax.axis_index("py")]
    lane = lax.broadcasted_iota(jnp.int32, table.shape, 1) % 16
    expanded = [jnp.where(lane == o, table, 0.0).astype(jnp.bfloat16) for o in range(16)]
    columns = []
    for group in range(4):
        columns.append(
            jnp.concatenate(
                [values_ref[(h * 4 + group) * 4 + q] for h in range(2) for q in range(4)], axis=0
            )
        )
    packed = jnp.concatenate(columns, axis=1)
    z_values = lax.dot_general(
        packed,
        z_ref[...].astype(jnp.bfloat16),
        (((0,), (0,)), ((), ())),
        preferred_element_type=jnp.float32,
    ).astype(jnp.bfloat16)
    copies = []
    for half in range(2):
        sides = []
        for x in range(2):
            parts = []
            for part in range(2):
                lanes = slice((x * 2 + part) * 128, (x * 2 + part + 1) * 128)
                parts += [
                    z_values[ky * 32 + half * 16 : ky * 32 + half * 16 + 16, lanes]
                    for ky in range(KY)
                ]
            sides.append(jnp.concatenate(parts, axis=0))
        right = jnp.concatenate(sides, axis=1)
        for block in range(4):
            spectral = jnp.dot(
                jnp.concatenate(expanded[block * 4 : block * 4 + 4], axis=0),
                right,
                preferred_element_type=jnp.float32,
            )
            for o4 in range(4):
                o = half * 16 + block * 4 + o4
                for x in range(2):
                    inner, edge = conv_ref[o, x], edge_ref[o, x]
                    convolved = jnp.concatenate(
                        [
                            jnp.where(upper, edge, inner[:8]),
                            inner[8:-8],
                            jnp.where(upper, inner[-8:], edge),
                        ],
                        axis=0,
                    )
                    total = spectral[o4 * 32 : o4 * 32 + 32, x * 128 : (x + 1) * 128]
                    total = total + convolved + bias_ref[o]
                    out_ref[o, x] = gelu(total).astype(jnp.bfloat16)
            number = half * 4 + block
            copy = pltpu.make_async_copy(
                out_ref.at[pl.ds(number * 4, 4)], out_hbm.at[pl.ds(number * 4, 4)], sems.at[number]
            )
            copy.start()
            copies.append(copy)
    for copy in copies:
        copy.wait()


def finish(bias, values, z_table, y_table, convolved, edges):
    vmem = pl.BlockSpec(memory_space=pltpu.VMEM)
    return pl.pallas_call(
        finish_kernel,
        out_shape=jax.ShapeDtypeStruct(convolved.shape, jnp.bfloat16),
        in_specs=[pl.BlockSpec(memory_space=pltpu.SMEM)] + [vmem] * 5,
        out_specs=pl.BlockSpec(memory_space=pltpu.HBM),
        scratch_shapes=[
            pltpu.VMEM(convolved.shape, jnp.bfloat16),
            pltpu.SemaphoreType.DMA((8,)),
        ],
        compiler_params=pltpu.CompilerParams(vmem_limit_bytes=16 * 2**20),
        cost_estimate=pl.CostEstimate(flops=2**28, bytes_accessed=2**22, transcendentals=2**18),
        name="finish_layer",
    )(bias, values, z_table, y_table, convolved, edges)


def exchanged(value):
    return lax.all_to_all(value, ("px", "py"), split_axis=0, concat_axis=0, tiled=True)


def swaps(first, second, axis):
    count = lax.axis_size(axis)
    inside = [(i, i ^ 1) for i in range(count)]
    across = [(i, i + 1 if i % 2 else i - 1) for i in range(1, count - 1)]
    return lax.ppermute(first, axis, across), lax.ppermute(second, axis, inside)


def body(state_field, conv_weight, conv_bias, spectral_weight):
    channels, cells_x, cells_y, depth = state_field.shape
    sizes = (lax.axis_size("px"), lax.axis_size("py"), cells_x, cells_y, depth)
    if sizes != (8, 4, 2, 32, 128):
        return general_body(state_field, conv_weight, conv_bias, spectral_weight)
    z_forward, y_forward, x_forward, x_inverse, z_inverse, y_inverse = tables(*sizes)
    spectral_weight = spectral_weight.swapaxes(4, 5)
    sent, held, real_weight = forward_modes(
        state_field.reshape(channels * cells_x, cells_y, depth),
        z_forward,
        y_forward,
        spectral_weight,
    )
    modes = exchanged(sent)
    first_own, second_own, token = arrange(held.reshape(state_field.shape))
    weights, taps = pack(
        token, real_weight, spectral_weight, conv_weight.transpose(2, 3, 4, 0, 1)
    )
    first_plane, second_plane = swaps(first_own, second_own, "px")
    values = exchanged(mix_modes(modes, x_forward, weights, x_inverse))
    planes = (first_plane, first_own, second_own, second_plane)
    first_row, second_row = swaps(*edge_rows(planes), "py")
    rows = channels * cells_x
    interior = convolve(interior_kernel, "convolve_interior", planes + (taps,), rows * cells_y)
    edges = convolve(
        edge_kernel, "convolve_edges", planes + (first_row, second_row, taps), rows * 8
    )
    return finish(
        conv_bias,
        values,
        z_inverse,
        y_inverse,
        interior.reshape(channels, cells_x, cells_y, depth),
        edges.reshape(channels, cells_x, 8, depth),
    )


def solution(mesh):
    in_specs = (P(None, "px", "py", None), P(), P(), P(None, "py", "px", None, None, None))
    out_specs = P(None, "px", "py", None)
    return jax.shard_map(body, mesh=mesh, in_specs=in_specs, out_specs=out_specs, check_vma=False)
```

```python
import functools
import math

import jax
import jax.numpy as jnp
import ml_dtypes
import numpy as np
from jax import lax
from jax.experimental import pallas as pl
from jax.experimental.pallas import tpu as pltpu
from jax.sharding import PartitionSpec as P

KX = 16
KY = 16
KZ = 16


def extended(cells, sides, width):
    for axis, dim in sides:
        count = lax.axis_size(axis)
        ends = count - 1
        head = lax.slice_in_dim(cells, 0, width, axis=dim)
        tail = lax.slice_in_dim(cells, cells.shape[dim] - width, cells.shape[dim], axis=dim)
        cells = jnp.concatenate(
            [
                lax.ppermute(tail, axis, [(i, (i + 1) % count) for i in range(ends)]),
                cells,
                lax.ppermute(head, axis, [((i + 1) % count, i) for i in range(ends)]),
            ],
            axis=dim,
        )
    return cells


def swapped(value, axis, distance):
    mask = 2**distance
    pairs = [(source, source ^ mask) for source in range(lax.axis_size(axis))]
    return lax.ppermute(value, axis, pairs)


def mode_numbers(count):
    indices = jnp.arange(count, dtype=jnp.int32)
    return jnp.where(indices < count // 2, indices, indices - count)


def trig_pair(numbers, points, length, factor, out_type):
    positions = jnp.arange(points, dtype=jnp.int32)
    phases = positions[:, None] * numbers[None, :] % length
    angles = phases.astype(jnp.float32) * (2.0 * math.pi / length)
    return (
        (jnp.cos(angles) * factor).astype(out_type),
        (jnp.sin(angles) * factor).astype(out_type),
    )


def last_product(source, table, precision=None):
    flat = source.reshape(-1, source.shape[-1])
    result = jnp.dot(flat, table, preferred_element_type=jnp.float32, precision=precision)
    return result.reshape(source.shape[:-1] + (table.shape[1],))


def forward_last(source, cosine, sine_table, precision=None):
    real_part = source[..., 0, :]
    imag_part = source[..., 1, :]
    real_out = last_product(real_part, cosine, precision) + last_product(
        imag_part, sine_table, precision
    )
    imag_out = last_product(imag_part, cosine, precision) - last_product(
        real_part, sine_table, precision
    )
    return jnp.stack([real_out, imag_out], axis=-2)


def inverse_last(source, cosine, sine_table, precision=None):
    real_part = source[..., 0, :]
    imag_part = source[..., 1, :]
    real_out = last_product(real_part, cosine, precision) - last_product(
        imag_part, sine_table, precision
    )
    imag_out = last_product(real_part, sine_table, precision) + last_product(
        imag_part, cosine, precision
    )
    return jnp.stack([real_out, imag_out], axis=-2)


def mix_block(spectral_weight, x_block):
    highest = lax.Precision.HIGHEST
    real_in = x_block[:, :, :, 0, :]
    imag_in = x_block[:, :, :, 1, :]
    partial_real = jnp.einsum(
        "zucok,uzck->uzok", spectral_weight[0], real_in, precision=highest
    ) - jnp.einsum("zucok,uzck->uzok", spectral_weight[1], imag_in, precision=highest)
    partial_imag = jnp.einsum(
        "zucok,uzck->uzok", spectral_weight[0], imag_in, precision=highest
    ) + jnp.einsum("zucok,uzck->uzok", spectral_weight[1], real_in, precision=highest)
    return jnp.stack([partial_real, partial_imag], axis=3)


def general_body(state_field, conv_weight, conv_bias, spectral_weight):
    channels, cells_x, cells_y, depth = state_field.shape
    count_x = lax.axis_size("px")
    count_y = lax.axis_size("py")
    width_x = cells_x * count_x
    width_y = cells_y * count_y
    index_x = lax.axis_index("px")
    kz_local = KZ // count_y
    units = 2 * KY // count_x
    highest = lax.Precision.HIGHEST
    padded = extended(state_field, (("px", 1), ("py", 2)), 1)
    convolved = lax.conv_general_dilated(
        padded[None],
        conv_weight,
        (1, 1, 1),
        ((0, 0), (0, 0), (1, 1)),
        dimension_numbers=("NCDHW", "OIDHW", "NCDHW"),
        preferred_element_type=jnp.float32,
    )[0]
    z_cos, z_sin = trig_pair(
        jnp.arange(KZ, dtype=jnp.int32), depth, depth, depth ** (-0.5), jnp.bfloat16
    )
    z_table = jnp.stack([z_cos, -z_sin], axis=1)
    z_modes = jnp.einsum(
        "cxyn,nwk->kcxwy", state_field, z_table, preferred_element_type=jnp.float32
    ).astype(jnp.bfloat16)
    y_cos, y_sin = trig_pair(mode_numbers(KY), width_y, width_y, width_y ** (-0.5), jnp.bfloat16)
    full_rows = lax.all_to_all(z_modes, "py", split_axis=0, concat_axis=4, tiled=True)
    y_modes = forward_last(full_rows, y_cos, y_sin)
    y_modes = y_modes.astype(jnp.bfloat16)
    by_unit = y_modes.reshape(kz_local, 2, channels // 2, cells_x, 2, KY).transpose(
        1, 5, 0, 2, 4, 3
    )
    by_unit = by_unit.reshape(2 * KY, kz_local, channels // 2, 2, cells_x)
    x_rows = lax.all_to_all(by_unit, "px", split_axis=0, concat_axis=4, tiled=True)
    x_cos, x_sin = trig_pair(mode_numbers(KX), width_x, width_x, width_x ** (-0.5), jnp.bfloat16)
    x_modes = forward_last(x_rows, x_cos, x_sin)
    partial_modes = mix_block(spectral_weight, x_modes)
    partial_modes = partial_modes.reshape(units, kz_local, 2, channels // 2, 2, KX)
    half_index = index_x * units // KY
    own_half = lax.dynamic_index_in_dim(partial_modes, half_index, 2, keepdims=False)
    other_half = lax.dynamic_index_in_dim(partial_modes, 1 - half_index, 2, keepdims=False)
    mixed_modes = own_half + swapped(other_half, "px", count_x.bit_length() - 2)
    ix_cos, ix_sin = trig_pair(mode_numbers(KX), width_x, width_x, KX ** (-0.5), jnp.float32)
    x_values = inverse_last(mixed_modes, ix_cos.T, ix_sin.T, highest).astype(jnp.bfloat16)
    returned = lax.all_to_all(x_values, "px", split_axis=4, concat_axis=0, tiled=True)
    returned = returned.reshape(2, KY, kz_local, channels // 2, 2, cells_x).transpose(
        2, 0, 3, 5, 4, 1
    )
    returned = returned.reshape(kz_local, channels, cells_x, 2, KY)
    iy_cos, iy_sin = trig_pair(mode_numbers(KY), width_y, width_y, KY ** (-0.5), jnp.bfloat16)
    expanded = inverse_last(returned, iy_cos.T, iy_sin.T).astype(jnp.bfloat16)
    y_values = lax.all_to_all(expanded, "py", split_axis=4, concat_axis=0, tiled=True)
    iz_cos, iz_sin = trig_pair(
        jnp.arange(KZ, dtype=jnp.int32), depth, depth, KZ ** (-0.5), jnp.bfloat16
    )
    iz_table = jnp.stack([iz_cos.T, -iz_sin.T], axis=0)
    spectral = jnp.einsum("kcxwy,wkn->cxyn", y_values, iz_table, preferred_element_type=jnp.float32)
    total = convolved + spectral + conv_bias[:, None, None, None]
    return jax.nn.gelu(total, approximate=False).astype(jnp.bfloat16)


def angle_tables(numbers, points, length, factor):
    phases = (np.arange(points)[:, None] * numbers[None, :]) % length
    angles = phases.astype(np.float32) * np.float32(2.0 * math.pi / length)
    return (
        np.cos(angles).astype(np.float32) * np.float32(factor),
        np.sin(angles).astype(np.float32) * np.float32(factor),
    )


def signed_modes(count):
    indices = np.arange(count)
    return np.where(indices < count // 2, indices, indices - count)


def narrow(table):
    return table.astype(ml_dtypes.bfloat16).astype(np.float32)


def forward_pair(cosine, sine):
    return np.stack([np.stack([cosine, -sine]), np.stack([sine, cosine])])


def inverse_pair(cosine, sine):
    return np.stack([np.stack([cosine, sine]), np.stack([-sine, cosine])])


@functools.cache
def tables(count_x, count_y, cells_x, cells_y, depth):
    width_x, width_y = count_x * cells_x, count_y * cells_y
    kzl, units = KZ // count_y, 2 * KY // count_x
    groups = KY // units
    zc, zs = angle_tables(np.arange(KZ), depth, depth, depth**-0.5)
    z_forward = np.concatenate([zc.T, -zs.T])
    yc, ys = angle_tables(signed_modes(KY), width_y, width_y, width_y**-0.5)
    pair = forward_pair(yc, ys).reshape(2, 2, count_y, cells_y, groups, units)
    y_forward = np.einsum("rsqygk,d,w->qrygwskd", pair, np.ones(8), np.ones(cells_x))
    y_forward = y_forward.reshape(count_y, 2 * cells_y, groups * 2 * cells_x * units * 8)
    xc, xs = angle_tables(signed_modes(KX), width_x, width_x, width_x**-0.5)
    pair = forward_pair(xc, xs).reshape(2, 2, count_x, cells_x, KX)
    x_forward = np.einsum("rspxk,gh,q->gskpqhxr", pair, np.eye(2), np.ones(count_y))
    x_forward = x_forward.reshape(4 * KX, count_x * count_y * 4 * cells_x)
    xc, xs = angle_tables(signed_modes(KX), width_x, width_x, KX**-0.5)
    pair = inverse_pair(xc, xs).reshape(2, 2, count_x, cells_x, KX)
    x_inverse = np.einsum("rspxk,zv->pxzsvrk", pair, np.eye(kzl))
    x_inverse = x_inverse.reshape(count_x * cells_x * kzl * 2, kzl * 2 * KX)
    zc, zs = angle_tables(np.arange(KZ), depth, depth, KZ**-0.5)
    pair = inverse_pair(zc, zs).reshape(2, 2, depth, count_y, kzl)
    z_inverse = np.einsum("rsnqz,xw,h->hqxzrwsn", pair, np.eye(cells_x), np.ones(2))
    z_inverse = z_inverse.reshape(4 * cells_x * KZ, cells_x * 2 * depth)
    yc, ys = angle_tables(signed_modes(KY), width_y, width_y, KY**-0.5)
    pair = np.stack([yc, -ys]).reshape(2, count_y, cells_y, KY)
    y_inverse = np.einsum("rqyk,i->qyrki", pair, np.ones(16))
    y_inverse = y_inverse.reshape(count_y, cells_y, 32 * KY)
    return (
        narrow(z_forward),
        narrow(y_forward),
        narrow(x_forward),
        np.concatenate(
            [narrow(x_inverse), narrow(x_inverse - narrow(x_inverse))], axis=1
        ),
        narrow(z_inverse),
        narrow(y_inverse),
    )


def block_moves(value):
    rows = value.shape[0]
    tiles = value.reshape(rows // 8, 8, 128)
    row = lax.broadcasted_iota(jnp.int32, tiles.shape, 1) % 4
    block = lax.broadcasted_iota(jnp.int32, tiles.shape, 2) // 32
    result = tiles
    for lane_step in (1, 2, 3):
        moved = pltpu.roll(tiles, 128 - 32 * lane_step, 2)
        result = jnp.where(row - block == lane_step, pltpu.roll(moved, lane_step, 1), result)
        result = jnp.where(
            row - block == lane_step - 4, pltpu.roll(moved, 8 + lane_step - 4, 1), result
        )
    return result


def forward_kernel(state_hbm, z_hbm, y_hbm, out_ref, state_ref, z_ref, y_ref, table_ref, sems):
    count = state_ref.shape[0] // 4
    span = state_ref.shape[1]
    y_copy = pltpu.make_async_copy(y_hbm.at[lax.axis_index("py")], y_ref, sems.at[0])
    z_copy = pltpu.make_async_copy(z_hbm, z_ref, sems.at[1])
    copies = [
        pltpu.make_async_copy(
            state_hbm.at[pl.ds(g * count, count)],
            state_ref.at[pl.ds(g * count, count)],
            sems.at[2 + g],
        )
        for g in range(4)
    ]
    for copy in [y_copy, z_copy] + copies:
        copy.start()
    y_copy.wait()
    table = y_ref[...]
    lane = lax.broadcasted_iota(jnp.int32, (span, table.shape[1]), 1)
    for x in range(2):
        for c in range(8):
            own = (lane % 8 == c) & (lane // 64 % 2 == x)
            for part in range(2):
                first = part * 16 * span + (c * 2 + x) * span
                block = jnp.where(own, table[part * span : (part + 1) * span], 0.0)
                table_ref[first : first + span] = block.astype(jnp.bfloat16)
    z_copy.wait()
    z_table = z_ref[...].astype(jnp.bfloat16)
    pieces = []
    for g in range(4):
        copies[g].wait()
        cells = state_ref[g * count : (g + 1) * count].reshape(count * span, state_ref.shape[2])
        z_modes = lax.dot_general(
            z_table, cells, (((1,), (1,)), ((), ())), preferred_element_type=jnp.float32
        ).astype(jnp.bfloat16)
        pieces.append(jnp.concatenate([z_modes[:KZ], z_modes[KZ:]], axis=1))
    stacked = jnp.concatenate(pieces, axis=0)
    modes = jnp.dot(stacked, table_ref[...], preferred_element_type=jnp.float32)
    for group in range(4):
        moved = block_moves(modes[:, group * 128 : (group + 1) * 128])
        for half in range(2):
            for pair in range(2):
                first = moved[half * 4 + pair]
                second = moved[half * 4 + 2 + pair]
                for side in range(2):
                    rows4 = slice(4 * side, 4 * side + 4)
                    chunk = jnp.concatenate([first[rows4], second[rows4]], axis=0)
                    out_ref[(half * 4 + group) * 4 + 2 * pair + side] = chunk.astype(jnp.bfloat16)


def forward_modes(state, z_table, y_table):
    return pl.pallas_call(
        forward_kernel,
        out_shape=(
            jax.ShapeDtypeStruct((32, 8, 128), jnp.bfloat16),
            jax.ShapeDtypeStruct(state.shape, jnp.bfloat16),
        ),
        in_specs=[pl.BlockSpec(memory_space=pltpu.HBM)] * 3,
        out_specs=(pl.BlockSpec(memory_space=pltpu.VMEM),) * 2,
        scratch_shapes=[
            pltpu.VMEM(z_table.shape, jnp.float32),
            pltpu.VMEM(y_table.shape[1:], jnp.float32),
            pltpu.VMEM((32 * state.shape[1], y_table.shape[2]), jnp.bfloat16),
            pltpu.SemaphoreType.DMA((6,)),
        ],
        compiler_params=pltpu.CompilerParams(vmem_limit_bytes=16 * 2**20),
        cost_estimate=pl.CostEstimate(flops=2**27, bytes_accessed=2**21, transcendentals=0),
        name="forward_modes",
    )(*(pltpu.with_memory_space_constraint(v, pltpu.HBM) for v in (state, z_table, y_table)))


def arrange_kernel(state_ref, first_ref, second_ref, sent_hbm, token_ref, wide, sem):
    odd_x = lax.rem(lax.axis_index("px"), 2)
    cells_y = state_ref.shape[2]
    copy = pltpu.make_async_copy(first_ref, sent_hbm, sem)
    for slot, (out_ref, x) in enumerate(((first_ref, odd_x), (second_ref, 1 - odd_x))):
        wide[slot] = state_ref[:, x].astype(jnp.float32).reshape(32 * cells_y, 128)
        for y in range(cells_y):
            out_ref[y] = wide[slot, pl.ds(y, 32, stride=cells_y), :].astype(jnp.bfloat16)
        if slot == 0:
            copy.start()
    token_ref[...] = jnp.zeros_like(token_ref)
    copy.wait()


def arrange(state):
    vmem = pl.BlockSpec(memory_space=pltpu.VMEM)
    cells_y = state.shape[2]
    plane = jax.ShapeDtypeStruct((cells_y, 32, 128), jnp.bfloat16)
    return pl.pallas_call(
        arrange_kernel,
        out_shape=(plane, plane, plane, jax.ShapeDtypeStruct((8, 128), jnp.float32)),
        in_specs=[vmem],
        out_specs=(vmem, vmem, pl.BlockSpec(memory_space=pltpu.HBM), vmem),
        scratch_shapes=[
            pltpu.VMEM((2, 32 * cells_y, 128), jnp.float32),
            pltpu.SemaphoreType.DMA,
        ],
        compiler_params=pltpu.CompilerParams(vmem_limit_bytes=16 * 2**20),
        cost_estimate=pl.CostEstimate(flops=2**10, bytes_accessed=2**10, transcendentals=0),
        name="arrange_cells",
    )(state)


def pack_kernel(
    after_ref, weight_hbm, conv_hbm, weight_out, conv_out, weight_ref, conv_ref, sems
):
    conv_copy = pltpu.make_async_copy(conv_hbm, conv_ref, sems.at[8])
    copies = [
        pltpu.make_async_copy(
            weight_hbm.at[part, kz], weight_ref.at[part, kz], sems.at[part * 4 + kz]
        )
        for part in range(2)
        for kz in range(4)
    ]
    for copy in [conv_copy] + copies:
        copy.start()
    index_x = lax.axis_index("px")
    odd_x = lax.rem(index_x, 2) == 1
    outer = (index_x == 0) | (index_x == lax.axis_size("px") - 1)
    conv_copy.wait()
    zero = jnp.zeros((32, 32), jnp.float32)
    for dz in range(3):
        taps = {
            (dx, dy): conv_ref[dx, dy, dz].astype(jnp.float32)
            for dx in range(3)
            for dy in range(3)
        }
        for y_at in range(2):
            for x_at in range(2):
                row = ((dz * 2 + y_at) * 2 + x_at) * 32
                for y_in in range(4):
                    blocks = [taps.get((x_in - x_at, y_in - y_at), zero) for x_in in range(4)]
                    blocks = [jnp.where(odd_x, blocks[3 - i], blocks[i]) for i in range(4)]
                    blocks[0] = jnp.where(outer, zero, blocks[0])
                    conv_out[row : row + 32, y_in * 128 : (y_in + 1) * 128] = jnp.concatenate(
                        blocks, axis=1
                    ).astype(jnp.bfloat16)
    for part in range(2):
        for kz in range(4):
            copies[part * 4 + kz].wait()
            for c in range(16):
                weight_out[part, kz, c] = jnp.concatenate(
                    [weight_ref[part, kz, u, c] for u in range(4)], axis=1
                )


def pack(after, spectral_weight, conv_weight):
    vmem = pl.BlockSpec(memory_space=pltpu.VMEM)
    return pl.pallas_call(
        pack_kernel,
        out_shape=(
            jax.ShapeDtypeStruct((2, 4, 16, KX, 128), jnp.float32),
            jax.ShapeDtypeStruct((384, 512), jnp.bfloat16),
        ),
        in_specs=[pl.BlockSpec(memory_space=pl.ANY)] + [pl.BlockSpec(memory_space=pltpu.HBM)] * 2,
        out_specs=(vmem, vmem),
        scratch_shapes=[
            pltpu.VMEM(spectral_weight.shape, jnp.float32),
            pltpu.VMEM(conv_weight.shape, jnp.bfloat16),
            pltpu.SemaphoreType.DMA((9,)),
        ],
        compiler_params=pltpu.CompilerParams(vmem_limit_bytes=16 * 2**20),
        cost_estimate=pl.CostEstimate(flops=2**10, bytes_accessed=2**10, transcendentals=0),
        name="pack_weights",
    )(
        after,
        *(pltpu.with_memory_space_constraint(v, pltpu.HBM) for v in (spectral_weight, conv_weight)),
    )


def mix_kernel(modes_ref, forward_ref, weight_ref, inverse_ref, out_ref):
    received = modes_ref[...].astype(jnp.float32).reshape(256, 128).astype(jnp.bfloat16)
    x_modes = jnp.dot(
        forward_ref[...].astype(jnp.bfloat16), received, preferred_element_type=jnp.float32)
    lane = lax.broadcasted_iota(jnp.int32, (16, 128), 1)
    base = (lane // 32) * 8
    mixed = []
    for kz in range(4):
        real_sum = imag_sum = None
        for c in range(16):
            half, c8 = c // 8, c % 8
            index = base + (kz * 32 + c8)
            real_in = jnp.take_along_axis(x_modes[half * 32 : half * 32 + 16], index, axis=1)
            imag_in = jnp.take_along_axis(x_modes[half * 32 + 16 : half * 32 + 32], index, axis=1)
            real_weight = weight_ref[0, kz, c]
            imag_weight = weight_ref[1, kz, c]
            real_term = real_weight * real_in - imag_weight * imag_in
            imag_term = real_weight * imag_in + imag_weight * real_in
            real_sum = real_term if real_sum is None else real_sum + real_term
            imag_sum = imag_term if imag_sum is None else imag_sum + imag_term
        mixed += [real_sum, imag_sum]
    mixed = jnp.concatenate(mixed, axis=0)
    inverse = inverse_ref[...].astype(jnp.bfloat16)
    high = mixed.astype(jnp.bfloat16)
    low = (mixed - high.astype(jnp.float32)).astype(jnp.bfloat16)
    values = jnp.dot(
        jnp.concatenate([inverse[:, :128], inverse], axis=1),
        jnp.concatenate([high, low, high], axis=0),
        preferred_element_type=jnp.float32,
    ).astype(jnp.bfloat16)
    for x in range(8):
        for y in range(4):
            out_ref[x * 4 + y] = values[16 * x : 16 * x + 16]


def mix_modes(modes, forward_table, weights, inverse_table):
    vmem = pl.BlockSpec(memory_space=pltpu.VMEM)
    return pl.pallas_call(
        mix_kernel,
        out_shape=jax.ShapeDtypeStruct((32, 16, 128), jnp.bfloat16),
        in_specs=[vmem] * 4,
        out_specs=vmem,
        compiler_params=pltpu.CompilerParams(vmem_limit_bytes=16 * 2**20),
        cost_estimate=pl.CostEstimate(flops=2**35, bytes_accessed=2**21, transcendentals=0),
        name="mix_modes",
    )(modes, forward_table, weights, inverse_table)


def cell_row(planes, y):
    return jnp.concatenate([plane[y] for plane in planes], axis=0)


def edge_rows_kernel(
    gathered_ref, own_ref, other_ref, inside_ref, plane_ref, first_ref, second_ref, sem
):
    copy = pltpu.make_async_copy(
        gathered_ref.at[lax.rem(lax.axis_index("px"), 2)], plane_ref, sem
    )
    copy.start()
    copy.wait()
    planes = (plane_ref, own_ref, other_ref, inside_ref)
    end = plane_ref.shape[0] - 1
    odd_y = lax.rem(lax.axis_index("py"), 2)
    first_ref[...] = cell_row(planes, odd_y * end)
    second_ref[...] = cell_row(planes, (1 - odd_y) * end)


def edge_rows(gathered, own, other, inside):
    vmem = pl.BlockSpec(memory_space=pltpu.VMEM)
    row = jax.ShapeDtypeStruct((128, 128), jnp.bfloat16)
    return pl.pallas_call(
        edge_rows_kernel,
        out_shape=(jax.ShapeDtypeStruct(own.shape, jnp.bfloat16), row, row),
        in_specs=[pl.BlockSpec(memory_space=pltpu.HBM)] + [vmem] * 3,
        out_specs=(vmem,) * 3,
        scratch_shapes=[pltpu.SemaphoreType.DMA],
        compiler_params=pltpu.CompilerParams(vmem_limit_bytes=16 * 2**20),
        cost_estimate=pl.CostEstimate(flops=2**10, bytes_accessed=2**17, transcendentals=0),
        name="edge_rows",
    )(pltpu.with_memory_space_constraint(gathered, pltpu.HBM), own, other, inside)


def convolve_quad(quad, row, weight, place, out_ref):
    lane = lax.broadcasted_iota(jnp.int32, (128, 256), 1) % 128
    windows = []
    for pair in range(2):
        start = quad * 4 + pair * 2 - 1
        windows.append(jnp.concatenate([row(start + i) for i in range(4)], axis=0))
    product = jnp.dot(weight, jnp.concatenate(windows, axis=1), preferred_element_type=jnp.float32)
    below = pltpu.roll(product[:128], 1, 1)
    above = pltpu.roll(product[256:], 255, 1)
    total = product[128:256] + jnp.where(lane == 0, 0.0, below)
    total = total + jnp.where(lane == 127, 0.0, above)
    for pair in range(2):
        for y_out in range(2):
            for x_out in range(2):
                first = (y_out * 2 + x_out) * 32
                value = total[first : first + 32, pair * 128 : (pair + 1) * 128]
                y = quad * 4 + pair * 2 + y_out
                at, span = place(y)
                out_ref[pl.ds(x_out * span + at, 32, stride=2 * span), :] = value


def interior_kernel(*refs):
    *planes, weight_ref, out_ref = refs
    cells_y = planes[0].shape[0]
    weight = weight_ref[...]
    for quad in range(1, cells_y // 4 - 1):
        convolve_quad(
            quad, lambda y: cell_row(planes, y), weight, lambda y: (y, cells_y), out_ref
        )


def edge_kernel(*refs):
    *planes, first_row, second_row, weight_ref, out_ref = refs
    cells_y = planes[0].shape[0]
    odd_y = lax.rem(lax.axis_index("py"), 2) == 1

    def row(y):
        if y < 0:
            return jnp.where(odd_y, second_row[...], first_row[...])
        if y >= cells_y:
            return jnp.where(odd_y, first_row[...], second_row[...])
        return cell_row(planes, y)

    weight = weight_ref[...]
    for quad in (0, cells_y // 4 - 1):
        convolve_quad(quad, row, weight, lambda y: (y % 8, 8), out_ref)


def convolve(kernel, name, operands, rows):
    vmem = pl.BlockSpec(memory_space=pltpu.VMEM)
    return pl.pallas_call(
        kernel,
        out_shape=jax.ShapeDtypeStruct((rows, 128), jnp.float32),
        in_specs=[vmem] * len(operands),
        out_specs=vmem,
        compiler_params=pltpu.CompilerParams(vmem_limit_bytes=16 * 2**20),
        cost_estimate=pl.CostEstimate(flops=2**30, bytes_accessed=2**21, transcendentals=0),
        name=name,
    )(*operands)


def gelu(value):
    return 0.5 * value * (1.0 + lax.erf(value * math.sqrt(0.5)))


def finish_kernel(
    bias_ref, values_ref, z_ref, y_ref, conv_ref, edge_ref, out_hbm, out_ref, sems
):
    upper = lax.broadcasted_iota(jnp.int32, (8, 128), 0) < 4
    table = y_ref[lax.axis_index("py")]
    lane = lax.broadcasted_iota(jnp.int32, table.shape, 1) % 16
    expanded = [jnp.where(lane == o, table, 0.0).astype(jnp.bfloat16) for o in range(16)]
    columns = []
    for group in range(4):
        columns.append(
            jnp.concatenate(
                [values_ref[(h * 4 + group) * 4 + q] for h in range(2) for q in range(4)], axis=0
            )
        )
    packed = jnp.concatenate(columns, axis=1)
    z_values = lax.dot_general(
        packed,
        z_ref[...].astype(jnp.bfloat16),
        (((0,), (0,)), ((), ())),
        preferred_element_type=jnp.float32,
    ).astype(jnp.bfloat16)
    copies = []
    for half in range(2):
        sides = []
        for x in range(2):
            parts = []
            for part in range(2):
                lanes = slice((x * 2 + part) * 128, (x * 2 + part + 1) * 128)
                parts += [
                    z_values[ky * 32 + half * 16 : ky * 32 + half * 16 + 16, lanes]
                    for ky in range(KY)
                ]
            sides.append(jnp.concatenate(parts, axis=0))
        right = jnp.concatenate(sides, axis=1)
        for block in range(4):
            spectral = jnp.dot(
                jnp.concatenate(expanded[block * 4 : block * 4 + 4], axis=0),
                right,
                preferred_element_type=jnp.float32,
            )
            for o4 in range(4):
                o = half * 16 + block * 4 + o4
                for x in range(2):
                    inner, edge = conv_ref[o, x], edge_ref[o, x]
                    convolved = jnp.concatenate(
                        [
                            jnp.where(upper, edge, inner[:8]),
                            inner[8:-8],
                            jnp.where(upper, inner[-8:], edge),
                        ],
                        axis=0,
                    )
                    total = spectral[o4 * 32 : o4 * 32 + 32, x * 128 : (x + 1) * 128]
                    total = total + convolved + bias_ref[o]
                    out_ref[o, x] = gelu(total).astype(jnp.bfloat16)
            number = half * 4 + block
            copy = pltpu.make_async_copy(
                out_ref.at[pl.ds(number * 4, 4)], out_hbm.at[pl.ds(number * 4, 4)], sems.at[number]
            )
            copy.start()
            copies.append(copy)
    for copy in copies:
        copy.wait()


def finish(bias, values, z_table, y_table, convolved, edges):
    vmem = pl.BlockSpec(memory_space=pltpu.VMEM)
    return pl.pallas_call(
        finish_kernel,
        out_shape=jax.ShapeDtypeStruct(convolved.shape, jnp.bfloat16),
        in_specs=[pl.BlockSpec(memory_space=pltpu.SMEM)] + [vmem] * 5,
        out_specs=pl.BlockSpec(memory_space=pltpu.HBM),
        scratch_shapes=[
            pltpu.VMEM(convolved.shape, jnp.bfloat16),
            pltpu.SemaphoreType.DMA((8,)),
        ],
        compiler_params=pltpu.CompilerParams(vmem_limit_bytes=16 * 2**20),
        cost_estimate=pl.CostEstimate(flops=2**28, bytes_accessed=2**22, transcendentals=2**18),
        name="finish_layer",
    )(bias, values, z_table, y_table, convolved, edges)


def exchanged(value):
    return lax.all_to_all(value, ("px", "py"), split_axis=0, concat_axis=0, tiled=True)


def pairs_inside(count):
    return [(i, i ^ 1) for i in range(count)]


def pairs_across(count):
    return [(i, i + 1 if i % 2 else i - 1) for i in range(1, count - 1)]


def gathered_across(value, axis):
    count = lax.axis_size(axis)
    groups = [[i, (i + 1) % count] for i in range(1, count, 2)]
    return lax.all_gather(value, axis, axis_index_groups=groups)


def body(state_field, conv_weight, conv_bias, spectral_weight):
    channels, cells_x, cells_y, depth = state_field.shape
    sizes = (lax.axis_size("px"), lax.axis_size("py"), cells_x, cells_y, depth)
    if sizes != (8, 4, 2, 32, 128):
        return general_body(state_field, conv_weight, conv_bias, spectral_weight)
    z_forward, y_forward, x_forward, x_inverse, z_inverse, y_inverse = tables(*sizes)
    sent, held = forward_modes(
        state_field.reshape(channels * cells_x, cells_y, depth), z_forward, y_forward
    )
    modes = exchanged(sent)
    first_own, second_own, leaving, token = arrange(held.reshape(state_field.shape))
    weights, taps = pack(
        token, spectral_weight.swapaxes(4, 5), conv_weight.transpose(2, 3, 4, 0, 1)
    )
    gathered = gathered_across(leaving, "px")
    inside = lax.ppermute(second_own, "px", pairs_inside(sizes[0]))
    values = exchanged(mix_modes(modes, x_forward, weights, x_inverse))
    across, *edges = edge_rows(gathered, first_own, second_own, inside)
    planes = (across, first_own, second_own, inside)
    first_row = lax.ppermute(edges[0], "py", pairs_across(sizes[1]))
    second_row = lax.ppermute(edges[1], "py", pairs_inside(sizes[1]))
    rows = channels * cells_x
    interior = convolve(interior_kernel, "convolve_interior", planes + (taps,), rows * cells_y)
    edges = convolve(
        edge_kernel, "convolve_edges", planes + (first_row, second_row, taps), rows * 8
    )
    return finish(
        conv_bias,
        values,
        z_inverse,
        y_inverse,
        interior.reshape(channels, cells_x, cells_y, depth),
        edges.reshape(channels, cells_x, 8, depth),
    )


def solution(mesh):
    in_specs = (P(None, "px", "py", None), P(), P(), P(None, "py", "px", None, None, None))
    out_specs = P(None, "px", "py", None)
    return jax.shard_map(body, mesh=mesh, in_specs=in_specs, out_specs=out_specs, check_vma=False)
```

```python
import functools
import math

import jax
import jax.numpy as jnp
import ml_dtypes
import numpy as np
from jax import lax
from jax.experimental import pallas as pl
from jax.experimental.pallas import tpu as pltpu
from jax.sharding import PartitionSpec as P

KX = 16
KY = 16
KZ = 16


def extended(cells, sides, width):
    for axis, dim in sides:
        count = lax.axis_size(axis)
        ends = count - 1
        head = lax.slice_in_dim(cells, 0, width, axis=dim)
        tail = lax.slice_in_dim(cells, cells.shape[dim] - width, cells.shape[dim], axis=dim)
        cells = jnp.concatenate(
            [
                lax.ppermute(tail, axis, [(i, (i + 1) % count) for i in range(ends)]),
                cells,
                lax.ppermute(head, axis, [((i + 1) % count, i) for i in range(ends)]),
            ],
            axis=dim,
        )
    return cells


def swapped(value, axis, distance):
    mask = 2**distance
    pairs = [(source, source ^ mask) for source in range(lax.axis_size(axis))]
    return lax.ppermute(value, axis, pairs)


def mode_numbers(count):
    indices = jnp.arange(count, dtype=jnp.int32)
    return jnp.where(indices < count // 2, indices, indices - count)


def trig_pair(numbers, points, length, factor, out_type):
    positions = jnp.arange(points, dtype=jnp.int32)
    phases = positions[:, None] * numbers[None, :] % length
    angles = phases.astype(jnp.float32) * (2.0 * math.pi / length)
    return (
        (jnp.cos(angles) * factor).astype(out_type),
        (jnp.sin(angles) * factor).astype(out_type),
    )


def last_product(source, table, precision=None):
    flat = source.reshape(-1, source.shape[-1])
    result = jnp.dot(flat, table, preferred_element_type=jnp.float32, precision=precision)
    return result.reshape(source.shape[:-1] + (table.shape[1],))


def forward_last(source, cosine, sine_table, precision=None):
    real_part = source[..., 0, :]
    imag_part = source[..., 1, :]
    real_out = last_product(real_part, cosine, precision) + last_product(
        imag_part, sine_table, precision
    )
    imag_out = last_product(imag_part, cosine, precision) - last_product(
        real_part, sine_table, precision
    )
    return jnp.stack([real_out, imag_out], axis=-2)


def inverse_last(source, cosine, sine_table, precision=None):
    real_part = source[..., 0, :]
    imag_part = source[..., 1, :]
    real_out = last_product(real_part, cosine, precision) - last_product(
        imag_part, sine_table, precision
    )
    imag_out = last_product(real_part, sine_table, precision) + last_product(
        imag_part, cosine, precision
    )
    return jnp.stack([real_out, imag_out], axis=-2)


def mix_block(spectral_weight, x_block):
    highest = lax.Precision.HIGHEST
    real_in = x_block[:, :, :, 0, :]
    imag_in = x_block[:, :, :, 1, :]
    partial_real = jnp.einsum(
        "zucok,uzck->uzok", spectral_weight[0], real_in, precision=highest
    ) - jnp.einsum("zucok,uzck->uzok", spectral_weight[1], imag_in, precision=highest)
    partial_imag = jnp.einsum(
        "zucok,uzck->uzok", spectral_weight[0], imag_in, precision=highest
    ) + jnp.einsum("zucok,uzck->uzok", spectral_weight[1], real_in, precision=highest)
    return jnp.stack([partial_real, partial_imag], axis=3)


def general_body(state_field, conv_weight, conv_bias, spectral_weight):
    channels, cells_x, cells_y, depth = state_field.shape
    count_x = lax.axis_size("px")
    count_y = lax.axis_size("py")
    width_x = cells_x * count_x
    width_y = cells_y * count_y
    index_x = lax.axis_index("px")
    kz_local = KZ // count_y
    units = 2 * KY // count_x
    highest = lax.Precision.HIGHEST
    padded = extended(state_field, (("px", 1), ("py", 2)), 1)
    convolved = lax.conv_general_dilated(
        padded[None],
        conv_weight,
        (1, 1, 1),
        ((0, 0), (0, 0), (1, 1)),
        dimension_numbers=("NCDHW", "OIDHW", "NCDHW"),
        preferred_element_type=jnp.float32,
    )[0]
    z_cos, z_sin = trig_pair(
        jnp.arange(KZ, dtype=jnp.int32), depth, depth, depth ** (-0.5), jnp.bfloat16
    )
    z_table = jnp.stack([z_cos, -z_sin], axis=1)
    z_modes = jnp.einsum(
        "cxyn,nwk->kcxwy", state_field, z_table, preferred_element_type=jnp.float32
    ).astype(jnp.bfloat16)
    y_cos, y_sin = trig_pair(mode_numbers(KY), width_y, width_y, width_y ** (-0.5), jnp.bfloat16)
    full_rows = lax.all_to_all(z_modes, "py", split_axis=0, concat_axis=4, tiled=True)
    y_modes = forward_last(full_rows, y_cos, y_sin)
    y_modes = y_modes.astype(jnp.bfloat16)
    by_unit = y_modes.reshape(kz_local, 2, channels // 2, cells_x, 2, KY).transpose(
        1, 5, 0, 2, 4, 3
    )
    by_unit = by_unit.reshape(2 * KY, kz_local, channels // 2, 2, cells_x)
    x_rows = lax.all_to_all(by_unit, "px", split_axis=0, concat_axis=4, tiled=True)
    x_cos, x_sin = trig_pair(mode_numbers(KX), width_x, width_x, width_x ** (-0.5), jnp.bfloat16)
    x_modes = forward_last(x_rows, x_cos, x_sin)
    partial_modes = mix_block(spectral_weight, x_modes)
    partial_modes = partial_modes.reshape(units, kz_local, 2, channels // 2, 2, KX)
    half_index = index_x * units // KY
    own_half = lax.dynamic_index_in_dim(partial_modes, half_index, 2, keepdims=False)
    other_half = lax.dynamic_index_in_dim(partial_modes, 1 - half_index, 2, keepdims=False)
    mixed_modes = own_half + swapped(other_half, "px", count_x.bit_length() - 2)
    ix_cos, ix_sin = trig_pair(mode_numbers(KX), width_x, width_x, KX ** (-0.5), jnp.float32)
    x_values = inverse_last(mixed_modes, ix_cos.T, ix_sin.T, highest).astype(jnp.bfloat16)
    returned = lax.all_to_all(x_values, "px", split_axis=4, concat_axis=0, tiled=True)
    returned = returned.reshape(2, KY, kz_local, channels // 2, 2, cells_x).transpose(
        2, 0, 3, 5, 4, 1
    )
    returned = returned.reshape(kz_local, channels, cells_x, 2, KY)
    iy_cos, iy_sin = trig_pair(mode_numbers(KY), width_y, width_y, KY ** (-0.5), jnp.bfloat16)
    expanded = inverse_last(returned, iy_cos.T, iy_sin.T).astype(jnp.bfloat16)
    y_values = lax.all_to_all(expanded, "py", split_axis=4, concat_axis=0, tiled=True)
    iz_cos, iz_sin = trig_pair(
        jnp.arange(KZ, dtype=jnp.int32), depth, depth, KZ ** (-0.5), jnp.bfloat16
    )
    iz_table = jnp.stack([iz_cos.T, -iz_sin.T], axis=0)
    spectral = jnp.einsum("kcxwy,wkn->cxyn", y_values, iz_table, preferred_element_type=jnp.float32)
    total = convolved + spectral + conv_bias[:, None, None, None]
    return jax.nn.gelu(total, approximate=False).astype(jnp.bfloat16)


def angle_tables(numbers, points, length, factor):
    phases = (np.arange(points)[:, None] * numbers[None, :]) % length
    angles = phases.astype(np.float32) * np.float32(2.0 * math.pi / length)
    return (
        np.cos(angles).astype(np.float32) * np.float32(factor),
        np.sin(angles).astype(np.float32) * np.float32(factor),
    )


def signed_modes(count):
    indices = np.arange(count)
    return np.where(indices < count // 2, indices, indices - count)


def narrow(table):
    return table.astype(ml_dtypes.bfloat16).astype(np.float32)


def forward_pair(cosine, sine):
    return np.stack([np.stack([cosine, -sine]), np.stack([sine, cosine])])


def inverse_pair(cosine, sine):
    return np.stack([np.stack([cosine, sine]), np.stack([-sine, cosine])])


@functools.cache
def tables(count_x, count_y, cells_x, cells_y, depth):
    width_x, width_y = count_x * cells_x, count_y * cells_y
    kzl, units = KZ // count_y, 2 * KY // count_x
    groups = KY // units
    zc, zs = angle_tables(np.arange(KZ), depth, depth, depth**-0.5)
    z_forward = np.concatenate([zc.T, -zs.T])
    yc, ys = angle_tables(signed_modes(KY), width_y, width_y, width_y**-0.5)
    pair = forward_pair(yc, ys).reshape(2, 2, count_y, cells_y, groups, units)
    y_forward = np.einsum("rsqygk,d,w->qrygwskd", pair, np.ones(8), np.ones(cells_x))
    y_forward = y_forward.reshape(count_y, 2 * cells_y, groups * 2 * cells_x * units * 8)
    xc, xs = angle_tables(signed_modes(KX), width_x, width_x, width_x**-0.5)
    pair = forward_pair(xc, xs).reshape(2, 2, count_x, cells_x, KX)
    x_forward = np.einsum("rspxk,gh,q->gskpqhxr", pair, np.eye(2), np.ones(count_y))
    x_forward = x_forward.reshape(4 * KX, count_x * count_y * 4 * cells_x)
    xc, xs = angle_tables(signed_modes(KX), width_x, width_x, KX**-0.5)
    pair = inverse_pair(xc, xs).reshape(2, 2, count_x, cells_x, KX)
    x_inverse = np.einsum("rspxk,zv->pxzsvrk", pair, np.eye(kzl))
    x_inverse = x_inverse.reshape(count_x * cells_x * kzl * 2, kzl * 2 * KX)
    zc, zs = angle_tables(np.arange(KZ), depth, depth, KZ**-0.5)
    pair = inverse_pair(zc, zs).reshape(2, 2, depth, count_y, kzl)
    z_inverse = np.einsum("rsnqz,xw,h->hqxzrwsn", pair, np.eye(cells_x), np.ones(2))
    z_inverse = z_inverse.reshape(4 * cells_x * KZ, cells_x * 2 * depth)
    yc, ys = angle_tables(signed_modes(KY), width_y, width_y, KY**-0.5)
    pair = np.stack([yc, -ys]).reshape(2, count_y, cells_y, KY)
    y_inverse = np.einsum("rqyk,i->qyrki", pair, np.ones(16))
    y_inverse = y_inverse.reshape(count_y, cells_y, 32 * KY)
    return (
        narrow(z_forward),
        narrow(y_forward),
        narrow(x_forward),
        np.concatenate(
            [narrow(x_inverse), narrow(x_inverse - narrow(x_inverse))], axis=1
        ),
        narrow(z_inverse),
        narrow(y_inverse),
    )


def block_moves(value):
    rows = value.shape[0]
    tiles = value.reshape(rows // 8, 8, 128)
    row = lax.broadcasted_iota(jnp.int32, tiles.shape, 1) % 4
    block = lax.broadcasted_iota(jnp.int32, tiles.shape, 2) // 32
    result = tiles
    for lane_step in (1, 2, 3):
        moved = pltpu.roll(tiles, 128 - 32 * lane_step, 2)
        result = jnp.where(row - block == lane_step, pltpu.roll(moved, lane_step, 1), result)
        result = jnp.where(
            row - block == lane_step - 4, pltpu.roll(moved, 8 + lane_step - 4, 1), result
        )
    return result


def forward_kernel(
    state_hbm,
    z_hbm,
    y_hbm,
    weight_hbm,
    conv_hbm,
    out_hbm,
    state_ref,
    packed_ref,
    conv_ref,
    out_ref,
    z_ref,
    y_ref,
    table_ref,
    weight_ref,
    sems,
):
    count = state_ref.shape[0] // 4
    span = state_ref.shape[1]
    y_copy = pltpu.make_async_copy(y_hbm.at[lax.axis_index("py")], y_ref, sems.at[0])
    z_copy = pltpu.make_async_copy(z_hbm, z_ref, sems.at[1])
    copies = [
        pltpu.make_async_copy(
            state_hbm.at[pl.ds(g * count, count)],
            state_ref.at[pl.ds(g * count, count)],
            sems.at[2 + g],
        )
        for g in range(4)
    ]
    conv_copy = pltpu.make_async_copy(conv_hbm, conv_ref, sems.at[6])
    weight_copies = [
        pltpu.make_async_copy(
            weight_hbm.at[part, kz], weight_ref.at[part, kz], sems.at[7 + part * 4 + kz]
        )
        for part in range(2)
        for kz in range(4)
    ]
    for copy in [y_copy, z_copy] + copies + weight_copies + [conv_copy]:
        copy.start()
    y_copy.wait()
    table = y_ref[...]
    lane = lax.broadcasted_iota(jnp.int32, (span, table.shape[1]), 1)
    for x in range(2):
        for c in range(8):
            own = (lane % 8 == c) & (lane // 64 % 2 == x)
            for part in range(2):
                first = part * 16 * span + (c * 2 + x) * span
                block = jnp.where(own, table[part * span : (part + 1) * span], 0.0)
                table_ref[first : first + span] = block.astype(jnp.bfloat16)
    z_copy.wait()
    z_table = z_ref[...].astype(jnp.bfloat16)
    pieces = []
    for g in range(4):
        copies[g].wait()
        cells = state_ref[g * count : (g + 1) * count].reshape(count * span, state_ref.shape[2])
        z_modes = lax.dot_general(
            z_table, cells, (((1,), (1,)), ((), ())), preferred_element_type=jnp.float32
        ).astype(jnp.bfloat16)
        pieces.append(jnp.concatenate([z_modes[:KZ], z_modes[KZ:]], axis=1))
    stacked = jnp.concatenate(pieces, axis=0)
    modes = jnp.dot(stacked, table_ref[...], preferred_element_type=jnp.float32)
    for group in range(4):
        moved = block_moves(modes[:, group * 128 : (group + 1) * 128])
        for half in range(2):
            for pair in range(2):
                first = moved[half * 4 + pair]
                second = moved[half * 4 + 2 + pair]
                for side in range(2):
                    rows4 = slice(4 * side, 4 * side + 4)
                    chunk = jnp.concatenate([first[rows4], second[rows4]], axis=0)
                    out_ref[(half * 4 + group) * 4 + 2 * pair + side] = chunk.astype(jnp.bfloat16)
    out_copy = pltpu.make_async_copy(out_ref, out_hbm, sems.at[15])
    out_copy.start()
    for part in range(2):
        for kz in range(4):
            weight_copies[part * 4 + kz].wait()
            for c in range(16):
                packed_ref[part, kz, c] = jnp.concatenate(
                    [weight_ref[part, kz, u, c] for u in range(4)], axis=1
                )
    conv_copy.wait()
    out_copy.wait()


def forward_modes(state, z_table, y_table, spectral_weight, conv_weight):
    vmem, hbm = (pl.BlockSpec(memory_space=space) for space in (pltpu.VMEM, pltpu.HBM))
    sent = (32, 8, 128)
    return pl.pallas_call(
        forward_kernel,
        out_shape=(
            jax.ShapeDtypeStruct(sent, jnp.bfloat16),
            jax.ShapeDtypeStruct(state.shape, jnp.bfloat16),
            jax.ShapeDtypeStruct((2, 4, 16, KX, 128), jnp.float32),
            jax.ShapeDtypeStruct(conv_weight.shape, jnp.bfloat16),
        ),
        in_specs=[hbm] * 5,
        out_specs=(hbm, vmem, vmem, vmem),
        scratch_shapes=[
            pltpu.VMEM(sent, jnp.bfloat16),
            pltpu.VMEM(z_table.shape, jnp.float32),
            pltpu.VMEM(y_table.shape[1:], jnp.float32),
            pltpu.VMEM((32 * state.shape[1], y_table.shape[2]), jnp.bfloat16),
            pltpu.VMEM(spectral_weight.shape, jnp.float32),
            pltpu.SemaphoreType.DMA((16,)),
        ],
        compiler_params=pltpu.CompilerParams(vmem_limit_bytes=16 * 2**20),
        cost_estimate=pl.CostEstimate(flops=2**27, bytes_accessed=2**21, transcendentals=0),
        name="forward_modes",
    )(
        *(
            pltpu.with_memory_space_constraint(v, pltpu.HBM)
            for v in (state, z_table, y_table, spectral_weight, conv_weight)
        )
    )


def arrange_kernel(state_ref, conv_ref, first_ref, second_ref, conv_out, wide):
    odd_x = lax.rem(lax.axis_index("px"), 2)
    cells_y = state_ref.shape[2]
    for slot, (out_ref, x) in enumerate(((first_ref, odd_x), (second_ref, 1 - odd_x))):
        wide[slot] = state_ref[:, x].astype(jnp.float32).reshape(32 * cells_y, 128)
        for y in range(cells_y):
            out_ref[y] = wide[slot, pl.ds(y, 32, stride=cells_y), :].astype(jnp.bfloat16)
    zero = jnp.zeros((32, 32), jnp.float32)
    for dz in range(3):
        taps = {
            (dx, dy): conv_ref[dx, dy, dz].astype(jnp.float32)
            for dx in range(3)
            for dy in range(3)
        }
        for y_at in range(2):
            for x_at in range(2):
                row = ((dz * 2 + y_at) * 2 + x_at) * 32
                for y_in in range(4):
                    blocks = [taps.get((x_in - x_at, y_in - y_at), zero) for x_in in range(4)]
                    blocks = [jnp.where(odd_x == 1, blocks[3 - i], blocks[i]) for i in range(4)]
                    conv_out[row : row + 32, y_in * 128 : (y_in + 1) * 128] = jnp.concatenate(
                        blocks, axis=1
                    ).astype(jnp.bfloat16)


def arrange(state, conv_weight):
    vmem = pl.BlockSpec(memory_space=pltpu.VMEM)
    cells_y = state.shape[2]
    plane = jax.ShapeDtypeStruct((cells_y, 32, 128), jnp.bfloat16)
    return pl.pallas_call(
        arrange_kernel,
        out_shape=(plane, plane, jax.ShapeDtypeStruct((384, 512), jnp.bfloat16)),
        in_specs=[vmem] * 2,
        out_specs=(vmem,) * 3,
        scratch_shapes=[pltpu.VMEM((2, 32 * cells_y, 128), jnp.float32)],
        compiler_params=pltpu.CompilerParams(vmem_limit_bytes=16 * 2**20),
        cost_estimate=pl.CostEstimate(flops=2**10, bytes_accessed=2**10, transcendentals=0),
        name="arrange_cells",
    )(state, conv_weight)


def mix_kernel(modes_ref, forward_ref, weight_ref, inverse_ref, out_ref):
    received = modes_ref[...].astype(jnp.float32).reshape(256, 128).astype(jnp.bfloat16)
    x_modes = jnp.dot(
        forward_ref[...].astype(jnp.bfloat16), received, preferred_element_type=jnp.float32)
    lane = lax.broadcasted_iota(jnp.int32, (16, 128), 1)
    base = (lane // 32) * 8
    mixed = []
    for kz in range(4):
        real_sum = imag_sum = None
        for c in range(16):
            half, c8 = c // 8, c % 8
            index = base + (kz * 32 + c8)
            real_in = jnp.take_along_axis(x_modes[half * 32 : half * 32 + 16], index, axis=1)
            imag_in = jnp.take_along_axis(x_modes[half * 32 + 16 : half * 32 + 32], index, axis=1)
            real_weight = weight_ref[0, kz, c]
            imag_weight = weight_ref[1, kz, c]
            real_term = real_weight * real_in - imag_weight * imag_in
            imag_term = real_weight * imag_in + imag_weight * real_in
            real_sum = real_term if real_sum is None else real_sum + real_term
            imag_sum = imag_term if imag_sum is None else imag_sum + imag_term
        mixed += [real_sum, imag_sum]
    mixed = jnp.concatenate(mixed, axis=0)
    inverse = inverse_ref[...].astype(jnp.bfloat16)
    high = mixed.astype(jnp.bfloat16)
    low = (mixed - high.astype(jnp.float32)).astype(jnp.bfloat16)
    values = jnp.dot(
        jnp.concatenate([inverse[:, :128], inverse], axis=1),
        jnp.concatenate([high, low, high], axis=0),
        preferred_element_type=jnp.float32,
    ).astype(jnp.bfloat16)
    for x in range(8):
        for y in range(4):
            out_ref[x * 4 + y] = values[16 * x : 16 * x + 16]


def mix_modes(modes, forward_table, weights, inverse_table):
    vmem = pl.BlockSpec(memory_space=pltpu.VMEM)
    return pl.pallas_call(
        mix_kernel,
        out_shape=jax.ShapeDtypeStruct((32, 16, 128), jnp.bfloat16),
        in_specs=[vmem] * 4,
        out_specs=vmem,
        compiler_params=pltpu.CompilerParams(vmem_limit_bytes=16 * 2**20),
        cost_estimate=pl.CostEstimate(flops=2**35, bytes_accessed=2**21, transcendentals=0),
        name="mix_modes",
    )(modes, forward_table, weights, inverse_table)


def cell_row(planes, y):
    return jnp.concatenate([plane[y] for plane in planes], axis=0)


def edge_rows_kernel(*refs):
    *planes, first_ref, second_ref = refs
    end = planes[0].shape[0] - 1
    odd_y = lax.rem(lax.axis_index("py"), 2)
    first_ref[...] = cell_row(planes, odd_y * end)
    second_ref[...] = cell_row(planes, (1 - odd_y) * end)


def edge_rows(planes):
    vmem = pl.BlockSpec(memory_space=pltpu.VMEM)
    row = jax.ShapeDtypeStruct((128, 128), jnp.bfloat16)
    return pl.pallas_call(
        edge_rows_kernel,
        out_shape=(row, row),
        in_specs=[vmem] * 4,
        out_specs=(vmem, vmem),
        compiler_params=pltpu.CompilerParams(vmem_limit_bytes=16 * 2**20),
        cost_estimate=pl.CostEstimate(flops=2**10, bytes_accessed=2**17, transcendentals=0),
        name="edge_rows",
    )(*planes)


def convolve_quad(quad, row, weight, place, out_ref):
    lane = lax.broadcasted_iota(jnp.int32, (128, 256), 1) % 128
    windows = []
    for pair in range(2):
        start = quad * 4 + pair * 2 - 1
        windows.append(jnp.concatenate([row(start + i) for i in range(4)], axis=0))
    product = jnp.dot(weight, jnp.concatenate(windows, axis=1), preferred_element_type=jnp.float32)
    below = pltpu.roll(product[:128], 1, 1)
    above = pltpu.roll(product[256:], 255, 1)
    total = product[128:256] + jnp.where(lane == 0, 0.0, below)
    total = total + jnp.where(lane == 127, 0.0, above)
    for pair in range(2):
        for y_out in range(2):
            for x_out in range(2):
                first = (y_out * 2 + x_out) * 32
                value = total[first : first + 32, pair * 128 : (pair + 1) * 128]
                y = quad * 4 + pair * 2 + y_out
                at, span = place(y)
                out_ref[pl.ds(x_out * span + at, 32, stride=2 * span), :] = value


def interior_kernel(*refs):
    *planes, weight_ref, out_ref = refs
    cells_y = planes[0].shape[0]
    weight = weight_ref[...]
    for quad in range(1, cells_y // 4 - 1):
        convolve_quad(
            quad, lambda y: cell_row(planes, y), weight, lambda y: (y, cells_y), out_ref
        )


def edge_kernel(*refs):
    *planes, first_row, second_row, weight_ref, out_ref = refs
    cells_y = planes[0].shape[0]
    odd_y = lax.rem(lax.axis_index("py"), 2) == 1

    def row(y):
        if y < 0:
            return jnp.where(odd_y, second_row[...], first_row[...])
        if y >= cells_y:
            return jnp.where(odd_y, first_row[...], second_row[...])
        return cell_row(planes, y)

    weight = weight_ref[...]
    for quad in (0, cells_y // 4 - 1):
        convolve_quad(quad, row, weight, lambda y: (y % 8, 8), out_ref)


def convolve(kernel, name, operands, rows):
    vmem = pl.BlockSpec(memory_space=pltpu.VMEM)
    return pl.pallas_call(
        kernel,
        out_shape=jax.ShapeDtypeStruct((rows, 128), jnp.float32),
        in_specs=[vmem] * len(operands),
        out_specs=vmem,
        compiler_params=pltpu.CompilerParams(vmem_limit_bytes=16 * 2**20),
        cost_estimate=pl.CostEstimate(flops=2**30, bytes_accessed=2**21, transcendentals=0),
        name=name,
    )(*operands)


def gelu(value):
    return 0.5 * value * (1.0 + lax.erf(value * math.sqrt(0.5)))


def finish_kernel(
    bias_ref, values_ref, z_ref, y_ref, conv_ref, edge_ref, out_hbm, out_ref, sems
):
    upper = lax.broadcasted_iota(jnp.int32, (8, 128), 0) < 4
    table = y_ref[lax.axis_index("py")]
    lane = lax.broadcasted_iota(jnp.int32, table.shape, 1) % 16
    expanded = [jnp.where(lane == o, table, 0.0).astype(jnp.bfloat16) for o in range(16)]
    columns = []
    for group in range(4):
        columns.append(
            jnp.concatenate(
                [values_ref[(h * 4 + group) * 4 + q] for h in range(2) for q in range(4)], axis=0
            )
        )
    packed = jnp.concatenate(columns, axis=1)
    z_values = lax.dot_general(
        packed,
        z_ref[...].astype(jnp.bfloat16),
        (((0,), (0,)), ((), ())),
        preferred_element_type=jnp.float32,
    ).astype(jnp.bfloat16)
    copies = []
    for half in range(2):
        sides = []
        for x in range(2):
            parts = []
            for part in range(2):
                lanes = slice((x * 2 + part) * 128, (x * 2 + part + 1) * 128)
                parts += [
                    z_values[ky * 32 + half * 16 : ky * 32 + half * 16 + 16, lanes]
                    for ky in range(KY)
                ]
            sides.append(jnp.concatenate(parts, axis=0))
        right = jnp.concatenate(sides, axis=1)
        for block in range(4):
            spectral = jnp.dot(
                jnp.concatenate(expanded[block * 4 : block * 4 + 4], axis=0),
                right,
                preferred_element_type=jnp.float32,
            )
            for o4 in range(4):
                o = half * 16 + block * 4 + o4
                for x in range(2):
                    inner, edge = conv_ref[o, x], edge_ref[o, x]
                    convolved = jnp.concatenate(
                        [
                            jnp.where(upper, edge, inner[:8]),
                            inner[8:-8],
                            jnp.where(upper, inner[-8:], edge),
                        ],
                        axis=0,
                    )
                    total = spectral[o4 * 32 : o4 * 32 + 32, x * 128 : (x + 1) * 128]
                    total = total + convolved + bias_ref[o]
                    out_ref[o, x] = gelu(total).astype(jnp.bfloat16)
            number = half * 4 + block
            copy = pltpu.make_async_copy(
                out_ref.at[pl.ds(number * 4, 4)], out_hbm.at[pl.ds(number * 4, 4)], sems.at[number]
            )
            copy.start()
            copies.append(copy)
    for copy in copies:
        copy.wait()


def finish(bias, values, z_table, y_table, convolved, edges):
    vmem = pl.BlockSpec(memory_space=pltpu.VMEM)
    return pl.pallas_call(
        finish_kernel,
        out_shape=jax.ShapeDtypeStruct(convolved.shape, jnp.bfloat16),
        in_specs=[pl.BlockSpec(memory_space=pltpu.SMEM)] + [vmem] * 5,
        out_specs=pl.BlockSpec(memory_space=pltpu.HBM),
        scratch_shapes=[
            pltpu.VMEM(convolved.shape, jnp.bfloat16),
            pltpu.SemaphoreType.DMA((8,)),
        ],
        compiler_params=pltpu.CompilerParams(vmem_limit_bytes=16 * 2**20),
        cost_estimate=pl.CostEstimate(flops=2**28, bytes_accessed=2**22, transcendentals=2**18),
        name="finish_layer",
    )(bias, values, z_table, y_table, convolved, edges)


def exchanged(value):
    return lax.all_to_all(value, ("px", "py"), split_axis=0, concat_axis=0, tiled=True)


def swaps(first, second, axis):
    count = lax.axis_size(axis)
    inside = [(i, i ^ 1) for i in range(count)]
    across = [(i, i + 1 if i % 2 else i - 1) for i in range(1, count - 1)]
    return lax.ppermute(first, axis, across), lax.ppermute(second, axis, inside)


def body(state_field, conv_weight, conv_bias, spectral_weight):
    channels, cells_x, cells_y, depth = state_field.shape
    sizes = (lax.axis_size("px"), lax.axis_size("py"), cells_x, cells_y, depth)
    if sizes != (8, 4, 2, 32, 128):
        return general_body(state_field, conv_weight, conv_bias, spectral_weight)
    z_forward, y_forward, x_forward, x_inverse, z_inverse, y_inverse = tables(*sizes)
    sent, held, weights, conv_held = forward_modes(
        state_field.reshape(channels * cells_x, cells_y, depth),
        z_forward,
        y_forward,
        spectral_weight.swapaxes(4, 5),
        conv_weight.transpose(2, 3, 4, 0, 1),
    )
    modes = exchanged(sent)
    first_own, second_own, taps = arrange(held.reshape(state_field.shape), conv_held)
    first_plane, second_plane = swaps(first_own, second_own, "px")
    values = exchanged(mix_modes(modes, x_forward, weights, x_inverse))
    planes = (first_plane, first_own, second_own, second_plane)
    first_row, second_row = swaps(*edge_rows(planes), "py")
    rows = channels * cells_x
    interior = convolve(interior_kernel, "convolve_interior", planes + (taps,), rows * cells_y)
    edges = convolve(
        edge_kernel, "convolve_edges", planes + (first_row, second_row, taps), rows * 8
    )
    return finish(
        conv_bias,
        values,
        z_inverse,
        y_inverse,
        interior.reshape(channels, cells_x, cells_y, depth),
        edges.reshape(channels, cells_x, 8, depth),
    )


def solution(mesh):
    in_specs = (P(None, "px", "py", None), P(), P(), P(None, "py", "px", None, None, None))
    out_specs = P(None, "px", "py", None)
    return jax.shard_map(body, mesh=mesh, in_specs=in_specs, out_specs=out_specs, check_vma=False)
```

```python
import functools
import math

import jax
import jax.numpy as jnp
import ml_dtypes
import numpy as np
from jax import lax
from jax.experimental import pallas as pl
from jax.experimental.pallas import tpu as pltpu
from jax.sharding import PartitionSpec as P

KX = 16
KY = 16
KZ = 16


def extended(cells, sides, width):
    for axis, dim in sides:
        count = lax.axis_size(axis)
        ends = count - 1
        head = lax.slice_in_dim(cells, 0, width, axis=dim)
        tail = lax.slice_in_dim(cells, cells.shape[dim] - width, cells.shape[dim], axis=dim)
        cells = jnp.concatenate(
            [
                lax.ppermute(tail, axis, [(i, (i + 1) % count) for i in range(ends)]),
                cells,
                lax.ppermute(head, axis, [((i + 1) % count, i) for i in range(ends)]),
            ],
            axis=dim,
        )
    return cells


def swapped(value, axis, distance):
    mask = 2**distance
    pairs = [(source, source ^ mask) for source in range(lax.axis_size(axis))]
    return lax.ppermute(value, axis, pairs)


def mode_numbers(count):
    indices = jnp.arange(count, dtype=jnp.int32)
    return jnp.where(indices < count // 2, indices, indices - count)


def trig_pair(numbers, points, length, factor, out_type):
    positions = jnp.arange(points, dtype=jnp.int32)
    phases = positions[:, None] * numbers[None, :] % length
    angles = phases.astype(jnp.float32) * (2.0 * math.pi / length)
    return (
        (jnp.cos(angles) * factor).astype(out_type),
        (jnp.sin(angles) * factor).astype(out_type),
    )


def last_product(source, table, precision=None):
    flat = source.reshape(-1, source.shape[-1])
    result = jnp.dot(flat, table, preferred_element_type=jnp.float32, precision=precision)
    return result.reshape(source.shape[:-1] + (table.shape[1],))


def forward_last(source, cosine, sine_table, precision=None):
    real_part = source[..., 0, :]
    imag_part = source[..., 1, :]
    real_out = last_product(real_part, cosine, precision) + last_product(
        imag_part, sine_table, precision
    )
    imag_out = last_product(imag_part, cosine, precision) - last_product(
        real_part, sine_table, precision
    )
    return jnp.stack([real_out, imag_out], axis=-2)


def inverse_last(source, cosine, sine_table, precision=None):
    real_part = source[..., 0, :]
    imag_part = source[..., 1, :]
    real_out = last_product(real_part, cosine, precision) - last_product(
        imag_part, sine_table, precision
    )
    imag_out = last_product(real_part, sine_table, precision) + last_product(
        imag_part, cosine, precision
    )
    return jnp.stack([real_out, imag_out], axis=-2)


def mix_block(spectral_weight, x_block):
    highest = lax.Precision.HIGHEST
    real_in = x_block[:, :, :, 0, :]
    imag_in = x_block[:, :, :, 1, :]
    partial_real = jnp.einsum(
        "zucok,uzck->uzok", spectral_weight[0], real_in, precision=highest
    ) - jnp.einsum("zucok,uzck->uzok", spectral_weight[1], imag_in, precision=highest)
    partial_imag = jnp.einsum(
        "zucok,uzck->uzok", spectral_weight[0], imag_in, precision=highest
    ) + jnp.einsum("zucok,uzck->uzok", spectral_weight[1], real_in, precision=highest)
    return jnp.stack([partial_real, partial_imag], axis=3)


def general_body(state_field, conv_weight, conv_bias, spectral_weight):
    channels, cells_x, cells_y, depth = state_field.shape
    count_x = lax.axis_size("px")
    count_y = lax.axis_size("py")
    width_x = cells_x * count_x
    width_y = cells_y * count_y
    index_x = lax.axis_index("px")
    kz_local = KZ // count_y
    units = 2 * KY // count_x
    highest = lax.Precision.HIGHEST
    padded = extended(state_field, (("px", 1), ("py", 2)), 1)
    convolved = lax.conv_general_dilated(
        padded[None],
        conv_weight,
        (1, 1, 1),
        ((0, 0), (0, 0), (1, 1)),
        dimension_numbers=("NCDHW", "OIDHW", "NCDHW"),
        preferred_element_type=jnp.float32,
    )[0]
    z_cos, z_sin = trig_pair(
        jnp.arange(KZ, dtype=jnp.int32), depth, depth, depth ** (-0.5), jnp.bfloat16
    )
    z_table = jnp.stack([z_cos, -z_sin], axis=1)
    z_modes = jnp.einsum(
        "cxyn,nwk->kcxwy", state_field, z_table, preferred_element_type=jnp.float32
    ).astype(jnp.bfloat16)
    y_cos, y_sin = trig_pair(mode_numbers(KY), width_y, width_y, width_y ** (-0.5), jnp.bfloat16)
    full_rows = lax.all_to_all(z_modes, "py", split_axis=0, concat_axis=4, tiled=True)
    y_modes = forward_last(full_rows, y_cos, y_sin)
    y_modes = y_modes.astype(jnp.bfloat16)
    by_unit = y_modes.reshape(kz_local, 2, channels // 2, cells_x, 2, KY).transpose(
        1, 5, 0, 2, 4, 3
    )
    by_unit = by_unit.reshape(2 * KY, kz_local, channels // 2, 2, cells_x)
    x_rows = lax.all_to_all(by_unit, "px", split_axis=0, concat_axis=4, tiled=True)
    x_cos, x_sin = trig_pair(mode_numbers(KX), width_x, width_x, width_x ** (-0.5), jnp.bfloat16)
    x_modes = forward_last(x_rows, x_cos, x_sin)
    partial_modes = mix_block(spectral_weight, x_modes)
    partial_modes = partial_modes.reshape(units, kz_local, 2, channels // 2, 2, KX)
    half_index = index_x * units // KY
    own_half = lax.dynamic_index_in_dim(partial_modes, half_index, 2, keepdims=False)
    other_half = lax.dynamic_index_in_dim(partial_modes, 1 - half_index, 2, keepdims=False)
    mixed_modes = own_half + swapped(other_half, "px", count_x.bit_length() - 2)
    ix_cos, ix_sin = trig_pair(mode_numbers(KX), width_x, width_x, KX ** (-0.5), jnp.float32)
    x_values = inverse_last(mixed_modes, ix_cos.T, ix_sin.T, highest).astype(jnp.bfloat16)
    returned = lax.all_to_all(x_values, "px", split_axis=4, concat_axis=0, tiled=True)
    returned = returned.reshape(2, KY, kz_local, channels // 2, 2, cells_x).transpose(
        2, 0, 3, 5, 4, 1
    )
    returned = returned.reshape(kz_local, channels, cells_x, 2, KY)
    iy_cos, iy_sin = trig_pair(mode_numbers(KY), width_y, width_y, KY ** (-0.5), jnp.bfloat16)
    expanded = inverse_last(returned, iy_cos.T, iy_sin.T).astype(jnp.bfloat16)
    y_values = lax.all_to_all(expanded, "py", split_axis=4, concat_axis=0, tiled=True)
    iz_cos, iz_sin = trig_pair(
        jnp.arange(KZ, dtype=jnp.int32), depth, depth, KZ ** (-0.5), jnp.bfloat16
    )
    iz_table = jnp.stack([iz_cos.T, -iz_sin.T], axis=0)
    spectral = jnp.einsum("kcxwy,wkn->cxyn", y_values, iz_table, preferred_element_type=jnp.float32)
    total = convolved + spectral + conv_bias[:, None, None, None]
    return jax.nn.gelu(total, approximate=False).astype(jnp.bfloat16)


def angle_tables(numbers, points, length, factor):
    phases = (np.arange(points)[:, None] * numbers[None, :]) % length
    angles = phases.astype(np.float32) * np.float32(2.0 * math.pi / length)
    return (
        np.cos(angles).astype(np.float32) * np.float32(factor),
        np.sin(angles).astype(np.float32) * np.float32(factor),
    )


def signed_modes(count):
    indices = np.arange(count)
    return np.where(indices < count // 2, indices, indices - count)


def narrow(table):
    return table.astype(ml_dtypes.bfloat16).astype(np.float32)


def forward_pair(cosine, sine):
    return np.stack([np.stack([cosine, -sine]), np.stack([sine, cosine])])


def inverse_pair(cosine, sine):
    return np.stack([np.stack([cosine, sine]), np.stack([-sine, cosine])])


@functools.cache
def tables(count_x, count_y, cells_x, cells_y, depth):
    width_x, width_y = count_x * cells_x, count_y * cells_y
    kzl, units = KZ // count_y, 2 * KY // count_x
    groups = KY // units
    zc, zs = angle_tables(np.arange(KZ), depth, depth, depth**-0.5)
    z_forward = np.concatenate([zc.T, -zs.T])
    yc, ys = angle_tables(signed_modes(KY), width_y, width_y, width_y**-0.5)
    pair = forward_pair(yc, ys).reshape(2, 2, count_y, cells_y, groups, units)
    y_forward = np.einsum("rsqygk,d,w->qrygwskd", pair, np.ones(8), np.ones(cells_x))
    y_forward = y_forward.reshape(count_y, 2 * cells_y, groups * 2 * cells_x * units * 8)
    xc, xs = angle_tables(signed_modes(KX), width_x, width_x, width_x**-0.5)
    pair = forward_pair(xc, xs).reshape(2, 2, count_x, cells_x, KX)
    x_forward = np.einsum("rspxk,gh,q->gskpqhxr", pair, np.eye(2), np.ones(count_y))
    x_forward = x_forward.reshape(4 * KX, count_x * count_y * 4 * cells_x)
    xc, xs = angle_tables(signed_modes(KX), width_x, width_x, KX**-0.5)
    pair = inverse_pair(xc, xs).reshape(2, 2, count_x, cells_x, KX)
    x_inverse = np.einsum("rspxk,zv->pxzsvrk", pair, np.eye(kzl))
    x_inverse = x_inverse.reshape(count_x * cells_x * kzl * 2, kzl * 2 * KX)
    zc, zs = angle_tables(np.arange(KZ), depth, depth, KZ**-0.5)
    pair = inverse_pair(zc, zs).reshape(2, 2, depth, count_y, kzl)
    z_inverse = np.einsum("rsnqz,xw,h->hqxzrwsn", pair, np.eye(cells_x), np.ones(2))
    z_inverse = z_inverse.reshape(4 * cells_x * KZ, cells_x * 2 * depth)
    yc, ys = angle_tables(signed_modes(KY), width_y, width_y, KY**-0.5)
    pair = np.stack([yc, -ys]).reshape(2, count_y, cells_y, KY)
    y_inverse = np.einsum("rqyk,i->qyrki", pair, np.ones(16))
    y_inverse = y_inverse.reshape(count_y, cells_y, 32 * KY)
    return (
        narrow(z_forward),
        narrow(y_forward),
        narrow(x_forward),
        np.concatenate(
            [narrow(x_inverse), narrow(x_inverse - narrow(x_inverse))], axis=1
        ),
        narrow(z_inverse),
        narrow(y_inverse),
    )


def block_moves(value):
    rows = value.shape[0]
    tiles = value.reshape(rows // 8, 8, 128)
    row = lax.broadcasted_iota(jnp.int32, tiles.shape, 1) % 4
    block = lax.broadcasted_iota(jnp.int32, tiles.shape, 2) // 32
    result = tiles
    for lane_step in (1, 2, 3):
        moved = pltpu.roll(tiles, 128 - 32 * lane_step, 2)
        result = jnp.where(row - block == lane_step, pltpu.roll(moved, lane_step, 1), result)
        result = jnp.where(
            row - block == lane_step - 4, pltpu.roll(moved, 8 + lane_step - 4, 1), result
        )
    return result


def forward_kernel(
    state_hbm,
    z_hbm,
    y_hbm,
    weight_hbm,
    conv_hbm,
    out_hbm,
    state_ref,
    packed_ref,
    conv_ref,
    out_ref,
    z_ref,
    y_ref,
    table_ref,
    weight_ref,
    sems,
):
    count = state_ref.shape[0] // 4
    span = state_ref.shape[1]
    y_copy = pltpu.make_async_copy(y_hbm.at[lax.axis_index("py")], y_ref, sems.at[0])
    z_copy = pltpu.make_async_copy(z_hbm, z_ref, sems.at[1])
    copies = [
        pltpu.make_async_copy(
            state_hbm.at[pl.ds(g * count, count)],
            state_ref.at[pl.ds(g * count, count)],
            sems.at[2 + g],
        )
        for g in range(4)
    ]
    conv_copy = pltpu.make_async_copy(conv_hbm, conv_ref, sems.at[6])
    weight_copies = [
        pltpu.make_async_copy(
            weight_hbm.at[part, kz], weight_ref.at[part, kz], sems.at[7 + part * 4 + kz]
        )
        for part in range(2)
        for kz in range(4)
    ]
    for copy in [y_copy, z_copy] + copies + weight_copies + [conv_copy]:
        copy.start()
    y_copy.wait()
    table = y_ref[...]
    lane = lax.broadcasted_iota(jnp.int32, (span, table.shape[1]), 1)
    for x in range(2):
        for c in range(8):
            own = (lane % 8 == c) & (lane // 64 % 2 == x)
            for part in range(2):
                first = part * 16 * span + (c * 2 + x) * span
                block = jnp.where(own, table[part * span : (part + 1) * span], 0.0)
                table_ref[first : first + span] = block.astype(jnp.bfloat16)
    z_copy.wait()
    z_table = z_ref[...].astype(jnp.bfloat16)
    pieces = []
    for g in range(4):
        copies[g].wait()
        cells = state_ref[g * count : (g + 1) * count].reshape(count * span, state_ref.shape[2])
        z_modes = lax.dot_general(
            z_table, cells, (((1,), (1,)), ((), ())), preferred_element_type=jnp.float32
        ).astype(jnp.bfloat16)
        pieces.append(jnp.concatenate([z_modes[:KZ], z_modes[KZ:]], axis=1))
    stacked = jnp.concatenate(pieces, axis=0)
    modes = jnp.dot(stacked, table_ref[...], preferred_element_type=jnp.float32)
    for group in range(4):
        moved = block_moves(modes[:, group * 128 : (group + 1) * 128])
        for half in range(2):
            for pair in range(2):
                first = moved[half * 4 + pair]
                second = moved[half * 4 + 2 + pair]
                for side in range(2):
                    rows4 = slice(4 * side, 4 * side + 4)
                    chunk = jnp.concatenate([first[rows4], second[rows4]], axis=0)
                    out_ref[(half * 4 + group) * 4 + 2 * pair + side] = chunk.astype(jnp.bfloat16)
    out_copy = pltpu.make_async_copy(out_ref, out_hbm, sems.at[15])
    out_copy.start()
    for part in range(2):
        for kz in range(4):
            weight_copies[part * 4 + kz].wait()
            for c in range(16):
                packed_ref[part, kz, c] = jnp.concatenate(
                    [weight_ref[part, kz, u, c] for u in range(4)], axis=1
                )
    conv_copy.wait()
    out_copy.wait()


def forward_modes(state, z_table, y_table, spectral_weight, conv_weight):
    vmem, hbm = (pl.BlockSpec(memory_space=space) for space in (pltpu.VMEM, pltpu.HBM))
    sent = (32, 8, 128)
    return pl.pallas_call(
        forward_kernel,
        out_shape=(
            jax.ShapeDtypeStruct(sent, jnp.bfloat16),
            jax.ShapeDtypeStruct(state.shape, jnp.bfloat16),
            jax.ShapeDtypeStruct((2, 4, 16, KX, 128), jnp.float32),
            jax.ShapeDtypeStruct(conv_weight.shape, jnp.bfloat16),
        ),
        in_specs=[hbm] * 5,
        out_specs=(hbm, vmem, vmem, vmem),
        scratch_shapes=[
            pltpu.VMEM(sent, jnp.bfloat16),
            pltpu.VMEM(z_table.shape, jnp.float32),
            pltpu.VMEM(y_table.shape[1:], jnp.float32),
            pltpu.VMEM((32 * state.shape[1], y_table.shape[2]), jnp.bfloat16),
            pltpu.VMEM(spectral_weight.shape, jnp.float32),
            pltpu.SemaphoreType.DMA((16,)),
        ],
        compiler_params=pltpu.CompilerParams(vmem_limit_bytes=16 * 2**20),
        cost_estimate=pl.CostEstimate(flops=2**27, bytes_accessed=2**21, transcendentals=0),
        name="forward_modes",
    )(
        *(
            pltpu.with_memory_space_constraint(v, pltpu.HBM)
            for v in (state, z_table, y_table, spectral_weight, conv_weight)
        )
    )


def arrange_kernel(state_ref, conv_ref, first_ref, second_ref, conv_out, wide):
    odd_x = lax.rem(lax.axis_index("px"), 2)
    cells_y = state_ref.shape[2]
    for slot, (out_ref, x) in enumerate(((first_ref, odd_x), (second_ref, 1 - odd_x))):
        wide[slot] = state_ref[:, x].astype(jnp.float32).reshape(32 * cells_y, 128)
        for y in range(cells_y):
            out_ref[y] = wide[slot, pl.ds(y, 32, stride=cells_y), :].astype(jnp.bfloat16)
    zero = jnp.zeros((32, 32), jnp.float32)
    for dz in range(3):
        for dy in range(3):
            taps = [conv_ref[dx, dy, dz].astype(jnp.float32) for dx in range(3)]
            for x_at in range(2):
                blocks = [zero] * x_at + taps + [zero] * (1 - x_at)
                blocks = [jnp.where(odd_x == 1, blocks[i], blocks[3 - i]) for i in range(4)]
                conv_out[dz, 32 * x_at : 32 * x_at + 32, 128 * dy : 128 * dy + 128] = (
                    jnp.concatenate(blocks, axis=1).astype(jnp.bfloat16)
                )


def arrange(state, conv_weight):
    vmem = pl.BlockSpec(memory_space=pltpu.VMEM)
    cells_y = state.shape[2]
    plane = jax.ShapeDtypeStruct((cells_y, 32, 128), jnp.bfloat16)
    return pl.pallas_call(
        arrange_kernel,
        out_shape=(plane, plane, jax.ShapeDtypeStruct((3, 64, 384), jnp.bfloat16)),
        in_specs=[vmem] * 2,
        out_specs=(vmem,) * 3,
        scratch_shapes=[pltpu.VMEM((2, 32 * cells_y, 128), jnp.float32)],
        compiler_params=pltpu.CompilerParams(vmem_limit_bytes=16 * 2**20),
        cost_estimate=pl.CostEstimate(flops=2**10, bytes_accessed=2**10, transcendentals=0),
        name="arrange_cells",
    )(state, conv_weight)


def mix_kernel(modes_ref, forward_ref, weight_ref, inverse_ref, out_ref):
    received = modes_ref[...].astype(jnp.float32).reshape(256, 128).astype(jnp.bfloat16)
    x_modes = jnp.dot(
        forward_ref[...].astype(jnp.bfloat16), received, preferred_element_type=jnp.float32)
    lane = lax.broadcasted_iota(jnp.int32, (16, 128), 1)
    base = (lane // 32) * 8
    mixed = []
    for kz in range(4):
        real_sum = imag_sum = None
        for c in range(16):
            half, c8 = c // 8, c % 8
            index = base + (kz * 32 + c8)
            real_in = jnp.take_along_axis(x_modes[half * 32 : half * 32 + 16], index, axis=1)
            imag_in = jnp.take_along_axis(x_modes[half * 32 + 16 : half * 32 + 32], index, axis=1)
            real_weight = weight_ref[0, kz, c]
            imag_weight = weight_ref[1, kz, c]
            real_term = real_weight * real_in - imag_weight * imag_in
            imag_term = real_weight * imag_in + imag_weight * real_in
            real_sum = real_term if real_sum is None else real_sum + real_term
            imag_sum = imag_term if imag_sum is None else imag_sum + imag_term
        mixed += [real_sum, imag_sum]
    mixed = jnp.concatenate(mixed, axis=0)
    inverse = inverse_ref[...].astype(jnp.bfloat16)
    high = mixed.astype(jnp.bfloat16)
    low = (mixed - high.astype(jnp.float32)).astype(jnp.bfloat16)
    values = jnp.dot(
        jnp.concatenate([inverse[:, :128], inverse], axis=1),
        jnp.concatenate([high, low, high], axis=0),
        preferred_element_type=jnp.float32,
    ).astype(jnp.bfloat16)
    for x in range(8):
        for y in range(4):
            out_ref[x * 4 + y] = values[16 * x : 16 * x + 16]


def mix_modes(modes, forward_table, weights, inverse_table):
    vmem = pl.BlockSpec(memory_space=pltpu.VMEM)
    return pl.pallas_call(
        mix_kernel,
        out_shape=jax.ShapeDtypeStruct((32, 16, 128), jnp.bfloat16),
        in_specs=[vmem] * 4,
        out_specs=vmem,
        compiler_params=pltpu.CompilerParams(vmem_limit_bytes=16 * 2**20),
        cost_estimate=pl.CostEstimate(flops=2**35, bytes_accessed=2**21, transcendentals=0),
        name="mix_modes",
    )(modes, forward_table, weights, inverse_table)


def cell_row(planes, y):
    return jnp.concatenate([plane[y] for plane in planes], axis=0)


def edge_rows_kernel(*refs):
    *planes, first_ref, second_ref = refs
    end = planes[0].shape[0] - 1
    odd_y = lax.rem(lax.axis_index("py"), 2)
    first_ref[...] = cell_row(planes, odd_y * end)
    second_ref[...] = cell_row(planes, (1 - odd_y) * end)


def edge_rows(planes):
    vmem = pl.BlockSpec(memory_space=pltpu.VMEM)
    row = jax.ShapeDtypeStruct((128, 128), jnp.bfloat16)
    return pl.pallas_call(
        edge_rows_kernel,
        out_shape=(row, row),
        in_specs=[vmem] * 4,
        out_specs=(vmem, vmem),
        compiler_params=pltpu.CompilerParams(vmem_limit_bytes=16 * 2**20),
        cost_estimate=pl.CostEstimate(flops=2**10, bytes_accessed=2**17, transcendentals=0),
        name="edge_rows",
    )(*planes)


def window_matrix(taps_ref):
    gap = jnp.zeros((64, 128), jnp.bfloat16)
    rows = []
    for dz in range(3):
        rows.append(jnp.concatenate([taps_ref[dz], gap], axis=1))
        rows.append(jnp.concatenate([gap, taps_ref[dz]], axis=1))
    return jnp.concatenate(rows, axis=0)


def convolve_quad(quad, row, weight, place, out_ref):
    lane = lax.broadcasted_iota(jnp.int32, (128, 256), 1) % 128
    windows = []
    for pair in range(2):
        start = quad * 4 + pair * 2 - 1
        windows.append(jnp.concatenate([row(start + i) for i in range(4)], axis=0))
    product = jnp.dot(weight, jnp.concatenate(windows, axis=1), preferred_element_type=jnp.float32)
    below = pltpu.roll(product[:128], 1, 1)
    above = pltpu.roll(product[256:], 255, 1)
    total = product[128:256] + jnp.where(lane == 0, 0.0, below)
    total = total + jnp.where(lane == 127, 0.0, above)
    for pair in range(2):
        for y_out in range(2):
            for x_out in range(2):
                first = (y_out * 2 + x_out) * 32
                value = total[first : first + 32, pair * 128 : (pair + 1) * 128]
                y = quad * 4 + pair * 2 + y_out
                at, span = place(y)
                out_ref[pl.ds(x_out * span + at, 32, stride=2 * span), :] = value


def interior_kernel(*refs):
    *planes, weight_ref, out_ref = refs
    cells_y = planes[0].shape[0]
    weight = window_matrix(weight_ref)
    for quad in range(1, cells_y // 4 - 1):
        convolve_quad(
            quad, lambda y: cell_row(planes, y), weight, lambda y: (y, cells_y), out_ref
        )


def edge_kernel(*refs):
    *planes, first_row, second_row, weight_ref, out_ref = refs
    cells_y = planes[0].shape[0]
    odd_y = lax.rem(lax.axis_index("py"), 2) == 1

    def row(y):
        if y < 0:
            return jnp.where(odd_y, second_row[...], first_row[...])
        if y >= cells_y:
            return jnp.where(odd_y, first_row[...], second_row[...])
        return cell_row(planes, y)

    weight = window_matrix(weight_ref)
    for quad in (0, cells_y // 4 - 1):
        convolve_quad(quad, row, weight, lambda y: (y % 8, 8), out_ref)


def convolve(kernel, name, operands, rows):
    vmem = pl.BlockSpec(memory_space=pltpu.VMEM)
    return pl.pallas_call(
        kernel,
        out_shape=jax.ShapeDtypeStruct((rows, 128), jnp.float32),
        in_specs=[vmem] * len(operands),
        out_specs=vmem,
        compiler_params=pltpu.CompilerParams(vmem_limit_bytes=16 * 2**20),
        cost_estimate=pl.CostEstimate(flops=2**30, bytes_accessed=2**21, transcendentals=0),
        name=name,
    )(*operands)


def gelu(value):
    return 0.5 * value * (1.0 + lax.erf(value * math.sqrt(0.5)))


def finish_kernel(
    bias_ref, values_ref, z_ref, y_ref, conv_ref, edge_ref, out_hbm, out_ref, sems
):
    upper = lax.broadcasted_iota(jnp.int32, (8, 128), 0) < 4
    table = y_ref[lax.axis_index("py")]
    lane = lax.broadcasted_iota(jnp.int32, table.shape, 1) % 16
    expanded = [jnp.where(lane == o, table, 0.0).astype(jnp.bfloat16) for o in range(16)]
    columns = []
    for group in range(4):
        columns.append(
            jnp.concatenate(
                [values_ref[(h * 4 + group) * 4 + q] for h in range(2) for q in range(4)], axis=0
            )
        )
    packed = jnp.concatenate(columns, axis=1)
    z_values = lax.dot_general(
        packed,
        z_ref[...].astype(jnp.bfloat16),
        (((0,), (0,)), ((), ())),
        preferred_element_type=jnp.float32,
    ).astype(jnp.bfloat16)
    copies = []
    for half in range(2):
        sides = []
        for x in range(2):
            parts = []
            for part in range(2):
                lanes = slice((x * 2 + part) * 128, (x * 2 + part + 1) * 128)
                parts += [
                    z_values[ky * 32 + half * 16 : ky * 32 + half * 16 + 16, lanes]
                    for ky in range(KY)
                ]
            sides.append(jnp.concatenate(parts, axis=0))
        right = jnp.concatenate(sides, axis=1)
        for block in range(4):
            spectral = jnp.dot(
                jnp.concatenate(expanded[block * 4 : block * 4 + 4], axis=0),
                right,
                preferred_element_type=jnp.float32,
            )
            for o4 in range(4):
                o = half * 16 + block * 4 + o4
                for x in range(2):
                    inner, edge = conv_ref[o, x], edge_ref[o, x]
                    convolved = jnp.concatenate(
                        [
                            jnp.where(upper, edge, inner[:8]),
                            inner[8:-8],
                            jnp.where(upper, inner[-8:], edge),
                        ],
                        axis=0,
                    )
                    total = spectral[o4 * 32 : o4 * 32 + 32, x * 128 : (x + 1) * 128]
                    total = total + convolved + bias_ref[o]
                    out_ref[o, x] = gelu(total).astype(jnp.bfloat16)
            number = half * 4 + block
            copy = pltpu.make_async_copy(
                out_ref.at[pl.ds(number * 4, 4)], out_hbm.at[pl.ds(number * 4, 4)], sems.at[number]
            )
            copy.start()
            copies.append(copy)
    for copy in copies:
        copy.wait()


def finish(bias, values, z_table, y_table, convolved, edges):
    vmem = pl.BlockSpec(memory_space=pltpu.VMEM)
    return pl.pallas_call(
        finish_kernel,
        out_shape=jax.ShapeDtypeStruct(convolved.shape, jnp.bfloat16),
        in_specs=[pl.BlockSpec(memory_space=pltpu.SMEM)] + [vmem] * 5,
        out_specs=pl.BlockSpec(memory_space=pltpu.HBM),
        scratch_shapes=[
            pltpu.VMEM(convolved.shape, jnp.bfloat16),
            pltpu.SemaphoreType.DMA((8,)),
        ],
        compiler_params=pltpu.CompilerParams(vmem_limit_bytes=16 * 2**20),
        cost_estimate=pl.CostEstimate(flops=2**28, bytes_accessed=2**22, transcendentals=2**18),
        name="finish_layer",
    )(bias, values, z_table, y_table, convolved, edges)


def exchanged(value):
    return lax.all_to_all(value, ("px", "py"), split_axis=0, concat_axis=0, tiled=True)


def swaps(first, second, axis):
    count = lax.axis_size(axis)
    inside = [(i, i ^ 1) for i in range(count)]
    across = [(i, i + 1 if i % 2 else i - 1) for i in range(1, count - 1)]
    second = lax.ppermute(second, axis, inside)
    return lax.ppermute(first, axis, across), second


def body(state_field, conv_weight, conv_bias, spectral_weight):
    channels, cells_x, cells_y, depth = state_field.shape
    sizes = (lax.axis_size("px"), lax.axis_size("py"), cells_x, cells_y, depth)
    if sizes != (8, 4, 2, 32, 128):
        return general_body(state_field, conv_weight, conv_bias, spectral_weight)
    z_forward, y_forward, x_forward, x_inverse, z_inverse, y_inverse = tables(*sizes)
    sent, held, weights, conv_held = forward_modes(
        state_field.reshape(channels * cells_x, cells_y, depth),
        z_forward,
        y_forward,
        spectral_weight.swapaxes(4, 5),
        conv_weight.transpose(2, 3, 4, 0, 1),
    )
    modes = exchanged(sent)
    first_own, second_own, taps = arrange(held.reshape(state_field.shape), conv_held)
    first_plane, second_plane = swaps(first_own, second_own, "px")
    values = exchanged(mix_modes(modes, x_forward, weights, x_inverse))
    planes = (second_plane, second_own, first_own, first_plane)
    first_row, second_row = swaps(*edge_rows(planes), "py")
    rows = channels * cells_x
    interior = convolve(interior_kernel, "convolve_interior", planes + (taps,), rows * cells_y)
    edges = convolve(
        edge_kernel, "convolve_edges", planes + (first_row, second_row, taps), rows * 8
    )
    return finish(
        conv_bias,
        values,
        z_inverse,
        y_inverse,
        interior.reshape(channels, cells_x, cells_y, depth),
        edges.reshape(channels, cells_x, 8, depth),
    )


def solution(mesh):
    in_specs = (P(None, "px", "py", None), P(), P(), P(None, "py", "px", None, None, None))
    out_specs = P(None, "px", "py", None)
    return jax.shard_map(body, mesh=mesh, in_specs=in_specs, out_specs=out_specs, check_vma=False)
```

```python
import functools
import math

import jax
import jax.numpy as jnp
import ml_dtypes
import numpy as np
from jax import lax
from jax.experimental import pallas as pl
from jax.experimental.pallas import tpu as pltpu
from jax.sharding import PartitionSpec as P

KX = 16
KY = 16
KZ = 16


def extended(cells, sides, width):
    for axis, dim in sides:
        count = lax.axis_size(axis)
        ends = count - 1
        head = lax.slice_in_dim(cells, 0, width, axis=dim)
        tail = lax.slice_in_dim(cells, cells.shape[dim] - width, cells.shape[dim], axis=dim)
        cells = jnp.concatenate(
            [
                lax.ppermute(tail, axis, [(i, (i + 1) % count) for i in range(ends)]),
                cells,
                lax.ppermute(head, axis, [((i + 1) % count, i) for i in range(ends)]),
            ],
            axis=dim,
        )
    return cells


def swapped(value, axis, distance):
    mask = 2**distance
    pairs = [(source, source ^ mask) for source in range(lax.axis_size(axis))]
    return lax.ppermute(value, axis, pairs)


def mode_numbers(count):
    indices = jnp.arange(count, dtype=jnp.int32)
    return jnp.where(indices < count // 2, indices, indices - count)


def trig_pair(numbers, points, length, factor, out_type):
    positions = jnp.arange(points, dtype=jnp.int32)
    phases = positions[:, None] * numbers[None, :] % length
    angles = phases.astype(jnp.float32) * (2.0 * math.pi / length)
    return (
        (jnp.cos(angles) * factor).astype(out_type),
        (jnp.sin(angles) * factor).astype(out_type),
    )


def last_product(source, table, precision=None):
    flat = source.reshape(-1, source.shape[-1])
    result = jnp.dot(flat, table, preferred_element_type=jnp.float32, precision=precision)
    return result.reshape(source.shape[:-1] + (table.shape[1],))


def forward_last(source, cosine, sine_table, precision=None):
    real_part = source[..., 0, :]
    imag_part = source[..., 1, :]
    real_out = last_product(real_part, cosine, precision) + last_product(
        imag_part, sine_table, precision
    )
    imag_out = last_product(imag_part, cosine, precision) - last_product(
        real_part, sine_table, precision
    )
    return jnp.stack([real_out, imag_out], axis=-2)


def inverse_last(source, cosine, sine_table, precision=None):
    real_part = source[..., 0, :]
    imag_part = source[..., 1, :]
    real_out = last_product(real_part, cosine, precision) - last_product(
        imag_part, sine_table, precision
    )
    imag_out = last_product(real_part, sine_table, precision) + last_product(
        imag_part, cosine, precision
    )
    return jnp.stack([real_out, imag_out], axis=-2)


def mix_block(spectral_weight, x_block):
    highest = lax.Precision.HIGHEST
    real_in = x_block[:, :, :, 0, :]
    imag_in = x_block[:, :, :, 1, :]
    partial_real = jnp.einsum(
        "zucok,uzck->uzok", spectral_weight[0], real_in, precision=highest
    ) - jnp.einsum("zucok,uzck->uzok", spectral_weight[1], imag_in, precision=highest)
    partial_imag = jnp.einsum(
        "zucok,uzck->uzok", spectral_weight[0], imag_in, precision=highest
    ) + jnp.einsum("zucok,uzck->uzok", spectral_weight[1], real_in, precision=highest)
    return jnp.stack([partial_real, partial_imag], axis=3)


def general_body(state_field, conv_weight, conv_bias, spectral_weight):
    channels, cells_x, cells_y, depth = state_field.shape
    count_x = lax.axis_size("px")
    count_y = lax.axis_size("py")
    width_x = cells_x * count_x
    width_y = cells_y * count_y
    index_x = lax.axis_index("px")
    kz_local = KZ // count_y
    units = 2 * KY // count_x
    highest = lax.Precision.HIGHEST
    padded = extended(state_field, (("px", 1), ("py", 2)), 1)
    convolved = lax.conv_general_dilated(
        padded[None],
        conv_weight,
        (1, 1, 1),
        ((0, 0), (0, 0), (1, 1)),
        dimension_numbers=("NCDHW", "OIDHW", "NCDHW"),
        preferred_element_type=jnp.float32,
    )[0]
    z_cos, z_sin = trig_pair(
        jnp.arange(KZ, dtype=jnp.int32), depth, depth, depth ** (-0.5), jnp.bfloat16
    )
    z_table = jnp.stack([z_cos, -z_sin], axis=1)
    z_modes = jnp.einsum(
        "cxyn,nwk->kcxwy", state_field, z_table, preferred_element_type=jnp.float32
    ).astype(jnp.bfloat16)
    y_cos, y_sin = trig_pair(mode_numbers(KY), width_y, width_y, width_y ** (-0.5), jnp.bfloat16)
    full_rows = lax.all_to_all(z_modes, "py", split_axis=0, concat_axis=4, tiled=True)
    y_modes = forward_last(full_rows, y_cos, y_sin)
    y_modes = y_modes.astype(jnp.bfloat16)
    by_unit = y_modes.reshape(kz_local, 2, channels // 2, cells_x, 2, KY).transpose(
        1, 5, 0, 2, 4, 3
    )
    by_unit = by_unit.reshape(2 * KY, kz_local, channels // 2, 2, cells_x)
    x_rows = lax.all_to_all(by_unit, "px", split_axis=0, concat_axis=4, tiled=True)
    x_cos, x_sin = trig_pair(mode_numbers(KX), width_x, width_x, width_x ** (-0.5), jnp.bfloat16)
    x_modes = forward_last(x_rows, x_cos, x_sin)
    partial_modes = mix_block(spectral_weight, x_modes)
    partial_modes = partial_modes.reshape(units, kz_local, 2, channels // 2, 2, KX)
    half_index = index_x * units // KY
    own_half = lax.dynamic_index_in_dim(partial_modes, half_index, 2, keepdims=False)
    other_half = lax.dynamic_index_in_dim(partial_modes, 1 - half_index, 2, keepdims=False)
    mixed_modes = own_half + swapped(other_half, "px", count_x.bit_length() - 2)
    ix_cos, ix_sin = trig_pair(mode_numbers(KX), width_x, width_x, KX ** (-0.5), jnp.float32)
    x_values = inverse_last(mixed_modes, ix_cos.T, ix_sin.T, highest).astype(jnp.bfloat16)
    returned = lax.all_to_all(x_values, "px", split_axis=4, concat_axis=0, tiled=True)
    returned = returned.reshape(2, KY, kz_local, channels // 2, 2, cells_x).transpose(
        2, 0, 3, 5, 4, 1
    )
    returned = returned.reshape(kz_local, channels, cells_x, 2, KY)
    iy_cos, iy_sin = trig_pair(mode_numbers(KY), width_y, width_y, KY ** (-0.5), jnp.bfloat16)
    expanded = inverse_last(returned, iy_cos.T, iy_sin.T).astype(jnp.bfloat16)
    y_values = lax.all_to_all(expanded, "py", split_axis=4, concat_axis=0, tiled=True)
    iz_cos, iz_sin = trig_pair(
        jnp.arange(KZ, dtype=jnp.int32), depth, depth, KZ ** (-0.5), jnp.bfloat16
    )
    iz_table = jnp.stack([iz_cos.T, -iz_sin.T], axis=0)
    spectral = jnp.einsum("kcxwy,wkn->cxyn", y_values, iz_table, preferred_element_type=jnp.float32)
    total = convolved + spectral + conv_bias[:, None, None, None]
    return jax.nn.gelu(total, approximate=False).astype(jnp.bfloat16)


def angle_tables(numbers, points, length, factor):
    phases = (np.arange(points)[:, None] * numbers[None, :]) % length
    angles = phases.astype(np.float32) * np.float32(2.0 * math.pi / length)
    return (
        np.cos(angles).astype(np.float32) * np.float32(factor),
        np.sin(angles).astype(np.float32) * np.float32(factor),
    )


def signed_modes(count):
    indices = np.arange(count)
    return np.where(indices < count // 2, indices, indices - count)


def narrow(table):
    return table.astype(ml_dtypes.bfloat16).astype(np.float32)


def forward_pair(cosine, sine):
    return np.stack([np.stack([cosine, -sine]), np.stack([sine, cosine])])


def inverse_pair(cosine, sine):
    return np.stack([np.stack([cosine, sine]), np.stack([-sine, cosine])])


@functools.cache
def tables(count_x, count_y, cells_x, cells_y, depth):
    width_x, width_y = count_x * cells_x, count_y * cells_y
    kzl, units = KZ // count_y, 2 * KY // count_x
    groups = KY // units
    zc, zs = angle_tables(np.arange(KZ), depth, depth, depth**-0.5)
    z_forward = np.concatenate([zc.T, -zs.T])
    yc, ys = angle_tables(signed_modes(KY), width_y, width_y, width_y**-0.5)
    pair = forward_pair(yc, ys).reshape(2, 2, count_y, cells_y, groups, units)
    y_forward = np.einsum("rsqygk,d,w->qrygwskd", pair, np.ones(8), np.ones(cells_x))
    y_forward = y_forward.reshape(count_y, 2 * cells_y, groups * 2 * cells_x * units * 8)
    xc, xs = angle_tables(signed_modes(KX), width_x, width_x, width_x**-0.5)
    pair = forward_pair(xc, xs).reshape(2, 2, count_x, cells_x, KX)
    x_forward = np.einsum("rspxk,gh,q->gskpqhxr", pair, np.eye(2), np.ones(count_y))
    x_forward = x_forward.reshape(4 * KX, count_x * count_y * 4 * cells_x)
    xc, xs = angle_tables(signed_modes(KX), width_x, width_x, KX**-0.5)
    pair = inverse_pair(xc, xs).reshape(2, 2, count_x, cells_x, KX)
    x_inverse = np.einsum("rspxk,zv->pxzsvrk", pair, np.eye(kzl))
    x_inverse = x_inverse.reshape(count_x * cells_x * kzl * 2, kzl * 2 * KX)
    zc, zs = angle_tables(np.arange(KZ), depth, depth, KZ**-0.5)
    pair = inverse_pair(zc, zs).reshape(2, 2, depth, count_y, kzl)
    z_inverse = np.einsum("rsnqz,xw,h->hqxzrwsn", pair, np.eye(cells_x), np.ones(2))
    z_inverse = z_inverse.reshape(4 * cells_x * KZ, cells_x * 2 * depth)
    yc, ys = angle_tables(signed_modes(KY), width_y, width_y, KY**-0.5)
    pair = np.stack([yc, -ys]).reshape(2, count_y, cells_y, KY)
    y_inverse = np.einsum("rqyk,i->qyrki", pair, np.ones(16))
    y_inverse = y_inverse.reshape(count_y, cells_y, 32 * KY)
    return (
        narrow(z_forward),
        narrow(y_forward),
        narrow(x_forward),
        np.concatenate(
            [narrow(x_inverse), narrow(x_inverse - narrow(x_inverse))], axis=1
        ),
        narrow(z_inverse),
        narrow(y_inverse),
    )


def block_moves(value):
    rows = value.shape[0]
    tiles = value.reshape(rows // 8, 8, 128)
    row = lax.broadcasted_iota(jnp.int32, tiles.shape, 1) % 4
    block = lax.broadcasted_iota(jnp.int32, tiles.shape, 2) // 32
    result = tiles
    for lane_step in (1, 2, 3):
        moved = pltpu.roll(tiles, 128 - 32 * lane_step, 2)
        result = jnp.where(row - block == lane_step, pltpu.roll(moved, lane_step, 1), result)
        result = jnp.where(
            row - block == lane_step - 4, pltpu.roll(moved, 8 + lane_step - 4, 1), result
        )
    return result


def forward_kernel(
    state_hbm,
    z_hbm,
    y_hbm,
    weight_hbm,
    conv_hbm,
    out_hbm,
    first_ref,
    second_ref,
    taps_ref,
    packed_ref,
    out_ref,
    state_ref,
    z_ref,
    y_ref,
    table_ref,
    weight_ref,
    conv_ref,
    wide,
    sems,
):
    count = state_ref.shape[0] // 4
    span = state_ref.shape[2]
    y_copy = pltpu.make_async_copy(y_hbm.at[lax.axis_index("py")], y_ref, sems.at[0])
    z_copy = pltpu.make_async_copy(z_hbm, z_ref, sems.at[1])
    copies = [
        pltpu.make_async_copy(
            state_hbm.at[pl.ds(g * count, count)],
            state_ref.at[pl.ds(g * count, count)],
            sems.at[2 + g],
        )
        for g in range(4)
    ]
    conv_copy = pltpu.make_async_copy(conv_hbm, conv_ref, sems.at[6])
    weight_copies = [
        pltpu.make_async_copy(
            weight_hbm.at[part, kz], weight_ref.at[part, kz], sems.at[7 + part * 4 + kz]
        )
        for part in range(2)
        for kz in range(4)
    ]
    for copy in [y_copy, z_copy] + copies + weight_copies + [conv_copy]:
        copy.start()
    y_copy.wait()
    table = y_ref[...]
    lane = lax.broadcasted_iota(jnp.int32, (span, table.shape[1]), 1)
    for x in range(2):
        for c in range(8):
            own = (lane % 8 == c) & (lane // 64 % 2 == x)
            for part in range(2):
                first = part * 16 * span + (c * 2 + x) * span
                block = jnp.where(own, table[part * span : (part + 1) * span], 0.0)
                table_ref[first : first + span] = block.astype(jnp.bfloat16)
    z_copy.wait()
    z_table = z_ref[...].astype(jnp.bfloat16)
    pieces = []
    for g in range(4):
        copies[g].wait()
        cells = state_ref[g * count : (g + 1) * count].reshape(2 * count * span, 128)
        z_modes = lax.dot_general(
            z_table, cells, (((1,), (1,)), ((), ())), preferred_element_type=jnp.float32
        ).astype(jnp.bfloat16)
        pieces.append(jnp.concatenate([z_modes[:KZ], z_modes[KZ:]], axis=1))
    stacked = jnp.concatenate(pieces, axis=0)
    modes = jnp.dot(stacked, table_ref[...], preferred_element_type=jnp.float32)
    for group in range(4):
        moved = block_moves(modes[:, group * 128 : (group + 1) * 128])
        for half in range(2):
            for pair in range(2):
                first = moved[half * 4 + pair]
                second = moved[half * 4 + 2 + pair]
                for side in range(2):
                    rows4 = slice(4 * side, 4 * side + 4)
                    chunk = jnp.concatenate([first[rows4], second[rows4]], axis=0)
                    out_ref[(half * 4 + group) * 4 + 2 * pair + side] = chunk.astype(jnp.bfloat16)
    out_copy = pltpu.make_async_copy(out_ref, out_hbm, sems.at[15])
    out_copy.start()
    odd_x = lax.rem(lax.axis_index("px"), 2)
    for slot, (plane_ref, x) in enumerate(((first_ref, odd_x), (second_ref, 1 - odd_x))):
        wide[slot] = state_ref[:, x].astype(jnp.float32).reshape(32 * span, 128)
        for y in range(span):
            plane_ref[y] = wide[slot, pl.ds(y, 32, stride=span), :].astype(jnp.bfloat16)
    conv_copy.wait()
    zero = jnp.zeros((32, 32), jnp.float32)
    for dz in range(3):
        for dy in range(3):
            taps = [conv_ref[dx, dy, dz].astype(jnp.float32) for dx in range(3)]
            for x_at in range(2):
                blocks = [zero] * x_at + taps + [zero] * (1 - x_at)
                blocks = [jnp.where(odd_x == 1, blocks[i], blocks[3 - i]) for i in range(4)]
                taps_ref[dz, 32 * x_at : 32 * x_at + 32, 128 * dy : 128 * dy + 128] = (
                    jnp.concatenate(blocks, axis=1).astype(jnp.bfloat16)
                )
    for part in range(2):
        for kz in range(4):
            weight_copies[part * 4 + kz].wait()
            for c in range(16):
                packed_ref[part, kz, c] = jnp.concatenate(
                    [weight_ref[part, kz, u, c] for u in range(4)], axis=1
                )
    out_copy.wait()


def forward_modes(state, z_table, y_table, spectral_weight, conv_weight):
    vmem, hbm = (pl.BlockSpec(memory_space=space) for space in (pltpu.VMEM, pltpu.HBM))
    sent = (32, 8, 128)
    plane = jax.ShapeDtypeStruct((state.shape[2], 32, 128), jnp.bfloat16)
    return pl.pallas_call(
        forward_kernel,
        out_shape=(
            jax.ShapeDtypeStruct(sent, jnp.bfloat16),
            plane,
            plane,
            jax.ShapeDtypeStruct((3, 64, 384), jnp.bfloat16),
            jax.ShapeDtypeStruct((2, 4, 16, KX, 128), jnp.float32),
        ),
        in_specs=[hbm] * 5,
        out_specs=(hbm, vmem, vmem, vmem, vmem),
        scratch_shapes=[
            pltpu.VMEM(sent, jnp.bfloat16),
            pltpu.VMEM(state.shape, jnp.bfloat16),
            pltpu.VMEM(z_table.shape, jnp.float32),
            pltpu.VMEM(y_table.shape[1:], jnp.float32),
            pltpu.VMEM((32 * state.shape[2], y_table.shape[2]), jnp.bfloat16),
            pltpu.VMEM(spectral_weight.shape, jnp.float32),
            pltpu.VMEM(conv_weight.shape, jnp.bfloat16),
            pltpu.VMEM((2, 32 * state.shape[2], 128), jnp.float32),
            pltpu.SemaphoreType.DMA((16,)),
        ],
        compiler_params=pltpu.CompilerParams(vmem_limit_bytes=16 * 2**20),
        cost_estimate=pl.CostEstimate(flops=2**27, bytes_accessed=2**21, transcendentals=0),
        name="forward_modes",
    )(
        *(
            pltpu.with_memory_space_constraint(v, pltpu.HBM)
            for v in (state, z_table, y_table, spectral_weight, conv_weight)
        )
    )


def mix_kernel(modes_ref, forward_ref, weight_ref, inverse_ref, out_ref):
    received = modes_ref[...].astype(jnp.float32).reshape(256, 128).astype(jnp.bfloat16)
    x_modes = jnp.dot(
        forward_ref[...].astype(jnp.bfloat16), received, preferred_element_type=jnp.float32)
    lane = lax.broadcasted_iota(jnp.int32, (16, 128), 1)
    base = (lane // 32) * 8
    mixed = []
    for kz in range(4):
        real_sum = imag_sum = None
        for c in range(16):
            half, c8 = c // 8, c % 8
            index = base + (kz * 32 + c8)
            real_in = jnp.take_along_axis(x_modes[half * 32 : half * 32 + 16], index, axis=1)
            imag_in = jnp.take_along_axis(x_modes[half * 32 + 16 : half * 32 + 32], index, axis=1)
            real_weight = weight_ref[0, kz, c]
            imag_weight = weight_ref[1, kz, c]
            real_term = real_weight * real_in - imag_weight * imag_in
            imag_term = real_weight * imag_in + imag_weight * real_in
            real_sum = real_term if real_sum is None else real_sum + real_term
            imag_sum = imag_term if imag_sum is None else imag_sum + imag_term
        mixed += [real_sum, imag_sum]
    mixed = jnp.concatenate(mixed, axis=0)
    inverse = inverse_ref[...].astype(jnp.bfloat16)
    high = mixed.astype(jnp.bfloat16)
    low = (mixed - high.astype(jnp.float32)).astype(jnp.bfloat16)
    values = jnp.dot(
        jnp.concatenate([inverse[:, :128], inverse], axis=1),
        jnp.concatenate([high, low, high], axis=0),
        preferred_element_type=jnp.float32,
    ).astype(jnp.bfloat16)
    for x in range(8):
        for y in range(4):
            out_ref[x * 4 + y] = values[16 * x : 16 * x + 16]


def mix_modes(modes, forward_table, weights, inverse_table):
    vmem = pl.BlockSpec(memory_space=pltpu.VMEM)
    return pl.pallas_call(
        mix_kernel,
        out_shape=jax.ShapeDtypeStruct((32, 16, 128), jnp.bfloat16),
        in_specs=[vmem] * 4,
        out_specs=vmem,
        compiler_params=pltpu.CompilerParams(vmem_limit_bytes=16 * 2**20),
        cost_estimate=pl.CostEstimate(flops=2**35, bytes_accessed=2**21, transcendentals=0),
        name="mix_modes",
    )(modes, forward_table, weights, inverse_table)


def cell_row(planes, y):
    return jnp.concatenate([plane[y] for plane in planes], axis=0)


def edge_rows_kernel(*refs):
    *planes, first_ref, second_ref = refs
    end = planes[0].shape[0] - 1
    odd_y = lax.rem(lax.axis_index("py"), 2)
    first_ref[...] = cell_row(planes, odd_y * end)
    second_ref[...] = cell_row(planes, (1 - odd_y) * end)


def edge_rows(planes):
    vmem = pl.BlockSpec(memory_space=pltpu.VMEM)
    row = jax.ShapeDtypeStruct((128, 128), jnp.bfloat16)
    return pl.pallas_call(
        edge_rows_kernel,
        out_shape=(row, row),
        in_specs=[vmem] * 4,
        out_specs=(vmem, vmem),
        compiler_params=pltpu.CompilerParams(vmem_limit_bytes=16 * 2**20),
        cost_estimate=pl.CostEstimate(flops=2**10, bytes_accessed=2**17, transcendentals=0),
        name="edge_rows",
    )(*planes)


def window_matrix(taps_ref):
    gap = jnp.zeros((64, 128), jnp.bfloat16)
    rows = []
    for dz in range(3):
        rows.append(jnp.concatenate([taps_ref[dz], gap], axis=1))
        rows.append(jnp.concatenate([gap, taps_ref[dz]], axis=1))
    return jnp.concatenate(rows, axis=0)


def convolve_quad(quad, row, weight, place, out_ref):
    lane = lax.broadcasted_iota(jnp.int32, (128, 256), 1) % 128
    windows = []
    for pair in range(2):
        start = quad * 4 + pair * 2 - 1
        windows.append(jnp.concatenate([row(start + i) for i in range(4)], axis=0))
    product = jnp.dot(weight, jnp.concatenate(windows, axis=1), preferred_element_type=jnp.float32)
    below = pltpu.roll(product[:128], 1, 1)
    above = pltpu.roll(product[256:], 255, 1)
    total = product[128:256] + jnp.where(lane == 0, 0.0, below)
    total = total + jnp.where(lane == 127, 0.0, above)
    for pair in range(2):
        for y_out in range(2):
            for x_out in range(2):
                first = (y_out * 2 + x_out) * 32
                value = total[first : first + 32, pair * 128 : (pair + 1) * 128]
                y = quad * 4 + pair * 2 + y_out
                at, span = place(y)
                out_ref[pl.ds(x_out * span + at, 32, stride=2 * span), :] = value


def interior_kernel(*refs):
    *planes, weight_ref, out_ref = refs
    cells_y = planes[0].shape[0]
    weight = window_matrix(weight_ref)
    for quad in range(1, cells_y // 4 - 1):
        convolve_quad(
            quad, lambda y: cell_row(planes, y), weight, lambda y: (y, cells_y), out_ref
        )


def edge_kernel(*refs):
    *planes, first_row, second_row, weight_ref, out_ref = refs
    cells_y = planes[0].shape[0]
    odd_y = lax.rem(lax.axis_index("py"), 2) == 1

    def row(y):
        if y < 0:
            return jnp.where(odd_y, second_row[...], first_row[...])
        if y >= cells_y:
            return jnp.where(odd_y, first_row[...], second_row[...])
        return cell_row(planes, y)

    weight = window_matrix(weight_ref)
    for quad in (0, cells_y // 4 - 1):
        convolve_quad(quad, row, weight, lambda y: (y % 8, 8), out_ref)


def convolve(kernel, name, operands, rows):
    vmem = pl.BlockSpec(memory_space=pltpu.VMEM)
    return pl.pallas_call(
        kernel,
        out_shape=jax.ShapeDtypeStruct((rows, 128), jnp.float32),
        in_specs=[vmem] * len(operands),
        out_specs=vmem,
        compiler_params=pltpu.CompilerParams(vmem_limit_bytes=16 * 2**20),
        cost_estimate=pl.CostEstimate(flops=2**30, bytes_accessed=2**21, transcendentals=0),
        name=name,
    )(*operands)


def gelu(value):
    return 0.5 * value * (1.0 + lax.erf(value * math.sqrt(0.5)))


def finish_kernel(
    bias_ref, values_ref, z_ref, y_ref, conv_ref, edge_ref, out_hbm, out_ref, sems
):
    upper = lax.broadcasted_iota(jnp.int32, (8, 128), 0) < 4
    table = y_ref[lax.axis_index("py")]
    lane = lax.broadcasted_iota(jnp.int32, table.shape, 1) % 16
    expanded = [jnp.where(lane == o, table, 0.0).astype(jnp.bfloat16) for o in range(16)]
    columns = []
    for group in range(4):
        columns.append(
            jnp.concatenate(
                [values_ref[(h * 4 + group) * 4 + q] for h in range(2) for q in range(4)], axis=0
            )
        )
    packed = jnp.concatenate(columns, axis=1)
    z_values = lax.dot_general(
        packed,
        z_ref[...].astype(jnp.bfloat16),
        (((0,), (0,)), ((), ())),
        preferred_element_type=jnp.float32,
    ).astype(jnp.bfloat16)
    copies = []
    for half in range(2):
        sides = []
        for x in range(2):
            parts = []
            for part in range(2):
                lanes = slice((x * 2 + part) * 128, (x * 2 + part + 1) * 128)
                parts += [
                    z_values[ky * 32 + half * 16 : ky * 32 + half * 16 + 16, lanes]
                    for ky in range(KY)
                ]
            sides.append(jnp.concatenate(parts, axis=0))
        right = jnp.concatenate(sides, axis=1)
        for block in range(4):
            spectral = jnp.dot(
                jnp.concatenate(expanded[block * 4 : block * 4 + 4], axis=0),
                right,
                preferred_element_type=jnp.float32,
            )
            for o4 in range(4):
                o = half * 16 + block * 4 + o4
                for x in range(2):
                    inner, edge = conv_ref[o, x], edge_ref[o, x]
                    convolved = jnp.concatenate(
                        [
                            jnp.where(upper, edge, inner[:8]),
                            inner[8:-8],
                            jnp.where(upper, inner[-8:], edge),
                        ],
                        axis=0,
                    )
                    total = spectral[o4 * 32 : o4 * 32 + 32, x * 128 : (x + 1) * 128]
                    total = total + convolved + bias_ref[o]
                    out_ref[o, x] = gelu(total).astype(jnp.bfloat16)
            number = half * 4 + block
            copy = pltpu.make_async_copy(
                out_ref.at[pl.ds(number * 4, 4)], out_hbm.at[pl.ds(number * 4, 4)], sems.at[number]
            )
            copy.start()
            copies.append(copy)
    for copy in copies:
        copy.wait()


def finish(bias, values, z_table, y_table, convolved, edges):
    vmem = pl.BlockSpec(memory_space=pltpu.VMEM)
    return pl.pallas_call(
        finish_kernel,
        out_shape=jax.ShapeDtypeStruct(convolved.shape, jnp.bfloat16),
        in_specs=[pl.BlockSpec(memory_space=pltpu.SMEM)] + [vmem] * 5,
        out_specs=pl.BlockSpec(memory_space=pltpu.HBM),
        scratch_shapes=[
            pltpu.VMEM(convolved.shape, jnp.bfloat16),
            pltpu.SemaphoreType.DMA((8,)),
        ],
        compiler_params=pltpu.CompilerParams(vmem_limit_bytes=16 * 2**20),
        cost_estimate=pl.CostEstimate(flops=2**28, bytes_accessed=2**22, transcendentals=2**18),
        name="finish_layer",
    )(bias, values, z_table, y_table, convolved, edges)


def exchanged(value):
    return lax.all_to_all(value, ("px", "py"), split_axis=0, concat_axis=0, tiled=True)


def swaps(first, second, axis):
    count = lax.axis_size(axis)
    inside = [(i, i ^ 1) for i in range(count)]
    across = [(i, i + 1 if i % 2 else i - 1) for i in range(1, count - 1)]
    second = lax.ppermute(second, axis, inside)
    return lax.ppermute(first, axis, across), second


def body(state_field, conv_weight, conv_bias, spectral_weight):
    channels, cells_x, cells_y, depth = state_field.shape
    sizes = (lax.axis_size("px"), lax.axis_size("py"), cells_x, cells_y, depth)
    if sizes != (8, 4, 2, 32, 128):
        return general_body(state_field, conv_weight, conv_bias, spectral_weight)
    z_forward, y_forward, x_forward, x_inverse, z_inverse, y_inverse = tables(*sizes)
    sent, first_own, second_own, taps, weights = forward_modes(
        state_field,
        z_forward,
        y_forward,
        spectral_weight.swapaxes(4, 5),
        conv_weight.transpose(2, 3, 4, 0, 1),
    )
    modes = exchanged(sent)
    first_plane, second_plane = swaps(first_own, second_own, "px")
    values = exchanged(mix_modes(modes, x_forward, weights, x_inverse))
    planes = (second_plane, second_own, first_own, first_plane)
    first_row, second_row = swaps(*edge_rows(planes), "py")
    rows = channels * cells_x
    interior = convolve(interior_kernel, "convolve_interior", planes + (taps,), rows * cells_y)
    edges = convolve(
        edge_kernel, "convolve_edges", planes + (first_row, second_row, taps), rows * 8
    )
    return finish(
        conv_bias,
        values,
        z_inverse,
        y_inverse,
        interior.reshape(channels, cells_x, cells_y, depth),
        edges.reshape(channels, cells_x, 8, depth),
    )


def solution(mesh):
    in_specs = (P(None, "px", "py", None), P(), P(), P(None, "py", "px", None, None, None))
    out_specs = P(None, "px", "py", None)
    return jax.shard_map(body, mesh=mesh, in_specs=in_specs, out_specs=out_specs, check_vma=False)
```

```python
import functools
import math

import jax
import jax.numpy as jnp
import ml_dtypes
import numpy as np
from jax import lax
from jax.experimental import pallas as pl
from jax.experimental.pallas import tpu as pltpu
from jax.sharding import PartitionSpec as P

KX = 16
KY = 16
KZ = 16


def extended(cells, sides, width):
    for axis, dim in sides:
        count = lax.axis_size(axis)
        ends = count - 1
        head = lax.slice_in_dim(cells, 0, width, axis=dim)
        tail = lax.slice_in_dim(cells, cells.shape[dim] - width, cells.shape[dim], axis=dim)
        cells = jnp.concatenate(
            [
                lax.ppermute(tail, axis, [(i, (i + 1) % count) for i in range(ends)]),
                cells,
                lax.ppermute(head, axis, [((i + 1) % count, i) for i in range(ends)]),
            ],
            axis=dim,
        )
    return cells


def swapped(value, axis, distance):
    mask = 2**distance
    pairs = [(source, source ^ mask) for source in range(lax.axis_size(axis))]
    return lax.ppermute(value, axis, pairs)


def mode_numbers(count):
    indices = jnp.arange(count, dtype=jnp.int32)
    return jnp.where(indices < count // 2, indices, indices - count)


def trig_pair(numbers, points, length, factor, out_type):
    positions = jnp.arange(points, dtype=jnp.int32)
    phases = positions[:, None] * numbers[None, :] % length
    angles = phases.astype(jnp.float32) * (2.0 * math.pi / length)
    return (
        (jnp.cos(angles) * factor).astype(out_type),
        (jnp.sin(angles) * factor).astype(out_type),
    )


def last_product(source, table, precision=None):
    flat = source.reshape(-1, source.shape[-1])
    result = jnp.dot(flat, table, preferred_element_type=jnp.float32, precision=precision)
    return result.reshape(source.shape[:-1] + (table.shape[1],))


def forward_last(source, cosine, sine_table, precision=None):
    real_part = source[..., 0, :]
    imag_part = source[..., 1, :]
    real_out = last_product(real_part, cosine, precision) + last_product(
        imag_part, sine_table, precision
    )
    imag_out = last_product(imag_part, cosine, precision) - last_product(
        real_part, sine_table, precision
    )
    return jnp.stack([real_out, imag_out], axis=-2)


def inverse_last(source, cosine, sine_table, precision=None):
    real_part = source[..., 0, :]
    imag_part = source[..., 1, :]
    real_out = last_product(real_part, cosine, precision) - last_product(
        imag_part, sine_table, precision
    )
    imag_out = last_product(real_part, sine_table, precision) + last_product(
        imag_part, cosine, precision
    )
    return jnp.stack([real_out, imag_out], axis=-2)


def mix_block(spectral_weight, x_block):
    highest = lax.Precision.HIGHEST
    real_in = x_block[:, :, :, 0, :]
    imag_in = x_block[:, :, :, 1, :]
    partial_real = jnp.einsum(
        "zucok,uzck->uzok", spectral_weight[0], real_in, precision=highest
    ) - jnp.einsum("zucok,uzck->uzok", spectral_weight[1], imag_in, precision=highest)
    partial_imag = jnp.einsum(
        "zucok,uzck->uzok", spectral_weight[0], imag_in, precision=highest
    ) + jnp.einsum("zucok,uzck->uzok", spectral_weight[1], real_in, precision=highest)
    return jnp.stack([partial_real, partial_imag], axis=3)


def general_body(state_field, conv_weight, conv_bias, spectral_weight):
    channels, cells_x, cells_y, depth = state_field.shape
    count_x = lax.axis_size("px")
    count_y = lax.axis_size("py")
    width_x = cells_x * count_x
    width_y = cells_y * count_y
    index_x = lax.axis_index("px")
    kz_local = KZ // count_y
    units = 2 * KY // count_x
    highest = lax.Precision.HIGHEST
    padded = extended(state_field, (("px", 1), ("py", 2)), 1)
    convolved = lax.conv_general_dilated(
        padded[None],
        conv_weight,
        (1, 1, 1),
        ((0, 0), (0, 0), (1, 1)),
        dimension_numbers=("NCDHW", "OIDHW", "NCDHW"),
        preferred_element_type=jnp.float32,
    )[0]
    z_cos, z_sin = trig_pair(
        jnp.arange(KZ, dtype=jnp.int32), depth, depth, depth ** (-0.5), jnp.bfloat16
    )
    z_table = jnp.stack([z_cos, -z_sin], axis=1)
    z_modes = jnp.einsum(
        "cxyn,nwk->kcxwy", state_field, z_table, preferred_element_type=jnp.float32
    ).astype(jnp.bfloat16)
    y_cos, y_sin = trig_pair(mode_numbers(KY), width_y, width_y, width_y ** (-0.5), jnp.bfloat16)
    full_rows = lax.all_to_all(z_modes, "py", split_axis=0, concat_axis=4, tiled=True)
    y_modes = forward_last(full_rows, y_cos, y_sin)
    y_modes = y_modes.astype(jnp.bfloat16)
    by_unit = y_modes.reshape(kz_local, 2, channels // 2, cells_x, 2, KY).transpose(
        1, 5, 0, 2, 4, 3
    )
    by_unit = by_unit.reshape(2 * KY, kz_local, channels // 2, 2, cells_x)
    x_rows = lax.all_to_all(by_unit, "px", split_axis=0, concat_axis=4, tiled=True)
    x_cos, x_sin = trig_pair(mode_numbers(KX), width_x, width_x, width_x ** (-0.5), jnp.bfloat16)
    x_modes = forward_last(x_rows, x_cos, x_sin)
    partial_modes = mix_block(spectral_weight, x_modes)
    partial_modes = partial_modes.reshape(units, kz_local, 2, channels // 2, 2, KX)
    half_index = index_x * units // KY
    own_half = lax.dynamic_index_in_dim(partial_modes, half_index, 2, keepdims=False)
    other_half = lax.dynamic_index_in_dim(partial_modes, 1 - half_index, 2, keepdims=False)
    mixed_modes = own_half + swapped(other_half, "px", count_x.bit_length() - 2)
    ix_cos, ix_sin = trig_pair(mode_numbers(KX), width_x, width_x, KX ** (-0.5), jnp.float32)
    x_values = inverse_last(mixed_modes, ix_cos.T, ix_sin.T, highest).astype(jnp.bfloat16)
    returned = lax.all_to_all(x_values, "px", split_axis=4, concat_axis=0, tiled=True)
    returned = returned.reshape(2, KY, kz_local, channels // 2, 2, cells_x).transpose(
        2, 0, 3, 5, 4, 1
    )
    returned = returned.reshape(kz_local, channels, cells_x, 2, KY)
    iy_cos, iy_sin = trig_pair(mode_numbers(KY), width_y, width_y, KY ** (-0.5), jnp.bfloat16)
    expanded = inverse_last(returned, iy_cos.T, iy_sin.T).astype(jnp.bfloat16)
    y_values = lax.all_to_all(expanded, "py", split_axis=4, concat_axis=0, tiled=True)
    iz_cos, iz_sin = trig_pair(
        jnp.arange(KZ, dtype=jnp.int32), depth, depth, KZ ** (-0.5), jnp.bfloat16
    )
    iz_table = jnp.stack([iz_cos.T, -iz_sin.T], axis=0)
    spectral = jnp.einsum("kcxwy,wkn->cxyn", y_values, iz_table, preferred_element_type=jnp.float32)
    total = convolved + spectral + conv_bias[:, None, None, None]
    return jax.nn.gelu(total, approximate=False).astype(jnp.bfloat16)


def angle_tables(numbers, points, length, factor):
    phases = (np.arange(points)[:, None] * numbers[None, :]) % length
    angles = phases.astype(np.float32) * np.float32(2.0 * math.pi / length)
    return (
        np.cos(angles).astype(np.float32) * np.float32(factor),
        np.sin(angles).astype(np.float32) * np.float32(factor),
    )


def signed_modes(count):
    indices = np.arange(count)
    return np.where(indices < count // 2, indices, indices - count)


def narrow(table):
    return table.astype(ml_dtypes.bfloat16).astype(np.float32)


def forward_pair(cosine, sine):
    return np.stack([np.stack([cosine, -sine]), np.stack([sine, cosine])])


def inverse_pair(cosine, sine):
    return np.stack([np.stack([cosine, sine]), np.stack([-sine, cosine])])


@functools.cache
def tables(count_x, count_y, cells_x, cells_y, depth):
    width_x, width_y = count_x * cells_x, count_y * cells_y
    kzl, units = KZ // count_y, 2 * KY // count_x
    groups = KY // units
    zc, zs = angle_tables(np.arange(KZ), depth, depth, depth**-0.5)
    z_forward = np.concatenate([zc.T, -zs.T])
    yc, ys = angle_tables(signed_modes(KY), width_y, width_y, width_y**-0.5)
    pair = forward_pair(yc, ys).reshape(2, 2, count_y, cells_y, groups, units)
    y_forward = np.einsum("rsqygk,d,w->qrygwskd", pair, np.ones(8), np.ones(cells_x))
    y_forward = y_forward.reshape(count_y, 2 * cells_y, groups * 2 * cells_x * units * 8)
    xc, xs = angle_tables(signed_modes(KX), width_x, width_x, width_x**-0.5)
    pair = forward_pair(xc, xs).reshape(2, 2, count_x, cells_x, KX)
    x_forward = np.einsum("rspxk,gh,q->gskpqhxr", pair, np.eye(2), np.ones(count_y))
    x_forward = x_forward.reshape(4 * KX, count_x * count_y * 4 * cells_x)
    xc, xs = angle_tables(signed_modes(KX), width_x, width_x, KX**-0.5)
    pair = inverse_pair(xc, xs).reshape(2, 2, count_x, cells_x, KX)
    x_inverse = np.einsum("rspxk,zv->pxzsvrk", pair, np.eye(kzl))
    x_inverse = x_inverse.reshape(count_x * cells_x * kzl * 2, kzl * 2 * KX)
    zc, zs = angle_tables(np.arange(KZ), depth, depth, KZ**-0.5)
    pair = inverse_pair(zc, zs).reshape(2, 2, depth, count_y, kzl)
    z_inverse = np.einsum("rsnqz,xw,h->hqxzrwsn", pair, np.eye(cells_x), np.ones(2))
    z_inverse = z_inverse.reshape(4 * cells_x * KZ, cells_x * 2 * depth)
    yc, ys = angle_tables(signed_modes(KY), width_y, width_y, KY**-0.5)
    pair = np.stack([yc, -ys]).reshape(2, count_y, cells_y, KY)
    y_inverse = np.einsum("rqyk,i->qyrki", pair, np.ones(16))
    y_inverse = y_inverse.reshape(count_y, cells_y, 32 * KY)
    return (
        narrow(z_forward),
        narrow(y_forward),
        narrow(x_forward),
        np.concatenate(
            [narrow(x_inverse), narrow(x_inverse - narrow(x_inverse))], axis=1
        ),
        narrow(z_inverse),
        narrow(y_inverse),
    )


def block_moves(value):
    rows = value.shape[0]
    tiles = value.reshape(rows // 8, 8, 128)
    row = lax.broadcasted_iota(jnp.int32, tiles.shape, 1) % 4
    block = lax.broadcasted_iota(jnp.int32, tiles.shape, 2) // 32
    result = tiles
    for lane_step in (1, 2, 3):
        moved = pltpu.roll(tiles, 128 - 32 * lane_step, 2)
        result = jnp.where(row - block == lane_step, pltpu.roll(moved, lane_step, 1), result)
        result = jnp.where(
            row - block == lane_step - 4, pltpu.roll(moved, 8 + lane_step - 4, 1), result
        )
    return result


def forward_kernel(
    state_hbm,
    z_hbm,
    y_hbm,
    weight_hbm,
    conv_hbm,
    out_hbm,
    first_ref,
    second_ref,
    taps_ref,
    packed_ref,
    out_ref,
    state_ref,
    z_ref,
    y_ref,
    table_ref,
    weight_ref,
    conv_ref,
    wide,
    sems,
):
    count = state_ref.shape[0] // 4
    span = state_ref.shape[2]
    y_copy = pltpu.make_async_copy(y_hbm.at[lax.axis_index("py")], y_ref, sems.at[0])
    z_copy = pltpu.make_async_copy(z_hbm, z_ref, sems.at[1])
    copies = [
        pltpu.make_async_copy(
            state_hbm.at[pl.ds(g * count, count)],
            state_ref.at[pl.ds(g * count, count)],
            sems.at[2 + g],
        )
        for g in range(4)
    ]
    conv_copy = pltpu.make_async_copy(conv_hbm, conv_ref, sems.at[6])
    weight_copies = [
        pltpu.make_async_copy(
            weight_hbm.at[part, kz], weight_ref.at[part, kz], sems.at[7 + part * 4 + kz]
        )
        for part in range(2)
        for kz in range(4)
    ]
    for copy in [y_copy, z_copy] + copies:
        copy.start()
    y_copy.wait()
    table = y_ref[...]
    lane = lax.broadcasted_iota(jnp.int32, (span, table.shape[1]), 1)
    for x in range(2):
        for c in range(8):
            own = (lane % 8 == c) & (lane // 64 % 2 == x)
            for part in range(2):
                first = part * 16 * span + (c * 2 + x) * span
                block = jnp.where(own, table[part * span : (part + 1) * span], 0.0)
                table_ref[first : first + span] = block.astype(jnp.bfloat16)
    z_copy.wait()
    z_table = z_ref[...].astype(jnp.bfloat16)
    pieces = []
    for g in range(4):
        copies[g].wait()
        if g == 3:
            for copy in [conv_copy] + weight_copies:
                copy.start()
        cells = state_ref[g * count : (g + 1) * count].reshape(2 * count * span, 128)
        z_modes = lax.dot_general(
            z_table, cells, (((1,), (1,)), ((), ())), preferred_element_type=jnp.float32
        ).astype(jnp.bfloat16)
        pieces.append(jnp.concatenate([z_modes[:KZ], z_modes[KZ:]], axis=1))
    stacked = jnp.concatenate(pieces, axis=0)
    modes = jnp.dot(stacked, table_ref[...], preferred_element_type=jnp.float32)
    for group in range(4):
        moved = block_moves(modes[:, group * 128 : (group + 1) * 128])
        for half in range(2):
            for pair in range(2):
                first = moved[half * 4 + pair]
                second = moved[half * 4 + 2 + pair]
                for side in range(2):
                    rows4 = slice(4 * side, 4 * side + 4)
                    chunk = jnp.concatenate([first[rows4], second[rows4]], axis=0)
                    out_ref[(half * 4 + group) * 4 + 2 * pair + side] = chunk.astype(jnp.bfloat16)
    out_copy = pltpu.make_async_copy(out_ref, out_hbm, sems.at[15])
    out_copy.start()
    odd_x = lax.rem(lax.axis_index("px"), 2)
    for slot, (plane_ref, x) in enumerate(((first_ref, odd_x), (second_ref, 1 - odd_x))):
        wide[slot] = state_ref[:, x].astype(jnp.float32).reshape(32 * span, 128)
        for y in range(span):
            plane_ref[y] = wide[slot, pl.ds(y, 32, stride=span), :].astype(jnp.bfloat16)
    conv_copy.wait()
    zero = jnp.zeros((32, 32), jnp.float32)
    for dz in range(3):
        for dy in range(3):
            taps = [conv_ref[dx, dy, dz].astype(jnp.float32) for dx in range(3)]
            for x_at in range(2):
                blocks = [zero] * x_at + taps + [zero] * (1 - x_at)
                blocks = [jnp.where(odd_x == 1, blocks[i], blocks[3 - i]) for i in range(4)]
                taps_ref[dz, 32 * x_at : 32 * x_at + 32, 128 * dy : 128 * dy + 128] = (
                    jnp.concatenate(blocks, axis=1).astype(jnp.bfloat16)
                )
    for part in range(2):
        for kz in range(4):
            weight_copies[part * 4 + kz].wait()
            for c in range(16):
                packed_ref[part, kz, c] = jnp.concatenate(
                    [weight_ref[part, kz, u, c].astype(jnp.bfloat16) for u in range(4)], axis=1
                )
    out_copy.wait()


def forward_modes(state, z_table, y_table, spectral_weight, conv_weight):
    vmem, hbm = (pl.BlockSpec(memory_space=space) for space in (pltpu.VMEM, pltpu.HBM))
    sent = (32, 8, 128)
    plane = jax.ShapeDtypeStruct((state.shape[2], 32, 128), jnp.bfloat16)
    return pl.pallas_call(
        forward_kernel,
        out_shape=(
            jax.ShapeDtypeStruct(sent, jnp.bfloat16),
            plane,
            plane,
            jax.ShapeDtypeStruct((3, 64, 384), jnp.bfloat16),
            jax.ShapeDtypeStruct((2, 4, 16, KX, 128), jnp.bfloat16),
        ),
        in_specs=[hbm] * 5,
        out_specs=(hbm, vmem, vmem, vmem, vmem),
        scratch_shapes=[
            pltpu.VMEM(sent, jnp.bfloat16),
            pltpu.VMEM(state.shape, jnp.bfloat16),
            pltpu.VMEM(z_table.shape, jnp.float32),
            pltpu.VMEM(y_table.shape[1:], jnp.float32),
            pltpu.VMEM((32 * state.shape[2], y_table.shape[2]), jnp.bfloat16),
            pltpu.VMEM(spectral_weight.shape, jnp.float32),
            pltpu.VMEM(conv_weight.shape, jnp.bfloat16),
            pltpu.VMEM((2, 32 * state.shape[2], 128), jnp.float32),
            pltpu.SemaphoreType.DMA((16,)),
        ],
        compiler_params=pltpu.CompilerParams(vmem_limit_bytes=16 * 2**20),
        cost_estimate=pl.CostEstimate(flops=2**27, bytes_accessed=2**21, transcendentals=0),
        name="forward_modes",
    )(
        *(
            pltpu.with_memory_space_constraint(v, pltpu.HBM)
            for v in (state, z_table, y_table, spectral_weight, conv_weight)
        )
    )


def mix_kernel(modes_ref, forward_ref, weight_ref, inverse_ref, out_ref):
    received = modes_ref[...].astype(jnp.float32).reshape(256, 128).astype(jnp.bfloat16)
    x_modes = jnp.dot(
        forward_ref[...].astype(jnp.bfloat16), received, preferred_element_type=jnp.float32)
    lane = lax.broadcasted_iota(jnp.int32, (16, 128), 1)
    base = (lane // 32) * 8
    mixed = []
    for kz in range(4):
        real_sum = imag_sum = None
        for c in range(16):
            half, c8 = c // 8, c % 8
            index = base + (kz * 32 + c8)
            real_in = jnp.take_along_axis(x_modes[half * 32 : half * 32 + 16], index, axis=1)
            imag_in = jnp.take_along_axis(x_modes[half * 32 + 16 : half * 32 + 32], index, axis=1)
            real_weight = weight_ref[0, kz, c].astype(jnp.float32)
            imag_weight = weight_ref[1, kz, c].astype(jnp.float32)
            real_term = real_weight * real_in - imag_weight * imag_in
            imag_term = real_weight * imag_in + imag_weight * real_in
            real_sum = real_term if real_sum is None else real_sum + real_term
            imag_sum = imag_term if imag_sum is None else imag_sum + imag_term
        mixed += [real_sum, imag_sum]
    mixed = jnp.concatenate(mixed, axis=0)
    inverse = inverse_ref[...].astype(jnp.bfloat16)
    high = mixed.astype(jnp.bfloat16)
    low = (mixed - high.astype(jnp.float32)).astype(jnp.bfloat16)
    values = jnp.dot(
        jnp.concatenate([inverse[:, :128], inverse], axis=1),
        jnp.concatenate([high, low, high], axis=0),
        preferred_element_type=jnp.float32,
    ).astype(jnp.bfloat16)
    for x in range(8):
        for y in range(4):
            out_ref[x * 4 + y] = values[16 * x : 16 * x + 16]


def mix_modes(modes, forward_table, weights, inverse_table):
    vmem = pl.BlockSpec(memory_space=pltpu.VMEM)
    return pl.pallas_call(
        mix_kernel,
        out_shape=jax.ShapeDtypeStruct((32, 16, 128), jnp.bfloat16),
        in_specs=[vmem] * 4,
        out_specs=vmem,
        compiler_params=pltpu.CompilerParams(vmem_limit_bytes=16 * 2**20),
        cost_estimate=pl.CostEstimate(flops=2**35, bytes_accessed=2**21, transcendentals=0),
        name="mix_modes",
    )(modes, forward_table, weights, inverse_table)


def cell_row(planes, y):
    return jnp.concatenate([plane[y] for plane in planes], axis=0)


def edge_rows_kernel(*refs):
    *planes, first_ref, second_ref = refs
    end = planes[0].shape[0] - 1
    odd_y = lax.rem(lax.axis_index("py"), 2)
    first_ref[...] = cell_row(planes, odd_y * end)
    second_ref[...] = cell_row(planes, (1 - odd_y) * end)


def edge_rows(planes):
    vmem = pl.BlockSpec(memory_space=pltpu.VMEM)
    row = jax.ShapeDtypeStruct((128, 128), jnp.bfloat16)
    return pl.pallas_call(
        edge_rows_kernel,
        out_shape=(row, row),
        in_specs=[vmem] * 4,
        out_specs=(vmem, vmem),
        compiler_params=pltpu.CompilerParams(vmem_limit_bytes=16 * 2**20),
        cost_estimate=pl.CostEstimate(flops=2**10, bytes_accessed=2**17, transcendentals=0),
        name="edge_rows",
    )(*planes)


def window_matrix(taps_ref):
    gap = jnp.zeros((64, 128), jnp.bfloat16)
    rows = []
    for dz in range(3):
        rows.append(jnp.concatenate([taps_ref[dz], gap], axis=1))
        rows.append(jnp.concatenate([gap, taps_ref[dz]], axis=1))
    return jnp.concatenate(rows, axis=0)


def convolve_quad(quad, row, weight, place, out_ref):
    lane = lax.broadcasted_iota(jnp.int32, (128, 256), 1) % 128
    windows = []
    for pair in range(2):
        start = quad * 4 + pair * 2 - 1
        windows.append(jnp.concatenate([row(start + i) for i in range(4)], axis=0))
    product = jnp.dot(weight, jnp.concatenate(windows, axis=1), preferred_element_type=jnp.float32)
    below = pltpu.roll(product[:128], 1, 1)
    above = pltpu.roll(product[256:], 255, 1)
    total = product[128:256] + jnp.where(lane == 0, 0.0, below)
    total = total + jnp.where(lane == 127, 0.0, above)
    for pair in range(2):
        for y_out in range(2):
            for x_out in range(2):
                first = (y_out * 2 + x_out) * 32
                value = total[first : first + 32, pair * 128 : (pair + 1) * 128]
                y = quad * 4 + pair * 2 + y_out
                at, span = place(y)
                out_ref[pl.ds(x_out * span + at, 32, stride=2 * span), :] = value


def interior_kernel(*refs):
    *planes, weight_ref, out_ref = refs
    cells_y = planes[0].shape[0]
    weight = window_matrix(weight_ref)
    for quad in range(1, cells_y // 4 - 1):
        convolve_quad(
            quad, lambda y: cell_row(planes, y), weight, lambda y: (y, cells_y), out_ref
        )


def edge_kernel(*refs):
    *planes, first_row, second_row, weight_ref, out_ref = refs
    cells_y = planes[0].shape[0]
    odd_y = lax.rem(lax.axis_index("py"), 2) == 1

    def row(y):
        if y < 0:
            return jnp.where(odd_y, second_row[...], first_row[...])
        if y >= cells_y:
            return jnp.where(odd_y, first_row[...], second_row[...])
        return cell_row(planes, y)

    weight = window_matrix(weight_ref)
    for quad in (0, cells_y // 4 - 1):
        convolve_quad(quad, row, weight, lambda y: (y % 8, 8), out_ref)


def convolve(kernel, name, operands, rows):
    vmem = pl.BlockSpec(memory_space=pltpu.VMEM)
    return pl.pallas_call(
        kernel,
        out_shape=jax.ShapeDtypeStruct((rows, 128), jnp.float32),
        in_specs=[vmem] * len(operands),
        out_specs=vmem,
        compiler_params=pltpu.CompilerParams(vmem_limit_bytes=16 * 2**20),
        cost_estimate=pl.CostEstimate(flops=2**30, bytes_accessed=2**21, transcendentals=0),
        name=name,
    )(*operands)


def gelu(value):
    return 0.5 * value * (1.0 + lax.erf(value * math.sqrt(0.5)))


def finish_kernel(
    bias_ref, values_ref, z_ref, y_ref, conv_ref, edge_ref, out_hbm, out_ref, sems
):
    upper = lax.broadcasted_iota(jnp.int32, (8, 128), 0) < 4
    table = y_ref[lax.axis_index("py")]
    lane = lax.broadcasted_iota(jnp.int32, table.shape, 1) % 16
    expanded = [jnp.where(lane == o, table, 0.0).astype(jnp.bfloat16) for o in range(16)]
    columns = []
    for group in range(4):
        columns.append(
            jnp.concatenate(
                [values_ref[(h * 4 + group) * 4 + q] for h in range(2) for q in range(4)], axis=0
            )
        )
    packed = jnp.concatenate(columns, axis=1)
    z_values = lax.dot_general(
        packed,
        z_ref[...].astype(jnp.bfloat16),
        (((0,), (0,)), ((), ())),
        preferred_element_type=jnp.float32,
    ).astype(jnp.bfloat16)
    copies = []
    for half in range(2):
        sides = []
        for x in range(2):
            parts = []
            for part in range(2):
                lanes = slice((x * 2 + part) * 128, (x * 2 + part + 1) * 128)
                parts += [
                    z_values[ky * 32 + half * 16 : ky * 32 + half * 16 + 16, lanes]
                    for ky in range(KY)
                ]
            sides.append(jnp.concatenate(parts, axis=0))
        right = jnp.concatenate(sides, axis=1)
        for block in range(4):
            spectral = jnp.dot(
                jnp.concatenate(expanded[block * 4 : block * 4 + 4], axis=0),
                right,
                preferred_element_type=jnp.float32,
            )
            for o4 in range(4):
                o = half * 16 + block * 4 + o4
                for x in range(2):
                    inner, edge = conv_ref[o, x], edge_ref[o, x]
                    convolved = jnp.concatenate(
                        [
                            jnp.where(upper, edge, inner[:8]),
                            inner[8:-8],
                            jnp.where(upper, inner[-8:], edge),
                        ],
                        axis=0,
                    )
                    total = spectral[o4 * 32 : o4 * 32 + 32, x * 128 : (x + 1) * 128]
                    total = total + convolved + bias_ref[o]
                    out_ref[o, x] = gelu(total).astype(jnp.bfloat16)
            number = half * 4 + block
            copy = pltpu.make_async_copy(
                out_ref.at[pl.ds(number * 4, 4)], out_hbm.at[pl.ds(number * 4, 4)], sems.at[number]
            )
            copy.start()
            copies.append(copy)
    for copy in copies:
        copy.wait()


def finish(bias, values, z_table, y_table, convolved, edges):
    vmem = pl.BlockSpec(memory_space=pltpu.VMEM)
    return pl.pallas_call(
        finish_kernel,
        out_shape=jax.ShapeDtypeStruct(convolved.shape, jnp.bfloat16),
        in_specs=[pl.BlockSpec(memory_space=pltpu.SMEM)] + [vmem] * 5,
        out_specs=pl.BlockSpec(memory_space=pltpu.HBM),
        scratch_shapes=[
            pltpu.VMEM(convolved.shape, jnp.bfloat16),
            pltpu.SemaphoreType.DMA((8,)),
        ],
        compiler_params=pltpu.CompilerParams(vmem_limit_bytes=16 * 2**20),
        cost_estimate=pl.CostEstimate(flops=2**28, bytes_accessed=2**22, transcendentals=2**18),
        name="finish_layer",
    )(bias, values, z_table, y_table, convolved, edges)


def exchanged(value):
    return lax.all_to_all(value, ("px", "py"), split_axis=0, concat_axis=0, tiled=True)


def swaps(first, second, axis):
    count = lax.axis_size(axis)
    inside = [(i, i ^ 1) for i in range(count)]
    across = [(i, i + 1 if i % 2 else i - 1) for i in range(1, count - 1)]
    second = lax.ppermute(second, axis, inside)
    return lax.ppermute(first, axis, across), second


def body(state_field, conv_weight, conv_bias, spectral_weight):
    channels, cells_x, cells_y, depth = state_field.shape
    sizes = (lax.axis_size("px"), lax.axis_size("py"), cells_x, cells_y, depth)
    if sizes != (8, 4, 2, 32, 128):
        return general_body(state_field, conv_weight, conv_bias, spectral_weight)
    z_forward, y_forward, x_forward, x_inverse, z_inverse, y_inverse = tables(*sizes)
    sent, first_own, second_own, taps, weights = forward_modes(
        state_field,
        z_forward,
        y_forward,
        spectral_weight.swapaxes(4, 5),
        conv_weight.transpose(2, 3, 4, 0, 1),
    )
    modes = exchanged(sent)
    first_plane, second_plane = swaps(first_own, second_own, "px")
    values = exchanged(mix_modes(modes, x_forward, weights, x_inverse))
    planes = (second_plane, second_own, first_own, first_plane)
    first_row, second_row = swaps(*edge_rows(planes), "py")
    rows = channels * cells_x
    interior = convolve(interior_kernel, "convolve_interior", planes + (taps,), rows * cells_y)
    edges = convolve(
        edge_kernel, "convolve_edges", planes + (first_row, second_row, taps), rows * 8
    )
    return finish(
        conv_bias,
        values,
        z_inverse,
        y_inverse,
        interior.reshape(channels, cells_x, cells_y, depth),
        edges.reshape(channels, cells_x, 8, depth),
    )


def solution(mesh):
    in_specs = (P(None, "px", "py", None), P(), P(), P(None, "py", "px", None, None, None))
    out_specs = P(None, "px", "py", None)
    return jax.shard_map(body, mesh=mesh, in_specs=in_specs, out_specs=out_specs, check_vma=False)
```

```python
import functools
import math

import jax
import jax.numpy as jnp
import ml_dtypes
import numpy as np
from jax import lax
from jax.experimental import pallas as pl
from jax.experimental.pallas import tpu as pltpu
from jax.sharding import PartitionSpec as P

KX = 16
KY = 16
KZ = 16


def extended(cells, sides, width):
    for axis, dim in sides:
        count = lax.axis_size(axis)
        ends = count - 1
        head = lax.slice_in_dim(cells, 0, width, axis=dim)
        tail = lax.slice_in_dim(cells, cells.shape[dim] - width, cells.shape[dim], axis=dim)
        cells = jnp.concatenate(
            [
                lax.ppermute(tail, axis, [(i, (i + 1) % count) for i in range(ends)]),
                cells,
                lax.ppermute(head, axis, [((i + 1) % count, i) for i in range(ends)]),
            ],
            axis=dim,
        )
    return cells


def swapped(value, axis, distance):
    mask = 2**distance
    pairs = [(source, source ^ mask) for source in range(lax.axis_size(axis))]
    return lax.ppermute(value, axis, pairs)


def mode_numbers(count):
    indices = jnp.arange(count, dtype=jnp.int32)
    return jnp.where(indices < count // 2, indices, indices - count)


def trig_pair(numbers, points, length, factor, out_type):
    positions = jnp.arange(points, dtype=jnp.int32)
    phases = positions[:, None] * numbers[None, :] % length
    angles = phases.astype(jnp.float32) * (2.0 * math.pi / length)
    return (
        (jnp.cos(angles) * factor).astype(out_type),
        (jnp.sin(angles) * factor).astype(out_type),
    )


def last_product(source, table, precision=None):
    flat = source.reshape(-1, source.shape[-1])
    result = jnp.dot(flat, table, preferred_element_type=jnp.float32, precision=precision)
    return result.reshape(source.shape[:-1] + (table.shape[1],))


def forward_last(source, cosine, sine_table, precision=None):
    real_part = source[..., 0, :]
    imag_part = source[..., 1, :]
    real_out = last_product(real_part, cosine, precision) + last_product(
        imag_part, sine_table, precision
    )
    imag_out = last_product(imag_part, cosine, precision) - last_product(
        real_part, sine_table, precision
    )
    return jnp.stack([real_out, imag_out], axis=-2)


def inverse_last(source, cosine, sine_table, precision=None):
    real_part = source[..., 0, :]
    imag_part = source[..., 1, :]
    real_out = last_product(real_part, cosine, precision) - last_product(
        imag_part, sine_table, precision
    )
    imag_out = last_product(real_part, sine_table, precision) + last_product(
        imag_part, cosine, precision
    )
    return jnp.stack([real_out, imag_out], axis=-2)


def mix_block(spectral_weight, x_block):
    highest = lax.Precision.HIGHEST
    real_in = x_block[:, :, :, 0, :]
    imag_in = x_block[:, :, :, 1, :]
    partial_real = jnp.einsum(
        "zucok,uzck->uzok", spectral_weight[0], real_in, precision=highest
    ) - jnp.einsum("zucok,uzck->uzok", spectral_weight[1], imag_in, precision=highest)
    partial_imag = jnp.einsum(
        "zucok,uzck->uzok", spectral_weight[0], imag_in, precision=highest
    ) + jnp.einsum("zucok,uzck->uzok", spectral_weight[1], real_in, precision=highest)
    return jnp.stack([partial_real, partial_imag], axis=3)


def general_body(state_field, conv_weight, conv_bias, spectral_weight):
    channels, cells_x, cells_y, depth = state_field.shape
    count_x = lax.axis_size("px")
    count_y = lax.axis_size("py")
    width_x = cells_x * count_x
    width_y = cells_y * count_y
    index_x = lax.axis_index("px")
    kz_local = KZ // count_y
    units = 2 * KY // count_x
    highest = lax.Precision.HIGHEST
    padded = extended(state_field, (("px", 1), ("py", 2)), 1)
    convolved = lax.conv_general_dilated(
        padded[None],
        conv_weight,
        (1, 1, 1),
        ((0, 0), (0, 0), (1, 1)),
        dimension_numbers=("NCDHW", "OIDHW", "NCDHW"),
        preferred_element_type=jnp.float32,
    )[0]
    z_cos, z_sin = trig_pair(
        jnp.arange(KZ, dtype=jnp.int32), depth, depth, depth ** (-0.5), jnp.bfloat16
    )
    z_table = jnp.stack([z_cos, -z_sin], axis=1)
    z_modes = jnp.einsum(
        "cxyn,nwk->kcxwy", state_field, z_table, preferred_element_type=jnp.float32
    ).astype(jnp.bfloat16)
    y_cos, y_sin = trig_pair(mode_numbers(KY), width_y, width_y, width_y ** (-0.5), jnp.bfloat16)
    full_rows = lax.all_to_all(z_modes, "py", split_axis=0, concat_axis=4, tiled=True)
    y_modes = forward_last(full_rows, y_cos, y_sin)
    y_modes = y_modes.astype(jnp.bfloat16)
    by_unit = y_modes.reshape(kz_local, 2, channels // 2, cells_x, 2, KY).transpose(
        1, 5, 0, 2, 4, 3
    )
    by_unit = by_unit.reshape(2 * KY, kz_local, channels // 2, 2, cells_x)
    x_rows = lax.all_to_all(by_unit, "px", split_axis=0, concat_axis=4, tiled=True)
    x_cos, x_sin = trig_pair(mode_numbers(KX), width_x, width_x, width_x ** (-0.5), jnp.bfloat16)
    x_modes = forward_last(x_rows, x_cos, x_sin)
    partial_modes = mix_block(spectral_weight, x_modes)
    partial_modes = partial_modes.reshape(units, kz_local, 2, channels // 2, 2, KX)
    half_index = index_x * units // KY
    own_half = lax.dynamic_index_in_dim(partial_modes, half_index, 2, keepdims=False)
    other_half = lax.dynamic_index_in_dim(partial_modes, 1 - half_index, 2, keepdims=False)
    mixed_modes = own_half + swapped(other_half, "px", count_x.bit_length() - 2)
    ix_cos, ix_sin = trig_pair(mode_numbers(KX), width_x, width_x, KX ** (-0.5), jnp.float32)
    x_values = inverse_last(mixed_modes, ix_cos.T, ix_sin.T, highest).astype(jnp.bfloat16)
    returned = lax.all_to_all(x_values, "px", split_axis=4, concat_axis=0, tiled=True)
    returned = returned.reshape(2, KY, kz_local, channels // 2, 2, cells_x).transpose(
        2, 0, 3, 5, 4, 1
    )
    returned = returned.reshape(kz_local, channels, cells_x, 2, KY)
    iy_cos, iy_sin = trig_pair(mode_numbers(KY), width_y, width_y, KY ** (-0.5), jnp.bfloat16)
    expanded = inverse_last(returned, iy_cos.T, iy_sin.T).astype(jnp.bfloat16)
    y_values = lax.all_to_all(expanded, "py", split_axis=4, concat_axis=0, tiled=True)
    iz_cos, iz_sin = trig_pair(
        jnp.arange(KZ, dtype=jnp.int32), depth, depth, KZ ** (-0.5), jnp.bfloat16
    )
    iz_table = jnp.stack([iz_cos.T, -iz_sin.T], axis=0)
    spectral = jnp.einsum("kcxwy,wkn->cxyn", y_values, iz_table, preferred_element_type=jnp.float32)
    total = convolved + spectral + conv_bias[:, None, None, None]
    return jax.nn.gelu(total, approximate=False).astype(jnp.bfloat16)


def angle_tables(numbers, points, length, factor):
    phases = (np.arange(points)[:, None] * numbers[None, :]) % length
    angles = phases.astype(np.float32) * np.float32(2.0 * math.pi / length)
    return (
        np.cos(angles).astype(np.float32) * np.float32(factor),
        np.sin(angles).astype(np.float32) * np.float32(factor),
    )


def signed_modes(count):
    indices = np.arange(count)
    return np.where(indices < count // 2, indices, indices - count)


def narrow(table):
    return table.astype(ml_dtypes.bfloat16).astype(np.float32)


def forward_pair(cosine, sine):
    return np.stack([np.stack([cosine, -sine]), np.stack([sine, cosine])])


def inverse_pair(cosine, sine):
    return np.stack([np.stack([cosine, sine]), np.stack([-sine, cosine])])


@functools.cache
def tables(count_x, count_y, cells_x, cells_y, depth):
    width_x, width_y = count_x * cells_x, count_y * cells_y
    kzl, units = KZ // count_y, 2 * KY // count_x
    groups = KY // units
    zc, zs = angle_tables(np.arange(KZ), depth, depth, depth**-0.5)
    z_forward = np.concatenate([zc.T, -zs.T])
    yc, ys = angle_tables(signed_modes(KY), width_y, width_y, width_y**-0.5)
    pair = forward_pair(yc, ys).reshape(2, 2, count_y, cells_y, groups, units)
    y_forward = np.einsum("rsqygk,d,w->qrygwskd", pair, np.ones(8), np.ones(cells_x))
    y_forward = y_forward.reshape(count_y, 2 * cells_y, groups * 2 * cells_x * units * 8)
    xc, xs = angle_tables(signed_modes(KX), width_x, width_x, width_x**-0.5)
    pair = forward_pair(xc, xs).reshape(2, 2, count_x, cells_x, KX)
    x_forward = np.einsum("rspxk,gh,q->gskpqhxr", pair, np.eye(2), np.ones(count_y))
    x_forward = x_forward.reshape(4 * KX, count_x * count_y * 4 * cells_x)
    xc, xs = angle_tables(signed_modes(KX), width_x, width_x, KX**-0.5)
    pair = inverse_pair(xc, xs).reshape(2, 2, count_x, cells_x, KX)
    x_inverse = np.einsum("rspxk,zv->pxzsvrk", pair, np.eye(kzl))
    x_inverse = x_inverse.reshape(count_x * cells_x * kzl * 2, kzl * 2 * KX)
    zc, zs = angle_tables(np.arange(KZ), depth, depth, KZ**-0.5)
    pair = inverse_pair(zc, zs).reshape(2, 2, depth, count_y, kzl)
    z_inverse = np.einsum("rsnqz,xw,h->hqxzrwsn", pair, np.eye(cells_x), np.ones(2))
    z_inverse = z_inverse.reshape(4 * cells_x * KZ, cells_x * 2 * depth)
    yc, ys = angle_tables(signed_modes(KY), width_y, width_y, KY**-0.5)
    pair = np.stack([yc, -ys]).reshape(2, count_y, cells_y, KY)
    y_inverse = np.einsum("rqyk,i->qyrki", pair, np.ones(16))
    y_inverse = y_inverse.reshape(count_y, cells_y, 32 * KY)
    return (
        narrow(z_forward),
        narrow(y_forward),
        narrow(x_forward),
        np.concatenate(
            [narrow(x_inverse), narrow(x_inverse - narrow(x_inverse))], axis=1
        ),
        narrow(z_inverse),
        narrow(y_inverse),
    )


def block_moves(value):
    rows = value.shape[0]
    tiles = value.reshape(rows // 8, 8, 128)
    row = lax.broadcasted_iota(jnp.int32, tiles.shape, 1) % 4
    block = lax.broadcasted_iota(jnp.int32, tiles.shape, 2) // 32
    result = tiles
    for lane_step in (1, 2, 3):
        moved = pltpu.roll(tiles, 128 - 32 * lane_step, 2)
        result = jnp.where(row - block == lane_step, pltpu.roll(moved, lane_step, 1), result)
        result = jnp.where(
            row - block == lane_step - 4, pltpu.roll(moved, 8 + lane_step - 4, 1), result
        )
    return result


def forward_kernel(
    state_hbm,
    z_hbm,
    y_hbm,
    weight_hbm,
    conv_hbm,
    out_hbm,
    state_ref,
    packed_ref,
    conv_ref,
    out_ref,
    z_ref,
    y_ref,
    table_ref,
    weight_ref,
    sems,
):
    count = state_ref.shape[0] // 4
    span = state_ref.shape[1]
    y_copy = pltpu.make_async_copy(y_hbm.at[lax.axis_index("py")], y_ref, sems.at[0])
    z_copy = pltpu.make_async_copy(z_hbm, z_ref, sems.at[1])
    copies = [
        pltpu.make_async_copy(
            state_hbm.at[pl.ds(g * count, count)],
            state_ref.at[pl.ds(g * count, count)],
            sems.at[2 + g],
        )
        for g in range(4)
    ]
    conv_copy = pltpu.make_async_copy(conv_hbm, conv_ref, sems.at[6])
    weight_copies = [
        pltpu.make_async_copy(
            weight_hbm.at[part, kz], weight_ref.at[part, kz], sems.at[7 + part * 4 + kz]
        )
        for part in range(2)
        for kz in range(4)
    ]
    for copy in [y_copy, z_copy] + copies + weight_copies + [conv_copy]:
        copy.start()
    y_copy.wait()
    table = y_ref[...]
    lane = lax.broadcasted_iota(jnp.int32, (span, table.shape[1]), 1)
    for x in range(2):
        for c in range(8):
            own = (lane % 8 == c) & (lane // 64 % 2 == x)
            for part in range(2):
                first = part * 16 * span + (c * 2 + x) * span
                block = jnp.where(own, table[part * span : (part + 1) * span], 0.0)
                table_ref[first : first + span] = block.astype(jnp.bfloat16)
    z_copy.wait()
    z_table = z_ref[...].astype(jnp.bfloat16)
    pieces = []
    for g in range(4):
        copies[g].wait()
        cells = state_ref[g * count : (g + 1) * count].reshape(count * span, state_ref.shape[2])
        z_modes = lax.dot_general(
            z_table, cells, (((1,), (1,)), ((), ())), preferred_element_type=jnp.float32
        ).astype(jnp.bfloat16)
        pieces.append(jnp.concatenate([z_modes[:KZ], z_modes[KZ:]], axis=1))
    stacked = jnp.concatenate(pieces, axis=0)
    modes = jnp.dot(stacked, table_ref[...], preferred_element_type=jnp.float32)
    for group in range(4):
        moved = block_moves(modes[:, group * 128 : (group + 1) * 128])
        for half in range(2):
            for pair in range(2):
                first = moved[half * 4 + pair]
                second = moved[half * 4 + 2 + pair]
                for side in range(2):
                    rows4 = slice(4 * side, 4 * side + 4)
                    chunk = jnp.concatenate([first[rows4], second[rows4]], axis=0)
                    out_ref[(half * 4 + group) * 4 + 2 * pair + side] = chunk.astype(jnp.bfloat16)
    out_copy = pltpu.make_async_copy(out_ref, out_hbm, sems.at[15])
    out_copy.start()
    for part in range(2):
        for kz in range(4):
            weight_copies[part * 4 + kz].wait()
            for c in range(16):
                packed_ref[part, kz, c] = jnp.concatenate(
                    [weight_ref[part, kz, u, c].astype(jnp.bfloat16) for u in range(4)], axis=1
                )
    conv_copy.wait()
    out_copy.wait()


def forward_modes(state, z_table, y_table, spectral_weight, conv_weight):
    vmem, hbm = (pl.BlockSpec(memory_space=space) for space in (pltpu.VMEM, pltpu.HBM))
    sent = (32, 8, 128)
    return pl.pallas_call(
        forward_kernel,
        out_shape=(
            jax.ShapeDtypeStruct(sent, jnp.bfloat16),
            jax.ShapeDtypeStruct(state.shape, jnp.bfloat16),
            jax.ShapeDtypeStruct((2, 4, 16, KX, 128), jnp.bfloat16),
            jax.ShapeDtypeStruct(conv_weight.shape, jnp.bfloat16),
        ),
        in_specs=[hbm] * 5,
        out_specs=(hbm, vmem, vmem, vmem),
        scratch_shapes=[
            pltpu.VMEM(sent, jnp.bfloat16),
            pltpu.VMEM(z_table.shape, jnp.float32),
            pltpu.VMEM(y_table.shape[1:], jnp.float32),
            pltpu.VMEM((32 * state.shape[1], y_table.shape[2]), jnp.bfloat16),
            pltpu.VMEM(spectral_weight.shape, jnp.float32),
            pltpu.SemaphoreType.DMA((16,)),
        ],
        compiler_params=pltpu.CompilerParams(vmem_limit_bytes=16 * 2**20),
        cost_estimate=pl.CostEstimate(flops=2**27, bytes_accessed=2**21, transcendentals=0),
        name="forward_modes",
    )(
        *(
            pltpu.with_memory_space_constraint(v, pltpu.HBM)
            for v in (state, z_table, y_table, spectral_weight, conv_weight)
        )
    )


def arrange_kernel(state_ref, conv_ref, first_ref, second_ref, conv_out, wide):
    odd_x = lax.rem(lax.axis_index("px"), 2)
    cells_y = state_ref.shape[2]
    for slot, (out_ref, x) in enumerate(((first_ref, odd_x), (second_ref, 1 - odd_x))):
        wide[slot] = state_ref[:, x].astype(jnp.float32).reshape(32 * cells_y, 128)
        for y in range(cells_y):
            out_ref[y] = wide[slot, pl.ds(y, 32, stride=cells_y), :].astype(jnp.bfloat16)
    zero = jnp.zeros((32, 32), jnp.float32)
    for dz in range(3):
        for dy in range(3):
            taps = [conv_ref[dx, dy, dz].astype(jnp.float32) for dx in range(3)]
            for x_at in range(2):
                blocks = [zero] * x_at + taps + [zero] * (1 - x_at)
                blocks = [jnp.where(odd_x == 1, blocks[i], blocks[3 - i]) for i in range(4)]
                conv_out[dz, 32 * x_at : 32 * x_at + 32, 128 * dy : 128 * dy + 128] = (
                    jnp.concatenate(blocks, axis=1).astype(jnp.bfloat16)
                )


def arrange(state, conv_weight):
    vmem = pl.BlockSpec(memory_space=pltpu.VMEM)
    cells_y = state.shape[2]
    plane = jax.ShapeDtypeStruct((cells_y, 32, 128), jnp.bfloat16)
    return pl.pallas_call(
        arrange_kernel,
        out_shape=(plane, plane, jax.ShapeDtypeStruct((3, 64, 384), jnp.bfloat16)),
        in_specs=[vmem] * 2,
        out_specs=(vmem,) * 3,
        scratch_shapes=[pltpu.VMEM((2, 32 * cells_y, 128), jnp.float32)],
        compiler_params=pltpu.CompilerParams(vmem_limit_bytes=16 * 2**20),
        cost_estimate=pl.CostEstimate(flops=2**10, bytes_accessed=2**10, transcendentals=0),
        name="arrange_cells",
    )(state, conv_weight)


def mix_kernel(modes_ref, forward_ref, weight_ref, inverse_ref, out_ref):
    received = modes_ref[...].astype(jnp.float32).reshape(256, 128).astype(jnp.bfloat16)
    x_modes = jnp.dot(
        forward_ref[...].astype(jnp.bfloat16), received, preferred_element_type=jnp.float32)
    lane = lax.broadcasted_iota(jnp.int32, (16, 128), 1)
    base = (lane // 32) * 8
    mixed = []
    for kz in range(4):
        real_sum = imag_sum = None
        for c in range(16):
            half, c8 = c // 8, c % 8
            index = base + (kz * 32 + c8)
            real_in = jnp.take_along_axis(x_modes[half * 32 : half * 32 + 16], index, axis=1)
            imag_in = jnp.take_along_axis(x_modes[half * 32 + 16 : half * 32 + 32], index, axis=1)
            real_weight = weight_ref[0, kz, c].astype(jnp.float32)
            imag_weight = weight_ref[1, kz, c].astype(jnp.float32)
            real_term = real_weight * real_in - imag_weight * imag_in
            imag_term = real_weight * imag_in + imag_weight * real_in
            real_sum = real_term if real_sum is None else real_sum + real_term
            imag_sum = imag_term if imag_sum is None else imag_sum + imag_term
        mixed += [real_sum, imag_sum]
    mixed = jnp.concatenate(mixed, axis=0)
    inverse = inverse_ref[...].astype(jnp.bfloat16)
    high = mixed.astype(jnp.bfloat16)
    low = (mixed - high.astype(jnp.float32)).astype(jnp.bfloat16)
    values = jnp.dot(
        jnp.concatenate([inverse[:, :128], inverse], axis=1),
        jnp.concatenate([high, low, high], axis=0),
        preferred_element_type=jnp.float32,
    ).astype(jnp.bfloat16)
    for x in range(8):
        for y in range(4):
            out_ref[x * 4 + y] = values[16 * x : 16 * x + 16]


def mix_modes(modes, forward_table, weights, inverse_table):
    vmem = pl.BlockSpec(memory_space=pltpu.VMEM)
    return pl.pallas_call(
        mix_kernel,
        out_shape=jax.ShapeDtypeStruct((32, 16, 128), jnp.bfloat16),
        in_specs=[vmem] * 4,
        out_specs=vmem,
        compiler_params=pltpu.CompilerParams(vmem_limit_bytes=16 * 2**20),
        cost_estimate=pl.CostEstimate(flops=2**35, bytes_accessed=2**21, transcendentals=0),
        name="mix_modes",
    )(modes, forward_table, weights, inverse_table)


def cell_row(planes, y):
    return jnp.concatenate([plane[y] for plane in planes], axis=0)


def edge_rows_kernel(*refs):
    *planes, first_ref, second_ref = refs
    end = planes[0].shape[0] - 1
    odd_y = lax.rem(lax.axis_index("py"), 2)
    first_ref[...] = cell_row(planes, odd_y * end)
    second_ref[...] = cell_row(planes, (1 - odd_y) * end)


def edge_rows(planes):
    vmem = pl.BlockSpec(memory_space=pltpu.VMEM)
    row = jax.ShapeDtypeStruct((128, 128), jnp.bfloat16)
    return pl.pallas_call(
        edge_rows_kernel,
        out_shape=(row, row),
        in_specs=[vmem] * 4,
        out_specs=(vmem, vmem),
        compiler_params=pltpu.CompilerParams(vmem_limit_bytes=16 * 2**20),
        cost_estimate=pl.CostEstimate(flops=2**10, bytes_accessed=2**17, transcendentals=0),
        name="edge_rows",
    )(*planes)


def window_matrix(taps_ref):
    gap = jnp.zeros((64, 128), jnp.bfloat16)
    rows = []
    for dz in range(3):
        rows.append(jnp.concatenate([taps_ref[dz], gap], axis=1))
        rows.append(jnp.concatenate([gap, taps_ref[dz]], axis=1))
    return jnp.concatenate(rows, axis=0)


def convolve_quad(quad, row, weight, place, out_ref):
    lane = lax.broadcasted_iota(jnp.int32, (128, 256), 1) % 128
    windows = []
    for pair in range(2):
        start = quad * 4 + pair * 2 - 1
        windows.append(jnp.concatenate([row(start + i) for i in range(4)], axis=0))
    product = jnp.dot(weight, jnp.concatenate(windows, axis=1), preferred_element_type=jnp.float32)
    below = pltpu.roll(product[:128], 1, 1)
    above = pltpu.roll(product[256:], 255, 1)
    total = product[128:256] + jnp.where(lane == 0, 0.0, below)
    total = total + jnp.where(lane == 127, 0.0, above)
    for pair in range(2):
        for y_out in range(2):
            for x_out in range(2):
                first = (y_out * 2 + x_out) * 32
                value = total[first : first + 32, pair * 128 : (pair + 1) * 128]
                y = quad * 4 + pair * 2 + y_out
                at, span = place(y)
                out_ref[pl.ds(x_out * span + at, 32, stride=2 * span), :] = value


def interior_kernel(*refs):
    *planes, weight_ref, out_ref = refs
    cells_y = planes[0].shape[0]
    weight = window_matrix(weight_ref)
    for quad in range(1, cells_y // 4 - 1):
        convolve_quad(
            quad, lambda y: cell_row(planes, y), weight, lambda y: (y, cells_y), out_ref
        )


def edge_kernel(*refs):
    *planes, first_row, second_row, weight_ref, out_ref = refs
    cells_y = planes[0].shape[0]
    odd_y = lax.rem(lax.axis_index("py"), 2) == 1

    def row(y):
        if y < 0:
            return jnp.where(odd_y, second_row[...], first_row[...])
        if y >= cells_y:
            return jnp.where(odd_y, first_row[...], second_row[...])
        return cell_row(planes, y)

    weight = window_matrix(weight_ref)
    for quad in (0, cells_y // 4 - 1):
        convolve_quad(quad, row, weight, lambda y: (y % 8, 8), out_ref)


def convolve(kernel, name, operands, rows):
    vmem = pl.BlockSpec(memory_space=pltpu.VMEM)
    return pl.pallas_call(
        kernel,
        out_shape=jax.ShapeDtypeStruct((rows, 128), jnp.float32),
        in_specs=[vmem] * len(operands),
        out_specs=vmem,
        compiler_params=pltpu.CompilerParams(vmem_limit_bytes=16 * 2**20),
        cost_estimate=pl.CostEstimate(flops=2**30, bytes_accessed=2**21, transcendentals=0),
        name=name,
    )(*operands)


def gelu(value):
    return 0.5 * value * (1.0 + lax.erf(value * math.sqrt(0.5)))


def finish_kernel(
    bias_ref, values_ref, z_ref, y_ref, conv_ref, edge_ref, out_hbm, out_ref, sems
):
    upper = lax.broadcasted_iota(jnp.int32, (8, 128), 0) < 4
    table = y_ref[lax.axis_index("py")]
    lane = lax.broadcasted_iota(jnp.int32, table.shape, 1) % 16
    expanded = [jnp.where(lane == o, table, 0.0).astype(jnp.bfloat16) for o in range(16)]
    columns = []
    for group in range(4):
        columns.append(
            jnp.concatenate(
                [values_ref[(h * 4 + group) * 4 + q] for h in range(2) for q in range(4)], axis=0
            )
        )
    packed = jnp.concatenate(columns, axis=1)
    z_values = lax.dot_general(
        packed,
        z_ref[...].astype(jnp.bfloat16),
        (((0,), (0,)), ((), ())),
        preferred_element_type=jnp.float32,
    ).astype(jnp.bfloat16)
    copies = []
    for half in range(2):
        sides = []
        for x in range(2):
            parts = []
            for part in range(2):
                lanes = slice((x * 2 + part) * 128, (x * 2 + part + 1) * 128)
                parts += [
                    z_values[ky * 32 + half * 16 : ky * 32 + half * 16 + 16, lanes]
                    for ky in range(KY)
                ]
            sides.append(jnp.concatenate(parts, axis=0))
        right = jnp.concatenate(sides, axis=1)
        for block in range(4):
            spectral = jnp.dot(
                jnp.concatenate(expanded[block * 4 : block * 4 + 4], axis=0),
                right,
                preferred_element_type=jnp.float32,
            )
            for o4 in range(4):
                o = half * 16 + block * 4 + o4
                for x in range(2):
                    inner, edge = conv_ref[o, x], edge_ref[o, x]
                    convolved = jnp.concatenate(
                        [
                            jnp.where(upper, edge, inner[:8]),
                            inner[8:-8],
                            jnp.where(upper, inner[-8:], edge),
                        ],
                        axis=0,
                    )
                    total = spectral[o4 * 32 : o4 * 32 + 32, x * 128 : (x + 1) * 128]
                    total = total + convolved + bias_ref[o]
                    out_ref[o, x] = gelu(total).astype(jnp.bfloat16)
            number = half * 4 + block
            copy = pltpu.make_async_copy(
                out_ref.at[pl.ds(number * 4, 4)], out_hbm.at[pl.ds(number * 4, 4)], sems.at[number]
            )
            copy.start()
            copies.append(copy)
    for copy in copies:
        copy.wait()


def finish(bias, values, z_table, y_table, convolved, edges):
    vmem = pl.BlockSpec(memory_space=pltpu.VMEM)
    return pl.pallas_call(
        finish_kernel,
        out_shape=jax.ShapeDtypeStruct(convolved.shape, jnp.bfloat16),
        in_specs=[pl.BlockSpec(memory_space=pltpu.SMEM)] + [vmem] * 5,
        out_specs=pl.BlockSpec(memory_space=pltpu.HBM),
        scratch_shapes=[
            pltpu.VMEM(convolved.shape, jnp.bfloat16),
            pltpu.SemaphoreType.DMA((8,)),
        ],
        compiler_params=pltpu.CompilerParams(vmem_limit_bytes=16 * 2**20),
        cost_estimate=pl.CostEstimate(flops=2**28, bytes_accessed=2**22, transcendentals=2**18),
        name="finish_layer",
    )(bias, values, z_table, y_table, convolved, edges)


def exchanged(value):
    return lax.all_to_all(value, ("px", "py"), split_axis=0, concat_axis=0, tiled=True)


def swaps(first, second, axis):
    count = lax.axis_size(axis)
    inside = [(i, i ^ 1) for i in range(count)]
    across = [(i, i + 1 if i % 2 else i - 1) for i in range(1, count - 1)]
    second = lax.ppermute(second, axis, inside)
    return lax.ppermute(first, axis, across), second


def body(state_field, conv_weight, conv_bias, spectral_weight):
    channels, cells_x, cells_y, depth = state_field.shape
    sizes = (lax.axis_size("px"), lax.axis_size("py"), cells_x, cells_y, depth)
    if sizes != (8, 4, 2, 32, 128):
        return general_body(state_field, conv_weight, conv_bias, spectral_weight)
    z_forward, y_forward, x_forward, x_inverse, z_inverse, y_inverse = tables(*sizes)
    sent, held, weights, conv_held = forward_modes(
        state_field.reshape(channels * cells_x, cells_y, depth),
        z_forward,
        y_forward,
        spectral_weight.swapaxes(4, 5),
        conv_weight.transpose(2, 3, 4, 0, 1),
    )
    modes = exchanged(sent)
    first_own, second_own, taps = arrange(held.reshape(state_field.shape), conv_held)
    first_plane, second_plane = swaps(first_own, second_own, "px")
    values = exchanged(mix_modes(modes, x_forward, weights, x_inverse))
    planes = (second_plane, second_own, first_own, first_plane)
    first_row, second_row = swaps(*edge_rows(planes), "py")
    rows = channels * cells_x
    interior = convolve(interior_kernel, "convolve_interior", planes + (taps,), rows * cells_y)
    edges = convolve(
        edge_kernel, "convolve_edges", planes + (first_row, second_row, taps), rows * 8
    )
    return finish(
        conv_bias,
        values,
        z_inverse,
        y_inverse,
        interior.reshape(channels, cells_x, cells_y, depth),
        edges.reshape(channels, cells_x, 8, depth),
    )


def solution(mesh):
    in_specs = (P(None, "px", "py", None), P(), P(), P(None, "py", "px", None, None, None))
    out_specs = P(None, "px", "py", None)
    return jax.shard_map(body, mesh=mesh, in_specs=in_specs, out_specs=out_specs, check_vma=False)
```

```python
import functools
import math

import jax
import jax.numpy as jnp
import ml_dtypes
import numpy as np
from jax import lax
from jax.experimental import pallas as pl
from jax.experimental.pallas import tpu as pltpu
from jax.sharding import PartitionSpec as P

KX = 16
KY = 16
KZ = 16


def extended(cells, sides, width):
    for axis, dim in sides:
        count = lax.axis_size(axis)
        ends = count - 1
        head = lax.slice_in_dim(cells, 0, width, axis=dim)
        tail = lax.slice_in_dim(cells, cells.shape[dim] - width, cells.shape[dim], axis=dim)
        cells = jnp.concatenate(
            [
                lax.ppermute(tail, axis, [(i, (i + 1) % count) for i in range(ends)]),
                cells,
                lax.ppermute(head, axis, [((i + 1) % count, i) for i in range(ends)]),
            ],
            axis=dim,
        )
    return cells


def swapped(value, axis, distance):
    mask = 2**distance
    pairs = [(source, source ^ mask) for source in range(lax.axis_size(axis))]
    return lax.ppermute(value, axis, pairs)


def mode_numbers(count):
    indices = jnp.arange(count, dtype=jnp.int32)
    return jnp.where(indices < count // 2, indices, indices - count)


def trig_pair(numbers, points, length, factor, out_type):
    positions = jnp.arange(points, dtype=jnp.int32)
    phases = positions[:, None] * numbers[None, :] % length
    angles = phases.astype(jnp.float32) * (2.0 * math.pi / length)
    return (
        (jnp.cos(angles) * factor).astype(out_type),
        (jnp.sin(angles) * factor).astype(out_type),
    )


def last_product(source, table, precision=None):
    flat = source.reshape(-1, source.shape[-1])
    result = jnp.dot(flat, table, preferred_element_type=jnp.float32, precision=precision)
    return result.reshape(source.shape[:-1] + (table.shape[1],))


def forward_last(source, cosine, sine_table, precision=None):
    real_part = source[..., 0, :]
    imag_part = source[..., 1, :]
    real_out = last_product(real_part, cosine, precision) + last_product(
        imag_part, sine_table, precision
    )
    imag_out = last_product(imag_part, cosine, precision) - last_product(
        real_part, sine_table, precision
    )
    return jnp.stack([real_out, imag_out], axis=-2)


def inverse_last(source, cosine, sine_table, precision=None):
    real_part = source[..., 0, :]
    imag_part = source[..., 1, :]
    real_out = last_product(real_part, cosine, precision) - last_product(
        imag_part, sine_table, precision
    )
    imag_out = last_product(real_part, sine_table, precision) + last_product(
        imag_part, cosine, precision
    )
    return jnp.stack([real_out, imag_out], axis=-2)


def mix_block(spectral_weight, x_block):
    highest = lax.Precision.HIGHEST
    real_in = x_block[:, :, :, 0, :]
    imag_in = x_block[:, :, :, 1, :]
    partial_real = jnp.einsum(
        "zucok,uzck->uzok", spectral_weight[0], real_in, precision=highest
    ) - jnp.einsum("zucok,uzck->uzok", spectral_weight[1], imag_in, precision=highest)
    partial_imag = jnp.einsum(
        "zucok,uzck->uzok", spectral_weight[0], imag_in, precision=highest
    ) + jnp.einsum("zucok,uzck->uzok", spectral_weight[1], real_in, precision=highest)
    return jnp.stack([partial_real, partial_imag], axis=3)


def general_body(state_field, conv_weight, conv_bias, spectral_weight):
    channels, cells_x, cells_y, depth = state_field.shape
    count_x = lax.axis_size("px")
    count_y = lax.axis_size("py")
    width_x = cells_x * count_x
    width_y = cells_y * count_y
    index_x = lax.axis_index("px")
    kz_local = KZ // count_y
    units = 2 * KY // count_x
    highest = lax.Precision.HIGHEST
    padded = extended(state_field, (("px", 1), ("py", 2)), 1)
    convolved = lax.conv_general_dilated(
        padded[None],
        conv_weight,
        (1, 1, 1),
        ((0, 0), (0, 0), (1, 1)),
        dimension_numbers=("NCDHW", "OIDHW", "NCDHW"),
        preferred_element_type=jnp.float32,
    )[0]
    z_cos, z_sin = trig_pair(
        jnp.arange(KZ, dtype=jnp.int32), depth, depth, depth ** (-0.5), jnp.bfloat16
    )
    z_table = jnp.stack([z_cos, -z_sin], axis=1)
    z_modes = jnp.einsum(
        "cxyn,nwk->kcxwy", state_field, z_table, preferred_element_type=jnp.float32
    ).astype(jnp.bfloat16)
    y_cos, y_sin = trig_pair(mode_numbers(KY), width_y, width_y, width_y ** (-0.5), jnp.bfloat16)
    full_rows = lax.all_to_all(z_modes, "py", split_axis=0, concat_axis=4, tiled=True)
    y_modes = forward_last(full_rows, y_cos, y_sin)
    y_modes = y_modes.astype(jnp.bfloat16)
    by_unit = y_modes.reshape(kz_local, 2, channels // 2, cells_x, 2, KY).transpose(
        1, 5, 0, 2, 4, 3
    )
    by_unit = by_unit.reshape(2 * KY, kz_local, channels // 2, 2, cells_x)
    x_rows = lax.all_to_all(by_unit, "px", split_axis=0, concat_axis=4, tiled=True)
    x_cos, x_sin = trig_pair(mode_numbers(KX), width_x, width_x, width_x ** (-0.5), jnp.bfloat16)
    x_modes = forward_last(x_rows, x_cos, x_sin)
    partial_modes = mix_block(spectral_weight, x_modes)
    partial_modes = partial_modes.reshape(units, kz_local, 2, channels // 2, 2, KX)
    half_index = index_x * units // KY
    own_half = lax.dynamic_index_in_dim(partial_modes, half_index, 2, keepdims=False)
    other_half = lax.dynamic_index_in_dim(partial_modes, 1 - half_index, 2, keepdims=False)
    mixed_modes = own_half + swapped(other_half, "px", count_x.bit_length() - 2)
    ix_cos, ix_sin = trig_pair(mode_numbers(KX), width_x, width_x, KX ** (-0.5), jnp.float32)
    x_values = inverse_last(mixed_modes, ix_cos.T, ix_sin.T, highest).astype(jnp.bfloat16)
    returned = lax.all_to_all(x_values, "px", split_axis=4, concat_axis=0, tiled=True)
    returned = returned.reshape(2, KY, kz_local, channels // 2, 2, cells_x).transpose(
        2, 0, 3, 5, 4, 1
    )
    returned = returned.reshape(kz_local, channels, cells_x, 2, KY)
    iy_cos, iy_sin = trig_pair(mode_numbers(KY), width_y, width_y, KY ** (-0.5), jnp.bfloat16)
    expanded = inverse_last(returned, iy_cos.T, iy_sin.T).astype(jnp.bfloat16)
    y_values = lax.all_to_all(expanded, "py", split_axis=4, concat_axis=0, tiled=True)
    iz_cos, iz_sin = trig_pair(
        jnp.arange(KZ, dtype=jnp.int32), depth, depth, KZ ** (-0.5), jnp.bfloat16
    )
    iz_table = jnp.stack([iz_cos.T, -iz_sin.T], axis=0)
    spectral = jnp.einsum("kcxwy,wkn->cxyn", y_values, iz_table, preferred_element_type=jnp.float32)
    total = convolved + spectral + conv_bias[:, None, None, None]
    return jax.nn.gelu(total, approximate=False).astype(jnp.bfloat16)


def angle_tables(numbers, points, length, factor):
    phases = (np.arange(points)[:, None] * numbers[None, :]) % length
    angles = phases.astype(np.float32) * np.float32(2.0 * math.pi / length)
    return (
        np.cos(angles).astype(np.float32) * np.float32(factor),
        np.sin(angles).astype(np.float32) * np.float32(factor),
    )


def signed_modes(count):
    indices = np.arange(count)
    return np.where(indices < count // 2, indices, indices - count)


def narrow(table):
    return table.astype(ml_dtypes.bfloat16).astype(np.float32)


def forward_pair(cosine, sine):
    return np.stack([np.stack([cosine, -sine]), np.stack([sine, cosine])])


def inverse_pair(cosine, sine):
    return np.stack([np.stack([cosine, sine]), np.stack([-sine, cosine])])


@functools.cache
def tables(count_x, count_y, cells_x, cells_y, depth):
    width_x, width_y = count_x * cells_x, count_y * cells_y
    kzl, units = KZ // count_y, 2 * KY // count_x
    groups = KY // units
    zc, zs = angle_tables(np.arange(KZ), depth, depth, depth**-0.5)
    z_forward = np.concatenate([zc.T, -zs.T])
    yc, ys = angle_tables(signed_modes(KY), width_y, width_y, width_y**-0.5)
    pair = forward_pair(yc, ys).reshape(2, 2, count_y, cells_y, groups, units)
    y_forward = np.einsum("rsqygk,d,w->qrygwskd", pair, np.ones(8), np.ones(cells_x))
    y_forward = y_forward.reshape(count_y, 2 * cells_y, groups * 2 * cells_x * units * 8)
    xc, xs = angle_tables(signed_modes(KX), width_x, width_x, width_x**-0.5)
    pair = forward_pair(xc, xs).reshape(2, 2, count_x, cells_x, KX)
    x_forward = np.einsum("rspxk,gh,q->gskpqhxr", pair, np.eye(2), np.ones(count_y))
    x_forward = x_forward.reshape(4 * KX, count_x * count_y * 4 * cells_x)
    xc, xs = angle_tables(signed_modes(KX), width_x, width_x, KX**-0.5)
    pair = inverse_pair(xc, xs).reshape(2, 2, count_x, cells_x, KX)
    x_inverse = np.einsum("rspxk,zv->pxzsvrk", pair, np.eye(kzl))
    x_inverse = x_inverse.reshape(count_x * cells_x * kzl * 2, kzl * 2 * KX)
    zc, zs = angle_tables(np.arange(KZ), depth, depth, KZ**-0.5)
    pair = inverse_pair(zc, zs).reshape(2, 2, depth, count_y, kzl)
    z_inverse = np.einsum("rsnqz,xw,h->hqxzrwsn", pair, np.eye(cells_x), np.ones(2))
    z_inverse = z_inverse.reshape(4 * cells_x * KZ, cells_x * 2 * depth)
    yc, ys = angle_tables(signed_modes(KY), width_y, width_y, KY**-0.5)
    pair = np.stack([yc, -ys]).reshape(2, count_y, cells_y, KY)
    y_inverse = np.einsum("rqyk,i->qyrki", pair, np.ones(16))
    y_inverse = y_inverse.reshape(count_y, cells_y, 32 * KY)
    return (
        narrow(z_forward),
        narrow(y_forward),
        narrow(x_forward),
        np.concatenate(
            [narrow(x_inverse), narrow(x_inverse - narrow(x_inverse))], axis=1
        ),
        narrow(z_inverse),
        narrow(y_inverse),
    )


def block_moves(value):
    rows = value.shape[0]
    tiles = value.reshape(rows // 8, 8, 128)
    row = lax.broadcasted_iota(jnp.int32, (1, 8, 128), 1) % 4
    block = lax.broadcasted_iota(jnp.int32, (1, 8, 128), 2) // 32
    result = tiles
    for lane_step in (1, 2, 3):
        moved = pltpu.roll(tiles, 128 - 32 * lane_step, 2)
        result = jnp.where(row - block == lane_step, pltpu.roll(moved, lane_step, 1), result)
        result = jnp.where(
            row - block == lane_step - 4, pltpu.roll(moved, 8 + lane_step - 4, 1), result
        )
    return result


def forward_kernel(
    state_hbm,
    z_hbm,
    y_hbm,
    weight_hbm,
    conv_hbm,
    out_hbm,
    state_ref,
    packed_ref,
    conv_ref,
    out_ref,
    z_ref,
    y_ref,
    table_ref,
    weight_ref,
    sems,
):
    count = state_ref.shape[0] // 4
    span = state_ref.shape[1]
    y_copy = pltpu.make_async_copy(y_hbm.at[lax.axis_index("py")], y_ref, sems.at[0])
    z_copy = pltpu.make_async_copy(z_hbm, z_ref, sems.at[1])
    copies = [
        pltpu.make_async_copy(
            state_hbm.at[pl.ds(g * count, count)],
            state_ref.at[pl.ds(g * count, count)],
            sems.at[2 + g],
        )
        for g in range(4)
    ]
    conv_copy = pltpu.make_async_copy(conv_hbm, conv_ref, sems.at[6])
    weight_copies = [
        pltpu.make_async_copy(
            weight_hbm.at[part, kz], weight_ref.at[part, kz], sems.at[7 + part * 4 + kz]
        )
        for part in range(2)
        for kz in range(4)
    ]
    for copy in [y_copy, z_copy] + copies + weight_copies + [conv_copy]:
        copy.start()
    y_copy.wait()
    table = y_ref[...]
    lane = lax.broadcasted_iota(jnp.int32, (1, 8, table.shape[1]), 2)
    halves = table.reshape(2, span // 8, 8, table.shape[1])
    for x in range(2):
        for c in range(8):
            own = (lane % 8 == c) & (lane // 64 % 2 == x)
            for part in range(2):
                first = part * 16 * span + (c * 2 + x) * span
                block = jnp.where(own, halves[part], 0.0).reshape(span, table.shape[1])
                table_ref[first : first + span] = block.astype(jnp.bfloat16)
    z_copy.wait()
    z_table = z_ref[...].astype(jnp.bfloat16)
    pieces = []
    for g in range(4):
        copies[g].wait()
        cells = state_ref[g * count : (g + 1) * count].reshape(count * span, state_ref.shape[2])
        z_modes = lax.dot_general(
            z_table, cells, (((1,), (1,)), ((), ())), preferred_element_type=jnp.float32
        ).astype(jnp.bfloat16)
        pieces.append(jnp.concatenate([z_modes[:KZ], z_modes[KZ:]], axis=1))
    stacked = jnp.concatenate(pieces, axis=0)
    modes = jnp.dot(stacked, table_ref[...], preferred_element_type=jnp.float32)
    for group in range(4):
        moved = block_moves(modes[:, group * 128 : (group + 1) * 128])
        for half in range(2):
            for pair in range(2):
                first = moved[half * 4 + pair]
                second = moved[half * 4 + 2 + pair]
                for side in range(2):
                    rows4 = slice(4 * side, 4 * side + 4)
                    chunk = jnp.concatenate([first[rows4], second[rows4]], axis=0)
                    out_ref[(half * 4 + group) * 4 + 2 * pair + side] = chunk.astype(jnp.bfloat16)
    out_copy = pltpu.make_async_copy(out_ref, out_hbm, sems.at[15])
    out_copy.start()
    for part in range(2):
        for kz in range(4):
            weight_copies[part * 4 + kz].wait()
            for c in range(16):
                packed_ref[part, kz, c] = jnp.concatenate(
                    [weight_ref[part, kz, u, c].astype(jnp.bfloat16) for u in range(4)], axis=1
                )
    conv_copy.wait()
    out_copy.wait()


def forward_modes(state, z_table, y_table, spectral_weight, conv_weight):
    vmem, hbm = (pl.BlockSpec(memory_space=space) for space in (pltpu.VMEM, pltpu.HBM))
    sent = (32, 8, 128)
    return pl.pallas_call(
        forward_kernel,
        out_shape=(
            jax.ShapeDtypeStruct(sent, jnp.bfloat16),
            jax.ShapeDtypeStruct(state.shape, jnp.bfloat16),
            jax.ShapeDtypeStruct((2, 4, 16, KX, 128), jnp.bfloat16),
            jax.ShapeDtypeStruct(conv_weight.shape, jnp.bfloat16),
        ),
        in_specs=[hbm] * 5,
        out_specs=(hbm, vmem, vmem, vmem),
        scratch_shapes=[
            pltpu.VMEM(sent, jnp.bfloat16),
            pltpu.VMEM(z_table.shape, jnp.float32),
            pltpu.VMEM(y_table.shape[1:], jnp.float32),
            pltpu.VMEM((32 * state.shape[1], y_table.shape[2]), jnp.bfloat16),
            pltpu.VMEM(spectral_weight.shape, jnp.float32),
            pltpu.SemaphoreType.DMA((16,)),
        ],
        compiler_params=pltpu.CompilerParams(vmem_limit_bytes=16 * 2**20),
        cost_estimate=pl.CostEstimate(flops=2**27, bytes_accessed=2**21, transcendentals=0),
        name="forward_modes",
    )(
        *(
            pltpu.with_memory_space_constraint(v, pltpu.HBM)
            for v in (state, z_table, y_table, spectral_weight, conv_weight)
        )
    )


def arrange_kernel(state_ref, conv_ref, first_ref, second_ref, conv_out, wide):
    odd_x = lax.rem(lax.axis_index("px"), 2)
    cells_y = state_ref.shape[2]
    for slot, (out_ref, x) in enumerate(((first_ref, odd_x), (second_ref, 1 - odd_x))):
        wide[slot] = state_ref[:, x].astype(jnp.float32).reshape(32 * cells_y, 128)
        for y in range(cells_y):
            out_ref[y] = wide[slot, pl.ds(y, 32, stride=cells_y), :].astype(jnp.bfloat16)
    zero = jnp.zeros((32, 32), jnp.float32)
    for dz in range(3):
        for dy in range(3):
            taps = [conv_ref[dx, dy, dz].astype(jnp.float32) for dx in range(3)]
            for x_at in range(2):
                blocks = [zero] * x_at + taps + [zero] * (1 - x_at)
                blocks = [jnp.where(odd_x == 1, blocks[i], blocks[3 - i]) for i in range(4)]
                conv_out[dz, 32 * x_at : 32 * x_at + 32, 128 * dy : 128 * dy + 128] = (
                    jnp.concatenate(blocks, axis=1).astype(jnp.bfloat16)
                )


def arrange(state, conv_weight):
    vmem = pl.BlockSpec(memory_space=pltpu.VMEM)
    cells_y = state.shape[2]
    plane = jax.ShapeDtypeStruct((cells_y, 32, 128), jnp.bfloat16)
    return pl.pallas_call(
        arrange_kernel,
        out_shape=(plane, plane, jax.ShapeDtypeStruct((3, 64, 384), jnp.bfloat16)),
        in_specs=[vmem] * 2,
        out_specs=(vmem,) * 3,
        scratch_shapes=[pltpu.VMEM((2, 32 * cells_y, 128), jnp.float32)],
        compiler_params=pltpu.CompilerParams(vmem_limit_bytes=16 * 2**20),
        cost_estimate=pl.CostEstimate(flops=2**10, bytes_accessed=2**10, transcendentals=0),
        name="arrange_cells",
    )(state, conv_weight)


def mix_kernel(modes_ref, forward_ref, weight_ref, inverse_ref, out_ref):
    received = modes_ref[...].astype(jnp.float32).reshape(256, 128).astype(jnp.bfloat16)
    x_modes = jnp.dot(
        forward_ref[...].astype(jnp.bfloat16), received, preferred_element_type=jnp.float32)
    lane = lax.broadcasted_iota(jnp.int32, (16, 128), 1)
    base = (lane // 32) * 8
    mixed = []
    for kz in range(4):
        real_sum = imag_sum = None
        for c in range(16):
            half, c8 = c // 8, c % 8
            index = base + (kz * 32 + c8)
            real_in = jnp.take_along_axis(x_modes[half * 32 : half * 32 + 16], index, axis=1)
            imag_in = jnp.take_along_axis(x_modes[half * 32 + 16 : half * 32 + 32], index, axis=1)
            real_weight = weight_ref[0, kz, c].astype(jnp.float32)
            imag_weight = weight_ref[1, kz, c].astype(jnp.float32)
            real_term = real_weight * real_in - imag_weight * imag_in
            imag_term = real_weight * imag_in + imag_weight * real_in
            real_sum = real_term if real_sum is None else real_sum + real_term
            imag_sum = imag_term if imag_sum is None else imag_sum + imag_term
        mixed += [real_sum, imag_sum]
    mixed = jnp.concatenate(mixed, axis=0)
    inverse = inverse_ref[...].astype(jnp.bfloat16)
    high = mixed.astype(jnp.bfloat16)
    low = (mixed - high.astype(jnp.float32)).astype(jnp.bfloat16)
    values = jnp.dot(
        jnp.concatenate([inverse[:, :128], inverse], axis=1),
        jnp.concatenate([high, low, high], axis=0),
        preferred_element_type=jnp.float32,
    ).astype(jnp.bfloat16)
    for x in range(8):
        for y in range(4):
            out_ref[x * 4 + y] = values[16 * x : 16 * x + 16]


def mix_modes(modes, forward_table, weights, inverse_table):
    vmem = pl.BlockSpec(memory_space=pltpu.VMEM)
    return pl.pallas_call(
        mix_kernel,
        out_shape=jax.ShapeDtypeStruct((32, 16, 128), jnp.bfloat16),
        in_specs=[vmem] * 4,
        out_specs=vmem,
        compiler_params=pltpu.CompilerParams(vmem_limit_bytes=16 * 2**20),
        cost_estimate=pl.CostEstimate(flops=2**35, bytes_accessed=2**21, transcendentals=0),
        name="mix_modes",
    )(modes, forward_table, weights, inverse_table)


def cell_row(planes, y):
    return jnp.concatenate([plane[y] for plane in planes], axis=0)


def edge_rows_kernel(*refs):
    *planes, first_ref, second_ref = refs
    end = planes[0].shape[0] - 1
    odd_y = lax.rem(lax.axis_index("py"), 2)
    first_ref[...] = cell_row(planes, odd_y * end)
    second_ref[...] = cell_row(planes, (1 - odd_y) * end)


def edge_rows(planes):
    vmem = pl.BlockSpec(memory_space=pltpu.VMEM)
    row = jax.ShapeDtypeStruct((128, 128), jnp.bfloat16)
    return pl.pallas_call(
        edge_rows_kernel,
        out_shape=(row, row),
        in_specs=[vmem] * 4,
        out_specs=(vmem, vmem),
        compiler_params=pltpu.CompilerParams(vmem_limit_bytes=16 * 2**20),
        cost_estimate=pl.CostEstimate(flops=2**10, bytes_accessed=2**17, transcendentals=0),
        name="edge_rows",
    )(*planes)


def window_matrix(taps_ref):
    gap = jnp.zeros((64, 128), jnp.bfloat16)
    rows = []
    for dz in range(3):
        rows.append(jnp.concatenate([taps_ref[dz], gap], axis=1))
        rows.append(jnp.concatenate([gap, taps_ref[dz]], axis=1))
    return jnp.concatenate(rows, axis=0)


def convolve_quad(quad, row, weight, place, out_ref):
    lane = lax.broadcasted_iota(jnp.int32, (128, 256), 1) % 128
    windows = []
    for pair in range(2):
        start = quad * 4 + pair * 2 - 1
        windows.append(jnp.concatenate([row(start + i) for i in range(4)], axis=0))
    product = jnp.dot(weight, jnp.concatenate(windows, axis=1), preferred_element_type=jnp.float32)
    below = pltpu.roll(product[:128], 1, 1)
    above = pltpu.roll(product[256:], 255, 1)
    total = product[128:256] + jnp.where(lane == 0, 0.0, below)
    total = total + jnp.where(lane == 127, 0.0, above)
    for pair in range(2):
        for y_out in range(2):
            for x_out in range(2):
                first = (y_out * 2 + x_out) * 32
                value = total[first : first + 32, pair * 128 : (pair + 1) * 128]
                y = quad * 4 + pair * 2 + y_out
                at, span = place(y)
                out_ref[pl.ds(x_out * span + at, 32, stride=2 * span), :] = value


def interior_kernel(*refs):
    *planes, weight_ref, out_ref = refs
    cells_y = planes[0].shape[0]
    weight = window_matrix(weight_ref)
    for quad in range(1, cells_y // 4 - 1):
        convolve_quad(
            quad, lambda y: cell_row(planes, y), weight, lambda y: (y, cells_y), out_ref
        )


def edge_kernel(*refs):
    *planes, first_row, second_row, weight_ref, out_ref = refs
    cells_y = planes[0].shape[0]
    odd_y = lax.rem(lax.axis_index("py"), 2) == 1

    def row(y):
        if y < 0:
            return jnp.where(odd_y, second_row[...], first_row[...])
        if y >= cells_y:
            return jnp.where(odd_y, first_row[...], second_row[...])
        return cell_row(planes, y)

    weight = window_matrix(weight_ref)
    for quad in (0, cells_y // 4 - 1):
        convolve_quad(quad, row, weight, lambda y: (y % 8, 8), out_ref)


def convolve(kernel, name, operands, rows):
    vmem = pl.BlockSpec(memory_space=pltpu.VMEM)
    return pl.pallas_call(
        kernel,
        out_shape=jax.ShapeDtypeStruct((rows, 128), jnp.float32),
        in_specs=[vmem] * len(operands),
        out_specs=vmem,
        compiler_params=pltpu.CompilerParams(vmem_limit_bytes=16 * 2**20),
        cost_estimate=pl.CostEstimate(flops=2**30, bytes_accessed=2**21, transcendentals=0),
        name=name,
    )(*operands)


def gelu(value):
    return 0.5 * value * (1.0 + lax.erf(value * math.sqrt(0.5)))


def finish_kernel(
    bias_ref, values_ref, z_ref, y_ref, conv_ref, edge_ref, out_hbm, out_ref, sems
):
    upper = lax.broadcasted_iota(jnp.int32, (8, 128), 0) < 4
    table = y_ref[lax.axis_index("py")]
    lane = lax.broadcasted_iota(jnp.int32, (1, 8, table.shape[1]), 2) % 16
    tiles = table.reshape(-1, 8, table.shape[1])
    expanded = [
        jnp.where(lane == o, tiles, 0.0).reshape(table.shape).astype(jnp.bfloat16)
        for o in range(16)
    ]
    columns = []
    for group in range(4):
        columns.append(
            jnp.concatenate(
                [values_ref[(h * 4 + group) * 4 + q] for h in range(2) for q in range(4)], axis=0
            )
        )
    packed = jnp.concatenate(columns, axis=1)
    z_values = lax.dot_general(
        packed,
        z_ref[...].astype(jnp.bfloat16),
        (((0,), (0,)), ((), ())),
        preferred_element_type=jnp.float32,
    ).astype(jnp.bfloat16)
    copies = []
    for half in range(2):
        sides = []
        for x in range(2):
            parts = []
            for part in range(2):
                lanes = slice((x * 2 + part) * 128, (x * 2 + part + 1) * 128)
                parts += [
                    z_values[ky * 32 + half * 16 : ky * 32 + half * 16 + 16, lanes]
                    for ky in range(KY)
                ]
            sides.append(jnp.concatenate(parts, axis=0))
        right = jnp.concatenate(sides, axis=1)
        for block in range(4):
            spectral = jnp.dot(
                jnp.concatenate(expanded[block * 4 : block * 4 + 4], axis=0),
                right,
                preferred_element_type=jnp.float32,
            )
            for o4 in range(4):
                o = half * 16 + block * 4 + o4
                for x in range(2):
                    inner, edge = conv_ref[o, x], edge_ref[o, x]
                    convolved = jnp.concatenate(
                        [
                            jnp.where(upper, edge, inner[:8]),
                            inner[8:-8],
                            jnp.where(upper, inner[-8:], edge),
                        ],
                        axis=0,
                    )
                    total = spectral[o4 * 32 : o4 * 32 + 32, x * 128 : (x + 1) * 128]
                    total = total + convolved + bias_ref[o]
                    out_ref[o, x] = gelu(total).astype(jnp.bfloat16)
            number = half * 4 + block
            copy = pltpu.make_async_copy(
                out_ref.at[pl.ds(number * 4, 4)], out_hbm.at[pl.ds(number * 4, 4)], sems.at[number]
            )
            copy.start()
            copies.append(copy)
    for copy in copies:
        copy.wait()


def finish(bias, values, z_table, y_table, convolved, edges):
    vmem = pl.BlockSpec(memory_space=pltpu.VMEM)
    return pl.pallas_call(
        finish_kernel,
        out_shape=jax.ShapeDtypeStruct(convolved.shape, jnp.bfloat16),
        in_specs=[pl.BlockSpec(memory_space=pltpu.SMEM)] + [vmem] * 5,
        out_specs=pl.BlockSpec(memory_space=pltpu.HBM),
        scratch_shapes=[
            pltpu.VMEM(convolved.shape, jnp.bfloat16),
            pltpu.SemaphoreType.DMA((8,)),
        ],
        compiler_params=pltpu.CompilerParams(vmem_limit_bytes=16 * 2**20),
        cost_estimate=pl.CostEstimate(flops=2**28, bytes_accessed=2**22, transcendentals=2**18),
        name="finish_layer",
    )(bias, values, z_table, y_table, convolved, edges)


def exchanged(value):
    return lax.all_to_all(value, ("px", "py"), split_axis=0, concat_axis=0, tiled=True)


def swaps(first, second, axis):
    count = lax.axis_size(axis)
    inside = [(i, i ^ 1) for i in range(count)]
    across = [(i, i + 1 if i % 2 else i - 1) for i in range(1, count - 1)]
    second = lax.ppermute(second, axis, inside)
    return lax.ppermute(first, axis, across), second


def body(state_field, conv_weight, conv_bias, spectral_weight):
    channels, cells_x, cells_y, depth = state_field.shape
    sizes = (lax.axis_size("px"), lax.axis_size("py"), cells_x, cells_y, depth)
    if sizes != (8, 4, 2, 32, 128):
        return general_body(state_field, conv_weight, conv_bias, spectral_weight)
    z_forward, y_forward, x_forward, x_inverse, z_inverse, y_inverse = tables(*sizes)
    sent, held, weights, conv_held = forward_modes(
        state_field.reshape(channels * cells_x, cells_y, depth),
        z_forward,
        y_forward,
        spectral_weight.swapaxes(4, 5),
        conv_weight.transpose(2, 3, 4, 0, 1),
    )
    modes = exchanged(sent)
    first_own, second_own, taps = arrange(held.reshape(state_field.shape), conv_held)
    first_plane, second_plane = swaps(first_own, second_own, "px")
    values = exchanged(mix_modes(modes, x_forward, weights, x_inverse))
    planes = (second_plane, second_own, first_own, first_plane)
    first_row, second_row = swaps(*edge_rows(planes), "py")
    rows = channels * cells_x
    interior = convolve(interior_kernel, "convolve_interior", planes + (taps,), rows * cells_y)
    edges = convolve(
        edge_kernel, "convolve_edges", planes + (first_row, second_row, taps), rows * 8
    )
    return finish(
        conv_bias,
        values,
        z_inverse,
        y_inverse,
        interior.reshape(channels, cells_x, cells_y, depth),
        edges.reshape(channels, cells_x, 8, depth),
    )


def solution(mesh):
    in_specs = (P(None, "px", "py", None), P(), P(), P(None, "py", "px", None, None, None))
    out_specs = P(None, "px", "py", None)
    return jax.shard_map(body, mesh=mesh, in_specs=in_specs, out_specs=out_specs, check_vma=False)
```
